32 devices in a mesh: groups: 2 (over x), tp: 8 (over z, y), section: 2 (over core).
Axes of the slice: x: 2, y: 2, z: 4, core: 2. Of those that a mesh axis runs over, the one named last changes fastest.
Arguments:
- hidden: bfloat16 [2, 64, 8192], P(None, 'groups', ('tp', 'section')), parts along dimension 1, may hold values from -16 to 16
- norm_gain: float32 [8192], replicated, may hold values from 0.25 to 1.75
- w_query: bfloat16 [8192, 8192], P(None, ('tp', 'section')), may hold values from -0.0625 to 0.0625
- key_value_weight: bfloat16 [8192, 2048], P(('tp', 'section')), may hold values from -0.09375 to 0.09375
- w_output: bfloat16 [8192, 8192], P(('tp', 'section')), may hold values from -0.0625 to 0.0625
- prompt_cache_pages: bfloat16 [512, 16, 2048], P(('groups', 'tp', 'section')), parts along dimension 0, may hold values from -4 to 4
- per_page_scales: bfloat16 [512, 16], P(('groups', 'tp', 'section')), parts along dimension 0, may hold values from 0.5 to 100
- lengths: int32 [8], P('groups'), parts along dimension 0, may hold values from 1 to 512, as said below
- block_table: int32 [8, 32], P('groups'), parts along dimension 0, may hold values from 0 to 255, as said below
Outputs:
- layer_out: bfloat16 [2, 64, 8192], P(None, 'groups', ('tp', 'section')), parts along dimension 1
The draws below stay inside these ranges and needn't reach their ends.
There are 2 independent parts, one for each index of `groups`. The reference program is written for one: setup_inputs(seed, part) draws one part's arguments, and reference() takes and returns one part's arrays. A program takes and returns all parts, laid end to end along the dimension named above; an argument that names none is the same for every part. Nothing has to cross between parts.
Inputs may be any that keep to these rules, and one draw needn't show every extreme that they name: `lengths`: one request has exactly 512 tokens. `block_table`: entry i of request r lies among the 16 pages of device r * 4 + i % 4 of the group (pages numbered device by device in the order of tp+section); entries on one device use distinct pages.
All inputs are finite; a program needn't handle non-finite values.
Results may differ from the reference program's by a relative error of at most 0.004.
The reference program's roundings to bfloat16 on the way count: a program that leaves them out, or rounds other values in their place, can miss the bound.
Values may be sent and summed in bfloat16 or wider, within the bound.
No kernel may reach another device: no remote copies, remote signals or barrier semaphores. Data moves between devices by JAX's collectives and lax.ppermute only.
A program may use at most 128 MiB of HBM per device.

```python
import math
import jax
import jax.numpy as jnp
from jax import lax

MODEL_WIDTH = 8192
QUERY_HEADS = 64
KEY_VALUE_HEADS = 8
HEAD_SIZE = 128
GROUP_REQUESTS = 4
SAMPLES = 8
PAGE_TOKENS = 16
PROMPT_LIMIT = 512
DECODE_ROWS = 32
NDEV = 16
SUBDEV = 4
REQUEST_PAGES = 32
PG_DEV = 16
GROUP_PAGES = 256


def draw_hidden(key, part):
    key = jax.random.fold_in(key, 11)
    base_random_key = jax.random.fold_in(key, 1)
    key_rows = jax.random.fold_in(key, 2)
    key_cols = jax.random.fold_in(key, 3)
    row_scale = jnp.exp(jax.random.uniform(key_rows, (2, DECODE_ROWS, 1), jnp.float32, math.log(0.2), math.log(2.0)))
    col_scale = jnp.exp(jax.random.uniform(key_cols, (MODEL_WIDTH,), jnp.float32, math.log(0.5), math.log(2.0)))
    start_offset = jax.random.normal(base_random_key, (2, DECODE_ROWS, MODEL_WIDTH), jnp.float32)
    start_offset = jnp.clip(start_offset, -4.0, 4.0)
    return (start_offset * row_scale * col_scale).astype(jnp.bfloat16)


def draw_per_page_scales(key, part):
    key = jax.random.fold_in(key, 13)
    base_random_key = jax.random.fold_in(key, 1)
    start_offset = jnp.exp(jax.random.uniform(base_random_key, (GROUP_PAGES, 2 * KEY_VALUE_HEADS), jnp.float32, math.log(0.5), math.log(4.0)))
    return start_offset.astype(jnp.bfloat16)


def draw_lengths(key, part):
    key = jax.random.fold_in(key, 17)
    key_others = jax.random.fold_in(key, 1)
    key_longest = jax.random.fold_in(key, 2)
    key_short = jax.random.fold_in(key, 3)
    others = jax.random.randint(key_others, (GROUP_REQUESTS,), 1, PROMPT_LIMIT + 1)
    short = jax.random.randint(key_short, (GROUP_REQUESTS,), 1, PAGE_TOKENS + 1)
    longest = jax.random.randint(key_longest, (), 0, GROUP_REQUESTS)
    index = jnp.arange(GROUP_REQUESTS)
    others = jnp.where(index == (longest + 1) % GROUP_REQUESTS, short, others)
    return jnp.where(index == longest, PROMPT_LIMIT, others).astype(jnp.int32)


def draw_block_table(key, part):
    key = jax.random.fold_in(key, 19)
    scores = jax.random.randint(key, (NDEV, PG_DEV), 0, 2 ** 20) * PG_DEV + jnp.arange(PG_DEV)[None, :]
    order = jnp.argsort(scores, axis=1, stable=True)
    logical = jnp.arange(REQUEST_PAGES)
    device = jnp.arange(GROUP_REQUESTS)[:, None] * SUBDEV + logical[None, :] % SUBDEV
    slot = logical // SUBDEV
    local = order[device, slot[None, :]]
    return (device * PG_DEV + local).astype(jnp.int32)


def with_spikes(entries, own_key, source, target, parts, factor):
    owner, partner = [(jnp.arange(entries.shape[dim]) // (entries.shape[dim] // parts)).reshape([-1 if axis == dim else 1 for axis in range(entries.ndim)]) for dim in (source, target)]
    chosen = jax.random.permutation(own_key, parts)[partner]
    strong = (owner == chosen) | (owner == (partner + parts // 2) % parts)
    return jnp.where(strong, factor * entries, entries)


def level_of(key, shape, shards, least, high):
    level = 1.0
    for position, shards_of in shards:
        draws = jax.random.uniform(jax.random.fold_in(jax.random.fold_in(key, 6), position), (shards_of,), jnp.float32, least / len(shards), high / len(shards))
        level = level * jnp.repeat(jnp.exp(draws), shape[position] // shards_of).reshape((-1,) + (1,) * (len(shape) - 1 - position))
    return level


def noise(rng, shape, width, most, shards=(), held_as=jnp.bfloat16):
    values = width * jax.random.normal(rng, shape, jnp.float32)
    if shards:
        values = values * level_of(rng, shape, shards, -0.22, 0.18)
    return jnp.clip(values, -most, most).astype(held_as)


def gaussian_with(stream_key, dims, width, reach, pieces, heavy, held_as=jnp.bfloat16):
    values = width * jax.random.normal(stream_key, dims, jnp.float32)
    if pieces:
        values = values * level_of(stream_key, dims, pieces, -0.22, 0.18)
    return jnp.clip(with_spikes(values, jax.random.fold_in(stream_key, 3), *heavy), -reach, reach).astype(held_as)


def setup_inputs(seed: int = 0, part: int = 0) -> dict:
    keys = jax.random.split(jax.random.key(seed), 10)
    part_keys = jax.random.split(jax.random.fold_in(keys[9], part), 10)
    hidden = draw_hidden(jax.random.fold_in(jax.random.fold_in(keys[9], part), 71), part)
    norm_gain = jnp.clip(1.0 + 0.15 * jax.random.normal(keys[1], (MODEL_WIDTH,), jnp.float32), 0.25, 1.75)
    w_query = noise(keys[2], (MODEL_WIDTH, QUERY_HEADS * HEAD_SIZE), MODEL_WIDTH ** -0.5, 0.0625, ((1, 16),))
    key_value_weight = gaussian_with(keys[3], (MODEL_WIDTH, 2 * KEY_VALUE_HEADS * HEAD_SIZE), MODEL_WIDTH ** -0.5, 0.09375, ((0, 16),), (0, 1, 16, 2.0))
    w_output = noise(keys[4], (QUERY_HEADS * HEAD_SIZE, MODEL_WIDTH), (QUERY_HEADS * HEAD_SIZE) ** -0.5, 0.0625, ((0, 16),))
    prompt_cache_pages = noise(part_keys[5], (GROUP_PAGES, PAGE_TOKENS, 2 * KEY_VALUE_HEADS * HEAD_SIZE), 1.0, 4.0, ((0, 16),))
    per_page_scales = draw_per_page_scales(jax.random.fold_in(jax.random.fold_in(keys[9], part), 71), part)
    lengths = draw_lengths(jax.random.fold_in(jax.random.fold_in(keys[9], part), 71), part)
    block_table = draw_block_table(jax.random.fold_in(jax.random.fold_in(keys[9], part), 71), part)
    return {"hidden": hidden, "norm_gain": norm_gain, "w_query": w_query, "key_value_weight": key_value_weight, "w_output": w_output, "prompt_cache_pages": prompt_cache_pages, "per_page_scales": per_page_scales, "lengths": lengths, "block_table": block_table}


theta_base = 500000.0
eps_norm = 1e-05

def rotate(vectors, positions):
    half = vectors.shape[-1] // 2
    freqs = jnp.exp(-jnp.log(theta_base) * jnp.arange(half, dtype=jnp.float32) * (2.0 / vectors.shape[-1]))
    angles = positions.astype(jnp.float32)[..., None] * freqs
    cosine = jnp.cos(angles)
    sine = jnp.sin(angles)
    first = vectors[..., :half]
    second = vectors[..., half:]
    return jnp.concatenate([first * cosine - second * sine, second * cosine + first * sine], axis=-1)

def normalize(rows, gain):
    wide = rows.astype(jnp.float32)
    scale = lax.rsqrt(lax.optimization_barrier(jnp.mean(wide * wide, axis=-1, keepdims=True)) + eps_norm)
    return (wide * scale * gain.astype(jnp.float32)).astype(jnp.bfloat16)

def widen_precision(array):
    return lax.optimization_barrier(array).astype(jnp.float32)

def reference(hidden, norm_gain, w_query, key_value_weight, w_output, prompt_cache_pages, per_page_scales, lengths, block_table):
    request_group = QUERY_HEADS // KEY_VALUE_HEADS
    flattened_page_table = block_table.reshape(-1).astype(jnp.int32)
    quantized_codes = jnp.take(prompt_cache_pages, flattened_page_table, axis=0).reshape(GROUP_REQUESTS, REQUEST_PAGES, PAGE_TOKENS, KEY_VALUE_HEADS, 2, HEAD_SIZE)
    dequant_scales = jnp.take(per_page_scales, flattened_page_table, axis=0).reshape(GROUP_REQUESTS, REQUEST_PAGES, 1, KEY_VALUE_HEADS, 2, 1)
    cache_pool = (quantized_codes.astype(jnp.float32) * dequant_scales.astype(jnp.float32)).astype(jnp.bfloat16)
    cache_pool = widen_precision(cache_pool).reshape(GROUP_REQUESTS, PROMPT_LIMIT, KEY_VALUE_HEADS, 2, HEAD_SIZE)
    visible = jnp.arange(PROMPT_LIMIT)[None, :] < lengths[:, None]
    base_positions = jnp.repeat(lengths, SAMPLES)
    factor = HEAD_SIZE ** (-0.5)
    fresh_keys = []
    fresh_values = []
    results = []
    for step in range(2):
        rows = hidden[step]
        positions = base_positions + step
        normalized_input = normalize(rows, norm_gain)
        query = jnp.dot(normalized_input, w_query, preferred_element_type=jnp.float32).reshape(DECODE_ROWS, QUERY_HEADS, HEAD_SIZE)
        query = widen_precision(rotate(query, positions[:, None]).astype(jnp.bfloat16))
        key_value_pair = jnp.dot(normalized_input, key_value_weight, preferred_element_type=jnp.float32).reshape(DECODE_ROWS, KEY_VALUE_HEADS, 2, HEAD_SIZE)
        fresh_keys.append(widen_precision(rotate(key_value_pair[:, :, 0], positions[:, None]).astype(jnp.bfloat16)))
        fresh_values.append(widen_precision(key_value_pair[:, :, 1].astype(jnp.bfloat16)))
        outputs = []
        for head_number in range(KEY_VALUE_HEADS):
            head_query = query[:, head_number * request_group:(head_number + 1) * request_group]
            grouped = head_query.reshape(GROUP_REQUESTS, SAMPLES, request_group, HEAD_SIZE)
            prompt = jnp.einsum('rsjd,rtd->rsjt', grouped, cache_pool[:, :, head_number, 0]) * factor
            prompt = jnp.where(visible[:, None, None, :], prompt, -jnp.inf).reshape(DECODE_ROWS, request_group, PROMPT_LIMIT)
            own = jnp.stack([jnp.einsum('bjd,bd->bj', head_query, fresh[:, head_number]) for fresh in fresh_keys], axis=-1) * factor
            scores = jnp.concatenate([prompt, own], axis=-1)
            highest = lax.optimization_barrier(jnp.max(scores, axis=-1, keepdims=True))
            weights = jnp.exp(scores - highest)
            weights = widen_precision((weights / lax.optimization_barrier(jnp.sum(weights, axis=-1, keepdims=True))).astype(jnp.bfloat16))
            spread = weights[..., :PROMPT_LIMIT].reshape(GROUP_REQUESTS, SAMPLES, request_group, PROMPT_LIMIT)
            mixed = jnp.einsum('rsjt,rtd->rsjd', spread, cache_pool[:, :, head_number, 1]).reshape(DECODE_ROWS, request_group, HEAD_SIZE)
            for index, fresh in enumerate(fresh_values):
                mixed = mixed + weights[..., PROMPT_LIMIT + index][..., None] * fresh[:, head_number][:, None, :]
            outputs.append(mixed)
        mixed_all = jnp.concatenate(outputs, axis=1).reshape(DECODE_ROWS, QUERY_HEADS * HEAD_SIZE).astype(jnp.bfloat16)
        result = jnp.dot(mixed_all, w_output, preferred_element_type=jnp.float32) + rows.astype(jnp.float32)
        results.append(result.astype(jnp.bfloat16))
    return jnp.stack(results)
```

```python
import functools

import jax
import jax.numpy as jnp
import numpy as np
from jax import lax
from jax.experimental import pallas as pl
from jax.experimental.pallas import tpu as pltpu
from jax.sharding import Mesh
from jax.sharding import PartitionSpec as P

QUERY_HEADS = 64
KEY_VALUE_HEADS = 8
HEAD_SIZE = 128
GROUP_REQUESTS = 4
SAMPLES = 8
PAGE_TOKENS = 16
STEPS = 2
ROWS = STEPS * SAMPLES
PAIR = 2 * HEAD_SIZE
DEVICES = ("req", "sub", "section")
PLANE = ("sub", "section")

theta_base = 500000.0
eps_norm = 1e-05
VMEM = 48 * 2**20


def params(**more):
    return pltpu.CompilerParams(vmem_limit_bytes=VMEM, **more)


def whole_spec(shape):
    return pl.BlockSpec(shape, lambda *_: (0,) * len(shape))


def turn(vectors, cosine, sine):
    return vectors * cosine + pltpu.roll(vectors, HEAD_SIZE // 2, vectors.ndim - 1) * sine


def pages_kernel(table, place, scales, page_ref, out_ref):
    e = pl.program_id(0)
    targets, heads = out_ref.shape[0], out_ref.shape[1]
    page = table[place[0], e * targets + place[1]] - place[2]
    repeats = targets * heads // KEY_VALUE_HEADS
    for target in range(targets):
        for h in range(heads):
            head = (target * heads) // repeats + h if repeats > 1 else target * heads + h
            for part in range(2):
                c = head * 2 + part
                block = page_ref[0, :, c * HEAD_SIZE : (c + 1) * HEAD_SIZE].astype(jnp.float32)
                out_ref[target, h, :, part * HEAD_SIZE : (part + 1) * HEAD_SIZE] = (
                    block * scales[page, c]
                ).astype(jnp.bfloat16)


def used_pages(pages, scales, table, place, targets, heads):
    entries = table.shape[1] // targets
    return pl.pallas_call(
        pages_kernel,
        grid_spec=pltpu.PrefetchScalarGridSpec(
            num_scalar_prefetch=3,
            grid=(entries,),
            in_specs=[
                pl.BlockSpec(
                    (1, PAGE_TOKENS, pages.shape[2]),
                    lambda e, table, place, scales: (
                        table[place[0], e * targets + place[1]] - place[2],
                        0,
                        0,
                    ),
                )
            ],
            out_specs=pl.BlockSpec(
                (targets, heads, PAGE_TOKENS, PAIR), lambda e, *_: (0, 0, e, 0)
            ),
        ),
        out_shape=jax.ShapeDtypeStruct(
            (targets, heads, entries * PAGE_TOKENS, PAIR), jnp.bfloat16
        ),
        compiler_params=params(),
        name="used_pages",
    )(table, place, scales.astype(jnp.float32), pages)


def norm_kernel(place, x_ref, gain_ref, weight_ref, normed_ref, pair_ref):
    blocks, rows, width = x_ref.shape
    total = jnp.zeros((rows, width), jnp.float32)
    for i in range(blocks):
        x = x_ref[i].astype(jnp.float32)
        total += x * x
    mean = jnp.sum(total, axis=-1, keepdims=True) / (blocks * width)
    scale = lax.rsqrt(mean + eps_norm)
    for i in range(blocks):
        x = x_ref[i].astype(jnp.float32)
        normed_ref[i] = (x * scale * gain_ref[i]).astype(jnp.bfloat16)
    mine = normed_ref[place[0]]
    requests, targets, _, wide = pair_ref.shape
    repeats = targets * wide // weight_ref.shape[1]
    for t in range(0, targets, repeats):
        first = (t // repeats) * wide
        part = jnp.dot(
            mine, weight_ref[:, first : first + wide], preferred_element_type=jnp.float32
        )
        for r in range(requests):
            for c in range(repeats):
                pair_ref[r, t + c] = part[r * ROWS : (r + 1) * ROWS]


def norm_and_pairs(x, gain, weight, device, targets, heads):
    blocks, rows, width = x.shape
    shapes = [
        jax.ShapeDtypeStruct((blocks, rows, width), jnp.bfloat16),
        jax.ShapeDtypeStruct((GROUP_REQUESTS, targets, ROWS, heads * PAIR), jnp.float32),
    ]
    return pl.pallas_call(
        norm_kernel,
        in_specs=[pl.BlockSpec(memory_space=pltpu.SMEM)]
        + [pl.BlockSpec(memory_space=pltpu.VMEM)] * 3,
        out_specs=[pl.BlockSpec(memory_space=pltpu.VMEM)] * 2,
        out_shape=shapes,
        compiler_params=params(),
        name="norm_and_pairs",
    )(device, x, gain.reshape(blocks, 1, width), weight)


def query_kernel(x_ref, weight_ref, cos_ref, sin_ref, out_ref, total):
    i = pl.program_id(0)

    @pl.when(i == 0)
    def _():
        total[...] = jnp.zeros_like(total)

    total[...] += jnp.dot(x_ref[0], weight_ref[...], preferred_element_type=jnp.float32)

    @pl.when(i == pl.num_programs(0) - 1)
    def _():
        for head in range(total.shape[1] // HEAD_SIZE):
            part = slice(head * HEAD_SIZE, (head + 1) * HEAD_SIZE)
            out_ref[:, part] = turn(total[:, part], cos_ref[...], sin_ref[...]).astype(
                jnp.bfloat16
            )


def queries(normed, weight, cosine, sine):
    blocks, rows, width = normed.shape
    columns = weight.shape[1]
    return pl.pallas_call(
        query_kernel,
        grid=(blocks,),
        in_specs=[
            pl.BlockSpec((1, rows, width), lambda i: (i, 0, 0)),
            pl.BlockSpec((width, columns), lambda i: (i, 0)),
            whole_spec(cosine.shape),
            whole_spec(sine.shape),
        ],
        out_specs=whole_spec((rows, columns)),
        out_shape=jax.ShapeDtypeStruct((rows, columns), jnp.bfloat16),
        scratch_shapes=[pltpu.VMEM((rows, columns), jnp.float32)],
        compiler_params=params(),
        name="queries",
    )(normed, weight, cosine, sine)


def attend_kernel(place, q_ref, cache_ref, pair_ref, cos_ref, sin_ref, out_ref):
    r, length = place[0], place[1]
    sources, heads, span, _ = cache_ref.shape
    quarter = q_ref.shape[2] // HEAD_SIZE
    parts = GROUP_REQUESTS // heads
    tokens = sources * span
    pairs = pair_ref[0]
    for i in range(1, pair_ref.shape[0]):
        pairs = pairs + pair_ref[i]
    column = lax.broadcasted_iota(jnp.int32, (1, tokens), 1)
    source, inside = column // span, column % span
    position = (inside // PAGE_TOKENS * sources + source) * PAGE_TOKENS + inside % PAGE_TOKENS
    visible = position < length
    count = parts * quarter * ROWS
    row = lax.broadcasted_iota(jnp.int32, (count, ROWS), 0) % ROWS
    other = lax.broadcasted_iota(jnp.int32, (count, ROWS), 1)
    own_visible = (row % SAMPLES == other % SAMPLES) & (other // SAMPLES <= row // SAMPLES)
    factor = HEAD_SIZE ** (-0.5)
    for h in range(heads):
        keys = cache_ref[:, h, :, :HEAD_SIZE].reshape(tokens, HEAD_SIZE)
        values = cache_ref[:, h, :, HEAD_SIZE:].reshape(tokens, HEAD_SIZE)
        new_key = turn(
            pairs[:, h * PAIR : h * PAIR + HEAD_SIZE], cos_ref[...], sin_ref[...]
        ).astype(jnp.bfloat16)
        new_value = pairs[:, h * PAIR + HEAD_SIZE : (h + 1) * PAIR].astype(jnp.bfloat16)
        slots = [lax.rem(r - k + GROUP_REQUESTS, GROUP_REQUESTS) for k in range(h * parts, (h + 1) * parts)]
        query = jnp.concatenate(
            [
                q_ref[slot, :, head * HEAD_SIZE : (head + 1) * HEAD_SIZE]
                for slot in slots
                for head in range(quarter)
            ],
            axis=0,
        )
        contract = (((1,), (1,)), ((), ()))
        scores = lax.dot_general(query, keys, contract, preferred_element_type=jnp.float32)
        scores = jnp.where(visible, scores * factor, -jnp.inf)
        own = lax.dot_general(query, new_key, contract, preferred_element_type=jnp.float32)
        own = jnp.where(own_visible, own * factor, -jnp.inf)
        highest = jnp.maximum(
            jnp.max(scores, axis=-1, keepdims=True), jnp.max(own, axis=-1, keepdims=True)
        )
        scores = jnp.exp(scores - highest)
        own = jnp.exp(own - highest)
        total = jnp.sum(scores, axis=-1, keepdims=True) + jnp.sum(own, axis=-1, keepdims=True)
        mixed = jnp.dot(
            (scores / total).astype(jnp.bfloat16), values, preferred_element_type=jnp.float32
        ) + jnp.dot(
            (own / total).astype(jnp.bfloat16), new_value, preferred_element_type=jnp.float32
        )
        mixed = mixed.astype(jnp.bfloat16)
        for i, slot in enumerate(slots):
            for head in range(quarter):
                first = (i * quarter + head) * ROWS
                out_ref[slot, :, head * HEAD_SIZE : (head + 1) * HEAD_SIZE] = mixed[
                    first : first + ROWS
                ]


def attend(query, cache, pairs, cosine, sine, place):
    return pl.pallas_call(
        attend_kernel,
        in_specs=[pl.BlockSpec(memory_space=pltpu.SMEM)]
        + [pl.BlockSpec(memory_space=pltpu.VMEM)] * 5,
        out_specs=pl.BlockSpec(memory_space=pltpu.VMEM),
        out_shape=jax.ShapeDtypeStruct(query.shape, jnp.bfloat16),
        compiler_params=params(),
        name="attend",
    )(place, query, cache, pairs, cosine, sine)


def output_kernel(x_ref, weight_ref, out_ref):
    out_ref[0] = jnp.dot(x_ref[...], weight_ref[...], preferred_element_type=jnp.float32)


def outputs(mixed, weight, blocks):
    rows, depth = mixed.shape
    width = weight.shape[1] // blocks
    return pl.pallas_call(
        output_kernel,
        grid=(blocks,),
        in_specs=[whole_spec((rows, depth)), pl.BlockSpec((depth, width), lambda i: (0, i))],
        out_specs=pl.BlockSpec((1, rows, width), lambda i: (i, 0, 0)),
        out_shape=jax.ShapeDtypeStruct((blocks, rows, width), jnp.float32),
        compiler_params=params(),
        name="outputs",
    )(mixed, weight)


def shards(
    hidden,
    norm_gain,
    w_query,
    key_value_weight,
    w_output,
    prompt_cache_pages,
    per_page_scales,
    lengths,
    block_table,
):
    devices = lax.axis_size(DEVICES)
    targets = lax.axis_size(PLANE)
    heads = max(1, KEY_VALUE_HEADS // targets)
    device = lax.axis_index(DEVICES)
    request = lax.axis_index("req")
    spot = lax.axis_index(PLANE)
    width = hidden.shape[2]

    rows = hidden.reshape(STEPS, GROUP_REQUESTS, SAMPLES, width)
    rows = jnp.swapaxes(rows, 0, 1).reshape(GROUP_REQUESTS * ROWS, width)
    gathered = lax.all_to_all(
        jnp.broadcast_to(rows[None], (devices,) + rows.shape), DEVICES, 0, 0, tiled=True
    )

    place = jnp.stack([request, spot, device * prompt_cache_pages.shape[0]]).astype(jnp.int32)
    send = used_pages(prompt_cache_pages, per_page_scales, block_table, place, targets, heads)
    cache = lax.all_to_all(send, PLANE, 0, 0, tiled=True)

    half = HEAD_SIZE // 2
    freqs = jnp.exp(
        -jnp.log(theta_base) * jnp.arange(half, dtype=jnp.float32) * (2.0 / HEAD_SIZE)
    )
    positions = (lengths[:, None] + jnp.arange(STEPS)[None, :]).astype(jnp.float32)
    angles = positions[..., None] * freqs
    cosine, sine = jnp.cos(angles), jnp.sin(angles)
    cosine = jnp.concatenate([cosine, cosine], axis=-1)
    sine = jnp.concatenate([-sine, sine], axis=-1)
    cosine = jnp.repeat(cosine, SAMPLES, axis=1)
    sine = jnp.repeat(sine, SAMPLES, axis=1)
    my_cosine = lax.dynamic_index_in_dim(cosine, request, 0, keepdims=False)
    my_sine = lax.dynamic_index_in_dim(sine, request, 0, keepdims=False)
    cosine = cosine.reshape(-1, HEAD_SIZE)
    sine = sine.reshape(-1, HEAD_SIZE)

    normed, pairs = norm_and_pairs(
        gathered, norm_gain, key_value_weight, device[None].astype(jnp.int32), targets, heads
    )
    pairs = lax.all_to_all(
        pairs.reshape(devices, ROWS, heads * PAIR), DEVICES, 0, 0, tiled=True
    )

    query = queries(normed, w_query, cosine, sine)
    query = query.reshape(GROUP_REQUESTS, ROWS, -1)
    group, member = device // GROUP_REQUESTS, device % GROUP_REQUESTS
    got = []
    for s in range(GROUP_REQUESTS):
        there = [
            (d, (d % GROUP_REQUESTS + s) % GROUP_REQUESTS * targets + d // GROUP_REQUESTS)
            for d in range(devices)
        ]
        block = lax.dynamic_index_in_dim(
            query, (member + s) % GROUP_REQUESTS, 0, keepdims=False
        )
        got.append(lax.ppermute(block, DEVICES, there))
    query = jnp.stack(got)

    my_length = lax.dynamic_index_in_dim(lengths, request, 0, keepdims=False)
    mixed = attend(
        query,
        cache,
        pairs,
        my_cosine,
        my_sine,
        jnp.stack([request, my_length]).astype(jnp.int32),
    )
    got = []
    for s in range(GROUP_REQUESTS):
        back = [
            ((d % GROUP_REQUESTS + s) % GROUP_REQUESTS * targets + d // GROUP_REQUESTS, d)
            for d in range(devices)
        ]
        got.append(lax.ppermute(mixed[s], DEVICES, back))
    mixed = jnp.stack(got)
    mixed = jnp.take(
        mixed, (jnp.arange(GROUP_REQUESTS) - member) % GROUP_REQUESTS, axis=0
    ).reshape(GROUP_REQUESTS * ROWS, -1)

    terms = outputs(mixed, w_output, devices)
    terms = lax.all_to_all(terms, DEVICES, 0, 0, tiled=True)
    result = jnp.sum(terms, axis=0) + rows.astype(jnp.float32)
    result = result.astype(jnp.bfloat16).reshape(GROUP_REQUESTS, STEPS, SAMPLES, width)
    return jnp.swapaxes(result, 0, 1).reshape(hidden.shape)


def solution(mesh):
    groups, tp, section = mesh.devices.shape
    finer = Mesh(
        mesh.devices.reshape(groups, GROUP_REQUESTS, tp // GROUP_REQUESTS, section),
        ("groups",) + DEVICES,
    )
    placed = (
        P(None, "groups", DEVICES),
        P(),
        P(None, DEVICES),
        P(DEVICES, None),
        P(DEVICES, None),
        P(("groups",) + DEVICES, None, None),
        P(("groups",) + DEVICES, None),
        P("groups"),
        P("groups", None),
    )
    return jax.shard_map(
        shards,
        mesh=finer,
        in_specs=placed,
        out_specs=P(None, "groups", DEVICES),
        check_vma=False,
    )
```

```python
import jax
import jax.numpy as jnp
from jax import lax
from jax.experimental import pallas as pl
from jax.experimental.pallas import tpu as pltpu
from jax.sharding import Mesh
from jax.sharding import PartitionSpec as P

QUERY_HEADS = 64
KEY_VALUE_HEADS = 8
HEAD_SIZE = 128
GROUP_REQUESTS = 4
SAMPLES = 8
PAGE_TOKENS = 16
STEPS = 2
ROWS = STEPS * SAMPLES
PAIR = 2 * HEAD_SIZE
DEVICES = ("req", "sub", "section")
PLANE = ("sub", "section")
CHIPS = ("req", "sub")

theta_base = 500000.0
eps_norm = 1e-05
VMEM = 16 * 2**20


def params(**more):
    return pltpu.CompilerParams(vmem_limit_bytes=VMEM, **more)


def whole_spec(shape):
    return pl.BlockSpec(shape, lambda *_: (0,) * len(shape))


def turn(vectors, cosine, sine):
    return vectors * cosine + pltpu.roll(vectors, HEAD_SIZE // 2, vectors.ndim - 1) * sine


def pages_kernel(table, place, scales, page_ref, *out_refs):
    e = pl.program_id(0)
    targets, heads = len(out_refs), out_refs[0].shape[0]
    page = table[place[0], e * targets + place[1]] - place[2]
    repeats = targets * heads // KEY_VALUE_HEADS
    for shift, out_ref in enumerate(out_refs):
        first = lax.rem(place[1] + shift, targets) * heads // repeats
        for h in range(heads):
            for part in range(2):
                c = (first + h) * 2 + part
                columns = pl.ds(pl.multiple_of(c * HEAD_SIZE, HEAD_SIZE), HEAD_SIZE)
                block = page_ref[0, :, columns].astype(jnp.float32)
                out_ref[h, :, part * HEAD_SIZE : (part + 1) * HEAD_SIZE] = (
                    block * scales[page, c]
                ).astype(jnp.bfloat16)


def used_pages(pages, scales, table, place, targets, heads):
    entries = table.shape[1] // targets
    return pl.pallas_call(
        pages_kernel,
        grid_spec=pltpu.PrefetchScalarGridSpec(
            num_scalar_prefetch=3,
            grid=(entries,),
            in_specs=[
                pl.BlockSpec(
                    (1, PAGE_TOKENS, pages.shape[2]),
                    lambda e, table, place, scales: (
                        table[place[0], e * targets + place[1]] - place[2],
                        0,
                        0,
                    ),
                )
            ],
            out_specs=[
                pl.BlockSpec((heads, PAGE_TOKENS, PAIR), lambda e, *_: (0, e, 0))
            ]
            * targets,
        ),
        out_shape=[
            jax.ShapeDtypeStruct((heads, entries * PAGE_TOKENS, PAIR), jnp.bfloat16)
        ]
        * targets,
        compiler_params=params(),
        name="used_pages",
    )(table, place, scales.astype(jnp.float32), pages)


def pairs_kernel(place, mine_ref, other_ref, rows_ref, gain_ref, weight_ref, scale_ref, pair_ref):
    blocks, rows, width = mine_ref.shape
    total = jnp.zeros((rows, width), jnp.float32)
    for ref in (mine_ref, other_ref):
        for i in range(blocks):
            x = ref[i].astype(jnp.float32)
            total += x * x
    mean = jnp.sum(total, axis=-1, keepdims=True) / (2 * blocks * width)
    scale = lax.rsqrt(mean + eps_norm)
    scale_ref[...] = jnp.broadcast_to(scale, scale_ref.shape)
    x = rows_ref[...].astype(jnp.float32)
    mine = (x * scale * gain_ref[place[0]]).astype(jnp.bfloat16)
    requests, targets, _, wide = pair_ref.shape
    repeats = targets * wide // weight_ref.shape[1]
    for t in range(0, targets, repeats):
        first = (t // repeats) * wide
        part = jnp.dot(
            mine, weight_ref[:, first : first + wide], preferred_element_type=jnp.float32
        )
        for r in range(requests):
            for step in range(STEPS):
                first = (step * requests + r) * SAMPLES
                for c in range(repeats):
                    pair_ref[r, t + c, step * SAMPLES : (step + 1) * SAMPLES] = part[
                        first : first + SAMPLES
                    ]


def scale_and_pairs(mine, other, rows, gain, weight, device, targets, heads):
    blocks, count, width = mine.shape
    shapes = [
        jax.ShapeDtypeStruct((count, HEAD_SIZE), jnp.float32),
        jax.ShapeDtypeStruct((GROUP_REQUESTS, targets, ROWS, heads * PAIR), jnp.float32),
    ]
    return pl.pallas_call(
        pairs_kernel,
        in_specs=[pl.BlockSpec(memory_space=pltpu.SMEM)]
        + [pl.BlockSpec(memory_space=pltpu.VMEM)] * 5,
        out_specs=[pl.BlockSpec(memory_space=pltpu.VMEM)] * 2,
        out_shape=shapes,
        compiler_params=params(),
        name="scale_and_pairs",
    )(device, mine, other, rows, gain, weight)


def query_kernel(
    place, mine_ref, other_ref, scale_ref, gain_ref, weight_ref, cos_ref, sin_ref, out_ref
):
    blocks, rows, width = mine_ref.shape
    columns = weight_ref.shape[1]
    scale = scale_ref[:, :1]
    total = jnp.zeros((rows, columns), jnp.float32)
    for i in range(blocks):
        for ref, core in ((mine_ref, place[1]), (other_ref, 1 - place[1])):
            block = 2 * i + core
            x = ref[i].astype(jnp.float32)
            x = (x * scale * gain_ref[block]).astype(jnp.bfloat16)
            depth = pl.ds(pl.multiple_of(block * width, width), width)
            total += jnp.dot(x, weight_ref[depth, :], preferred_element_type=jnp.float32)
    for head in range(columns // HEAD_SIZE):
        part = slice(head * HEAD_SIZE, (head + 1) * HEAD_SIZE)
        turned = turn(total[:, part], cos_ref[...], sin_ref[...])
        for r in range(GROUP_REQUESTS):
            first, second = r * SAMPLES, (GROUP_REQUESTS + r) * SAMPLES
            out_ref[r, :, part] = jnp.concatenate(
                [turned[first : first + SAMPLES], turned[second : second + SAMPLES]], axis=0
            ).astype(jnp.bfloat16)


def queries(place, mine, other, scale, gain, weight, cosine, sine):
    columns = weight.shape[1]
    return pl.pallas_call(
        query_kernel,
        in_specs=[pl.BlockSpec(memory_space=pltpu.SMEM)]
        + [pl.BlockSpec(memory_space=pltpu.VMEM)] * 7,
        out_specs=pl.BlockSpec(memory_space=pltpu.VMEM),
        out_shape=jax.ShapeDtypeStruct((GROUP_REQUESTS, ROWS, columns), jnp.bfloat16),
        compiler_params=params(),
        name="queries",
    )(place, mine, other, scale, gain, weight, cosine, sine)


def attend_kernel(place, *refs):
    r, length, spot = place[0], place[1], place[2]
    q_refs = refs[:GROUP_REQUESTS]
    out_refs = refs[-GROUP_REQUESTS:]
    pair_ref, cos_ref, sin_ref = refs[GROUP_REQUESTS : GROUP_REQUESTS + 3]
    cache_refs = refs[GROUP_REQUESTS + 3 : -GROUP_REQUESTS]
    sources = len(cache_refs)
    heads, span, _ = cache_refs[0].shape
    quarter = q_refs[0].shape[1] // HEAD_SIZE
    parts = GROUP_REQUESTS // heads
    tokens = sources * span
    pairs = pair_ref[0]
    for i in range(1, pair_ref.shape[0]):
        pairs = pairs + pair_ref[i]
    column = lax.broadcasted_iota(jnp.int32, (1, tokens), 1)
    shift, inside = column // span, column % span
    source = (spot - shift + sources) % sources
    position = (inside // PAGE_TOKENS * sources + source) * PAGE_TOKENS + inside % PAGE_TOKENS
    visible = position < length
    count = GROUP_REQUESTS * quarter * ROWS
    row = lax.broadcasted_iota(jnp.int32, (count, ROWS), 0) % ROWS
    other = lax.broadcasted_iota(jnp.int32, (count, ROWS), 1)
    own_visible = (row % SAMPLES == other % SAMPLES) & (other // SAMPLES <= row // SAMPLES)
    query = jnp.concatenate(
        [
            ref[:, head * HEAD_SIZE : (head + 1) * HEAD_SIZE]
            for ref in q_refs
            for head in range(quarter)
        ],
        axis=0,
    )
    block = quarter * ROWS
    factor = HEAD_SIZE ** (-0.5)
    contract = (((1,), (1,)), ((), ()))
    result = None
    for h in range(heads):
        keys = jnp.concatenate([ref[h, :, :HEAD_SIZE] for ref in cache_refs], axis=0)
        values = jnp.concatenate([ref[h, :, HEAD_SIZE:] for ref in cache_refs], axis=0)
        new_key = turn(
            pairs[:, h * PAIR : h * PAIR + HEAD_SIZE], cos_ref[...], sin_ref[...]
        ).astype(jnp.bfloat16)
        new_value = pairs[:, h * PAIR + HEAD_SIZE : (h + 1) * PAIR].astype(jnp.bfloat16)
        scores = lax.dot_general(query, keys, contract, preferred_element_type=jnp.float32)
        scores = jnp.where(visible, scores * factor, -jnp.inf)
        own = lax.dot_general(query, new_key, contract, preferred_element_type=jnp.float32)
        own = jnp.where(own_visible, own * factor, -jnp.inf)
        highest = jnp.maximum(
            jnp.max(scores, axis=-1, keepdims=True), jnp.max(own, axis=-1, keepdims=True)
        )
        scores = jnp.exp(scores - highest)
        own = jnp.exp(own - highest)
        total = jnp.sum(scores, axis=-1, keepdims=True) + jnp.sum(own, axis=-1, keepdims=True)
        mixed = jnp.dot(
            (scores / total).astype(jnp.bfloat16), values, preferred_element_type=jnp.float32
        ) + jnp.dot(
            (own / total).astype(jnp.bfloat16), new_value, preferred_element_type=jnp.float32
        )
        if result is None:
            result = mixed
        else:
            slot = lax.broadcasted_iota(jnp.int32, (count, 1), 0) // block
            source = (r - slot + GROUP_REQUESTS) % GROUP_REQUESTS
            result = jnp.where(source // parts == h, mixed, result)
    result = result.astype(jnp.bfloat16)
    for slot, out_ref in enumerate(out_refs):
        for head in range(quarter):
            first = slot * block + head * ROWS
            out_ref[:, head * HEAD_SIZE : (head + 1) * HEAD_SIZE] = result[first : first + ROWS]


def attend(place, query, pairs, cosine, sine, cache):
    shape = jax.ShapeDtypeStruct(query[0].shape, jnp.bfloat16)
    return pl.pallas_call(
        attend_kernel,
        in_specs=[pl.BlockSpec(memory_space=pltpu.SMEM)]
        + [pl.BlockSpec(memory_space=pltpu.VMEM)] * (len(query) + 3 + len(cache)),
        out_specs=[pl.BlockSpec(memory_space=pltpu.VMEM)] * GROUP_REQUESTS,
        out_shape=[shape] * GROUP_REQUESTS,
        compiler_params=params(),
        name="attend",
    )(place, *query, pairs, cosine, sine, *cache)


def output_kernel(place, *refs):
    x_refs, weight_ref, out_ref = refs[:GROUP_REQUESTS], refs[-2], refs[-1]
    blocks, rows, width = out_ref.shape
    order = [lax.rem(r - place[0] + GROUP_REQUESTS, GROUP_REQUESTS) for r in range(GROUP_REQUESTS)]
    x = jnp.stack([ref[...] for ref in x_refs])
    pieces = []
    for r in range(GROUP_REQUESTS):
        piece = x[0]
        for s in range(1, GROUP_REQUESTS):
            piece = jnp.where(order[r] == s, x[s], piece)
        pieces.append(piece)
    x = jnp.concatenate(pieces, axis=0)
    for i in range(blocks):
        columns = pl.ds(pl.multiple_of((2 * i + place[1]) * width, width), width)
        part = jnp.dot(x, weight_ref[:, columns], preferred_element_type=jnp.float32)
        for r in range(GROUP_REQUESTS):
            for step in range(STEPS):
                source = r * ROWS + step * SAMPLES
                target = (step * GROUP_REQUESTS + r) * SAMPLES
                out_ref[i, target : target + SAMPLES] = part[source : source + SAMPLES]


def outputs(place, mixed, weight, blocks):
    rows = GROUP_REQUESTS * ROWS
    width = weight.shape[1] // (2 * blocks)
    return pl.pallas_call(
        output_kernel,
        in_specs=[pl.BlockSpec(memory_space=pltpu.SMEM)]
        + [pl.BlockSpec(memory_space=pltpu.VMEM)] * (GROUP_REQUESTS + 1),
        out_specs=pl.BlockSpec(memory_space=pltpu.VMEM),
        out_shape=jax.ShapeDtypeStruct((blocks, rows, width), jnp.float32),
        compiler_params=params(),
        name="outputs",
    )(place, *mixed, weight)


def fold_core_kernel(place, mine_ref, got_ref, *out_refs):
    subs = len(out_refs)
    for shift, out_ref in enumerate(out_refs):
        sub = lax.rem(place[0] + shift, subs)
        for i in range(GROUP_REQUESTS):
            block = i * subs + sub
            out_ref[i] = mine_ref[block] + got_ref[block]


def fold_core(place, mine, got, subs):
    shape = jax.ShapeDtypeStruct((GROUP_REQUESTS,) + mine.shape[1:], jnp.float32)
    return pl.pallas_call(
        fold_core_kernel,
        in_specs=[pl.BlockSpec(memory_space=pltpu.SMEM)]
        + [pl.BlockSpec(memory_space=pltpu.VMEM)] * 2,
        out_specs=[pl.BlockSpec(memory_space=pltpu.VMEM)] * subs,
        out_shape=[shape] * subs,
        compiler_params=params(),
        name="fold_core",
    )(place, mine, got)


def fold_sub_kernel(place, *refs):
    in_refs, out_refs = refs[:-GROUP_REQUESTS], refs[-GROUP_REQUESTS:]
    for shift, out_ref in enumerate(out_refs):
        block = lax.rem(place[0] + shift, GROUP_REQUESTS)
        total = in_refs[0][block]
        for ref in in_refs[1:]:
            total = total + ref[block]
        out_ref[...] = total


def fold_sub(place, parts):
    shape = jax.ShapeDtypeStruct(parts[0].shape[1:], jnp.float32)
    return pl.pallas_call(
        fold_sub_kernel,
        in_specs=[pl.BlockSpec(memory_space=pltpu.SMEM)]
        + [pl.BlockSpec(memory_space=pltpu.VMEM)] * len(parts),
        out_specs=[pl.BlockSpec(memory_space=pltpu.VMEM)] * GROUP_REQUESTS,
        out_shape=[shape] * GROUP_REQUESTS,
        compiler_params=params(),
        name="fold_sub",
    )(place, *parts)


def finish_kernel(rows_ref, *refs):
    total = refs[0][...]
    for ref in refs[1:-1]:
        total = total + ref[...]
    refs[-1][...] = (total + rows_ref[...].astype(jnp.float32)).astype(jnp.bfloat16)


def finish(rows, parts):
    return pl.pallas_call(
        finish_kernel,
        in_specs=[pl.BlockSpec(memory_space=pltpu.VMEM)] * (1 + len(parts)),
        out_specs=pl.BlockSpec(memory_space=pltpu.VMEM),
        out_shape=jax.ShapeDtypeStruct(rows.shape, jnp.bfloat16),
        compiler_params=params(),
        name="finish",
    )(rows, *parts)


def passed(array, axis, shift):
    size = lax.axis_size(axis)
    return lax.ppermute(array, axis, [(i, (i + shift) % size) for i in range(size)])


def scalars(*values):
    return jnp.stack(values).astype(jnp.int32)


def shards(
    hidden,
    norm_gain,
    w_query,
    key_value_weight,
    w_output,
    prompt_cache_pages,
    per_page_scales,
    lengths,
    block_table,
):
    devices = lax.axis_size(DEVICES)
    targets = lax.axis_size(PLANE)
    subs = lax.axis_size("sub")
    chips = devices // 2
    heads = max(1, KEY_VALUE_HEADS // targets)
    device = lax.axis_index(DEVICES)
    request = lax.axis_index("req")
    sub = lax.axis_index("sub")
    core = lax.axis_index("section")
    spot = lax.axis_index(PLANE)
    group, member = device // GROUP_REQUESTS, device % GROUP_REQUESTS
    width = hidden.shape[2]

    rows = hidden.reshape(GROUP_REQUESTS * ROWS, width)
    mine = lax.all_to_all(
        jnp.broadcast_to(rows[None], (chips,) + rows.shape), CHIPS, 0, 0, tiled=True
    )
    other = passed(mine, "section", 1)

    place = scalars(request, spot, device * prompt_cache_pages.shape[0])
    send = used_pages(prompt_cache_pages, per_page_scales, block_table, place, targets, heads)
    cache = [send[0]]
    for s in range(1, targets):
        there = [(d, (d + s) % targets) for d in range(targets)]
        cache.append(lax.ppermute(send[s], PLANE, there))

    half = HEAD_SIZE // 2
    freqs = jnp.exp(
        -jnp.log(theta_base) * jnp.arange(half, dtype=jnp.float32) * (2.0 / HEAD_SIZE)
    )
    positions = (lengths[None, :] + jnp.arange(STEPS)[:, None]).astype(jnp.float32)
    angles = positions[..., None] * freqs
    cosine, sine = jnp.cos(angles), jnp.sin(angles)
    cosine = jnp.repeat(jnp.concatenate([cosine, cosine], axis=-1)[:, :, None], SAMPLES, axis=2)
    sine = jnp.repeat(jnp.concatenate([-sine, sine], axis=-1)[:, :, None], SAMPLES, axis=2)
    my_cosine = lax.dynamic_index_in_dim(cosine, request, 1, keepdims=False)
    my_sine = lax.dynamic_index_in_dim(sine, request, 1, keepdims=False)

    gain = norm_gain.reshape(devices, 1, width)
    scale, pairs = scale_and_pairs(
        mine, other, rows, gain, key_value_weight, scalars(device), targets, heads
    )
    pairs = lax.all_to_all(
        pairs.reshape(devices, ROWS, heads * PAIR), DEVICES, 0, 0, tiled=True
    )

    query = queries(
        scalars(device, core),
        mine,
        other,
        scale,
        gain,
        w_query,
        cosine.reshape(-1, HEAD_SIZE),
        sine.reshape(-1, HEAD_SIZE),
    )
    got = []
    for s in range(GROUP_REQUESTS):
        there = [
            (d, (d % GROUP_REQUESTS + s) % GROUP_REQUESTS * targets + d // GROUP_REQUESTS)
            for d in range(devices)
        ]
        block = lax.dynamic_index_in_dim(
            query, (member + s) % GROUP_REQUESTS, 0, keepdims=False
        )
        got.append(lax.ppermute(block, DEVICES, there))

    my_length = lax.dynamic_index_in_dim(lengths, request, 0, keepdims=False)
    mixed = attend(
        scalars(request, my_length, spot),
        got,
        pairs,
        my_cosine.reshape(ROWS, HEAD_SIZE),
        my_sine.reshape(ROWS, HEAD_SIZE),
        cache,
    )
    got = []
    for s in range(GROUP_REQUESTS):
        back = [
            ((d % GROUP_REQUESTS + s) % GROUP_REQUESTS * targets + d // GROUP_REQUESTS, d)
            for d in range(devices)
        ]
        got.append(lax.ppermute(mixed[s], DEVICES, back))

    away = outputs(scalars(member, 1 - core), got, w_output, chips)
    arrived = passed(away, "section", 1)
    kept = outputs(scalars(member, core), got, w_output, chips)
    parts = fold_core(scalars(sub), kept, arrived, subs)
    parts = [parts[0]] + [passed(parts[s], "sub", s) for s in range(1, subs)]
    parts = fold_sub(scalars(request), parts)
    parts = [parts[0]] + [passed(parts[s], "req", s) for s in range(1, GROUP_REQUESTS)]
    return finish(rows, parts).reshape(hidden.shape)


def solution(mesh):
    groups, tp, section = mesh.devices.shape
    finer = Mesh(
        mesh.devices.reshape(groups, GROUP_REQUESTS, tp // GROUP_REQUESTS, section),
        ("groups",) + DEVICES,
    )
    placed = (
        P(None, "groups", DEVICES),
        P(),
        P(None, DEVICES),
        P(DEVICES, None),
        P(DEVICES, None),
        P(("groups",) + DEVICES, None, None),
        P(("groups",) + DEVICES, None),
        P("groups"),
        P("groups", None),
    )
    return jax.shard_map(
        shards,
        mesh=finer,
        in_specs=placed,
        out_specs=P(None, "groups", DEVICES),
        check_vma=False,
    )
```

```python
import jax
import jax.numpy as jnp
from jax import lax
from jax.experimental import pallas as pl
from jax.experimental.pallas import tpu as pltpu
from jax.sharding import Mesh
from jax.sharding import PartitionSpec as P

QUERY_HEADS = 64
KEY_VALUE_HEADS = 8
HEAD_SIZE = 128
GROUP_REQUESTS = 4
SAMPLES = 8
PAGE_TOKENS = 16
STEPS = 2
ROWS = STEPS * SAMPLES
PAIR = 2 * HEAD_SIZE
LANES = 128
TAIL = 16
DEVICES = ("req", "sub", "section")
PLANE = ("sub", "section")
CHIPS = ("req", "sub")

theta_base = 500000.0
eps_norm = 1e-05
VMEM = 16 * 2**20


def params(**more):
    return pltpu.CompilerParams(vmem_limit_bytes=VMEM, **more)


def whole_spec(shape):
    return pl.BlockSpec(shape, lambda *_: (0,) * len(shape))


def turn(vectors, cosine, sine):
    return vectors * cosine + pltpu.roll(vectors, HEAD_SIZE // 2, vectors.ndim - 1) * sine


def stage_kernel(*refs):
    half = (len(refs) - 1) // 2
    copies = [
        pltpu.make_async_copy(refs[i], refs[half + i], refs[-1].at[i]) for i in range(half)
    ]
    for copy in copies:
        copy.start()
    for copy in copies:
        copy.wait()


def staged(*arrays):
    size = sum(array.size * array.dtype.itemsize for array in arrays)
    return pl.pallas_call(
        stage_kernel,
        in_specs=[pl.BlockSpec(memory_space=pltpu.HBM)] * len(arrays),
        out_specs=[pl.BlockSpec(memory_space=pltpu.VMEM)] * len(arrays),
        out_shape=[jax.ShapeDtypeStruct(array.shape, array.dtype) for array in arrays],
        scratch_shapes=[pltpu.SemaphoreType.DMA((len(arrays),))],
        compiler_params=pltpu.CompilerParams(vmem_limit_bytes=30 * 2**20),
        cost_estimate=pl.CostEstimate(flops=0, bytes_accessed=2 * size, transcendentals=0),
        name="staged",
    )(*arrays)


def pages_kernel(table, place, scales, page_ref, *out_refs):
    e = pl.program_id(0)
    targets, heads = len(out_refs), out_refs[0].shape[0]
    page = table[place[0], e * targets + place[1]] - place[2]
    repeats = targets * heads // KEY_VALUE_HEADS
    for shift, out_ref in enumerate(out_refs):
        first = lax.rem(place[1] + shift, targets) * heads // repeats
        for h in range(heads):
            for part in range(2):
                c = (first + h) * 2 + part
                columns = pl.ds(pl.multiple_of(c * HEAD_SIZE, HEAD_SIZE), HEAD_SIZE)
                block = page_ref[0, :, columns].astype(jnp.float32)
                out_ref[h, :, part * HEAD_SIZE : (part + 1) * HEAD_SIZE] = (
                    block * scales[page, c]
                ).astype(jnp.bfloat16)


def used_pages(pages, scales, table, place, targets, heads):
    entries = table.shape[1] // targets
    return pl.pallas_call(
        pages_kernel,
        grid_spec=pltpu.PrefetchScalarGridSpec(
            num_scalar_prefetch=3,
            grid=(entries,),
            in_specs=[
                pl.BlockSpec(
                    (1, PAGE_TOKENS, pages.shape[2]),
                    lambda e, table, place, scales: (
                        table[place[0], e * targets + place[1]] - place[2],
                        0,
                        0,
                    ),
                )
            ],
            out_specs=[
                pl.BlockSpec((heads, PAGE_TOKENS, PAIR), lambda e, *_: (0, e, 0))
            ]
            * targets,
        ),
        out_shape=[
            jax.ShapeDtypeStruct((heads, entries * PAGE_TOKENS, PAIR), jnp.bfloat16)
        ]
        * targets,
        compiler_params=params(),
        name="used_pages",
    )(table, place, scales.astype(jnp.float32), pages)


def pairs_kernel(place, mine_ref, other_ref, rows_ref, gain_ref, weight_ref, scale_ref, pair_ref):
    blocks, rows, width = mine_ref.shape
    total = jnp.zeros((rows, width), jnp.float32)
    for ref in (mine_ref, other_ref):
        for i in range(blocks):
            x = ref[i].astype(jnp.float32)
            total += x * x
    mean = jnp.sum(total, axis=-1, keepdims=True) / (2 * blocks * width)
    scale = lax.rsqrt(mean + eps_norm)
    scale_ref[...] = jnp.broadcast_to(scale, scale_ref.shape)
    x = rows_ref[...].astype(jnp.float32)
    mine = (x * scale * gain_ref[place[0]]).astype(jnp.bfloat16)
    requests, targets, _, wide = pair_ref.shape
    repeats = targets * wide // weight_ref.shape[1]
    for t in range(0, targets, repeats):
        first = (t // repeats) * wide
        part = jnp.dot(
            mine, weight_ref[:, first : first + wide], preferred_element_type=jnp.float32
        )
        for r in range(requests):
            for step in range(STEPS):
                first = (step * requests + r) * SAMPLES
                for c in range(repeats):
                    pair_ref[r, t + c, step * SAMPLES : (step + 1) * SAMPLES] = part[
                        first : first + SAMPLES
                    ]


def scale_and_pairs(mine, other, rows, gain, weight, device, targets, heads):
    blocks, count, width = mine.shape
    shapes = [
        jax.ShapeDtypeStruct((count, HEAD_SIZE), jnp.float32),
        jax.ShapeDtypeStruct((GROUP_REQUESTS, targets, ROWS, heads * PAIR), jnp.float32),
    ]
    return pl.pallas_call(
        pairs_kernel,
        in_specs=[pl.BlockSpec(memory_space=pltpu.SMEM)]
        + [pl.BlockSpec(memory_space=pltpu.VMEM)] * 5,
        out_specs=[pl.BlockSpec(memory_space=pltpu.VMEM)] * 2,
        out_shape=shapes,
        compiler_params=params(),
        name="scale_and_pairs",
    )(device, mine, other, rows, gain, weight)


def query_kernel(
    place, mine_ref, other_ref, scale_ref, gain_ref, weight_ref, cos_ref, sin_ref, out_ref
):
    blocks, rows, width = mine_ref.shape
    columns = weight_ref.shape[1]
    scale = scale_ref[:, :1]
    total = jnp.zeros((rows, columns), jnp.float32)
    for i in range(blocks):
        for ref, core in ((mine_ref, place[1]), (other_ref, 1 - place[1])):
            block = 2 * i + core
            x = ref[i].astype(jnp.float32)
            x = (x * scale * gain_ref[block]).astype(jnp.bfloat16)
            depth = pl.ds(pl.multiple_of(block * width, width), width)
            total += jnp.dot(x, weight_ref[depth, :], preferred_element_type=jnp.float32)
    for head in range(columns // HEAD_SIZE):
        part = slice(head * HEAD_SIZE, (head + 1) * HEAD_SIZE)
        turned = turn(total[:, part], cos_ref[...], sin_ref[...])
        for r in range(GROUP_REQUESTS):
            first, second = r * SAMPLES, (GROUP_REQUESTS + r) * SAMPLES
            out_ref[r, :, part] = jnp.concatenate(
                [turned[first : first + SAMPLES], turned[second : second + SAMPLES]], axis=0
            ).astype(jnp.bfloat16)


def queries(place, mine, other, scale, gain, weight, cosine, sine):
    columns = weight.shape[1]
    return pl.pallas_call(
        query_kernel,
        in_specs=[pl.BlockSpec(memory_space=pltpu.SMEM)]
        + [pl.BlockSpec(memory_space=pltpu.VMEM)] * 7,
        out_specs=pl.BlockSpec(memory_space=pltpu.VMEM),
        out_shape=jax.ShapeDtypeStruct((GROUP_REQUESTS, ROWS, columns), jnp.bfloat16),
        compiler_params=params(),
        name="queries",
    )(place, mine, other, scale, gain, weight, cosine, sine)


def attend_kernel(place, *refs):
    r, length, spot = place[0], place[1], place[2]
    q_refs = refs[:GROUP_REQUESTS]
    out_refs = refs[-GROUP_REQUESTS:]
    pair_ref, cos_ref, sin_ref = refs[GROUP_REQUESTS : GROUP_REQUESTS + 3]
    cache_refs = refs[GROUP_REQUESTS + 3 : -GROUP_REQUESTS]
    sources = len(cache_refs)
    heads, span, _ = cache_refs[0].shape
    quarter = q_refs[0].shape[1] // HEAD_SIZE
    parts = GROUP_REQUESTS // heads
    tokens = sources * span
    pairs = pair_ref[0]
    for i in range(1, pair_ref.shape[0]):
        pairs = pairs + pair_ref[i]
    column = lax.broadcasted_iota(jnp.int32, (1, tokens), 1)
    shift, inside = column // span, column % span
    source = (spot - shift + sources) % sources
    position = (inside // PAGE_TOKENS * sources + source) * PAGE_TOKENS + inside % PAGE_TOKENS
    visible = position < length
    count = GROUP_REQUESTS * quarter * ROWS
    row = lax.broadcasted_iota(jnp.int32, (count, ROWS), 0) % ROWS
    other = lax.broadcasted_iota(jnp.int32, (count, ROWS), 1)
    own_visible = (row % SAMPLES == other % SAMPLES) & (other // SAMPLES <= row // SAMPLES)
    query = jnp.concatenate(
        [
            ref[:, head * HEAD_SIZE : (head + 1) * HEAD_SIZE]
            for ref in q_refs
            for head in range(quarter)
        ],
        axis=0,
    )
    block = quarter * ROWS
    factor = HEAD_SIZE ** (-0.5)
    contract = (((1,), (1,)), ((), ()))
    result = None
    for h in range(heads):
        keys = jnp.concatenate([ref[h, :, :HEAD_SIZE] for ref in cache_refs], axis=0)
        values = jnp.concatenate([ref[h, :, HEAD_SIZE:] for ref in cache_refs], axis=0)
        new_key = turn(
            pairs[:, h * PAIR : h * PAIR + HEAD_SIZE], cos_ref[...], sin_ref[...]
        ).astype(jnp.bfloat16)
        new_value = pairs[:, h * PAIR + HEAD_SIZE : (h + 1) * PAIR].astype(jnp.bfloat16)
        scores = lax.dot_general(query, keys, contract, preferred_element_type=jnp.float32)
        scores = jnp.where(visible, scores * factor, -jnp.inf)
        own = lax.dot_general(query, new_key, contract, preferred_element_type=jnp.float32)
        own = jnp.where(own_visible, own * factor, -jnp.inf)
        highest = jnp.maximum(
            jnp.max(scores, axis=-1, keepdims=True), jnp.max(own, axis=-1, keepdims=True)
        )
        scores = jnp.exp(scores - highest)
        own = jnp.exp(own - highest)
        total = jnp.sum(scores, axis=-1, keepdims=True) + jnp.sum(own, axis=-1, keepdims=True)
        mixed = jnp.dot(
            (scores / total).astype(jnp.bfloat16), values, preferred_element_type=jnp.float32
        ) + jnp.dot(
            (own / total).astype(jnp.bfloat16), new_value, preferred_element_type=jnp.float32
        )
        if result is None:
            result = mixed
        else:
            slot = lax.broadcasted_iota(jnp.int32, (count, 1), 0) // block
            source = (r - slot + GROUP_REQUESTS) % GROUP_REQUESTS
            result = jnp.where(source // parts == h, mixed, result)
    result = result.astype(jnp.bfloat16)
    for slot, out_ref in enumerate(out_refs):
        for head in range(quarter):
            first = slot * block + head * ROWS
            out_ref[:, head * HEAD_SIZE : (head + 1) * HEAD_SIZE] = result[first : first + ROWS]


def attend(place, query, pairs, cosine, sine, cache):
    shape = jax.ShapeDtypeStruct(query[0].shape, jnp.bfloat16)
    return pl.pallas_call(
        attend_kernel,
        in_specs=[pl.BlockSpec(memory_space=pltpu.SMEM)]
        + [pl.BlockSpec(memory_space=pltpu.VMEM)] * (len(query) + 3 + len(cache)),
        out_specs=[pl.BlockSpec(memory_space=pltpu.VMEM)] * GROUP_REQUESTS,
        out_shape=[shape] * GROUP_REQUESTS,
        compiler_params=params(),
        name="attend",
    )(place, *query, pairs, cosine, sine, *cache)


def output_kernel(place, *refs):
    x_refs, weight_ref, out_ref = refs[:GROUP_REQUESTS], refs[-2], refs[-1]
    blocks, rows, width = out_ref.shape
    order = [lax.rem(r - place[0] + GROUP_REQUESTS, GROUP_REQUESTS) for r in range(GROUP_REQUESTS)]
    x = jnp.stack([ref[...] for ref in x_refs])
    pieces = []
    for r in range(GROUP_REQUESTS):
        piece = x[0]
        for s in range(1, GROUP_REQUESTS):
            piece = jnp.where(order[r] == s, x[s], piece)
        pieces.append(piece)
    x = jnp.concatenate(pieces, axis=0)
    for i in range(blocks):
        columns = pl.ds(pl.multiple_of((2 * i + place[1]) * width, width), width)
        part = jnp.dot(x, weight_ref[:, columns], preferred_element_type=jnp.float32)
        for r in range(GROUP_REQUESTS):
            for step in range(STEPS):
                source = r * ROWS + step * SAMPLES
                target = (step * GROUP_REQUESTS + r) * SAMPLES
                out_ref[i, target : target + SAMPLES] = part[source : source + SAMPLES]


def outputs(place, mixed, weight, blocks):
    rows = GROUP_REQUESTS * ROWS
    width = weight.shape[1] // (2 * blocks)
    return pl.pallas_call(
        output_kernel,
        in_specs=[pl.BlockSpec(memory_space=pltpu.SMEM)]
        + [pl.BlockSpec(memory_space=pltpu.VMEM)] * (GROUP_REQUESTS + 1),
        out_specs=pl.BlockSpec(memory_space=pltpu.VMEM),
        out_shape=jax.ShapeDtypeStruct((blocks, rows, width), jnp.float32),
        compiler_params=params(),
        name="outputs",
    )(place, *mixed, weight)


def pieces_of(block):
    return [block[:, c : c + LANES] for c in range(0, block.shape[1], LANES)]


def encode(out_ref, pieces):
    rows = pieces[0].shape[0]
    peak = jnp.abs(pieces[0])
    for piece in pieces[1:]:
        peak = jnp.maximum(peak, jnp.abs(piece))
    peak = jnp.maximum(jnp.max(peak, axis=0, keepdims=True), 1e-30)
    exponent = jnp.floor(jnp.log2(peak)) - 14.0
    inverse = jnp.exp2(-exponent)
    for i, piece in enumerate(pieces):
        code = jnp.clip(jnp.floor(piece * inverse + 0.5), -32767.0, 32767.0)
        out_ref[i * rows : (i + 1) * rows] = code.astype(jnp.int32).astype(jnp.int16)
    out_ref[len(pieces) * rows :] = (
        jnp.broadcast_to(exponent, (TAIL, LANES)).astype(jnp.int32).astype(jnp.int16)
    )


def step_of(ref):
    tail = ref[ref.shape[0] - TAIL :].astype(jnp.int32).astype(jnp.float32)
    return jnp.exp2(tail[:1])


def decoded(ref, first, rows, step):
    return ref[pl.ds(first, rows)].astype(jnp.int32).astype(jnp.float32) * step


def fold_core_kernel(place, mine_ref, got_ref, kept_ref, *out_refs):
    subs = 1 + len(out_refs)
    for shift in range(subs):
        sub = lax.rem(place[0] + shift, subs)
        pieces = []
        for i in range(GROUP_REQUESTS):
            block = mine_ref[i * subs + sub] + got_ref[i * subs + sub]
            if shift == 0:
                kept_ref[i] = block
            pieces += pieces_of(block)
        if shift:
            encode(out_refs[shift - 1], pieces)


def fold_core(place, mine, got, subs):
    _, rows, width = mine.shape
    kept = jax.ShapeDtypeStruct((GROUP_REQUESTS, rows, width), jnp.float32)
    sent = jax.ShapeDtypeStruct(
        (GROUP_REQUESTS * width // LANES * rows + TAIL, LANES), jnp.int16
    )
    return pl.pallas_call(
        fold_core_kernel,
        in_specs=[pl.BlockSpec(memory_space=pltpu.SMEM)]
        + [pl.BlockSpec(memory_space=pltpu.VMEM)] * 2,
        out_specs=[pl.BlockSpec(memory_space=pltpu.VMEM)] * subs,
        out_shape=[kept] + [sent] * (subs - 1),
        compiler_params=params(),
        name="fold_core",
    )(place, mine, got)


def fold_sub_kernel(place, kept_ref, *refs):
    in_refs, total_ref, out_refs = (
        refs[:-GROUP_REQUESTS],
        refs[-GROUP_REQUESTS],
        refs[1 - GROUP_REQUESTS :],
    )
    _, rows, width = kept_ref.shape
    steps = [step_of(ref) for ref in in_refs]
    for shift in range(GROUP_REQUESTS):
        block = lax.rem(place[0] + shift, GROUP_REQUESTS)
        pieces = pieces_of(kept_ref[block])
        for c in range(len(pieces)):
            first = pl.multiple_of((block * len(pieces) + c) * rows, rows)
            for ref, step in zip(in_refs, steps):
                pieces[c] = pieces[c] + decoded(ref, first, rows, step)
        if shift:
            encode(out_refs[shift - 1], pieces)
        else:
            for c, piece in enumerate(pieces):
                total_ref[:, c * LANES : (c + 1) * LANES] = piece


def fold_sub(place, kept, parts):
    _, rows, width = kept.shape
    total = jax.ShapeDtypeStruct((rows, width), jnp.float32)
    sent = jax.ShapeDtypeStruct((width // LANES * rows + TAIL, LANES), jnp.int16)
    return pl.pallas_call(
        fold_sub_kernel,
        in_specs=[pl.BlockSpec(memory_space=pltpu.SMEM)]
        + [pl.BlockSpec(memory_space=pltpu.VMEM)] * (1 + len(parts)),
        out_specs=[pl.BlockSpec(memory_space=pltpu.VMEM)] * GROUP_REQUESTS,
        out_shape=[total] + [sent] * (GROUP_REQUESTS - 1),
        compiler_params=params(),
        name="fold_sub",
    )(place, kept, *parts)


def finish_kernel(rows_ref, total_ref, *refs):
    rows = rows_ref.shape[0]
    steps = [step_of(ref) for ref in refs[:-1]]
    for c in range(rows_ref.shape[1] // LANES):
        part = slice(c * LANES, (c + 1) * LANES)
        total = total_ref[:, part]
        for ref, step in zip(refs[:-1], steps):
            total = total + decoded(ref, c * rows, rows, step)
        refs[-1][:, part] = (total + rows_ref[:, part].astype(jnp.float32)).astype(jnp.bfloat16)


def finish(rows, total, parts):
    return pl.pallas_call(
        finish_kernel,
        in_specs=[pl.BlockSpec(memory_space=pltpu.VMEM)] * (2 + len(parts)),
        out_specs=pl.BlockSpec(memory_space=pltpu.VMEM),
        out_shape=jax.ShapeDtypeStruct(rows.shape, jnp.bfloat16),
        compiler_params=params(),
        name="finish",
    )(rows, total, *parts)


def passed(array, axis, shift):
    size = lax.axis_size(axis)
    return lax.ppermute(array, axis, [(i, (i + shift) % size) for i in range(size)])


def scalars(*values):
    return jnp.stack(values).astype(jnp.int32)


def shards(
    hidden,
    norm_gain,
    w_query,
    key_value_weight,
    w_output,
    prompt_cache_pages,
    per_page_scales,
    lengths,
    block_table,
):
    devices = lax.axis_size(DEVICES)
    targets = lax.axis_size(PLANE)
    subs = lax.axis_size("sub")
    chips = devices // 2
    heads = max(1, KEY_VALUE_HEADS // targets)
    device = lax.axis_index(DEVICES)
    request = lax.axis_index("req")
    sub = lax.axis_index("sub")
    core = lax.axis_index("section")
    spot = lax.axis_index(PLANE)
    group, member = device // GROUP_REQUESTS, device % GROUP_REQUESTS
    width = hidden.shape[2]

    rows = hidden.reshape(GROUP_REQUESTS * ROWS, width)
    mine = lax.all_to_all(
        jnp.broadcast_to(rows[None], (chips,) + rows.shape), CHIPS, 0, 0, tiled=True
    )
    other = passed(mine, "section", 1)

    place = scalars(request, spot, device * prompt_cache_pages.shape[0])
    send = used_pages(prompt_cache_pages, per_page_scales, block_table, place, targets, heads)
    cache = [send[0]]
    for s in range(1, targets):
        there = [(d, (d + s) % targets) for d in range(targets)]
        cache.append(lax.ppermute(send[s], PLANE, there))

    half = HEAD_SIZE // 2
    freqs = jnp.exp(
        -jnp.log(theta_base) * jnp.arange(half, dtype=jnp.float32) * (2.0 / HEAD_SIZE)
    )
    positions = (lengths[None, :] + jnp.arange(STEPS)[:, None]).astype(jnp.float32)
    angles = positions[..., None] * freqs
    cosine, sine = jnp.cos(angles), jnp.sin(angles)
    cosine = jnp.repeat(jnp.concatenate([cosine, cosine], axis=-1)[:, :, None], SAMPLES, axis=2)
    sine = jnp.repeat(jnp.concatenate([-sine, sine], axis=-1)[:, :, None], SAMPLES, axis=2)
    my_cosine = lax.dynamic_index_in_dim(cosine, request, 1, keepdims=False)
    my_sine = lax.dynamic_index_in_dim(sine, request, 1, keepdims=False)

    rows, gain, key_value_weight, w_query, w_output = staged(
        rows, norm_gain.reshape(devices, 1, width), key_value_weight, w_query, w_output
    )
    scale, pairs = scale_and_pairs(
        mine, other, rows, gain, key_value_weight, scalars(device), targets, heads
    )
    pairs = lax.all_to_all(
        pairs.reshape(devices, ROWS, heads * PAIR), DEVICES, 0, 0, tiled=True
    )

    query = queries(
        scalars(device, core),
        mine,
        other,
        scale,
        gain,
        w_query,
        cosine.reshape(-1, HEAD_SIZE),
        sine.reshape(-1, HEAD_SIZE),
    )
    got = []
    for s in range(GROUP_REQUESTS):
        there = [
            (d, (d % GROUP_REQUESTS + s) % GROUP_REQUESTS * targets + d // GROUP_REQUESTS)
            for d in range(devices)
        ]
        block = lax.dynamic_index_in_dim(
            query, (member + s) % GROUP_REQUESTS, 0, keepdims=False
        )
        got.append(lax.ppermute(block, DEVICES, there))

    my_length = lax.dynamic_index_in_dim(lengths, request, 0, keepdims=False)
    mixed = attend(
        scalars(request, my_length, spot),
        got,
        pairs,
        my_cosine.reshape(ROWS, HEAD_SIZE),
        my_sine.reshape(ROWS, HEAD_SIZE),
        cache,
    )
    got = []
    for s in range(GROUP_REQUESTS):
        back = [
            ((d % GROUP_REQUESTS + s) % GROUP_REQUESTS * targets + d // GROUP_REQUESTS, d)
            for d in range(devices)
        ]
        got.append(lax.ppermute(mixed[s], DEVICES, back))

    away = outputs(scalars(member, 1 - core), got, w_output, chips)
    arrived = passed(away, "section", 1)
    kept = outputs(scalars(member, core), got, w_output, chips)
    kept, *parts = fold_core(scalars(sub), kept, arrived, subs)
    parts = [passed(part, "sub", s + 1) for s, part in enumerate(parts)]
    total, *parts = fold_sub(scalars(request), kept, parts)
    parts = [passed(part, "req", s + 1) for s, part in enumerate(parts)]
    return finish(rows, total, parts).reshape(hidden.shape)


def solution(mesh):
    groups, tp, section = mesh.devices.shape
    finer = Mesh(
        mesh.devices.reshape(groups, GROUP_REQUESTS, tp // GROUP_REQUESTS, section),
        ("groups",) + DEVICES,
    )
    placed = (
        P(None, "groups", DEVICES),
        P(),
        P(None, DEVICES),
        P(DEVICES, None),
        P(DEVICES, None),
        P(("groups",) + DEVICES, None, None),
        P(("groups",) + DEVICES, None),
        P("groups"),
        P("groups", None),
    )
    return jax.shard_map(
        shards,
        mesh=finer,
        in_specs=placed,
        out_specs=P(None, "groups", DEVICES),
        check_vma=False,
    )
```

```python
import jax
import jax.numpy as jnp
from jax import lax
from jax.experimental import pallas as pl
from jax.experimental.pallas import tpu as pltpu
from jax.sharding import Mesh
from jax.sharding import PartitionSpec as P

QUERY_HEADS = 64
KEY_VALUE_HEADS = 8
HEAD_SIZE = 128
GROUP_REQUESTS = 4
SAMPLES = 8
PAGE_TOKENS = 16
STEPS = 2
ROWS = STEPS * SAMPLES
PAIR = 2 * HEAD_SIZE
LANES = 128
TAIL = 16
DEVICES = ("req", "sub", "section")

theta_base = 500000.0
eps_norm = 1e-05
VMEM = 16 * 2**20


def params(**more):
    return pltpu.CompilerParams(vmem_limit_bytes=VMEM, **more)


def whole_spec(shape):
    return pl.BlockSpec(shape, lambda *_: (0,) * len(shape))


def turn(vectors, cosine, sine):
    return vectors * cosine + pltpu.roll(vectors, HEAD_SIZE // 2, vectors.ndim - 1) * sine


def stage_kernel(*refs):
    half = (len(refs) - 1) // 2
    copies = [
        pltpu.make_async_copy(refs[i], refs[half + i], refs[-1].at[i]) for i in range(half)
    ]
    for copy in copies:
        copy.start()
    for copy in copies:
        copy.wait()


def staged(*arrays):
    size = sum(array.size * array.dtype.itemsize for array in arrays)
    return pl.pallas_call(
        stage_kernel,
        in_specs=[pl.BlockSpec(memory_space=pltpu.HBM)] * len(arrays),
        out_specs=[pl.BlockSpec(memory_space=pltpu.VMEM)] * len(arrays),
        out_shape=[jax.ShapeDtypeStruct(array.shape, array.dtype) for array in arrays],
        scratch_shapes=[pltpu.SemaphoreType.DMA((len(arrays),))],
        compiler_params=pltpu.CompilerParams(vmem_limit_bytes=30 * 2**20),
        cost_estimate=pl.CostEstimate(flops=0, bytes_accessed=2 * size, transcendentals=0),
        name="staged",
    )(*arrays)


def pages_kernel(table, place, scales, page_ref, *out_refs):
    e = pl.program_id(0)
    subs = len(out_refs)
    targets = 2 * subs
    page = table[place[0], e * targets + place[1]] - place[2]
    for shift, out_ref in enumerate(out_refs):
        half = lax.rem(place[1] // 2 + shift, subs) // (subs // 2)
        for z in range(GROUP_REQUESTS):
            head = 2 * lax.rem(place[0] + z, GROUP_REQUESTS) + half
            for part in range(2):
                c = head * 2 + part
                columns = pl.ds(pl.multiple_of(c * HEAD_SIZE, HEAD_SIZE), HEAD_SIZE)
                block = page_ref[0, :, columns].astype(jnp.float32)
                out_ref[z, :, part * HEAD_SIZE : (part + 1) * HEAD_SIZE] = (
                    block * scales[page, c]
                ).astype(jnp.bfloat16)


def used_pages(pages, scales, table, place, subs):
    targets = 2 * subs
    entries = table.shape[1] // targets
    return pl.pallas_call(
        pages_kernel,
        grid_spec=pltpu.PrefetchScalarGridSpec(
            num_scalar_prefetch=3,
            grid=(entries,),
            in_specs=[
                pl.BlockSpec(
                    (1, PAGE_TOKENS, pages.shape[2]),
                    lambda e, table, place, scales: (
                        table[place[0], e * targets + place[1]] - place[2],
                        0,
                        0,
                    ),
                )
            ],
            out_specs=[
                pl.BlockSpec((GROUP_REQUESTS, PAGE_TOKENS, PAIR), lambda e, *_: (0, e, 0))
            ]
            * subs,
        ),
        out_shape=[
            jax.ShapeDtypeStruct((GROUP_REQUESTS, entries * PAGE_TOKENS, PAIR), jnp.bfloat16)
        ]
        * subs,
        compiler_params=params(),
        name="used_pages",
    )(table, place, scales.astype(jnp.float32), pages)


def regroup_kernel(*refs):
    ins, outs = refs[:-GROUP_REQUESTS], refs[-GROUP_REQUESTS:]
    for z, out_ref in enumerate(outs):
        for j, ref in enumerate(ins):
            out_ref[j] = ref[z]


def regroup(parts):
    shape = jax.ShapeDtypeStruct((len(parts),) + parts[0].shape[1:], parts[0].dtype)
    return pl.pallas_call(
        regroup_kernel,
        in_specs=[pl.BlockSpec(memory_space=pltpu.VMEM)] * len(parts),
        out_specs=[pl.BlockSpec(memory_space=pltpu.VMEM)] * GROUP_REQUESTS,
        out_shape=[shape] * GROUP_REQUESTS,
        compiler_params=params(),
        name="regroup",
    )(*parts)


def pack_kernel(*refs):
    for i, ref in enumerate(refs[:-1]):
        refs[-1][i] = ref[...]


def pack(parts):
    return pl.pallas_call(
        pack_kernel,
        in_specs=[pl.BlockSpec(memory_space=pltpu.VMEM)] * len(parts),
        out_specs=pl.BlockSpec(memory_space=pltpu.VMEM),
        out_shape=jax.ShapeDtypeStruct((len(parts),) + parts[0].shape, parts[0].dtype),
        compiler_params=params(),
        name="pack",
    )(*parts)


def blocks_of(place, refs):
    request, sub, core = place[0], place[1], place[2]
    subs = len(refs) // 2
    for i, ref in enumerate(refs):
        from_core = core if i < subs else 1 - core
        from_sub = lax.rem(sub - i % subs + subs, subs)
        for z in range(GROUP_REQUESTS):
            from_request = lax.rem(request - z + GROUP_REQUESTS, GROUP_REQUESTS)
            yield ref, z, (from_request * subs + from_sub) * 2 + from_core


def pairs_kernel(place, rows_ref, gain_ref, weight_ref, *refs):
    subs = (len(refs) - 1) // 3
    x_refs, scale_ref, kept_ref, out_refs = (
        refs[: 2 * subs],
        refs[2 * subs],
        refs[2 * subs + 1],
        refs[2 * subs + 2 :],
    )
    request, sub, core = place[0], place[1], place[2]
    rows, width = rows_ref.shape
    total = jnp.zeros((rows, LANES), jnp.float32)
    for ref in x_refs:
        for z in range(GROUP_REQUESTS):
            for piece in pieces_of(ref[z].astype(jnp.float32)):
                total += piece * piece
    mean = jnp.sum(total, axis=-1, keepdims=True) / (2 * subs * GROUP_REQUESTS * width)
    scale = lax.rsqrt(mean + eps_norm)
    scale_ref[...] = jnp.broadcast_to(scale, scale_ref.shape)
    device = (request * subs + sub) * 2 + core
    x = rows_ref[...].astype(jnp.float32)
    mine = (x * scale * gain_ref[device]).astype(jnp.bfloat16)
    for shift in range(subs):
        half = lax.rem(sub + shift, subs) // (subs // 2)
        pieces = []
        for z in range(GROUP_REQUESTS):
            head = 2 * lax.rem(request + z, GROUP_REQUESTS) + half
            columns = pl.ds(pl.multiple_of(head * PAIR, PAIR), PAIR)
            part = jnp.dot(mine, weight_ref[:, columns], preferred_element_type=jnp.float32)
            if shift == 0:
                kept_ref[z] = part
            pieces += pieces_of(part)
        if shift:
            encode(out_refs[shift - 1], pieces)


def scale_and_pairs(place, rows, gain, weight, gathered):
    subs = len(gathered) // 2
    count = rows.shape[0]
    sent = jax.ShapeDtypeStruct((2 * GROUP_REQUESTS * count + TAIL, LANES), jnp.int16)
    shapes = [
        jax.ShapeDtypeStruct((count, LANES), jnp.float32),
        jax.ShapeDtypeStruct((GROUP_REQUESTS, count, PAIR), jnp.float32),
    ] + [sent] * (subs - 1)
    return pl.pallas_call(
        pairs_kernel,
        in_specs=[pl.BlockSpec(memory_space=pltpu.SMEM)]
        + [pl.BlockSpec(memory_space=pltpu.VMEM)] * (3 + len(gathered)),
        out_specs=[pl.BlockSpec(memory_space=pltpu.VMEM)] * len(shapes),
        out_shape=shapes,
        compiler_params=params(),
        name="scale_and_pairs",
    )(place, rows, gain, weight, *gathered)


def query_kernel(place, scale_ref, gain_ref, weight_ref, cos_ref, sin_ref, *refs):
    out_ref = refs[-1]
    _, rows, width = refs[0].shape
    columns = weight_ref.shape[1]
    scale = scale_ref[:, :1]
    total = jnp.zeros((rows, columns), jnp.float32)
    for ref, z, block in blocks_of(place, refs[:-1]):
        x = ref[z].astype(jnp.float32)
        x = (x * scale * gain_ref[block]).astype(jnp.bfloat16)
        depth = pl.ds(pl.multiple_of(block * width, width), width)
        total += jnp.dot(x, weight_ref[depth, :], preferred_element_type=jnp.float32)
    for head in range(columns // HEAD_SIZE):
        part = slice(head * HEAD_SIZE, (head + 1) * HEAD_SIZE)
        turned = turn(total[:, part], cos_ref[...], sin_ref[...])
        for r in range(GROUP_REQUESTS):
            first, second = r * SAMPLES, (GROUP_REQUESTS + r) * SAMPLES
            out_ref[r, :, part] = jnp.concatenate(
                [turned[first : first + SAMPLES], turned[second : second + SAMPLES]], axis=0
            ).astype(jnp.bfloat16)


def queries(place, scale, gain, weight, cosine, sine, gathered):
    columns = weight.shape[1]
    return pl.pallas_call(
        query_kernel,
        in_specs=[pl.BlockSpec(memory_space=pltpu.SMEM)]
        + [pl.BlockSpec(memory_space=pltpu.VMEM)] * (5 + len(gathered)),
        out_specs=pl.BlockSpec(memory_space=pltpu.VMEM),
        out_shape=jax.ShapeDtypeStruct((GROUP_REQUESTS, ROWS, columns), jnp.bfloat16),
        compiler_params=params(),
        name="queries",
    )(place, scale, gain, weight, cosine, sine, *gathered)


def attend_kernel(place, lengths, q_ref, mine_ref, other_ref, cos_ref, sin_ref, *refs):
    caches, out_ref, key_ref, value_ref = refs[:-3], refs[-3], refs[-2], refs[-1]
    request, sub, core = place[0], place[1], place[2]
    subs, span, _ = caches[0].shape
    targets = 2 * subs
    tokens = targets * span
    quarter = q_ref.shape[2] // HEAD_SIZE
    pair = mine_ref[...] + other_ref[...]
    key_ref[...] = turn(pair[:, :HEAD_SIZE], cos_ref[...], sin_ref[...])
    value_ref[...] = pair[:, HEAD_SIZE:]
    column = lax.broadcasted_iota(jnp.int32, (1, tokens), 1)
    source, inside = column // span, column % span
    from_core = jnp.where(source < subs, core, 1 - core)
    from_sub = (sub - source % subs + subs) % subs
    entry = inside // PAGE_TOKENS * targets + from_sub * 2 + from_core
    position = entry * PAGE_TOKENS + inside % PAGE_TOKENS
    count = quarter * ROWS
    row = lax.broadcasted_iota(jnp.int32, (count, ROWS), 0) % ROWS
    other = lax.broadcasted_iota(jnp.int32, (count, ROWS), 1)
    own_visible = (row % SAMPLES == other % SAMPLES) & (other // SAMPLES <= row // SAMPLES)
    factor = HEAD_SIZE ** (-0.5)
    contract = (((1,), (1,)), ((), ()))
    for z in range(GROUP_REQUESTS):
        r = lax.rem(request - z + GROUP_REQUESTS, GROUP_REQUESTS)
        fresh = [
            pl.ds(pl.multiple_of((step * GROUP_REQUESTS + r) * SAMPLES, SAMPLES), SAMPLES)
            for step in range(STEPS)
        ]
        new_key = jnp.concatenate([key_ref[rows] for rows in fresh], axis=0)
        new_value = jnp.concatenate([value_ref[rows] for rows in fresh], axis=0)
        new_key, new_value = new_key.astype(jnp.bfloat16), new_value.astype(jnp.bfloat16)
        pair_of_caches = (caches[z], caches[GROUP_REQUESTS + z])
        keys = jnp.concatenate(
            [c[j, :, :HEAD_SIZE] for c in pair_of_caches for j in range(subs)], axis=0
        )
        values = jnp.concatenate(
            [c[j, :, HEAD_SIZE:] for c in pair_of_caches for j in range(subs)], axis=0
        )
        query = jnp.concatenate(
            [q_ref[r, :, h * HEAD_SIZE : (h + 1) * HEAD_SIZE] for h in range(quarter)], axis=0
        )
        scores = lax.dot_general(query, keys, contract, preferred_element_type=jnp.float32)
        scores = jnp.where(position < lengths[r], scores * factor, -jnp.inf)
        own = lax.dot_general(query, new_key, contract, preferred_element_type=jnp.float32)
        own = jnp.where(own_visible, own * factor, -jnp.inf)
        highest = jnp.maximum(
            jnp.max(scores, axis=-1, keepdims=True), jnp.max(own, axis=-1, keepdims=True)
        )
        scores = jnp.exp(scores - highest)
        own = jnp.exp(own - highest)
        total = jnp.sum(scores, axis=-1, keepdims=True) + jnp.sum(own, axis=-1, keepdims=True)
        mixed = jnp.dot(
            (scores / total).astype(jnp.bfloat16), values, preferred_element_type=jnp.float32
        ) + jnp.dot(
            (own / total).astype(jnp.bfloat16), new_value, preferred_element_type=jnp.float32
        )
        mixed = mixed.astype(jnp.bfloat16)
        for h in range(quarter):
            out_ref[r, :, h * HEAD_SIZE : (h + 1) * HEAD_SIZE] = mixed[
                h * ROWS : (h + 1) * ROWS
            ]


def attend(place, lengths, query, mine, other, cosine, sine, caches):
    return pl.pallas_call(
        attend_kernel,
        in_specs=[pl.BlockSpec(memory_space=pltpu.SMEM)] * 2
        + [pl.BlockSpec(memory_space=pltpu.VMEM)] * (5 + len(caches)),
        out_specs=pl.BlockSpec(memory_space=pltpu.VMEM),
        out_shape=jax.ShapeDtypeStruct(query.shape, jnp.bfloat16),
        scratch_shapes=[pltpu.VMEM(cosine.shape, jnp.float32)] * 2,
        compiler_params=params(),
        name="attend",
    )(place, lengths, query, mine, other, cosine, sine, *caches)


def output_kernel(place, x_ref, weight_ref, out_ref):
    blocks, rows, width = out_ref.shape
    x = x_ref[...].reshape(rows, -1)
    for i in range(blocks):
        columns = pl.ds(pl.multiple_of((2 * i + place[0]) * width, width), width)
        part = jnp.dot(x, weight_ref[:, columns], preferred_element_type=jnp.float32)
        for r in range(GROUP_REQUESTS):
            for step in range(STEPS):
                source = r * ROWS + step * SAMPLES
                target = (step * GROUP_REQUESTS + r) * SAMPLES
                out_ref[i, target : target + SAMPLES] = part[source : source + SAMPLES]


def outputs(place, mixed, weight, blocks):
    rows = GROUP_REQUESTS * ROWS
    width = weight.shape[1] // (2 * blocks)
    return pl.pallas_call(
        output_kernel,
        in_specs=[pl.BlockSpec(memory_space=pltpu.SMEM)]
        + [pl.BlockSpec(memory_space=pltpu.VMEM)] * 2,
        out_specs=pl.BlockSpec(memory_space=pltpu.VMEM),
        out_shape=jax.ShapeDtypeStruct((blocks, rows, width), jnp.float32),
        compiler_params=params(),
        name="outputs",
    )(place, mixed, weight)


def pieces_of(block):
    return [block[:, c : c + LANES] for c in range(0, block.shape[1], LANES)]


def encode(out_ref, pieces):
    rows = pieces[0].shape[0]
    peak = jnp.abs(pieces[0])
    for piece in pieces[1:]:
        peak = jnp.maximum(peak, jnp.abs(piece))
    peak = jnp.maximum(jnp.max(peak, axis=0, keepdims=True), 1e-30)
    exponent = jnp.floor(jnp.log2(peak)) - 14.0
    inverse = jnp.exp2(-exponent)
    for i, piece in enumerate(pieces):
        code = jnp.clip(jnp.floor(piece * inverse + 0.5), -32767.0, 32767.0)
        out_ref[i * rows : (i + 1) * rows] = code.astype(jnp.int32).astype(jnp.int16)
    out_ref[len(pieces) * rows :] = (
        jnp.broadcast_to(exponent, (TAIL, LANES)).astype(jnp.int32).astype(jnp.int16)
    )


def step_of(ref):
    tail = ref[ref.shape[0] - TAIL :].astype(jnp.int32).astype(jnp.float32)
    return jnp.exp2(tail[:1])


def decoded(ref, first, rows, step):
    return ref[pl.ds(first, rows)].astype(jnp.int32).astype(jnp.float32) * step


def fold_core_kernel(place, mine_ref, got_ref, kept_ref, *out_refs):
    subs = 1 + len(out_refs)
    for shift in range(subs):
        sub = lax.rem(place[0] + shift, subs)
        pieces = []
        for i in range(GROUP_REQUESTS):
            block = mine_ref[i * subs + sub] + got_ref[i * subs + sub]
            if shift == 0:
                kept_ref[i] = block
            pieces += pieces_of(block)
        if shift:
            encode(out_refs[shift - 1], pieces)


def fold_core(place, mine, got, subs):
    _, rows, width = mine.shape
    kept = jax.ShapeDtypeStruct((GROUP_REQUESTS, rows, width), jnp.float32)
    sent = jax.ShapeDtypeStruct(
        (GROUP_REQUESTS * width // LANES * rows + TAIL, LANES), jnp.int16
    )
    return pl.pallas_call(
        fold_core_kernel,
        in_specs=[pl.BlockSpec(memory_space=pltpu.SMEM)]
        + [pl.BlockSpec(memory_space=pltpu.VMEM)] * 2,
        out_specs=[pl.BlockSpec(memory_space=pltpu.VMEM)] * subs,
        out_shape=[kept] + [sent] * (subs - 1),
        compiler_params=params(),
        name="fold_core",
    )(place, mine, got)


def fold_sub_kernel(place, kept_ref, *refs):
    in_refs, total_ref, out_refs = (
        refs[:-GROUP_REQUESTS],
        refs[-GROUP_REQUESTS],
        refs[1 - GROUP_REQUESTS :],
    )
    _, rows, width = kept_ref.shape
    steps = [step_of(ref) for ref in in_refs]
    for shift in range(GROUP_REQUESTS):
        block = lax.rem(place[0] + shift, GROUP_REQUESTS)
        pieces = pieces_of(kept_ref[block])
        for c in range(len(pieces)):
            first = pl.multiple_of((block * len(pieces) + c) * rows, rows)
            for ref, step in zip(in_refs, steps):
                pieces[c] = pieces[c] + decoded(ref, first, rows, step)
        if shift:
            encode(out_refs[shift - 1], pieces)
        else:
            for c, piece in enumerate(pieces):
                total_ref[:, c * LANES : (c + 1) * LANES] = piece


def fold_sub(place, kept, parts):
    _, rows, width = kept.shape
    total = jax.ShapeDtypeStruct((rows, width), jnp.float32)
    sent = jax.ShapeDtypeStruct((width // LANES * rows + TAIL, LANES), jnp.int16)
    return pl.pallas_call(
        fold_sub_kernel,
        in_specs=[pl.BlockSpec(memory_space=pltpu.SMEM)]
        + [pl.BlockSpec(memory_space=pltpu.VMEM)] * (1 + len(parts)),
        out_specs=[pl.BlockSpec(memory_space=pltpu.VMEM)] * GROUP_REQUESTS,
        out_shape=[total] + [sent] * (GROUP_REQUESTS - 1),
        compiler_params=params(),
        name="fold_sub",
    )(place, kept, *parts)


def fold_pairs_kernel(total_ref, *refs):
    rows = total_ref.shape[0]
    steps = [step_of(ref) for ref in refs[:-1]]
    for c in range(total_ref.shape[1] // LANES):
        part = slice(c * LANES, (c + 1) * LANES)
        total = total_ref[:, part]
        for ref, step in zip(refs[:-1], steps):
            total = total + decoded(ref, c * rows, rows, step)
        refs[-1][:, part] = total


def fold_pairs(total, parts):
    return pl.pallas_call(
        fold_pairs_kernel,
        in_specs=[pl.BlockSpec(memory_space=pltpu.VMEM)] * (1 + len(parts)),
        out_specs=pl.BlockSpec(memory_space=pltpu.VMEM),
        out_shape=jax.ShapeDtypeStruct(total.shape, jnp.float32),
        compiler_params=params(),
        name="fold_pairs",
    )(total, *parts)


def finish_kernel(rows_ref, total_ref, *refs):
    rows = rows_ref.shape[0]
    steps = [step_of(ref) for ref in refs[:-1]]
    for c in range(rows_ref.shape[1] // LANES):
        part = slice(c * LANES, (c + 1) * LANES)
        total = total_ref[:, part]
        for ref, step in zip(refs[:-1], steps):
            total = total + decoded(ref, c * rows, rows, step)
        refs[-1][:, part] = (total + rows_ref[:, part].astype(jnp.float32)).astype(jnp.bfloat16)


def finish(rows, total, parts):
    return pl.pallas_call(
        finish_kernel,
        in_specs=[pl.BlockSpec(memory_space=pltpu.VMEM)] * (2 + len(parts)),
        out_specs=pl.BlockSpec(memory_space=pltpu.VMEM),
        out_shape=jax.ShapeDtypeStruct(rows.shape, jnp.bfloat16),
        compiler_params=params(),
        name="finish",
    )(rows, total, *parts)


def passed(array, axis, shift):
    size = lax.axis_size(axis)
    return lax.ppermute(array, axis, [(i, (i + shift) % size) for i in range(size)])


def scalars(*values):
    return jnp.stack([jnp.asarray(value, jnp.int32) for value in values])


def shards(
    hidden,
    norm_gain,
    w_query,
    key_value_weight,
    w_output,
    prompt_cache_pages,
    per_page_scales,
    lengths,
    block_table,
):
    devices = lax.axis_size(DEVICES)
    subs = lax.axis_size("sub")
    device = lax.axis_index(DEVICES)
    request = lax.axis_index("req")
    sub = lax.axis_index("sub")
    core = lax.axis_index("section")
    width = hidden.shape[2]
    place = scalars(request, sub, core)

    rows = hidden.reshape(GROUP_REQUESTS * ROWS, width)
    column = pack([rows] + [passed(rows, "req", s) for s in range(1, GROUP_REQUESTS)])
    gathered = [column] + [passed(column, "sub", s) for s in range(1, subs)]
    gathered = gathered + [passed(part, "section", 1) for part in gathered]

    where = scalars(request, sub * 2 + core, device * prompt_cache_pages.shape[0])
    parts = used_pages(prompt_cache_pages, per_page_scales, block_table, where, subs)
    parts = [parts[0]] + [passed(parts[s], "sub", s) for s in range(1, subs)]
    parts = regroup(parts)
    caches = [parts[0]] + [passed(parts[s], "req", s) for s in range(1, GROUP_REQUESTS)]
    caches = caches + [passed(part, "section", 1) for part in caches]

    half = HEAD_SIZE // 2
    freqs = jnp.exp(
        -jnp.log(theta_base) * jnp.arange(half, dtype=jnp.float32) * (2.0 / HEAD_SIZE)
    )
    positions = (lengths[None, :] + jnp.arange(STEPS)[:, None]).astype(jnp.float32)
    angles = positions[..., None] * freqs
    cosine, sine = jnp.cos(angles), jnp.sin(angles)
    cosine = jnp.repeat(jnp.concatenate([cosine, cosine], axis=-1)[:, :, None], SAMPLES, axis=2)
    sine = jnp.repeat(jnp.concatenate([-sine, sine], axis=-1)[:, :, None], SAMPLES, axis=2)
    cosine = cosine.reshape(-1, HEAD_SIZE)
    sine = sine.reshape(-1, HEAD_SIZE)

    rows, gain, key_value_weight, w_query = staged(
        rows, norm_gain.reshape(devices, 1, width), key_value_weight, w_query
    )
    (w_output,) = staged(w_output)
    scale, kept, *parts = scale_and_pairs(place, rows, gain, key_value_weight, gathered)
    parts = [passed(part, "sub", s + 1) for s, part in enumerate(parts)]
    total, *parts = fold_sub(scalars(0), kept, parts)
    parts = [passed(part, "req", s + 1) for s, part in enumerate(parts)]
    mine = fold_pairs(total, parts)
    other = passed(mine, "section", 1)

    query = queries(place, scale, gain, w_query, cosine, sine, gathered)
    mixed = attend(
        place, lengths.astype(jnp.int32), query, mine, other, cosine, sine, caches
    )

    away = outputs(scalars(1 - core), mixed, w_output, devices // 2)
    arrived = passed(away, "section", 1)
    kept = outputs(scalars(core), mixed, w_output, devices // 2)
    kept, *parts = fold_core(scalars(sub), kept, arrived, subs)
    parts = [passed(part, "sub", s + 1) for s, part in enumerate(parts)]
    total, *parts = fold_sub(scalars(request), kept, parts)
    parts = [passed(part, "req", s + 1) for s, part in enumerate(parts)]
    return finish(rows, total, parts).reshape(hidden.shape)


def solution(mesh):
    groups, tp, section = mesh.devices.shape
    finer = Mesh(
        mesh.devices.reshape(groups, GROUP_REQUESTS, tp // GROUP_REQUESTS, section),
        ("groups",) + DEVICES,
    )
    placed = (
        P(None, "groups", DEVICES),
        P(),
        P(None, DEVICES),
        P(DEVICES, None),
        P(DEVICES, None),
        P(("groups",) + DEVICES, None, None),
        P(("groups",) + DEVICES, None),
        P("groups"),
        P("groups", None),
    )
    return jax.shard_map(
        shards,
        mesh=finer,
        in_specs=placed,
        out_specs=P(None, "groups", DEVICES),
        check_vma=False,
    )
```

```python
import functools

import jax
import jax.numpy as jnp
from jax import lax
from jax.experimental import pallas as pl
from jax.experimental.pallas import tpu as pltpu
from jax.sharding import Mesh
from jax.sharding import PartitionSpec as P

QUERY_HEADS = 64
KEY_VALUE_HEADS = 8
HEAD_SIZE = 128
GROUP_REQUESTS = 4
SAMPLES = 8
PAGE_TOKENS = 16
STEPS = 2
ROWS = STEPS * SAMPLES
PAIR = 2 * HEAD_SIZE
LANES = 128
HALVES = ((0, 3), (1, 2))
TAIL = 16
DEVICES = ("req", "sub", "section")

theta_base = 500000.0
eps_norm = 1e-05
VMEM = 16 * 2**20
LARGE_VMEM = 51 * 2**20


def params(**more):
    return pltpu.CompilerParams(vmem_limit_bytes=VMEM, **more)


def cost(*groups, flops=0):
    size = sum(array.size * array.dtype.itemsize for arrays in groups for array in arrays)
    return pl.CostEstimate(flops=flops, bytes_accessed=size, transcendentals=0)


def unread(arrays):
    return [pl.BlockSpec(memory_space=pl.ANY)] * len(arrays)


def turn(vectors, cosine, sine):
    return vectors * cosine + pltpu.roll(vectors, HEAD_SIZE // 2, vectors.ndim - 1) * sine


def stage_kernel(count, *refs):
    ins, outs, sems = refs[:count], refs[-1 - count : -1], refs[-1]
    copies = [pltpu.make_async_copy(ins[i], outs[i], sems.at[i]) for i in range(count)]
    for copy in copies:
        copy.start()
    for copy in copies:
        copy.wait()


def staged(arrays, after=()):
    count = len(arrays)
    return pl.pallas_call(
        functools.partial(stage_kernel, count),
        in_specs=[pl.BlockSpec(memory_space=pltpu.HBM)] * count + unread(after),
        out_specs=[pl.BlockSpec(memory_space=pltpu.VMEM)] * count,
        out_shape=[jax.ShapeDtypeStruct(array.shape, array.dtype) for array in arrays],
        scratch_shapes=[pltpu.SemaphoreType.DMA((count,))],
        compiler_params=params(),
        cost_estimate=cost(arrays, arrays),
        name="staged",
    )(*arrays, *after)


def pages_kernel(table, place, scales, page_ref, *out_refs):
    e = pl.program_id(0)
    subs = len(out_refs)
    targets = 2 * subs
    page = table[place[0], e * targets + place[1]] - place[2]
    for shift, out_ref in enumerate(out_refs):
        half = lax.rem(place[1] // 2 + shift, subs) // (subs // 2)
        for z in range(GROUP_REQUESTS):
            head = 2 * lax.rem(place[0] + z, GROUP_REQUESTS) + half
            for part in range(2):
                c = head * 2 + part
                columns = pl.ds(pl.multiple_of(c * HEAD_SIZE, HEAD_SIZE), HEAD_SIZE)
                block = page_ref[0, :, columns].astype(jnp.float32)
                out_ref[z, :, part * HEAD_SIZE : (part + 1) * HEAD_SIZE] = (
                    block * scales[page, c]
                ).astype(jnp.bfloat16)


def used_pages(pages, scales, table, place, subs):
    targets = 2 * subs
    entries = table.shape[1] // targets
    return pl.pallas_call(
        pages_kernel,
        grid_spec=pltpu.PrefetchScalarGridSpec(
            num_scalar_prefetch=3,
            grid=(entries,),
            in_specs=[
                pl.BlockSpec(
                    (1, PAGE_TOKENS, pages.shape[2]),
                    lambda e, table, place, scales: (
                        table[place[0], e * targets + place[1]] - place[2],
                        0,
                        0,
                    ),
                )
            ],
            out_specs=[
                pl.BlockSpec((GROUP_REQUESTS, PAGE_TOKENS, PAIR), lambda e, *_: (0, e, 0))
            ]
            * subs,
        ),
        out_shape=[
            jax.ShapeDtypeStruct((GROUP_REQUESTS, entries * PAGE_TOKENS, PAIR), jnp.bfloat16)
        ]
        * subs,
        compiler_params=params(),
        cost_estimate=pl.CostEstimate(
            flops=0, bytes_accessed=4 * entries * PAGE_TOKENS * pages.shape[2], transcendentals=0
        ),
        name="used_pages",
    )(table, place, scales.astype(jnp.float32), pages)


def regroup_kernel(*refs):
    ins, outs = refs[:-GROUP_REQUESTS], refs[-GROUP_REQUESTS:]
    for z, out_ref in enumerate(outs):
        for j, ref in enumerate(ins):
            out_ref[j] = ref[z]


def regroup(parts):
    shape = jax.ShapeDtypeStruct((len(parts),) + parts[0].shape[1:], parts[0].dtype)
    return pl.pallas_call(
        regroup_kernel,
        in_specs=[pl.BlockSpec(memory_space=pltpu.VMEM)] * len(parts),
        out_specs=[pl.BlockSpec(memory_space=pltpu.VMEM)] * GROUP_REQUESTS,
        out_shape=[shape] * GROUP_REQUESTS,
        compiler_params=params(),
        cost_estimate=cost(parts, parts),
        name="regroup",
    )(*parts)


def pack_kernel(*refs):
    for i, ref in enumerate(refs[:-1]):
        refs[-1][i] = ref[...]


def pack(parts):
    return pl.pallas_call(
        pack_kernel,
        in_specs=[pl.BlockSpec(memory_space=pltpu.VMEM)] * len(parts),
        out_specs=pl.BlockSpec(memory_space=pltpu.VMEM),
        out_shape=jax.ShapeDtypeStruct((len(parts),) + parts[0].shape, parts[0].dtype),
        compiler_params=params(),
        cost_estimate=cost(parts, parts),
        name="pack",
    )(*parts)


def blocks_of(place, refs):
    request, sub, core = place[0], place[1], place[2]
    subs = len(refs) // 2
    for i, ref in enumerate(refs):
        from_core = core if i < subs else 1 - core
        from_sub = lax.rem(sub - i % subs + subs, subs)
        for z in range(GROUP_REQUESTS):
            from_request = lax.rem(request - z + GROUP_REQUESTS, GROUP_REQUESTS)
            yield ref, z, (from_request * subs + from_sub) * 2 + from_core


def pairs_kernel(place, gain_ref, weight_ref, *refs):
    subs = (len(refs) - 1) // 3
    x_refs, scale_ref, kept_ref, out_refs = (
        refs[: 2 * subs],
        refs[2 * subs],
        refs[2 * subs + 1],
        refs[2 * subs + 2 :],
    )
    request, sub, core = place[0], place[1], place[2]
    _, rows, width = x_refs[0].shape
    total = jnp.zeros((rows, LANES), jnp.float32)
    for ref in x_refs:
        for z in range(GROUP_REQUESTS):
            for piece in pieces_of(ref[z].astype(jnp.float32)):
                total += piece * piece
    mean = jnp.sum(total, axis=-1, keepdims=True) / (2 * subs * GROUP_REQUESTS * width)
    scale = lax.rsqrt(mean + eps_norm)
    scale_ref[...] = jnp.broadcast_to(scale, scale_ref.shape)
    device = (request * subs + sub) * 2 + core
    x = x_refs[0][0].astype(jnp.float32)
    mine = (x * scale * gain_ref[device]).astype(jnp.bfloat16)
    for shift in range(subs):
        half = lax.rem(sub + shift, subs) // (subs // 2)
        pieces = []
        for z in range(GROUP_REQUESTS):
            head = 2 * lax.rem(request + z, GROUP_REQUESTS) + half
            columns = pl.ds(pl.multiple_of(head * PAIR, PAIR), PAIR)
            part = jnp.dot(mine, weight_ref[:, columns], preferred_element_type=jnp.float32)
            if shift == 0:
                kept_ref[z] = part
            pieces += pieces_of(part)
        if shift:
            encode(out_refs[shift - 1], pieces)


def scale_and_pairs(place, gain, weight, gathered):
    subs = len(gathered) // 2
    count = gathered[0].shape[1]
    sent = jax.ShapeDtypeStruct((2 * GROUP_REQUESTS * count + TAIL, LANES), jnp.int16)
    shapes = [
        jax.ShapeDtypeStruct((count, LANES), jnp.float32),
        jax.ShapeDtypeStruct((GROUP_REQUESTS, count, PAIR), jnp.float32),
    ] + [sent] * (subs - 1)
    return pl.pallas_call(
        pairs_kernel,
        in_specs=[pl.BlockSpec(memory_space=pltpu.SMEM)]
        + [pl.BlockSpec(memory_space=pltpu.VMEM)] * (2 + len(gathered)),
        out_specs=[pl.BlockSpec(memory_space=pltpu.VMEM)] * len(shapes),
        out_shape=shapes,
        compiler_params=params(),
        cost_estimate=cost(gathered, [weight], flops=2 * count * weight.size),
        name="scale_and_pairs",
    )(place, gain, weight, *gathered)


def query_kernel(place, scale_ref, gain_ref, weight_ref, cos_ref, sin_ref, *refs):
    x_refs, out_ref, held, sems = refs[:-3], refs[-3], refs[-2], refs[-1]
    _, rows, width = x_refs[0].shape
    columns = weight_ref.shape[1]
    blocks = list(blocks_of(place, x_refs))
    copies = []
    for i, (_, _, block) in enumerate(blocks):
        depth = pl.ds(pl.multiple_of(block * width, width), width)
        copies.append(pltpu.make_async_copy(weight_ref.at[depth], held.at[i], sems.at[i]))
    for copy in copies:
        copy.start()
    scale = scale_ref[:, :1]
    total = jnp.zeros((rows, columns), jnp.float32)
    for i, (ref, z, block) in enumerate(blocks):
        x = ref[z].astype(jnp.float32)
        x = (x * scale * gain_ref[block]).astype(jnp.bfloat16)
        copies[i].wait()
        total += jnp.dot(x, held[i], preferred_element_type=jnp.float32)
    for head in range(columns // HEAD_SIZE):
        part = slice(head * HEAD_SIZE, (head + 1) * HEAD_SIZE)
        turned = turn(total[:, part], cos_ref[...], sin_ref[...])
        for r in range(GROUP_REQUESTS):
            first, second = r * SAMPLES, (GROUP_REQUESTS + r) * SAMPLES
            out_ref[r, :, part] = jnp.concatenate(
                [turned[first : first + SAMPLES], turned[second : second + SAMPLES]], axis=0
            ).astype(jnp.bfloat16)


def queries(place, scale, gain, weight, cosine, sine, gathered):
    columns = weight.shape[1]
    _, rows, width = gathered[0].shape
    blocks = weight.shape[0] // width
    return pl.pallas_call(
        query_kernel,
        in_specs=[pl.BlockSpec(memory_space=pltpu.SMEM)]
        + [pl.BlockSpec(memory_space=pltpu.VMEM)] * 2
        + [pl.BlockSpec(memory_space=pltpu.HBM)]
        + [pl.BlockSpec(memory_space=pltpu.VMEM)] * (2 + len(gathered)),
        out_specs=pl.BlockSpec(memory_space=pltpu.VMEM),
        out_shape=jax.ShapeDtypeStruct((GROUP_REQUESTS, ROWS, columns), jnp.bfloat16),
        scratch_shapes=[
            pltpu.VMEM((blocks, width, columns), jnp.bfloat16),
            pltpu.SemaphoreType.DMA((blocks,)),
        ],
        compiler_params=pltpu.CompilerParams(vmem_limit_bytes=LARGE_VMEM),
        cost_estimate=cost([weight], flops=2 * rows * weight.size),
        name="queries",
    )(place, scale, gain, weight, cosine, sine, *gathered)


def attend_kernel(place, lengths, q_ref, mine_ref, other_ref, cos_ref, sin_ref, *refs):
    caches, out_ref, key_ref, value_ref = refs[:-3], refs[-3], refs[-2], refs[-1]
    request, sub, core = place[0], place[1], place[2]
    subs, span, _ = caches[0].shape
    targets = 2 * subs
    tokens = targets * span
    quarter = q_ref.shape[2] // HEAD_SIZE
    pair = mine_ref[...] + other_ref[...]
    key_ref[...] = turn(pair[:, :HEAD_SIZE], cos_ref[...], sin_ref[...])
    value_ref[...] = pair[:, HEAD_SIZE:]
    column = lax.broadcasted_iota(jnp.int32, (1, tokens), 1)
    source, inside = column // span, column % span
    from_core = jnp.where(source < subs, core, 1 - core)
    from_sub = (sub - source % subs + subs) % subs
    entry = inside // PAGE_TOKENS * targets + from_sub * 2 + from_core
    position = entry * PAGE_TOKENS + inside % PAGE_TOKENS
    count = quarter * ROWS
    row = lax.broadcasted_iota(jnp.int32, (count, ROWS), 0) % ROWS
    other = lax.broadcasted_iota(jnp.int32, (count, ROWS), 1)
    own_visible = (row % SAMPLES == other % SAMPLES) & (other // SAMPLES <= row // SAMPLES)
    factor = HEAD_SIZE ** (-0.5)
    contract = (((1,), (1,)), ((), ()))
    for z in range(GROUP_REQUESTS):
        r = lax.rem(request - z + GROUP_REQUESTS, GROUP_REQUESTS)
        fresh = [
            pl.ds(pl.multiple_of((step * GROUP_REQUESTS + r) * SAMPLES, SAMPLES), SAMPLES)
            for step in range(STEPS)
        ]
        new_key = jnp.concatenate([key_ref[rows] for rows in fresh], axis=0)
        new_value = jnp.concatenate([value_ref[rows] for rows in fresh], axis=0)
        new_key, new_value = new_key.astype(jnp.bfloat16), new_value.astype(jnp.bfloat16)
        pair_of_caches = (caches[z], caches[GROUP_REQUESTS + z])
        keys = jnp.concatenate(
            [c[j, :, :HEAD_SIZE] for c in pair_of_caches for j in range(subs)], axis=0
        )
        values = jnp.concatenate(
            [c[j, :, HEAD_SIZE:] for c in pair_of_caches for j in range(subs)], axis=0
        )
        query = jnp.concatenate(
            [q_ref[r, :, h * HEAD_SIZE : (h + 1) * HEAD_SIZE] for h in range(quarter)], axis=0
        )
        scores = lax.dot_general(query, keys, contract, preferred_element_type=jnp.float32)
        scores = jnp.where(position < lengths[r], scores * factor, -jnp.inf)
        own = lax.dot_general(query, new_key, contract, preferred_element_type=jnp.float32)
        own = jnp.where(own_visible, own * factor, -jnp.inf)
        highest = jnp.maximum(
            jnp.max(scores, axis=-1, keepdims=True), jnp.max(own, axis=-1, keepdims=True)
        )
        scores = jnp.exp(scores - highest)
        own = jnp.exp(own - highest)
        total = jnp.sum(scores, axis=-1, keepdims=True) + jnp.sum(own, axis=-1, keepdims=True)
        mixed = jnp.dot(
            (scores / total).astype(jnp.bfloat16), values, preferred_element_type=jnp.float32
        ) + jnp.dot(
            (own / total).astype(jnp.bfloat16), new_value, preferred_element_type=jnp.float32
        )
        mixed = mixed.astype(jnp.bfloat16)
        for h in range(quarter):
            out_ref[r, :, h * HEAD_SIZE : (h + 1) * HEAD_SIZE] = mixed[
                h * ROWS : (h + 1) * ROWS
            ]


def attend(place, lengths, query, mine, other, cosine, sine, caches):
    return pl.pallas_call(
        attend_kernel,
        in_specs=[pl.BlockSpec(memory_space=pltpu.SMEM)] * 2
        + [pl.BlockSpec(memory_space=pltpu.VMEM)] * (5 + len(caches)),
        out_specs=pl.BlockSpec(memory_space=pltpu.VMEM),
        out_shape=jax.ShapeDtypeStruct(query.shape, jnp.bfloat16),
        scratch_shapes=[pltpu.VMEM(cosine.shape, jnp.float32)] * 2,
        compiler_params=params(),
        cost_estimate=cost(caches, caches, caches, flops=2**28),
        name="attend",
    )(place, lengths, query, mine, other, cosine, sine, *caches)


def output_kernel(place, x_ref, weight_ref, out_ref):
    blocks, rows, width = out_ref.shape
    x = x_ref[...].reshape(rows, -1)
    for i in range(blocks):
        columns = pl.ds(pl.multiple_of((2 * i + place[0]) * width, width), width)
        part = jnp.dot(x, weight_ref[:, columns], preferred_element_type=jnp.float32)
        for r in range(GROUP_REQUESTS):
            for step in range(STEPS):
                source = r * ROWS + step * SAMPLES
                target = (step * GROUP_REQUESTS + r) * SAMPLES
                out_ref[i, target : target + SAMPLES] = part[source : source + SAMPLES]


def outputs(place, mixed, weight, blocks):
    rows = GROUP_REQUESTS * ROWS
    width = weight.shape[1] // (2 * blocks)
    return pl.pallas_call(
        output_kernel,
        in_specs=[pl.BlockSpec(memory_space=pltpu.SMEM)]
        + [pl.BlockSpec(memory_space=pltpu.VMEM)] * 2,
        out_specs=pl.BlockSpec(memory_space=pltpu.VMEM),
        out_shape=jax.ShapeDtypeStruct((blocks, rows, width), jnp.float32),
        compiler_params=params(),
        cost_estimate=cost([weight], flops=rows * weight.size),
        name="outputs",
    )(place, mixed, weight)


def pieces_of(block):
    return [block[:, c : c + LANES] for c in range(0, block.shape[1], LANES)]


def encode(out_ref, pieces):
    rows = pieces[0].shape[0]
    peak = jnp.abs(pieces[0])
    for piece in pieces[1:]:
        peak = jnp.maximum(peak, jnp.abs(piece))
    peak = jnp.maximum(jnp.max(peak, axis=0, keepdims=True), 1e-30)
    exponent = jnp.floor(jnp.log2(peak)) - 14.0
    inverse = jnp.exp2(-exponent)
    for i, piece in enumerate(pieces):
        code = jnp.clip(jnp.floor(piece * inverse + 0.5), -32767.0, 32767.0)
        out_ref[i * rows : (i + 1) * rows] = code.astype(jnp.int32).astype(jnp.int16)
    out_ref[len(pieces) * rows :] = (
        jnp.broadcast_to(exponent, (TAIL, LANES)).astype(jnp.int32).astype(jnp.int16)
    )


def step_of(ref):
    tail = ref[ref.shape[0] - TAIL :].astype(jnp.int32).astype(jnp.float32)
    return jnp.exp2(tail[:1])


def decoded(ref, first, rows, step):
    return ref[pl.ds(first, rows)].astype(jnp.int32).astype(jnp.float32) * step


def fold_core_kernel(place, mine_ref, got_ref, kept_ref, *out_refs):
    subs = 1 + len(out_refs) // 2
    for shift in range(subs):
        sub = lax.rem(place[1] + shift, subs)
        for half in range(2):
            pieces = []
            for z in HALVES[half]:
                block = lax.rem(place[0] + z, GROUP_REQUESTS) * subs + sub
                block = mine_ref[block] + got_ref[block]
                if shift == 0:
                    kept_ref[z] = block
                pieces += pieces_of(block)
            if shift:
                encode(out_refs[(shift - 1) * 2 + half], pieces)


def fold_core(place, mine, got, subs):
    _, rows, width = mine.shape
    kept = jax.ShapeDtypeStruct((GROUP_REQUESTS, rows, width), jnp.float32)
    sent = jax.ShapeDtypeStruct((2 * width // LANES * rows + TAIL, LANES), jnp.int16)
    return pl.pallas_call(
        fold_core_kernel,
        in_specs=[pl.BlockSpec(memory_space=pltpu.SMEM)]
        + [pl.BlockSpec(memory_space=pltpu.VMEM)] * 2,
        out_specs=[pl.BlockSpec(memory_space=pltpu.VMEM)] * (2 * subs - 1),
        out_shape=[kept] + [sent] * (2 * subs - 2),
        compiler_params=params(),
        cost_estimate=cost([mine, got]),
        name="fold_core",
    )(place, mine, got)


def fold_sub_kernel(order, count, kept_ref, *refs):
    in_refs, out_refs = refs[:count], refs[-len(order) :]
    _, rows, width = kept_ref.shape
    steps = [step_of(ref) for ref in in_refs]
    for i, (z, out_ref) in enumerate(zip(order, out_refs)):
        pieces = pieces_of(kept_ref[z])
        for c in range(len(pieces)):
            for ref, step in zip(in_refs, steps):
                first = (i * len(pieces) + c) * rows
                pieces[c] = pieces[c] + decoded(ref, first, rows, step)
        if z:
            encode(out_ref, pieces)
        else:
            for c, piece in enumerate(pieces):
                out_ref[:, c * LANES : (c + 1) * LANES] = piece


def fold_sub(order, kept, parts, after=()):
    _, rows, width = kept.shape
    total = jax.ShapeDtypeStruct((rows, width), jnp.float32)
    sent = jax.ShapeDtypeStruct((width // LANES * rows + TAIL, LANES), jnp.int16)
    return pl.pallas_call(
        functools.partial(fold_sub_kernel, order, len(parts)),
        in_specs=[pl.BlockSpec(memory_space=pltpu.VMEM)] * (1 + len(parts)) + unread(after),
        out_specs=[pl.BlockSpec(memory_space=pltpu.VMEM)] * len(order),
        out_shape=[sent if z else total for z in order],
        compiler_params=params(),
        cost_estimate=cost([kept], parts),
        name="fold_sub",
    )(kept, *parts, *after)


def fold_pairs_kernel(count, total_ref, *refs):
    rows = total_ref.shape[0]
    refs, out_ref = refs[:count], refs[-1]
    steps = [step_of(ref) for ref in refs]
    for c in range(total_ref.shape[1] // LANES):
        part = slice(c * LANES, (c + 1) * LANES)
        total = total_ref[:, part]
        for ref, step in zip(refs, steps):
            total = total + decoded(ref, c * rows, rows, step)
        out_ref[:, part] = total


def fold_pairs(total, parts, after=()):
    return pl.pallas_call(
        functools.partial(fold_pairs_kernel, len(parts)),
        in_specs=[pl.BlockSpec(memory_space=pltpu.VMEM)] * (1 + len(parts)) + unread(after),
        out_specs=pl.BlockSpec(memory_space=pltpu.VMEM),
        out_shape=jax.ShapeDtypeStruct(total.shape, jnp.float32),
        compiler_params=params(),
        cost_estimate=cost([total], parts),
        name="fold_pairs",
    )(total, *parts, *after)


def finish_kernel(rows_ref, total_ref, *refs):
    rows = total_ref.shape[0]
    steps = [step_of(ref) for ref in refs[:-1]]
    for c in range(total_ref.shape[1] // LANES):
        part = slice(c * LANES, (c + 1) * LANES)
        total = total_ref[:, part]
        for ref, step in zip(refs[:-1], steps):
            total = total + decoded(ref, c * rows, rows, step)
        refs[-1][:, part] = (total + rows_ref[0, :, part].astype(jnp.float32)).astype(
            jnp.bfloat16
        )


def finish(rows, total, parts):
    return pl.pallas_call(
        finish_kernel,
        in_specs=[pl.BlockSpec(memory_space=pltpu.VMEM)] * (2 + len(parts)),
        out_specs=pl.BlockSpec(memory_space=pltpu.VMEM),
        out_shape=jax.ShapeDtypeStruct(total.shape, jnp.bfloat16),
        compiler_params=params(),
        cost_estimate=cost([total], parts),
        name="finish",
    )(rows, total, *parts)


def passed(array, axis, shift):
    size = lax.axis_size(axis)
    return lax.ppermute(array, axis, [(i, (i + shift) % size) for i in range(size)])


def scalars(*values):
    return jnp.stack([jnp.asarray(value, jnp.int32) for value in values])


def shards(
    hidden,
    norm_gain,
    w_query,
    key_value_weight,
    w_output,
    prompt_cache_pages,
    per_page_scales,
    lengths,
    block_table,
):
    devices = lax.axis_size(DEVICES)
    subs = lax.axis_size("sub")
    device = lax.axis_index(DEVICES)
    request = lax.axis_index("req")
    sub = lax.axis_index("sub")
    core = lax.axis_index("section")
    width = hidden.shape[2]
    place = scalars(request, sub, core)

    rows = hidden.reshape(GROUP_REQUESTS * ROWS, width)
    column = [rows] + [passed(rows, "req", s) for s in range(1, GROUP_REQUESTS)]
    gathered = [pack(column)]
    for s in range(1, subs):
        gathered.append(pack([passed(part, "sub", s) for part in column]))
    gathered = gathered + [passed(part, "section", 1) for part in gathered]

    where = scalars(request, sub * 2 + core, device * prompt_cache_pages.shape[0])
    parts = used_pages(prompt_cache_pages, per_page_scales, block_table, where, subs)
    parts = [parts[0]] + [passed(parts[s], "sub", s) for s in range(1, subs)]
    parts = regroup(parts)
    caches = [parts[0]] + [passed(parts[s], "req", s) for s in range(1, GROUP_REQUESTS)]
    caches = caches + [passed(part, "section", 1) for part in caches]

    half = HEAD_SIZE // 2
    freqs = jnp.exp(
        -jnp.log(theta_base) * jnp.arange(half, dtype=jnp.float32) * (2.0 / HEAD_SIZE)
    )
    positions = (lengths[None, :] + jnp.arange(STEPS)[:, None]).astype(jnp.float32)
    angles = positions[..., None] * freqs
    cosine, sine = jnp.cos(angles), jnp.sin(angles)
    cosine = jnp.repeat(jnp.concatenate([cosine, cosine], axis=-1)[:, :, None], SAMPLES, axis=2)
    sine = jnp.repeat(jnp.concatenate([-sine, sine], axis=-1)[:, :, None], SAMPLES, axis=2)
    cosine = cosine.reshape(-1, HEAD_SIZE)
    sine = sine.reshape(-1, HEAD_SIZE)

    gain, key_value_weight = staged([norm_gain.reshape(devices, 1, width), key_value_weight])
    scale, kept, *parts = scale_and_pairs(place, gain, key_value_weight, gathered)
    parts = [passed(part, "sub", s + 1) for s, part in enumerate(parts)]
    query = queries(place, scale, gain, w_query, cosine, sine, gathered)
    total, *parts = fold_sub((0, 1, 2, 3), kept, parts, after=[query])
    parts = [passed(part, "req", s + 1) for s, part in enumerate(parts)]
    (w_output,) = staged([w_output], after=[query])
    mine = fold_pairs(total, parts, after=[w_output])
    other = passed(mine, "section", 1)

    mixed = attend(
        place, lengths.astype(jnp.int32), query, mine, other, cosine, sine, caches
    )

    away = outputs(scalars(1 - core), mixed, w_output, devices // 2)
    arrived = passed(away, "section", 1)
    kept = outputs(scalars(core), mixed, w_output, devices // 2)
    kept, *parts = fold_core(place, kept, arrived, subs)
    parts = [passed(part, "sub", i // 2 + 1) for i, part in enumerate(parts)]
    last = {}
    for half, order in enumerate(HALVES):
        last.update(zip(order, fold_sub(order, kept, parts[half::2])))
    parts = [passed(last[s], "req", s) for s in range(1, GROUP_REQUESTS)]
    return finish(gathered[0], last[0], parts).reshape(hidden.shape)


def solution(mesh):
    groups, tp, section = mesh.devices.shape
    finer = Mesh(
        mesh.devices.reshape(groups, GROUP_REQUESTS, tp // GROUP_REQUESTS, section),
        ("groups",) + DEVICES,
    )
    placed = (
        P(None, "groups", DEVICES),
        P(),
        P(None, DEVICES),
        P(DEVICES, None),
        P(DEVICES, None),
        P(("groups",) + DEVICES, None, None),
        P(("groups",) + DEVICES, None),
        P("groups"),
        P("groups", None),
    )
    return jax.shard_map(
        shards,
        mesh=finer,
        in_specs=placed,
        out_specs=P(None, "groups", DEVICES),
        check_vma=False,
    )
```

```python
import functools

import jax
import jax.numpy as jnp
from jax import lax
from jax.experimental import pallas as pl
from jax.experimental.pallas import tpu as pltpu
from jax.sharding import Mesh
from jax.sharding import PartitionSpec as P

QUERY_HEADS = 64
KEY_VALUE_HEADS = 8
HEAD_SIZE = 128
GROUP_REQUESTS = 4
SAMPLES = 8
PAGE_TOKENS = 16
STEPS = 2
ROWS = STEPS * SAMPLES
PAIR = 2 * HEAD_SIZE
LANES = 128
HALVES = ((0, 3), (1, 2))
TAIL = 16
DEVICES = ("req", "sub", "section")

theta_base = 500000.0
eps_norm = 1e-05
VMEM = 16 * 2**20
LARGE_VMEM = 51 * 2**20


def params(**more):
    return pltpu.CompilerParams(vmem_limit_bytes=VMEM, **more)


def cost(*groups, flops=0):
    size = sum(array.size * array.dtype.itemsize for arrays in groups for array in arrays)
    return pl.CostEstimate(flops=flops, bytes_accessed=size, transcendentals=0)


def unread(arrays):
    return [pl.BlockSpec(memory_space=pl.ANY)] * len(arrays)


def turn(vectors, cosine, sine):
    return vectors * cosine + pltpu.roll(vectors, HEAD_SIZE // 2, vectors.ndim - 1) * sine


def stage_kernel(count, *refs):
    ins, outs, sems = refs[:count], refs[-2 - count : -1], refs[-1]
    copies = [pltpu.make_async_copy(ins[i], outs[i], sems.at[i]) for i in range(count)]
    for copy in copies:
        copy.start()
    outs[-1][...] = jnp.zeros_like(outs[-1])
    for copy in copies:
        copy.wait()


def staged(arrays, after=()):
    count = len(arrays)
    token = jax.ShapeDtypeStruct((8, LANES), jnp.float32)
    return pl.pallas_call(
        functools.partial(stage_kernel, count),
        in_specs=[pl.BlockSpec(memory_space=pltpu.HBM)] * count + unread(after),
        out_specs=[pl.BlockSpec(memory_space=pltpu.VMEM)] * (count + 1),
        out_shape=[jax.ShapeDtypeStruct(array.shape, array.dtype) for array in arrays] + [token],
        scratch_shapes=[pltpu.SemaphoreType.DMA((count,))],
        compiler_params=params(),
        cost_estimate=cost(arrays, arrays),
        name="staged",
    )(*arrays, *after)


def gate_kernel(*refs):
    pass


def gate(arrays, after):
    count = len(arrays)
    return pl.pallas_call(
        gate_kernel,
        in_specs=[pl.BlockSpec(memory_space=pl.ANY)] * count + unread(after),
        out_specs=[pl.BlockSpec(memory_space=pl.ANY)] * count,
        out_shape=[jax.ShapeDtypeStruct(array.shape, array.dtype) for array in arrays],
        input_output_aliases={i: i for i in range(count)},
        compiler_params=params(),
        name="gate",
    )(*arrays, *after)


def pages_kernel(table, place, scales, page_ref, *out_refs):
    e = pl.program_id(0)
    subs = out_refs[0].shape[0]
    targets = 2 * subs
    page = table[place[0], e * targets + place[1]] - place[2]
    for z, out_ref in enumerate(out_refs):
        for j in range(subs):
            half = (place[1] // 2 ^ j) // (subs // 2)
            head = 2 * (place[0] ^ z) + half
            for part in range(2):
                c = head * 2 + part
                columns = pl.ds(pl.multiple_of(c * HEAD_SIZE, HEAD_SIZE), HEAD_SIZE)
                block = page_ref[0, :, columns].astype(jnp.float32)
                out_ref[j, :, part * HEAD_SIZE : (part + 1) * HEAD_SIZE] = (
                    block * scales[page, c]
                ).astype(jnp.bfloat16)


def used_pages(pages, scales, table, place, subs):
    targets = 2 * subs
    entries = table.shape[1] // targets
    shape = jax.ShapeDtypeStruct((subs, entries * PAGE_TOKENS, PAIR), jnp.bfloat16)
    return pl.pallas_call(
        pages_kernel,
        grid_spec=pltpu.PrefetchScalarGridSpec(
            num_scalar_prefetch=3,
            grid=(entries,),
            in_specs=[
                pl.BlockSpec(
                    (1, PAGE_TOKENS, pages.shape[2]),
                    lambda e, table, place, scales: (
                        table[place[0], e * targets + place[1]] - place[2],
                        0,
                        0,
                    ),
                )
            ],
            out_specs=[pl.BlockSpec((subs, PAGE_TOKENS, PAIR), lambda e, *_: (0, e, 0))]
            * GROUP_REQUESTS,
        ),
        out_shape=[shape] * GROUP_REQUESTS,
        compiler_params=params(),
        cost_estimate=pl.CostEstimate(
            flops=0, bytes_accessed=4 * entries * PAGE_TOKENS * pages.shape[2], transcendentals=0
        ),
        name="used_pages",
    )(table, place, scales.astype(jnp.float32), pages)


def regroup_kernel(*refs):
    ins, outs = refs[:GROUP_REQUESTS], refs[-refs[0].shape[0] :]
    for j, out_ref in enumerate(outs):
        for z, ref in enumerate(ins):
            out_ref[z] = ref[j]


def regroup(parts, after=()):
    subs = parts[0].shape[0]
    shape = jax.ShapeDtypeStruct((len(parts),) + parts[0].shape[1:], parts[0].dtype)
    return pl.pallas_call(
        regroup_kernel,
        in_specs=[pl.BlockSpec(memory_space=pltpu.VMEM)] * len(parts) + unread(after),
        out_specs=[pl.BlockSpec(memory_space=pltpu.VMEM)] * subs,
        out_shape=[shape] * subs,
        compiler_params=params(),
        cost_estimate=cost(parts, parts),
        name="regroup",
    )(*parts, *after)


def pack_kernel(*refs):
    for i in range(refs[-1].shape[0]):
        refs[-1][i] = refs[i][...]


def pack(parts):
    return pl.pallas_call(
        pack_kernel,
        in_specs=[pl.BlockSpec(memory_space=pltpu.VMEM)] * len(parts),
        out_specs=pl.BlockSpec(memory_space=pltpu.VMEM),
        out_shape=jax.ShapeDtypeStruct((len(parts),) + parts[0].shape, parts[0].dtype),
        compiler_params=params(),
        cost_estimate=cost(parts, parts),
        name="pack",
    )(*parts)


def blocks_of(place, refs):
    request, sub, core = place[0], place[1], place[2]
    subs = len(refs) // 2
    for i, ref in enumerate(refs):
        from_core = core if i < subs else 1 - core
        for z in range(GROUP_REQUESTS):
            yield ref, z, ((request ^ z) * subs + (sub ^ i % subs)) * 2 + from_core


def pairs_kernel(place, gain_ref, weight_ref, *refs):
    subs = (len(refs) - 1) // 3
    x_refs, scale_ref, kept_ref, out_refs = (
        refs[: 2 * subs],
        refs[2 * subs],
        refs[2 * subs + 1],
        refs[2 * subs + 2 :],
    )
    request, sub, core = place[0], place[1], place[2]
    _, rows, width = x_refs[0].shape
    total = jnp.zeros((rows, LANES), jnp.float32)
    for ref in x_refs:
        for z in range(GROUP_REQUESTS):
            for piece in pieces_of(ref[z].astype(jnp.float32)):
                total += piece * piece
    mean = jnp.sum(total, axis=-1, keepdims=True) / (2 * subs * GROUP_REQUESTS * width)
    scale = lax.rsqrt(mean + eps_norm)
    scale_ref[...] = jnp.broadcast_to(scale, scale_ref.shape)
    device = (request * subs + sub) * 2 + core
    x = x_refs[0][0].astype(jnp.float32)
    mine = (x * scale * gain_ref[device]).astype(jnp.bfloat16)
    for shift in range(subs):
        half = (sub ^ shift) // (subs // 2)
        pieces = []
        for z in range(GROUP_REQUESTS):
            head = 2 * (request ^ z) + half
            columns = pl.ds(pl.multiple_of(head * PAIR, PAIR), PAIR)
            part = jnp.dot(mine, weight_ref[:, columns], preferred_element_type=jnp.float32)
            if shift == 0:
                kept_ref[z] = part
            pieces += pieces_of(part)
        if shift:
            encode(out_refs[shift - 1], pieces)


def scale_and_pairs(place, gain, weight, gathered):
    subs = len(gathered) // 2
    count = gathered[0].shape[1]
    sent = jax.ShapeDtypeStruct((2 * GROUP_REQUESTS * count + TAIL, LANES), jnp.int16)
    shapes = [
        jax.ShapeDtypeStruct((count, LANES), jnp.float32),
        jax.ShapeDtypeStruct((GROUP_REQUESTS, count, PAIR), jnp.float32),
    ] + [sent] * (subs - 1)
    return pl.pallas_call(
        pairs_kernel,
        in_specs=[pl.BlockSpec(memory_space=pltpu.SMEM)]
        + [pl.BlockSpec(memory_space=pltpu.VMEM)] * (2 + len(gathered)),
        out_specs=[pl.BlockSpec(memory_space=pltpu.VMEM)] * len(shapes),
        out_shape=shapes,
        compiler_params=params(),
        cost_estimate=cost(gathered, [weight], flops=2 * count * weight.size),
        name="scale_and_pairs",
    )(place, gain, weight, *gathered)


def query_kernel(place, scale_ref, gain_ref, weight_ref, cos_ref, sin_ref, *refs):
    x_refs, out_ref, held, sems = refs[:-3], refs[-3], refs[-2], refs[-1]
    _, rows, width = x_refs[0].shape
    columns = weight_ref.shape[1]
    blocks = list(blocks_of(place, x_refs))
    copies = []
    for i, (_, _, block) in enumerate(blocks):
        depth = pl.ds(pl.multiple_of(block * width, width), width)
        copies.append(pltpu.make_async_copy(weight_ref.at[depth], held.at[i], sems.at[i]))
    for copy in copies:
        copy.start()
    scale = scale_ref[:, :1]
    total = jnp.zeros((rows, columns), jnp.float32)
    for i, (ref, z, block) in enumerate(blocks):
        x = ref[z].astype(jnp.float32)
        x = (x * scale * gain_ref[block]).astype(jnp.bfloat16)
        copies[i].wait()
        total += jnp.dot(x, held[i], preferred_element_type=jnp.float32)
    for head in range(columns // HEAD_SIZE):
        part = slice(head * HEAD_SIZE, (head + 1) * HEAD_SIZE)
        turned = turn(total[:, part], cos_ref[...], sin_ref[...])
        for r in range(GROUP_REQUESTS):
            first, second = r * SAMPLES, (GROUP_REQUESTS + r) * SAMPLES
            out_ref[r, :, part] = jnp.concatenate(
                [turned[first : first + SAMPLES], turned[second : second + SAMPLES]], axis=0
            ).astype(jnp.bfloat16)


def queries(place, scale, gain, weight, cosine, sine, gathered):
    columns = weight.shape[1]
    _, rows, width = gathered[0].shape
    blocks = weight.shape[0] // width
    return pl.pallas_call(
        query_kernel,
        in_specs=[pl.BlockSpec(memory_space=pltpu.SMEM)]
        + [pl.BlockSpec(memory_space=pltpu.VMEM)] * 2
        + [pl.BlockSpec(memory_space=pltpu.HBM)]
        + [pl.BlockSpec(memory_space=pltpu.VMEM)] * (2 + len(gathered)),
        out_specs=pl.BlockSpec(memory_space=pltpu.VMEM),
        out_shape=jax.ShapeDtypeStruct((GROUP_REQUESTS, ROWS, columns), jnp.bfloat16),
        scratch_shapes=[
            pltpu.VMEM((blocks, width, columns), jnp.bfloat16),
            pltpu.SemaphoreType.DMA((blocks,)),
        ],
        compiler_params=pltpu.CompilerParams(vmem_limit_bytes=LARGE_VMEM),
        cost_estimate=cost([weight], flops=2 * rows * weight.size),
        name="queries",
    )(place, scale, gain, weight, cosine, sine, *gathered)


def attend_kernel(place, lengths, q_ref, mine_ref, other_ref, cos_ref, sin_ref, *refs):
    caches, out_ref, key_ref, value_ref = refs[:-3], refs[-3], refs[-2], refs[-1]
    request, sub, core = place[0], place[1], place[2]
    subs, span = len(caches) // 2, caches[0].shape[1]
    targets = 2 * subs
    tokens = targets * span
    quarter = q_ref.shape[2] // HEAD_SIZE
    pair = mine_ref[...] + other_ref[...]
    key_ref[...] = turn(pair[:, :HEAD_SIZE], cos_ref[...], sin_ref[...])
    value_ref[...] = pair[:, HEAD_SIZE:]
    column = lax.broadcasted_iota(jnp.int32, (1, tokens), 1)
    source, inside = column // span, column % span
    from_core = jnp.where(source < subs, core, 1 - core)
    from_sub = sub ^ source % subs
    entry = inside // PAGE_TOKENS * targets + from_sub * 2 + from_core
    position = entry * PAGE_TOKENS + inside % PAGE_TOKENS
    count = quarter * ROWS
    row = lax.broadcasted_iota(jnp.int32, (count, ROWS), 0) % ROWS
    other = lax.broadcasted_iota(jnp.int32, (count, ROWS), 1)
    own_visible = (row % SAMPLES == other % SAMPLES) & (other // SAMPLES <= row // SAMPLES)
    factor = HEAD_SIZE ** (-0.5)
    contract = (((1,), (1,)), ((), ()))
    for z in range(GROUP_REQUESTS):
        r = request ^ z
        fresh = [
            pl.ds(pl.multiple_of((step * GROUP_REQUESTS + r) * SAMPLES, SAMPLES), SAMPLES)
            for step in range(STEPS)
        ]
        new_key = jnp.concatenate([key_ref[rows] for rows in fresh], axis=0)
        new_value = jnp.concatenate([value_ref[rows] for rows in fresh], axis=0)
        new_key, new_value = new_key.astype(jnp.bfloat16), new_value.astype(jnp.bfloat16)
        keys = jnp.concatenate([ref[z, :, :HEAD_SIZE] for ref in caches], axis=0)
        values = jnp.concatenate([ref[z, :, HEAD_SIZE:] for ref in caches], axis=0)
        query = jnp.concatenate(
            [q_ref[r, :, h * HEAD_SIZE : (h + 1) * HEAD_SIZE] for h in range(quarter)], axis=0
        )
        scores = lax.dot_general(query, keys, contract, preferred_element_type=jnp.float32)
        scores = jnp.where(position < lengths[r], scores * factor, -jnp.inf)
        own = lax.dot_general(query, new_key, contract, preferred_element_type=jnp.float32)
        own = jnp.where(own_visible, own * factor, -jnp.inf)
        highest = jnp.maximum(
            jnp.max(scores, axis=-1, keepdims=True), jnp.max(own, axis=-1, keepdims=True)
        )
        scores = jnp.exp(scores - highest)
        own = jnp.exp(own - highest)
        total = jnp.sum(scores, axis=-1, keepdims=True) + jnp.sum(own, axis=-1, keepdims=True)
        mixed = jnp.dot(
            (scores / total).astype(jnp.bfloat16), values, preferred_element_type=jnp.float32
        ) + jnp.dot(
            (own / total).astype(jnp.bfloat16), new_value, preferred_element_type=jnp.float32
        )
        mixed = mixed.astype(jnp.bfloat16)
        for h in range(quarter):
            out_ref[r, :, h * HEAD_SIZE : (h + 1) * HEAD_SIZE] = mixed[
                h * ROWS : (h + 1) * ROWS
            ]


def attend(place, lengths, query, mine, other, cosine, sine, caches):
    return pl.pallas_call(
        attend_kernel,
        in_specs=[pl.BlockSpec(memory_space=pltpu.SMEM)] * 2
        + [pl.BlockSpec(memory_space=pltpu.VMEM)] * (5 + len(caches)),
        out_specs=pl.BlockSpec(memory_space=pltpu.VMEM),
        out_shape=jax.ShapeDtypeStruct(query.shape, jnp.bfloat16),
        scratch_shapes=[pltpu.VMEM(cosine.shape, jnp.float32)] * 2,
        compiler_params=params(),
        cost_estimate=cost(caches, caches, caches, flops=2**28),
        name="attend",
    )(place, lengths, query, mine, other, cosine, sine, *caches)


def output_kernel(place, x_ref, weight_ref, out_ref):
    blocks, rows, width = out_ref.shape
    x = x_ref[...].reshape(rows, -1)
    for i in range(blocks):
        columns = pl.ds(pl.multiple_of((2 * i + place[0]) * width, width), width)
        part = jnp.dot(x, weight_ref[:, columns], preferred_element_type=jnp.float32)
        for r in range(GROUP_REQUESTS):
            for step in range(STEPS):
                source = r * ROWS + step * SAMPLES
                target = (step * GROUP_REQUESTS + r) * SAMPLES
                out_ref[i, target : target + SAMPLES] = part[source : source + SAMPLES]


def outputs(place, mixed, weight, blocks):
    rows = GROUP_REQUESTS * ROWS
    width = weight.shape[1] // (2 * blocks)
    return pl.pallas_call(
        output_kernel,
        in_specs=[pl.BlockSpec(memory_space=pltpu.SMEM)]
        + [pl.BlockSpec(memory_space=pltpu.VMEM)] * 2,
        out_specs=pl.BlockSpec(memory_space=pltpu.VMEM),
        out_shape=jax.ShapeDtypeStruct((blocks, rows, width), jnp.float32),
        compiler_params=params(),
        cost_estimate=cost([weight], flops=rows * weight.size),
        name="outputs",
    )(place, mixed, weight)


def pieces_of(block):
    return [block[:, c : c + LANES] for c in range(0, block.shape[1], LANES)]


def encode(out_ref, pieces):
    rows = pieces[0].shape[0]
    peak = jnp.abs(pieces[0])
    for piece in pieces[1:]:
        peak = jnp.maximum(peak, jnp.abs(piece))
    peak = jnp.maximum(jnp.max(peak, axis=0, keepdims=True), 1e-30)
    exponent = jnp.floor(jnp.log2(peak)) - 14.0
    inverse = jnp.exp2(-exponent)
    for i, piece in enumerate(pieces):
        code = jnp.clip(jnp.floor(piece * inverse + 0.5), -32767.0, 32767.0)
        out_ref[i * rows : (i + 1) * rows] = code.astype(jnp.int32).astype(jnp.int16)
    out_ref[len(pieces) * rows :] = (
        jnp.broadcast_to(exponent, (TAIL, LANES)).astype(jnp.int32).astype(jnp.int16)
    )


def step_of(ref):
    tail = ref[ref.shape[0] - TAIL :].astype(jnp.int32).astype(jnp.float32)
    return jnp.exp2(tail[:1])


def decoded(ref, first, rows, step):
    return ref[pl.ds(first, rows)].astype(jnp.int32).astype(jnp.float32) * step


def fold_core_kernel(place, mine_ref, got_ref, kept_ref, *out_refs):
    subs = 1 + len(out_refs) // 2
    for shift in range(subs):
        sub = place[1] ^ shift
        for half in range(2):
            pieces = []
            for z in HALVES[half]:
                block = (place[0] ^ z) * subs + sub
                block = mine_ref[block] + got_ref[block]
                if shift == 0:
                    kept_ref[z] = block
                pieces += pieces_of(block)
            if shift:
                encode(out_refs[(shift - 1) * 2 + half], pieces)


def fold_core(place, mine, got, subs):
    _, rows, width = mine.shape
    kept = jax.ShapeDtypeStruct((GROUP_REQUESTS, rows, width), jnp.float32)
    sent = jax.ShapeDtypeStruct((2 * width // LANES * rows + TAIL, LANES), jnp.int16)
    return pl.pallas_call(
        fold_core_kernel,
        in_specs=[pl.BlockSpec(memory_space=pltpu.SMEM)]
        + [pl.BlockSpec(memory_space=pltpu.VMEM)] * 2,
        out_specs=[pl.BlockSpec(memory_space=pltpu.VMEM)] * (2 * subs - 1),
        out_shape=[kept] + [sent] * (2 * subs - 2),
        compiler_params=params(),
        cost_estimate=cost([mine, got]),
        name="fold_core",
    )(place, mine, got)


def fold_sub_kernel(order, count, kept_ref, *refs):
    in_refs, out_refs = refs[:count], refs[-len(order) :]
    _, rows, width = kept_ref.shape
    steps = [step_of(ref) for ref in in_refs]
    for i, (z, out_ref) in enumerate(zip(order, out_refs)):
        pieces = pieces_of(kept_ref[z])
        for c in range(len(pieces)):
            for ref, step in zip(in_refs, steps):
                first = (i * len(pieces) + c) * rows
                pieces[c] = pieces[c] + decoded(ref, first, rows, step)
        if z:
            encode(out_ref, pieces)
        else:
            for c, piece in enumerate(pieces):
                out_ref[:, c * LANES : (c + 1) * LANES] = piece


def fold_sub(order, kept, parts, after=()):
    _, rows, width = kept.shape
    total = jax.ShapeDtypeStruct((rows, width), jnp.float32)
    sent = jax.ShapeDtypeStruct((width // LANES * rows + TAIL, LANES), jnp.int16)
    return pl.pallas_call(
        functools.partial(fold_sub_kernel, order, len(parts)),
        in_specs=[pl.BlockSpec(memory_space=pltpu.VMEM)] * (1 + len(parts)) + unread(after),
        out_specs=[pl.BlockSpec(memory_space=pltpu.VMEM)] * len(order),
        out_shape=[sent if z else total for z in order],
        compiler_params=params(),
        cost_estimate=cost([kept], parts),
        name="fold_sub",
    )(kept, *parts, *after)


def fold_pairs_kernel(count, total_ref, *refs):
    rows = total_ref.shape[0]
    refs, out_ref = refs[:count], refs[-1]
    steps = [step_of(ref) for ref in refs]
    for c in range(total_ref.shape[1] // LANES):
        part = slice(c * LANES, (c + 1) * LANES)
        total = total_ref[:, part]
        for ref, step in zip(refs, steps):
            total = total + decoded(ref, c * rows, rows, step)
        out_ref[:, part] = total


def fold_pairs(total, parts, after=()):
    return pl.pallas_call(
        functools.partial(fold_pairs_kernel, len(parts)),
        in_specs=[pl.BlockSpec(memory_space=pltpu.VMEM)] * (1 + len(parts)) + unread(after),
        out_specs=pl.BlockSpec(memory_space=pltpu.VMEM),
        out_shape=jax.ShapeDtypeStruct(total.shape, jnp.float32),
        compiler_params=params(),
        cost_estimate=cost([total], parts),
        name="fold_pairs",
    )(total, *parts, *after)


def finish_kernel(rows_ref, total_ref, *refs):
    rows = total_ref.shape[0]
    steps = [step_of(ref) for ref in refs[:-1]]
    for c in range(total_ref.shape[1] // LANES):
        part = slice(c * LANES, (c + 1) * LANES)
        total = total_ref[:, part]
        for ref, step in zip(refs[:-1], steps):
            total = total + decoded(ref, c * rows, rows, step)
        refs[-1][:, part] = (total + rows_ref[0, :, part].astype(jnp.float32)).astype(
            jnp.bfloat16
        )


def finish(rows, total, parts):
    return pl.pallas_call(
        finish_kernel,
        in_specs=[pl.BlockSpec(memory_space=pltpu.VMEM)] * (2 + len(parts)),
        out_specs=pl.BlockSpec(memory_space=pltpu.VMEM),
        out_shape=jax.ShapeDtypeStruct(total.shape, jnp.bfloat16),
        compiler_params=params(),
        cost_estimate=cost([total], parts),
        name="finish",
    )(rows, total, *parts)


def passed(array, axis, shift):
    return lax.ppermute(array, axis, [(i, i ^ shift) for i in range(lax.axis_size(axis))])


def scalars(*values):
    return jnp.stack([jnp.asarray(value, jnp.int32) for value in values])


def shards(
    hidden,
    norm_gain,
    w_query,
    key_value_weight,
    w_output,
    prompt_cache_pages,
    per_page_scales,
    lengths,
    block_table,
):
    devices = lax.axis_size(DEVICES)
    subs = lax.axis_size("sub")
    device = lax.axis_index(DEVICES)
    request = lax.axis_index("req")
    sub = lax.axis_index("sub")
    core = lax.axis_index("section")
    width = hidden.shape[2]
    place = scalars(request, sub, core)

    rows = hidden.reshape(GROUP_REQUESTS * ROWS, width)
    column = [rows] + [passed(rows, "req", s) for s in range(1, GROUP_REQUESTS)]
    where = scalars(request, sub * 2 + core, device * prompt_cache_pages.shape[0])
    pages = list(used_pages(prompt_cache_pages, per_page_scales, block_table, where, subs))
    column = pack(column)
    gathered = [passed(column, "sub", s) for s in range(1, subs)]
    pages[1:] = [passed(pages[s], "req", s) for s in range(1, GROUP_REQUESTS)]
    gain, key_value_weight, ready = staged(
        [norm_gain.reshape(devices, 1, width), key_value_weight], after=[column]
    )
    gathered = [column] + list(gate(gathered, after=[ready]))
    gathered = gathered + [passed(part, "section", 1) for part in gathered]

    half = HEAD_SIZE // 2
    freqs = jnp.exp(
        -jnp.log(theta_base) * jnp.arange(half, dtype=jnp.float32) * (2.0 / HEAD_SIZE)
    )
    positions = (lengths[None, :] + jnp.arange(STEPS)[:, None]).astype(jnp.float32)
    angles = positions[..., None] * freqs
    cosine, sine = jnp.cos(angles), jnp.sin(angles)
    cosine = jnp.repeat(jnp.concatenate([cosine, cosine], axis=-1)[:, :, None], SAMPLES, axis=2)
    sine = jnp.repeat(jnp.concatenate([-sine, sine], axis=-1)[:, :, None], SAMPLES, axis=2)
    cosine = cosine.reshape(-1, HEAD_SIZE)
    sine = sine.reshape(-1, HEAD_SIZE)

    scale, kept, *parts = scale_and_pairs(place, gain, key_value_weight, gathered)
    parts = [passed(part, "sub", s + 1) for s, part in enumerate(parts)]
    query = queries(place, scale, gain, w_query, cosine, sine, gathered)
    total, *parts = fold_sub((0, 1, 2, 3), kept, parts, after=[query])
    parts = [passed(part, "req", s + 1) for s, part in enumerate(parts)]
    pages = regroup(pages, after=[total])
    caches = [passed(pages[s], "sub", s) for s in range(1, subs)]
    w_output, ready = staged([w_output], after=[query])
    mine = fold_pairs(total, parts, after=[ready])
    caches = list(pages[:1]) + list(gate(caches, after=[mine]))
    caches = caches + [passed(part, "section", 1) for part in caches]
    other = passed(mine, "section", 1)

    mixed = attend(
        place, lengths.astype(jnp.int32), query, mine, other, cosine, sine, caches
    )

    away = outputs(scalars(1 - core), mixed, w_output, devices // 2)
    arrived = passed(away, "section", 1)
    kept = outputs(scalars(core), mixed, w_output, devices // 2)
    kept, *parts = fold_core(place, kept, arrived, subs)
    parts = [passed(part, "sub", i // 2 + 1) for i, part in enumerate(parts)]
    last = {}
    for half, order in enumerate(HALVES):
        last.update(zip(order, fold_sub(order, kept, parts[half::2])))
    parts = [passed(last[s], "req", s) for s in range(1, GROUP_REQUESTS)]
    return finish(gathered[0], last[0], parts).reshape(hidden.shape)


def solution(mesh):
    groups, tp, section = mesh.devices.shape
    finer = Mesh(
        mesh.devices.reshape(groups, GROUP_REQUESTS, tp // GROUP_REQUESTS, section),
        ("groups",) + DEVICES,
    )
    placed = (
        P(None, "groups", DEVICES),
        P(),
        P(None, DEVICES),
        P(DEVICES, None),
        P(DEVICES, None),
        P(("groups",) + DEVICES, None, None),
        P(("groups",) + DEVICES, None),
        P("groups"),
        P("groups", None),
    )
    return jax.shard_map(
        shards,
        mesh=finer,
        in_specs=placed,
        out_specs=P(None, "groups", DEVICES),
        check_vma=False,
    )
```

```python
import functools

import jax
import jax.numpy as jnp
from jax import lax
from jax.experimental import pallas as pl
from jax.experimental.pallas import tpu as pltpu
from jax.sharding import Mesh
from jax.sharding import PartitionSpec as P

QUERY_HEADS = 64
KEY_VALUE_HEADS = 8
HEAD_SIZE = 128
GROUP_REQUESTS = 4
SAMPLES = 8
PAGE_TOKENS = 16
STEPS = 2
ROWS = STEPS * SAMPLES
PAIR = 2 * HEAD_SIZE
LANES = 128
HALVES = ((0, 3), (1, 2))
TAIL = 16
DEVICES = ("req", "sub", "section")

theta_base = 500000.0
eps_norm = 1e-05
VMEM = 16 * 2**20
LARGE_VMEM = 51 * 2**20


def params(**more):
    return pltpu.CompilerParams(vmem_limit_bytes=VMEM, **more)


def cost(*groups, flops=0):
    size = sum(array.size * array.dtype.itemsize for arrays in groups for array in arrays)
    return pl.CostEstimate(flops=flops, bytes_accessed=size, transcendentals=0)


def unread(arrays):
    return [pl.BlockSpec(memory_space=pl.ANY)] * len(arrays)


def turn(vectors, cosine, sine):
    return vectors * cosine + pltpu.roll(vectors, HEAD_SIZE // 2, vectors.ndim - 1) * sine


def stage_kernel(count, *refs):
    ins, outs, sems = refs[:count], refs[-2 - count : -1], refs[-1]
    copies = [pltpu.make_async_copy(ins[i], outs[i], sems.at[i]) for i in range(count)]
    for copy in copies:
        copy.start()
    outs[-1][...] = jnp.zeros_like(outs[-1])
    for copy in copies:
        copy.wait()


def staged(arrays, after=()):
    count = len(arrays)
    token = jax.ShapeDtypeStruct((8, LANES), jnp.float32)
    return pl.pallas_call(
        functools.partial(stage_kernel, count),
        in_specs=[pl.BlockSpec(memory_space=pltpu.HBM)] * count + unread(after),
        out_specs=[pl.BlockSpec(memory_space=pltpu.VMEM)] * (count + 1),
        out_shape=[jax.ShapeDtypeStruct(array.shape, array.dtype) for array in arrays] + [token],
        scratch_shapes=[pltpu.SemaphoreType.DMA((count,))],
        compiler_params=params(),
        cost_estimate=cost(arrays, arrays),
        name="staged",
    )(*arrays, *after)


def gate_kernel(*refs):
    pass


def gate(arrays, after):
    count = len(arrays)
    return pl.pallas_call(
        gate_kernel,
        in_specs=[pl.BlockSpec(memory_space=pl.ANY)] * count + unread(after),
        out_specs=[pl.BlockSpec(memory_space=pl.ANY)] * count,
        out_shape=[jax.ShapeDtypeStruct(array.shape, array.dtype) for array in arrays],
        input_output_aliases={i: i for i in range(count)},
        compiler_params=params(),
        name="gate",
    )(*arrays, *after)


def pages_kernel(table, place, scales, page_ref, rows_ref, rows_out_ref, *out_refs):
    e = pl.program_id(0)
    rows_out_ref[...] = rows_ref[...]
    subs = out_refs[0].shape[0]
    targets = 2 * subs
    page = table[place[0], e * targets + place[1]] - place[2]
    for z, out_ref in enumerate(out_refs):
        for j in range(subs):
            half = (place[1] // 2 ^ j) // (subs // 2)
            head = 2 * (place[0] ^ z) + half
            for part in range(2):
                c = head * 2 + part
                columns = pl.ds(pl.multiple_of(c * HEAD_SIZE, HEAD_SIZE), HEAD_SIZE)
                block = page_ref[0, :, columns].astype(jnp.float32)
                out_ref[j, :, part * HEAD_SIZE : (part + 1) * HEAD_SIZE] = (
                    block * scales[page, c]
                ).astype(jnp.bfloat16)


def used_pages(pages, scales, table, place, subs, rows):
    targets = 2 * subs
    entries = table.shape[1] // targets
    shape = jax.ShapeDtypeStruct((subs, entries * PAGE_TOKENS, PAIR), jnp.bfloat16)
    return pl.pallas_call(
        pages_kernel,
        grid_spec=pltpu.PrefetchScalarGridSpec(
            num_scalar_prefetch=3,
            grid=(entries,),
            in_specs=[
                pl.BlockSpec(
                    (1, PAGE_TOKENS, pages.shape[2]),
                    lambda e, table, place, scales: (
                        table[place[0], e * targets + place[1]] - place[2],
                        0,
                        0,
                    ),
                ),
                pl.BlockSpec(rows.shape, lambda e, *_: (0, 0)),
            ],
            out_specs=[pl.BlockSpec(rows.shape, lambda e, *_: (0, 0))]
            + [pl.BlockSpec((subs, PAGE_TOKENS, PAIR), lambda e, *_: (0, e, 0))]
            * GROUP_REQUESTS,
        ),
        out_shape=[jax.ShapeDtypeStruct(rows.shape, rows.dtype)] + [shape] * GROUP_REQUESTS,
        compiler_params=params(),
        cost_estimate=pl.CostEstimate(
            flops=0, bytes_accessed=4 * entries * PAGE_TOKENS * pages.shape[2], transcendentals=0
        ),
        name="used_pages",
    )(table, place, scales.astype(jnp.float32), pages, rows)


def regroup_kernel(*refs):
    ins, outs = refs[:GROUP_REQUESTS], refs[-refs[0].shape[0] :]
    for j, out_ref in enumerate(outs):
        for z, ref in enumerate(ins):
            out_ref[z] = ref[j]


def regroup(parts, after=()):
    subs = parts[0].shape[0]
    shape = jax.ShapeDtypeStruct((len(parts),) + parts[0].shape[1:], parts[0].dtype)
    return pl.pallas_call(
        regroup_kernel,
        in_specs=[pl.BlockSpec(memory_space=pltpu.VMEM)] * len(parts) + unread(after),
        out_specs=[pl.BlockSpec(memory_space=pltpu.VMEM)] * subs,
        out_shape=[shape] * subs,
        compiler_params=params(),
        cost_estimate=cost(parts, parts),
        name="regroup",
    )(*parts, *after)


def pack_kernel(*refs):
    for i in range(refs[-1].shape[0]):
        refs[-1][i] = refs[i][...]


def pack(parts):
    return pl.pallas_call(
        pack_kernel,
        in_specs=[pl.BlockSpec(memory_space=pltpu.VMEM)] * len(parts),
        out_specs=pl.BlockSpec(memory_space=pltpu.VMEM),
        out_shape=jax.ShapeDtypeStruct((len(parts),) + parts[0].shape, parts[0].dtype),
        compiler_params=params(),
        cost_estimate=cost(parts, parts),
        name="pack",
    )(*parts)


def blocks_of(place, refs):
    request, sub, core = place[0], place[1], place[2]
    subs = len(refs) // 2
    for i, ref in enumerate(refs):
        from_core = core if i < subs else 1 - core
        for z in range(GROUP_REQUESTS):
            yield ref, z, ((request ^ z) * subs + (sub ^ i % subs)) * 2 + from_core


def pairs_kernel(place, gain_ref, weight_ref, *refs):
    subs = (len(refs) - 1) // 3
    x_refs, scale_ref, kept_ref, out_refs = (
        refs[: 2 * subs],
        refs[2 * subs],
        refs[2 * subs + 1],
        refs[2 * subs + 2 :],
    )
    request, sub, core = place[0], place[1], place[2]
    _, rows, width = x_refs[0].shape
    total = jnp.zeros((rows, LANES), jnp.float32)
    for ref in x_refs:
        for z in range(GROUP_REQUESTS):
            for piece in pieces_of(ref[z].astype(jnp.float32)):
                total += piece * piece
    mean = jnp.sum(total, axis=-1, keepdims=True) / (2 * subs * GROUP_REQUESTS * width)
    scale = lax.rsqrt(mean + eps_norm)
    scale_ref[...] = jnp.broadcast_to(scale, scale_ref.shape)
    device = (request * subs + sub) * 2 + core
    x = x_refs[0][0].astype(jnp.float32)
    mine = (x * scale * gain_ref[device]).astype(jnp.bfloat16)
    for shift in range(subs):
        half = (sub ^ shift) // (subs // 2)
        pieces = []
        for z in range(GROUP_REQUESTS):
            head = 2 * (request ^ z) + half
            columns = pl.ds(pl.multiple_of(head * PAIR, PAIR), PAIR)
            part = jnp.dot(mine, weight_ref[:, columns], preferred_element_type=jnp.float32)
            if shift == 0:
                kept_ref[z] = part
            pieces += pieces_of(part)
        if shift:
            encode(out_refs[shift - 1], pieces)


def scale_and_pairs(place, gain, weight, gathered):
    subs = len(gathered) // 2
    count = gathered[0].shape[1]
    sent = jax.ShapeDtypeStruct((2 * GROUP_REQUESTS * count + TAIL, LANES), jnp.int16)
    shapes = [
        jax.ShapeDtypeStruct((count, LANES), jnp.float32),
        jax.ShapeDtypeStruct((GROUP_REQUESTS, count, PAIR), jnp.float32),
    ] + [sent] * (subs - 1)
    return pl.pallas_call(
        pairs_kernel,
        in_specs=[pl.BlockSpec(memory_space=pltpu.SMEM)]
        + [pl.BlockSpec(memory_space=pltpu.VMEM)] * (2 + len(gathered)),
        out_specs=[pl.BlockSpec(memory_space=pltpu.VMEM)] * len(shapes),
        out_shape=shapes,
        compiler_params=params(),
        cost_estimate=cost(gathered, [weight], flops=2 * count * weight.size),
        name="scale_and_pairs",
    )(place, gain, weight, *gathered)


def query_kernel(place, scale_ref, gain_ref, weight_ref, cos_ref, sin_ref, *refs):
    x_refs, out_ref, held, sems = refs[:-3], refs[-3], refs[-2], refs[-1]
    _, rows, width = x_refs[0].shape
    columns = weight_ref.shape[1]
    blocks = list(blocks_of(place, x_refs))
    copies = []
    for i, (_, _, block) in enumerate(blocks):
        depth = pl.ds(pl.multiple_of(block * width, width), width)
        copies.append(pltpu.make_async_copy(weight_ref.at[depth], held.at[i], sems.at[i]))
    for copy in copies:
        copy.start()
    scale = scale_ref[:, :1]
    total = jnp.zeros((rows, columns), jnp.float32)
    for i, (ref, z, block) in enumerate(blocks):
        x = ref[z].astype(jnp.float32)
        x = (x * scale * gain_ref[block]).astype(jnp.bfloat16)
        copies[i].wait()
        total += jnp.dot(x, held[i], preferred_element_type=jnp.float32)
    for head in range(columns // HEAD_SIZE):
        part = slice(head * HEAD_SIZE, (head + 1) * HEAD_SIZE)
        turned = turn(total[:, part], cos_ref[...], sin_ref[...])
        for r in range(GROUP_REQUESTS):
            first, second = r * SAMPLES, (GROUP_REQUESTS + r) * SAMPLES
            out_ref[r, :, part] = jnp.concatenate(
                [turned[first : first + SAMPLES], turned[second : second + SAMPLES]], axis=0
            ).astype(jnp.bfloat16)


def queries(place, scale, gain, weight, cosine, sine, gathered):
    columns = weight.shape[1]
    _, rows, width = gathered[0].shape
    blocks = weight.shape[0] // width
    return pl.pallas_call(
        query_kernel,
        in_specs=[pl.BlockSpec(memory_space=pltpu.SMEM)]
        + [pl.BlockSpec(memory_space=pltpu.VMEM)] * 2
        + [pl.BlockSpec(memory_space=pltpu.HBM)]
        + [pl.BlockSpec(memory_space=pltpu.VMEM)] * (2 + len(gathered)),
        out_specs=pl.BlockSpec(memory_space=pltpu.VMEM),
        out_shape=jax.ShapeDtypeStruct((GROUP_REQUESTS, ROWS, columns), jnp.bfloat16),
        scratch_shapes=[
            pltpu.VMEM((blocks, width, columns), jnp.bfloat16),
            pltpu.SemaphoreType.DMA((blocks,)),
        ],
        compiler_params=pltpu.CompilerParams(vmem_limit_bytes=LARGE_VMEM),
        cost_estimate=cost([weight], flops=2 * rows * weight.size),
        name="queries",
    )(place, scale, gain, weight, cosine, sine, *gathered)


def attend_kernel(place, lengths, q_ref, mine_ref, other_ref, cos_ref, sin_ref, *refs):
    caches, out_ref, key_ref, value_ref = refs[:-3], refs[-3], refs[-2], refs[-1]
    request, sub, core = place[0], place[1], place[2]
    subs, span = len(caches) // 2, caches[0].shape[1]
    targets = 2 * subs
    tokens = targets * span
    quarter = q_ref.shape[2] // HEAD_SIZE
    pair = mine_ref[...] + other_ref[...]
    key_ref[...] = turn(pair[:, :HEAD_SIZE], cos_ref[...], sin_ref[...])
    value_ref[...] = pair[:, HEAD_SIZE:]
    column = lax.broadcasted_iota(jnp.int32, (1, tokens), 1)
    source, inside = column // span, column % span
    from_core = jnp.where(source < subs, core, 1 - core)
    from_sub = sub ^ source % subs
    entry = inside // PAGE_TOKENS * targets + from_sub * 2 + from_core
    position = entry * PAGE_TOKENS + inside % PAGE_TOKENS
    count = quarter * ROWS
    row = lax.broadcasted_iota(jnp.int32, (count, ROWS), 0) % ROWS
    other = lax.broadcasted_iota(jnp.int32, (count, ROWS), 1)
    own_visible = (row % SAMPLES == other % SAMPLES) & (other // SAMPLES <= row // SAMPLES)
    factor = HEAD_SIZE ** (-0.5)
    contract = (((1,), (1,)), ((), ()))
    for z in range(GROUP_REQUESTS):
        r = request ^ z
        fresh = [
            pl.ds(pl.multiple_of((step * GROUP_REQUESTS + r) * SAMPLES, SAMPLES), SAMPLES)
            for step in range(STEPS)
        ]
        new_key = jnp.concatenate([key_ref[rows] for rows in fresh], axis=0)
        new_value = jnp.concatenate([value_ref[rows] for rows in fresh], axis=0)
        new_key, new_value = new_key.astype(jnp.bfloat16), new_value.astype(jnp.bfloat16)
        keys = jnp.concatenate([ref[z, :, :HEAD_SIZE] for ref in caches], axis=0)
        values = jnp.concatenate([ref[z, :, HEAD_SIZE:] for ref in caches], axis=0)
        query = jnp.concatenate(
            [q_ref[r, :, h * HEAD_SIZE : (h + 1) * HEAD_SIZE] for h in range(quarter)], axis=0
        )
        scores = lax.dot_general(query, keys, contract, preferred_element_type=jnp.float32)
        scores = jnp.where(position < lengths[r], scores * factor, -jnp.inf)
        own = lax.dot_general(query, new_key, contract, preferred_element_type=jnp.float32)
        own = jnp.where(own_visible, own * factor, -jnp.inf)
        highest = jnp.maximum(
            jnp.max(scores, axis=-1, keepdims=True), jnp.max(own, axis=-1, keepdims=True)
        )
        scores = jnp.exp(scores - highest)
        own = jnp.exp(own - highest)
        total = jnp.sum(scores, axis=-1, keepdims=True) + jnp.sum(own, axis=-1, keepdims=True)
        mixed = jnp.dot(
            (scores / total).astype(jnp.bfloat16), values, preferred_element_type=jnp.float32
        ) + jnp.dot(
            (own / total).astype(jnp.bfloat16), new_value, preferred_element_type=jnp.float32
        )
        mixed = mixed.astype(jnp.bfloat16)
        for h in range(quarter):
            out_ref[r, :, h * HEAD_SIZE : (h + 1) * HEAD_SIZE] = mixed[
                h * ROWS : (h + 1) * ROWS
            ]


def attend(place, lengths, query, mine, other, cosine, sine, caches):
    return pl.pallas_call(
        attend_kernel,
        in_specs=[pl.BlockSpec(memory_space=pltpu.SMEM)] * 2
        + [pl.BlockSpec(memory_space=pltpu.VMEM)] * (5 + len(caches)),
        out_specs=pl.BlockSpec(memory_space=pltpu.VMEM),
        out_shape=jax.ShapeDtypeStruct(query.shape, jnp.bfloat16),
        scratch_shapes=[pltpu.VMEM(cosine.shape, jnp.float32)] * 2,
        compiler_params=params(),
        cost_estimate=cost(caches, caches, caches, flops=2**28),
        name="attend",
    )(place, lengths, query, mine, other, cosine, sine, *caches)


def output_kernel(away, subs, shifts, place, x_ref, weight_ref, *refs):
    out_ref = refs[-1]
    blocks, rows, width = out_ref.shape
    core = 1 - place[2] if away else place[2]
    x = x_ref[...].reshape(rows, -1)
    for i in range(blocks):
        z, shift = i % GROUP_REQUESTS, shifts[i // GROUP_REQUESTS]
        block = ((place[0] ^ z) * subs + (place[1] ^ shift)) * 2 + core
        columns = pl.ds(pl.multiple_of(block * width, width), width)
        part = jnp.dot(x, weight_ref[:, columns], preferred_element_type=jnp.float32)
        for r in range(GROUP_REQUESTS):
            for step in range(STEPS):
                source = r * ROWS + step * SAMPLES
                target = (step * GROUP_REQUESTS + r) * SAMPLES
                out_ref[i, target : target + SAMPLES] = part[source : source + SAMPLES]


def outputs(place, mixed, weight, away, subs, shifts, after=()):
    rows = GROUP_REQUESTS * ROWS
    width = weight.shape[1] // (2 * GROUP_REQUESTS * subs)
    blocks = GROUP_REQUESTS * len(shifts)
    return pl.pallas_call(
        functools.partial(output_kernel, away, subs, shifts),
        in_specs=[pl.BlockSpec(memory_space=pltpu.SMEM)]
        + [pl.BlockSpec(memory_space=pltpu.VMEM)] * 2
        + unread(after),
        out_specs=pl.BlockSpec(memory_space=pltpu.VMEM),
        out_shape=jax.ShapeDtypeStruct((blocks, rows, width), jnp.float32),
        compiler_params=params(),
        cost_estimate=cost([mixed], flops=2 * rows * mixed.shape[2] * blocks * width),
        name="outputs",
    )(place, mixed, weight, *after)


def pieces_of(block):
    return [block[:, c : c + LANES] for c in range(0, block.shape[1], LANES)]


def encode(out_ref, pieces):
    rows = pieces[0].shape[0]
    peak = jnp.abs(pieces[0])
    for piece in pieces[1:]:
        peak = jnp.maximum(peak, jnp.abs(piece))
    peak = jnp.maximum(jnp.max(peak, axis=0, keepdims=True), 1e-30)
    exponent = jnp.floor(jnp.log2(peak)) - 14.0
    inverse = jnp.exp2(-exponent)
    for i, piece in enumerate(pieces):
        code = jnp.clip(jnp.floor(piece * inverse + 0.5), -32767.0, 32767.0)
        out_ref[i * rows : (i + 1) * rows] = code.astype(jnp.int32).astype(jnp.int16)
    out_ref[len(pieces) * rows :] = (
        jnp.broadcast_to(exponent, (TAIL, LANES)).astype(jnp.int32).astype(jnp.int16)
    )


def step_of(ref):
    tail = ref[ref.shape[0] - TAIL :].astype(jnp.int32).astype(jnp.float32)
    return jnp.exp2(tail[:1])


def decoded(ref, first, rows, step):
    return ref[pl.ds(first, rows)].astype(jnp.int32).astype(jnp.float32) * step


def fold_core_kernel(mine_ref, got_ref, *out_refs):
    for i, out_ref in enumerate(out_refs):
        pieces = []
        for z in HALVES[i % 2]:
            block = i // 2 * GROUP_REQUESTS + z
            pieces += pieces_of(mine_ref[block] + got_ref[block])
        encode(out_ref, pieces)


def fold_core(mine, got):
    blocks, rows, width = mine.shape
    count = 2 * (blocks // GROUP_REQUESTS)
    sent = jax.ShapeDtypeStruct((2 * width // LANES * rows + TAIL, LANES), jnp.int16)
    return pl.pallas_call(
        fold_core_kernel,
        in_specs=[pl.BlockSpec(memory_space=pltpu.VMEM)] * 2,
        out_specs=[pl.BlockSpec(memory_space=pltpu.VMEM)] * count,
        out_shape=[sent] * count,
        compiler_params=params(),
        cost_estimate=cost([mine, got]),
        name="fold_core",
    )(mine, got)


def fold_sub_kernel(order, count, own, *refs):
    own_refs, in_refs, out_refs = refs[:own], refs[own : own + count], refs[-len(order) :]
    _, rows, width = own_refs[0].shape
    steps = [step_of(ref) for ref in in_refs]
    for i, (z, out_ref) in enumerate(zip(order, out_refs)):
        block = own_refs[0][z]
        for ref in own_refs[1:]:
            block = block + ref[z]
        pieces = pieces_of(block)
        for c in range(len(pieces)):
            for ref, step in zip(in_refs, steps):
                first = (i * len(pieces) + c) * rows
                pieces[c] = pieces[c] + decoded(ref, first, rows, step)
        if z:
            encode(out_ref, pieces)
        else:
            for c, piece in enumerate(pieces):
                out_ref[:, c * LANES : (c + 1) * LANES] = piece


def fold_sub(order, own, parts, after=()):
    _, rows, width = own[0].shape
    total = jax.ShapeDtypeStruct((rows, width), jnp.float32)
    sent = jax.ShapeDtypeStruct((width // LANES * rows + TAIL, LANES), jnp.int16)
    return pl.pallas_call(
        functools.partial(fold_sub_kernel, order, len(parts), len(own)),
        in_specs=[pl.BlockSpec(memory_space=pltpu.VMEM)] * (len(own) + len(parts))
        + unread(after),
        out_specs=[pl.BlockSpec(memory_space=pltpu.VMEM)] * len(order),
        out_shape=[sent if z else total for z in order],
        compiler_params=params(),
        cost_estimate=cost(own, parts),
        name="fold_sub",
    )(*own, *parts, *after)


def fold_pairs_kernel(count, total_ref, *refs):
    rows = total_ref.shape[0]
    refs, out_ref = refs[:count], refs[-1]
    steps = [step_of(ref) for ref in refs]
    for c in range(total_ref.shape[1] // LANES):
        part = slice(c * LANES, (c + 1) * LANES)
        total = total_ref[:, part]
        for ref, step in zip(refs, steps):
            total = total + decoded(ref, c * rows, rows, step)
        out_ref[:, part] = total


def fold_pairs(total, parts, after=()):
    return pl.pallas_call(
        functools.partial(fold_pairs_kernel, len(parts)),
        in_specs=[pl.BlockSpec(memory_space=pltpu.VMEM)] * (1 + len(parts)) + unread(after),
        out_specs=pl.BlockSpec(memory_space=pltpu.VMEM),
        out_shape=jax.ShapeDtypeStruct(total.shape, jnp.float32),
        compiler_params=params(),
        cost_estimate=cost([total], parts),
        name="fold_pairs",
    )(total, *parts, *after)


def finish_kernel(rows_ref, total_ref, *refs):
    rows = total_ref.shape[0]
    steps = [step_of(ref) for ref in refs[:-1]]
    for c in range(total_ref.shape[1] // LANES):
        part = slice(c * LANES, (c + 1) * LANES)
        total = total_ref[:, part]
        for ref, step in zip(refs[:-1], steps):
            total = total + decoded(ref, c * rows, rows, step)
        refs[-1][:, part] = (total + rows_ref[0, :, part].astype(jnp.float32)).astype(
            jnp.bfloat16
        )


def finish(rows, total, parts):
    return pl.pallas_call(
        finish_kernel,
        in_specs=[pl.BlockSpec(memory_space=pltpu.VMEM)] * (2 + len(parts)),
        out_specs=pl.BlockSpec(memory_space=pltpu.VMEM),
        out_shape=jax.ShapeDtypeStruct(total.shape, jnp.bfloat16),
        compiler_params=params(),
        cost_estimate=cost([total], parts),
        name="finish",
    )(rows, total, *parts)


def passed(array, axis, shift):
    return lax.ppermute(array, axis, [(i, i ^ shift) for i in range(lax.axis_size(axis))])


def scalars(*values):
    return jnp.stack([jnp.asarray(value, jnp.int32) for value in values])


def shards(
    hidden,
    norm_gain,
    w_query,
    key_value_weight,
    w_output,
    prompt_cache_pages,
    per_page_scales,
    lengths,
    block_table,
):
    devices = lax.axis_size(DEVICES)
    subs = lax.axis_size("sub")
    device = lax.axis_index(DEVICES)
    request = lax.axis_index("req")
    sub = lax.axis_index("sub")
    core = lax.axis_index("section")
    width = hidden.shape[2]
    place = scalars(request, sub, core)

    rows = hidden.reshape(GROUP_REQUESTS * ROWS, width)
    column = [passed(rows, "req", s) for s in range(1, GROUP_REQUESTS)]
    where = scalars(request, sub * 2 + core, device * prompt_cache_pages.shape[0])
    rows, *pages = used_pages(
        prompt_cache_pages, per_page_scales, block_table, where, subs, rows
    )
    column = pack([rows] + column)
    gathered = [passed(column, "sub", s) for s in range(1, subs)]
    pages[1:] = [passed(pages[s], "req", s) for s in range(1, GROUP_REQUESTS)]
    gain, key_value_weight, ready = staged(
        [norm_gain.reshape(devices, 1, width), key_value_weight], after=[column]
    )
    gathered = [column] + list(gate(gathered, after=[ready]))
    gathered = gathered + [passed(part, "section", 1) for part in gathered]

    half = HEAD_SIZE // 2
    freqs = jnp.exp(
        -jnp.log(theta_base) * jnp.arange(half, dtype=jnp.float32) * (2.0 / HEAD_SIZE)
    )
    positions = (lengths[None, :] + jnp.arange(STEPS)[:, None]).astype(jnp.float32)
    angles = positions[..., None] * freqs
    cosine, sine = jnp.cos(angles), jnp.sin(angles)
    cosine = jnp.repeat(jnp.concatenate([cosine, cosine], axis=-1)[:, :, None], SAMPLES, axis=2)
    sine = jnp.repeat(jnp.concatenate([-sine, sine], axis=-1)[:, :, None], SAMPLES, axis=2)
    cosine = cosine.reshape(-1, HEAD_SIZE)
    sine = sine.reshape(-1, HEAD_SIZE)

    scale, kept, *parts = scale_and_pairs(place, gain, key_value_weight, gathered)
    parts = [passed(part, "sub", s + 1) for s, part in enumerate(parts)]
    query = queries(place, scale, gain, w_query, cosine, sine, gathered)
    total, *parts = fold_sub((0, 1, 2, 3), [kept], parts, after=[query])
    parts = [passed(part, "req", s + 1) for s, part in enumerate(parts)]
    pages = regroup(pages, after=[total])
    caches = [passed(pages[s], "sub", s) for s in range(1, subs)]
    w_output, ready = staged([w_output], after=[query])
    mine = fold_pairs(total, parts, after=[ready])
    caches = list(pages[:1]) + list(gate(caches, after=[mine]))
    caches = caches + [passed(part, "section", 1) for part in caches]
    other = passed(mine, "section", 1)

    mixed = attend(
        place, lengths.astype(jnp.int32), query, mine, other, cosine, sine, caches
    )

    others = tuple(range(1, subs))
    first = outputs(place, mixed, w_output, True, subs, others)
    got_first = passed(first, "section", 1)
    second = outputs(place, mixed, w_output, True, subs, (0,), after=[first])
    got_second = passed(second, "section", 1)
    kept = outputs(place, mixed, w_output, False, subs, others, after=[second])
    parts = fold_core(kept, got_first)
    kept = outputs(place, mixed, w_output, False, subs, (0,), after=parts[:1])
    parts = [passed(part, "sub", i // 2 + 1) for i, part in enumerate(parts)]
    last = {}
    for half, order in enumerate(HALVES):
        last.update(zip(order, fold_sub(order, [kept, got_second], parts[half::2])))
    parts = [passed(last[s], "req", s) for s in range(1, GROUP_REQUESTS)]
    return finish(gathered[0], last[0], parts).reshape(hidden.shape)


def solution(mesh):
    groups, tp, section = mesh.devices.shape
    finer = Mesh(
        mesh.devices.reshape(groups, GROUP_REQUESTS, tp // GROUP_REQUESTS, section),
        ("groups",) + DEVICES,
    )
    placed = (
        P(None, "groups", DEVICES),
        P(),
        P(None, DEVICES),
        P(DEVICES, None),
        P(DEVICES, None),
        P(("groups",) + DEVICES, None, None),
        P(("groups",) + DEVICES, None),
        P("groups"),
        P("groups", None),
    )
    return jax.shard_map(
        shards,
        mesh=finer,
        in_specs=placed,
        out_specs=P(None, "groups", DEVICES),
        check_vma=False,
    )
```

```python
import functools

import jax
import jax.numpy as jnp
from jax import lax
from jax.experimental import pallas as pl
from jax.experimental.pallas import tpu as pltpu
from jax.sharding import Mesh
from jax.sharding import PartitionSpec as P

QUERY_HEADS = 64
KEY_VALUE_HEADS = 8
HEAD_SIZE = 128
GROUP_REQUESTS = 4
SAMPLES = 8
PAGE_TOKENS = 16
STEPS = 2
ROWS = STEPS * SAMPLES
PAIR = 2 * HEAD_SIZE
LANES = 128
TAIL = 16
DEVICES = ("req", "sub", "section")

theta_base = 500000.0
eps_norm = 1e-05
VMEM = 16 * 2**20
LARGE_VMEM = 51 * 2**20
IN_FLIGHT = 4


def params(**more):
    return pltpu.CompilerParams(vmem_limit_bytes=VMEM, **more)


def cost(*groups, flops=0):
    size = sum(array.size * array.dtype.itemsize for arrays in groups for array in arrays)
    return pl.CostEstimate(flops=flops, bytes_accessed=size, transcendentals=0)


def unread(arrays):
    return [pl.BlockSpec(memory_space=pl.ANY)] * len(arrays)


def turn(vectors, cosine, sine):
    return vectors * cosine + pltpu.roll(vectors, HEAD_SIZE // 2, vectors.ndim - 1) * sine


def stage_kernel(order, count, place, block_ref, *refs):
    out_ref, token_ref, *outs, sems = refs[-3 - count :]
    width = out_ref.shape[2]
    copies = [
        pltpu.make_async_copy(refs[i], outs[i], sems.at[len(order) + i]) for i in range(count)
    ]
    for i, block in enumerate(order):
        columns = pl.ds(pl.multiple_of(block(place) * width, width), width)
        copies.append(pltpu.make_async_copy(block_ref.at[:, columns], out_ref.at[i], sems.at[i]))
    for copy in copies:
        copy.start()
    token_ref[...] = jnp.zeros_like(token_ref)
    for copy in copies:
        copy.wait()


def staged(place, array, width, order, more=(), after=()):
    rows, count = array.shape[0], len(order)
    return pl.pallas_call(
        functools.partial(stage_kernel, order, len(more)),
        in_specs=[pl.BlockSpec(memory_space=pltpu.SMEM)]
        + [pl.BlockSpec(memory_space=pltpu.HBM)] * (1 + len(more))
        + unread(after),
        out_specs=[pl.BlockSpec(memory_space=pltpu.VMEM)] * (2 + len(more)),
        out_shape=[
            jax.ShapeDtypeStruct((count, rows, width), array.dtype),
            jax.ShapeDtypeStruct((8, LANES), jnp.float32),
        ]
        + [jax.ShapeDtypeStruct(other.shape, other.dtype) for other in more],
        scratch_shapes=[pltpu.SemaphoreType.DMA((count + len(more),))],
        compiler_params=params(),
        cost_estimate=cost([array], [array]),
        name="staged",
    )(place, array, *more, *after)


def pair_order(subs):
    return [
        lambda place, j=j, z=z: 2 * (place[0] ^ z) + (place[1] ^ j) // (subs // 2)
        for j in range(subs)
        for z in range(GROUP_REQUESTS)
    ]


def output_order(subs):
    return [
        lambda place, c=c, j=j, z=z: ((place[0] ^ z) * subs + (place[1] ^ j)) * 2 + (place[2] ^ c)
        for c in range(2)
        for j in range(subs)
        for z in range(GROUP_REQUESTS)
    ]


def gate_kernel(*refs):
    pass


def gate(arrays, after):
    count = len(arrays)
    return pl.pallas_call(
        gate_kernel,
        in_specs=[pl.BlockSpec(memory_space=pl.ANY)] * count + unread(after),
        out_specs=[pl.BlockSpec(memory_space=pl.ANY)] * count,
        out_shape=[jax.ShapeDtypeStruct(array.shape, array.dtype) for array in arrays],
        input_output_aliases={i: i for i in range(count)},
        compiler_params=params(),
        name="gate",
    )(*arrays, *after)


def pages_kernel(table, place, scales, page_ref, rows_ref, rows_out_ref, *out_refs):
    e = pl.program_id(0)
    rows_out_ref[...] = rows_ref[...]
    subs = out_refs[0].shape[0]
    targets = 2 * subs
    page = table[place[0], e * targets + place[1]] - place[2]
    for z, out_ref in enumerate(out_refs):
        for j in range(subs):
            half = (place[1] // 2 ^ j) // (subs // 2)
            head = 2 * (place[0] ^ z) + half
            for part in range(2):
                c = head * 2 + part
                columns = pl.ds(pl.multiple_of(c * HEAD_SIZE, HEAD_SIZE), HEAD_SIZE)
                block = page_ref[0, :, columns].astype(jnp.float32)
                out_ref[j, :, part * HEAD_SIZE : (part + 1) * HEAD_SIZE] = (
                    block * scales[page, c]
                ).astype(jnp.bfloat16)


def used_pages(pages, scales, table, place, subs, rows):
    targets = 2 * subs
    entries = table.shape[1] // targets
    shape = jax.ShapeDtypeStruct((subs, entries * PAGE_TOKENS, PAIR), jnp.bfloat16)
    return pl.pallas_call(
        pages_kernel,
        grid_spec=pltpu.PrefetchScalarGridSpec(
            num_scalar_prefetch=3,
            grid=(entries,),
            in_specs=[
                pl.BlockSpec(
                    (1, PAGE_TOKENS, pages.shape[2]),
                    lambda e, table, place, scales: (
                        table[place[0], e * targets + place[1]] - place[2],
                        0,
                        0,
                    ),
                ),
                pl.BlockSpec(rows.shape, lambda e, *_: (0, 0)),
            ],
            out_specs=[pl.BlockSpec(rows.shape, lambda e, *_: (0, 0))]
            + [pl.BlockSpec((subs, PAGE_TOKENS, PAIR), lambda e, *_: (0, e, 0))]
            * GROUP_REQUESTS,
        ),
        out_shape=[jax.ShapeDtypeStruct(rows.shape, rows.dtype)] + [shape] * GROUP_REQUESTS,
        compiler_params=params(),
        cost_estimate=pl.CostEstimate(
            flops=0, bytes_accessed=4 * entries * PAGE_TOKENS * pages.shape[2], transcendentals=0
        ),
        name="used_pages",
    )(table, place, scales.astype(jnp.float32), pages, rows)


def regroup_kernel(*refs):
    ins, outs = refs[:GROUP_REQUESTS], refs[-refs[0].shape[0] :]
    for j, out_ref in enumerate(outs):
        for z, ref in enumerate(ins):
            out_ref[z] = ref[j]


def regroup(parts, after=()):
    subs = parts[0].shape[0]
    shape = jax.ShapeDtypeStruct((len(parts),) + parts[0].shape[1:], parts[0].dtype)
    return pl.pallas_call(
        regroup_kernel,
        in_specs=[pl.BlockSpec(memory_space=pltpu.VMEM)] * len(parts) + unread(after),
        out_specs=[pl.BlockSpec(memory_space=pltpu.VMEM)] * subs,
        out_shape=[shape] * subs,
        compiler_params=params(),
        cost_estimate=cost(parts, parts),
        name="regroup",
    )(*parts, *after)


def pack_kernel(*refs):
    for i in range(refs[-1].shape[0]):
        refs[-1][i] = refs[i][...]


def pack(parts):
    return pl.pallas_call(
        pack_kernel,
        in_specs=[pl.BlockSpec(memory_space=pltpu.VMEM)] * len(parts),
        out_specs=pl.BlockSpec(memory_space=pltpu.VMEM),
        out_shape=jax.ShapeDtypeStruct((len(parts),) + parts[0].shape, parts[0].dtype),
        compiler_params=params(),
        cost_estimate=cost(parts, parts),
        name="pack",
    )(*parts)


def blocks_of(place, refs):
    request, sub, core = place[0], place[1], place[2]
    subs = len(refs) // 2
    for i, ref in enumerate(refs):
        from_core = core if i < subs else 1 - core
        for z in range(GROUP_REQUESTS):
            yield ref, z, ((request ^ z) * subs + (sub ^ i % subs)) * 2 + from_core


def pairs_kernel(place, gain_ref, weight_ref, *refs):
    subs = (len(refs) - 1) // 3
    x_refs, scale_ref, kept_ref, out_refs = (
        refs[: 2 * subs],
        refs[2 * subs],
        refs[2 * subs + 1],
        refs[2 * subs + 2 :],
    )
    request, sub, core = place[0], place[1], place[2]
    _, rows, width = x_refs[0].shape
    total = jnp.zeros((rows, LANES), jnp.float32)
    for ref in x_refs:
        for z in range(GROUP_REQUESTS):
            for piece in pieces_of(ref[z].astype(jnp.float32)):
                total += piece * piece
    mean = jnp.sum(total, axis=-1, keepdims=True) / (2 * subs * GROUP_REQUESTS * width)
    scale = lax.rsqrt(mean + eps_norm)
    scale_ref[...] = jnp.broadcast_to(scale, scale_ref.shape)
    device = (request * subs + sub) * 2 + core
    x = x_refs[0][0].astype(jnp.float32)
    mine = (x * scale * gain_ref[device]).astype(jnp.bfloat16)
    for shift in range(subs):
        pieces = []
        for z in range(GROUP_REQUESTS):
            block = weight_ref[shift * GROUP_REQUESTS + z]
            part = jnp.dot(mine, block, preferred_element_type=jnp.float32)
            if shift == 0:
                kept_ref[z] = part
            pieces += pieces_of(part)
        if shift:
            encode(out_refs[shift - 1], pieces)


def scale_and_pairs(place, gain, weight, gathered):
    subs = len(gathered) // 2
    count = gathered[0].shape[1]
    sent = jax.ShapeDtypeStruct((2 * GROUP_REQUESTS * count + TAIL, LANES), jnp.int16)
    shapes = [
        jax.ShapeDtypeStruct((count, LANES), jnp.float32),
        jax.ShapeDtypeStruct((GROUP_REQUESTS, count, PAIR), jnp.float32),
    ] + [sent] * (subs - 1)
    return pl.pallas_call(
        pairs_kernel,
        in_specs=[pl.BlockSpec(memory_space=pltpu.SMEM)]
        + [pl.BlockSpec(memory_space=pltpu.VMEM)] * (2 + len(gathered)),
        out_specs=[pl.BlockSpec(memory_space=pltpu.VMEM)] * len(shapes),
        out_shape=shapes,
        compiler_params=params(),
        cost_estimate=cost(gathered, [weight], flops=2 * count * weight.size),
        name="scale_and_pairs",
    )(place, gain, weight, *gathered)


def query_kernel(place, scale_ref, gain_ref, weight_ref, cos_ref, sin_ref, *refs):
    x_refs, out_ref, held, sems = refs[:-3], refs[-3], refs[-2], refs[-1]
    _, rows, width = x_refs[0].shape
    columns = weight_ref.shape[1]
    blocks = list(blocks_of(place, x_refs))
    copies = []
    for i, (_, _, block) in enumerate(blocks):
        depth = pl.ds(pl.multiple_of(block * width, width), width)
        copies.append(pltpu.make_async_copy(weight_ref.at[depth], held.at[i], sems.at[i]))
    for copy in copies[:IN_FLIGHT]:
        copy.start()
    scale = scale_ref[:, :1]
    total = jnp.zeros((rows, columns), jnp.float32)
    for i, (ref, z, block) in enumerate(blocks):
        x = ref[z].astype(jnp.float32)
        x = (x * scale * gain_ref[block]).astype(jnp.bfloat16)
        copies[i].wait()
        if i + IN_FLIGHT < len(copies):
            copies[i + IN_FLIGHT].start()
        total += jnp.dot(x, held[i], preferred_element_type=jnp.float32)
    for head in range(columns // HEAD_SIZE):
        part = slice(head * HEAD_SIZE, (head + 1) * HEAD_SIZE)
        turned = turn(total[:, part], cos_ref[...], sin_ref[...])
        for r in range(GROUP_REQUESTS):
            first, second = r * SAMPLES, (GROUP_REQUESTS + r) * SAMPLES
            out_ref[r, :, part] = jnp.concatenate(
                [turned[first : first + SAMPLES], turned[second : second + SAMPLES]], axis=0
            ).astype(jnp.bfloat16)


def queries(place, scale, gain, weight, cosine, sine, gathered):
    columns = weight.shape[1]
    _, rows, width = gathered[0].shape
    blocks = weight.shape[0] // width
    return pl.pallas_call(
        query_kernel,
        in_specs=[pl.BlockSpec(memory_space=pltpu.SMEM)]
        + [pl.BlockSpec(memory_space=pltpu.VMEM)] * 2
        + [pl.BlockSpec(memory_space=pltpu.HBM)]
        + [pl.BlockSpec(memory_space=pltpu.VMEM)] * (2 + len(gathered)),
        out_specs=pl.BlockSpec(memory_space=pltpu.VMEM),
        out_shape=jax.ShapeDtypeStruct((GROUP_REQUESTS, ROWS, columns), jnp.bfloat16),
        scratch_shapes=[
            pltpu.VMEM((blocks, width, columns), jnp.bfloat16),
            pltpu.SemaphoreType.DMA((blocks,)),
        ],
        compiler_params=pltpu.CompilerParams(vmem_limit_bytes=LARGE_VMEM),
        cost_estimate=cost([weight], flops=2 * rows * weight.size),
        name="queries",
    )(place, scale, gain, weight, cosine, sine, *gathered)


def attend_kernel(place, lengths, q_ref, mine_ref, other_ref, cos_ref, sin_ref, *refs):
    caches, out_ref, key_ref, value_ref = refs[:-3], refs[-3], refs[-2], refs[-1]
    request, sub, core = place[0], place[1], place[2]
    subs, span = len(caches) // 2, caches[0].shape[1]
    targets = 2 * subs
    tokens = targets * span
    quarter = q_ref.shape[2] // HEAD_SIZE
    pair = mine_ref[...] + other_ref[...]
    key_ref[...] = turn(pair[:, :HEAD_SIZE], cos_ref[...], sin_ref[...])
    value_ref[...] = pair[:, HEAD_SIZE:]
    column = lax.broadcasted_iota(jnp.int32, (1, tokens), 1)
    source, inside = column // span, column % span
    from_core = jnp.where(source < subs, core, 1 - core)
    from_sub = sub ^ source % subs
    entry = inside // PAGE_TOKENS * targets + from_sub * 2 + from_core
    position = entry * PAGE_TOKENS + inside % PAGE_TOKENS
    count = quarter * ROWS
    row = lax.broadcasted_iota(jnp.int32, (count, ROWS), 0) % ROWS
    other = lax.broadcasted_iota(jnp.int32, (count, ROWS), 1)
    own_visible = (row % SAMPLES == other % SAMPLES) & (other // SAMPLES <= row // SAMPLES)
    factor = HEAD_SIZE ** (-0.5)
    contract = (((1,), (1,)), ((), ()))
    for z in range(GROUP_REQUESTS):
        r = request ^ z
        fresh = [
            pl.ds(pl.multiple_of((step * GROUP_REQUESTS + r) * SAMPLES, SAMPLES), SAMPLES)
            for step in range(STEPS)
        ]
        new_key = jnp.concatenate([key_ref[rows] for rows in fresh], axis=0)
        new_value = jnp.concatenate([value_ref[rows] for rows in fresh], axis=0)
        new_key, new_value = new_key.astype(jnp.bfloat16), new_value.astype(jnp.bfloat16)
        keys = jnp.concatenate([ref[z, :, :HEAD_SIZE] for ref in caches], axis=0)
        values = jnp.concatenate([ref[z, :, HEAD_SIZE:] for ref in caches], axis=0)
        query = jnp.concatenate(
            [q_ref[r, :, h * HEAD_SIZE : (h + 1) * HEAD_SIZE] for h in range(quarter)], axis=0
        )
        scores = lax.dot_general(query, keys, contract, preferred_element_type=jnp.float32)
        scores = jnp.where(position < lengths[r], scores * factor, -jnp.inf)
        own = lax.dot_general(query, new_key, contract, preferred_element_type=jnp.float32)
        own = jnp.where(own_visible, own * factor, -jnp.inf)
        highest = jnp.maximum(
            jnp.max(scores, axis=-1, keepdims=True), jnp.max(own, axis=-1, keepdims=True)
        )
        scores = jnp.exp(scores - highest)
        own = jnp.exp(own - highest)
        total = jnp.sum(scores, axis=-1, keepdims=True) + jnp.sum(own, axis=-1, keepdims=True)
        mixed = jnp.dot(
            (scores / total).astype(jnp.bfloat16), values, preferred_element_type=jnp.float32
        ) + jnp.dot(
            (own / total).astype(jnp.bfloat16), new_value, preferred_element_type=jnp.float32
        )
        mixed = mixed.astype(jnp.bfloat16)
        for h in range(quarter):
            out_ref[r, :, h * HEAD_SIZE : (h + 1) * HEAD_SIZE] = mixed[
                h * ROWS : (h + 1) * ROWS
            ]


def attend(place, lengths, query, mine, other, cosine, sine, caches):
    return pl.pallas_call(
        attend_kernel,
        in_specs=[pl.BlockSpec(memory_space=pltpu.SMEM)] * 2
        + [pl.BlockSpec(memory_space=pltpu.VMEM)] * (5 + len(caches)),
        out_specs=pl.BlockSpec(memory_space=pltpu.VMEM),
        out_shape=jax.ShapeDtypeStruct(query.shape, jnp.bfloat16),
        scratch_shapes=[pltpu.VMEM(cosine.shape, jnp.float32)] * 2,
        compiler_params=params(),
        cost_estimate=cost(caches, caches, caches, flops=2**28),
        name="attend",
    )(place, lengths, query, mine, other, cosine, sine, *caches)


def output_kernel(first, x_ref, weight_ref, *refs):
    out_ref = refs[-1]
    blocks, rows, width = out_ref.shape
    x = x_ref[...].reshape(rows, -1)
    for i in range(blocks):
        part = jnp.dot(x, weight_ref[first + i], preferred_element_type=jnp.float32)
        for r in range(GROUP_REQUESTS):
            for step in range(STEPS):
                source = r * ROWS + step * SAMPLES
                target = (step * GROUP_REQUESTS + r) * SAMPLES
                out_ref[i, target : target + SAMPLES] = part[source : source + SAMPLES]


def outputs(mixed, weight, first, blocks, after=()):
    rows, width = GROUP_REQUESTS * ROWS, weight.shape[2]
    return pl.pallas_call(
        functools.partial(output_kernel, first),
        in_specs=[pl.BlockSpec(memory_space=pltpu.VMEM)] * 2 + unread(after),
        out_specs=pl.BlockSpec(memory_space=pltpu.VMEM),
        out_shape=jax.ShapeDtypeStruct((blocks, rows, width), jnp.float32),
        compiler_params=params(),
        cost_estimate=cost([mixed], flops=2 * rows * mixed.shape[2] * blocks * width),
        name="outputs",
    )(mixed, weight, *after)


def pieces_of(block):
    return [block[:, c : c + LANES] for c in range(0, block.shape[1], LANES)]


def encode(out_ref, pieces):
    rows = pieces[0].shape[0]
    peak = jnp.abs(pieces[0])
    for piece in pieces[1:]:
        peak = jnp.maximum(peak, jnp.abs(piece))
    peak = jnp.maximum(jnp.max(peak, axis=0, keepdims=True), 1e-30)
    exponent = jnp.floor(jnp.log2(peak)) - 14.0
    inverse = jnp.exp2(-exponent)
    for i, piece in enumerate(pieces):
        code = jnp.clip(jnp.floor(piece * inverse + 0.5), -32767.0, 32767.0)
        out_ref[i * rows : (i + 1) * rows] = code.astype(jnp.int32).astype(jnp.int16)
    out_ref[len(pieces) * rows :] = (
        jnp.broadcast_to(exponent, (TAIL, LANES)).astype(jnp.int32).astype(jnp.int16)
    )


def step_of(ref):
    tail = ref[ref.shape[0] - TAIL :].astype(jnp.int32).astype(jnp.float32)
    return jnp.exp2(tail[:1])


def decoded(ref, first, rows, step):
    return ref[pl.ds(first, rows)].astype(jnp.int32).astype(jnp.float32) * step


def fold_core_kernel(mine_ref, got_ref, *out_refs):
    for i, out_ref in enumerate(out_refs):
        pieces = []
        for z in range(GROUP_REQUESTS):
            block = i * GROUP_REQUESTS + z
            pieces += pieces_of(mine_ref[block] + got_ref[block])
        encode(out_ref, pieces)


def fold_core(mine, got):
    blocks, rows, width = mine.shape
    count = blocks // GROUP_REQUESTS
    sent = jax.ShapeDtypeStruct(
        (GROUP_REQUESTS * width // LANES * rows + TAIL, LANES), jnp.int16
    )
    return pl.pallas_call(
        fold_core_kernel,
        in_specs=[pl.BlockSpec(memory_space=pltpu.VMEM)] * 2,
        out_specs=[pl.BlockSpec(memory_space=pltpu.VMEM)] * count,
        out_shape=[sent] * count,
        compiler_params=params(),
        cost_estimate=cost([mine, got]),
        name="fold_core",
    )(mine, got)


def fold_sub_kernel(count, own, *refs):
    own_refs, in_refs, out_refs = refs[:own], refs[own : own + count], refs[-GROUP_REQUESTS:]
    _, rows, width = own_refs[0].shape
    steps = [step_of(ref) for ref in in_refs]
    for z, out_ref in enumerate(out_refs):
        block = own_refs[0][z]
        for ref in own_refs[1:]:
            block = block + ref[z]
        pieces = pieces_of(block)
        for c in range(len(pieces)):
            for ref, step in zip(in_refs, steps):
                first = (z * len(pieces) + c) * rows
                pieces[c] = pieces[c] + decoded(ref, first, rows, step)
        if z:
            encode(out_ref, pieces)
        else:
            for c, piece in enumerate(pieces):
                out_ref[:, c * LANES : (c + 1) * LANES] = piece


def fold_sub(own, parts, after=()):
    _, rows, width = own[0].shape
    total = jax.ShapeDtypeStruct((rows, width), jnp.float32)
    sent = jax.ShapeDtypeStruct((width // LANES * rows + TAIL, LANES), jnp.int16)
    return pl.pallas_call(
        functools.partial(fold_sub_kernel, len(parts), len(own)),
        in_specs=[pl.BlockSpec(memory_space=pltpu.VMEM)] * (len(own) + len(parts))
        + unread(after),
        out_specs=[pl.BlockSpec(memory_space=pltpu.VMEM)] * GROUP_REQUESTS,
        out_shape=[total] + [sent] * (GROUP_REQUESTS - 1),
        compiler_params=params(),
        cost_estimate=cost(own, parts),
        name="fold_sub",
    )(*own, *parts, *after)


def fold_pairs_kernel(count, total_ref, *refs):
    rows = total_ref.shape[0]
    refs, out_ref = refs[:count], refs[-1]
    steps = [step_of(ref) for ref in refs]
    for c in range(total_ref.shape[1] // LANES):
        part = slice(c * LANES, (c + 1) * LANES)
        total = total_ref[:, part]
        for ref, step in zip(refs, steps):
            total = total + decoded(ref, c * rows, rows, step)
        out_ref[:, part] = total


def fold_pairs(total, parts, after=()):
    return pl.pallas_call(
        functools.partial(fold_pairs_kernel, len(parts)),
        in_specs=[pl.BlockSpec(memory_space=pltpu.VMEM)] * (1 + len(parts)) + unread(after),
        out_specs=pl.BlockSpec(memory_space=pltpu.VMEM),
        out_shape=jax.ShapeDtypeStruct(total.shape, jnp.float32),
        compiler_params=params(),
        cost_estimate=cost([total], parts),
        name="fold_pairs",
    )(total, *parts, *after)


def finish_kernel(rows_ref, total_ref, *refs):
    rows = total_ref.shape[0]
    steps = [step_of(ref) for ref in refs[:-1]]
    for c in range(total_ref.shape[1] // LANES):
        part = slice(c * LANES, (c + 1) * LANES)
        total = total_ref[:, part]
        for ref, step in zip(refs[:-1], steps):
            total = total + decoded(ref, c * rows, rows, step)
        refs[-1][:, part] = (total + rows_ref[0, :, part].astype(jnp.float32)).astype(
            jnp.bfloat16
        )


def finish(rows, total, parts):
    return pl.pallas_call(
        finish_kernel,
        in_specs=[pl.BlockSpec(memory_space=pltpu.VMEM)] * (2 + len(parts)),
        out_specs=pl.BlockSpec(memory_space=pltpu.VMEM),
        out_shape=jax.ShapeDtypeStruct(total.shape, jnp.bfloat16),
        compiler_params=params(),
        cost_estimate=cost([total], parts),
        name="finish",
    )(rows, total, *parts)


def passed(array, axis, shift):
    return lax.ppermute(array, axis, [(i, i ^ shift) for i in range(lax.axis_size(axis))])


def scalars(*values):
    return jnp.stack([jnp.asarray(value, jnp.int32) for value in values])


def shards(
    hidden,
    norm_gain,
    w_query,
    key_value_weight,
    w_output,
    prompt_cache_pages,
    per_page_scales,
    lengths,
    block_table,
):
    devices = lax.axis_size(DEVICES)
    subs = lax.axis_size("sub")
    device = lax.axis_index(DEVICES)
    request = lax.axis_index("req")
    sub = lax.axis_index("sub")
    core = lax.axis_index("section")
    width = hidden.shape[2]
    place = scalars(request, sub, core)

    rows = hidden.reshape(GROUP_REQUESTS * ROWS, width)
    column = [passed(rows, "req", s) for s in range(1, GROUP_REQUESTS)]
    where = scalars(request, sub * 2 + core, device * prompt_cache_pages.shape[0])
    rows, *pages = used_pages(
        prompt_cache_pages, per_page_scales, block_table, where, subs, rows
    )
    column = pack([rows] + column)
    gathered = [passed(column, "sub", s) for s in range(1, subs)]
    pages[1:] = [passed(pages[s], "req", s) for s in range(1, GROUP_REQUESTS)]
    key_value_weight, ready, gain = staged(
        place,
        key_value_weight,
        PAIR,
        pair_order(subs),
        more=[norm_gain.reshape(devices, 1, width)],
        after=[column],
    )
    gathered = [column] + list(gate(gathered, after=[ready]))
    gathered = gathered + [passed(part, "section", 1) for part in gathered]

    half = HEAD_SIZE // 2
    freqs = jnp.exp(
        -jnp.log(theta_base) * jnp.arange(half, dtype=jnp.float32) * (2.0 / HEAD_SIZE)
    )
    positions = (lengths[None, :] + jnp.arange(STEPS)[:, None]).astype(jnp.float32)
    angles = positions[..., None] * freqs
    cosine, sine = jnp.cos(angles), jnp.sin(angles)
    cosine = jnp.repeat(jnp.concatenate([cosine, cosine], axis=-1)[:, :, None], SAMPLES, axis=2)
    sine = jnp.repeat(jnp.concatenate([-sine, sine], axis=-1)[:, :, None], SAMPLES, axis=2)
    cosine = cosine.reshape(-1, HEAD_SIZE)
    sine = sine.reshape(-1, HEAD_SIZE)

    scale, kept, *parts = scale_and_pairs(place, gain, key_value_weight, gathered)
    parts = [passed(part, "sub", s + 1) for s, part in enumerate(parts)]
    query = queries(place, scale, gain, w_query, cosine, sine, gathered)
    total, *parts = fold_sub([kept], parts, after=[query])
    parts = [passed(part, "req", s + 1) for s, part in enumerate(parts)]
    pages = regroup(pages, after=[total])
    caches = [passed(pages[s], "sub", s) for s in range(1, subs)]
    w_output, ready = staged(place, w_output, width, output_order(subs), after=[query])
    mine = fold_pairs(total, parts, after=[ready])
    caches = list(pages[:1]) + list(gate(caches, after=[mine]))
    caches = caches + [passed(part, "section", 1) for part in caches]
    other = passed(mine, "section", 1)

    mixed = attend(
        place, lengths.astype(jnp.int32), query, mine, other, cosine, sine, caches
    )

    mid, end = GROUP_REQUESTS, GROUP_REQUESTS * subs
    first = outputs(mixed, w_output, end + mid, end - mid)
    got_first = passed(first, "section", 1)
    second = outputs(mixed, w_output, end, mid, after=[first])
    got_second = passed(second, "section", 1)
    kept = outputs(mixed, w_output, mid, end - mid, after=[second])
    parts = fold_core(kept, got_first)
    kept = outputs(mixed, w_output, 0, mid, after=parts[:1])
    parts = [passed(part, "sub", s + 1) for s, part in enumerate(parts)]
    total, *parts = fold_sub([kept, got_second], parts)
    parts = [passed(part, "req", s + 1) for s, part in enumerate(parts)]
    return finish(gathered[0], total, parts).reshape(hidden.shape)


def solution(mesh):
    groups, tp, section = mesh.devices.shape
    finer = Mesh(
        mesh.devices.reshape(groups, GROUP_REQUESTS, tp // GROUP_REQUESTS, section),
        ("groups",) + DEVICES,
    )
    placed = (
        P(None, "groups", DEVICES),
        P(),
        P(None, DEVICES),
        P(DEVICES, None),
        P(DEVICES, None),
        P(("groups",) + DEVICES, None, None),
        P(("groups",) + DEVICES, None),
        P("groups"),
        P("groups", None),
    )
    return jax.shard_map(
        shards,
        mesh=finer,
        in_specs=placed,
        out_specs=P(None, "groups", DEVICES),
        check_vma=False,
    )
```

```python
import functools

import jax
import jax.numpy as jnp
from jax import lax
from jax.experimental import pallas as pl
from jax.experimental.pallas import tpu as pltpu
from jax.sharding import Mesh
from jax.sharding import PartitionSpec as P

QUERY_HEADS = 64
KEY_VALUE_HEADS = 8
HEAD_SIZE = 128
GROUP_REQUESTS = 4
SAMPLES = 8
PAGE_TOKENS = 16
STEPS = 2
ROWS = STEPS * SAMPLES
PAIR = 2 * HEAD_SIZE
LANES = 128
TAIL = 16
HALVES = ((0, 3), (1, 2))
DEVICES = ("req", "sub", "section")

theta_base = 500000.0
eps_norm = 1e-05
VMEM = 16 * 2**20
LARGE_VMEM = 51 * 2**20


def params(**more):
    return pltpu.CompilerParams(vmem_limit_bytes=VMEM, **more)


def cost(*groups, flops=0):
    size = sum(array.size * array.dtype.itemsize for arrays in groups for array in arrays)
    return pl.CostEstimate(flops=flops, bytes_accessed=size, transcendentals=0)


def unread(arrays):
    return [pl.BlockSpec(memory_space=pl.ANY)] * len(arrays)


def turn(vectors, cosine, sine):
    return vectors * cosine + pltpu.roll(vectors, HEAD_SIZE // 2, vectors.ndim - 1) * sine


def stage_kernel(order, count, place, block_ref, *refs):
    out_ref, token_ref, *outs, sems = refs[-3 - count :]
    width = out_ref.shape[2]
    copies = [
        pltpu.make_async_copy(refs[i], outs[i], sems.at[len(order) + i]) for i in range(count)
    ]
    for i, block in enumerate(order):
        columns = pl.ds(pl.multiple_of(block(place) * width, width), width)
        copies.append(pltpu.make_async_copy(block_ref.at[:, columns], out_ref.at[i], sems.at[i]))
    for copy in copies:
        copy.start()
    token_ref[...] = jnp.zeros_like(token_ref)
    for copy in copies:
        copy.wait()


def staged(place, array, width, order, more=(), after=()):
    rows, count = array.shape[0], len(order)
    return pl.pallas_call(
        functools.partial(stage_kernel, order, len(more)),
        in_specs=[pl.BlockSpec(memory_space=pltpu.SMEM)]
        + [pl.BlockSpec(memory_space=pltpu.HBM)] * (1 + len(more))
        + unread(after),
        out_specs=[pl.BlockSpec(memory_space=pltpu.VMEM)] * (2 + len(more)),
        out_shape=[
            jax.ShapeDtypeStruct((count, rows, width), array.dtype),
            jax.ShapeDtypeStruct((8, LANES), jnp.float32),
        ]
        + [jax.ShapeDtypeStruct(other.shape, other.dtype) for other in more],
        scratch_shapes=[pltpu.SemaphoreType.DMA((count + len(more),))],
        compiler_params=params(),
        cost_estimate=cost([array] * 2),
        name="staged",
    )(place, array, *more, *after)


def pair_order(subs):
    return [
        lambda place, j=j, z=z: 2 * (place[0] ^ z) + (place[1] ^ j) // (subs // 2)
        for j in range(subs)
        for z in range(GROUP_REQUESTS)
    ]


def output_order(subs):
    return [
        lambda place, c=c, j=j, z=z: ((place[0] ^ z) * subs + (place[1] ^ j)) * 2 + (place[2] ^ c)
        for c in range(2)
        for j in range(subs)
        for z in range(GROUP_REQUESTS)
    ]


def gate_kernel(*refs):
    pass


def gate(arrays, after):
    count = len(arrays)
    return pl.pallas_call(
        gate_kernel,
        in_specs=[pl.BlockSpec(memory_space=pl.ANY)] * count + unread(after),
        out_specs=[pl.BlockSpec(memory_space=pl.ANY)] * count,
        out_shape=[jax.ShapeDtypeStruct(array.shape, array.dtype) for array in arrays],
        input_output_aliases={i: i for i in range(count)},
        compiler_params=params(),
        name="gate",
    )(*arrays, *after)


def pages_kernel(table, place, scales, page_ref, rows_ref, rows_out_ref, *out_refs):
    e = pl.program_id(0)
    rows_out_ref[...] = rows_ref[...]
    subs = out_refs[0].shape[0]
    targets = 2 * subs
    page = table[place[0], e * targets + place[1]] - place[2]
    for z, out_ref in enumerate(out_refs):
        for j in range(subs):
            half = (place[1] // 2 ^ j) // (subs // 2)
            head = 2 * (place[0] ^ z) + half
            for part in range(2):
                c = head * 2 + part
                columns = pl.ds(pl.multiple_of(c * HEAD_SIZE, HEAD_SIZE), HEAD_SIZE)
                block = page_ref[0, :, columns].astype(jnp.float32)
                out_ref[j, :, part * HEAD_SIZE : (part + 1) * HEAD_SIZE] = (
                    block * scales[page, c]
                ).astype(jnp.bfloat16)


def used_pages(pages, scales, table, place, subs, rows):
    targets = 2 * subs
    entries = table.shape[1] // targets
    shape = jax.ShapeDtypeStruct((subs, entries * PAGE_TOKENS, PAIR), jnp.bfloat16)
    return pl.pallas_call(
        pages_kernel,
        grid_spec=pltpu.PrefetchScalarGridSpec(
            num_scalar_prefetch=3,
            grid=(entries,),
            in_specs=[
                pl.BlockSpec(
                    (1, PAGE_TOKENS, pages.shape[2]),
                    lambda e, table, place, scales: (
                        table[place[0], e * targets + place[1]] - place[2],
                        0,
                        0,
                    ),
                ),
                pl.BlockSpec(rows.shape, lambda e, *_: (0, 0)),
            ],
            out_specs=[pl.BlockSpec(rows.shape, lambda e, *_: (0, 0))]
            + [pl.BlockSpec((subs, PAGE_TOKENS, PAIR), lambda e, *_: (0, e, 0))]
            * GROUP_REQUESTS,
        ),
        out_shape=[jax.ShapeDtypeStruct(rows.shape, rows.dtype)] + [shape] * GROUP_REQUESTS,
        compiler_params=params(),
        cost_estimate=pl.CostEstimate(
            flops=0, bytes_accessed=4 * entries * PAGE_TOKENS * pages.shape[2], transcendentals=0
        ),
        name="used_pages",
    )(table, place, scales.astype(jnp.float32), pages, rows)


def regroup_kernel(*refs):
    ins, outs = refs[:GROUP_REQUESTS], refs[-refs[0].shape[0] :]
    for j, out_ref in enumerate(outs):
        for z, ref in enumerate(ins):
            out_ref[z] = ref[j]


def regroup(parts, after=()):
    subs = parts[0].shape[0]
    shape = jax.ShapeDtypeStruct((len(parts),) + parts[0].shape[1:], parts[0].dtype)
    return pl.pallas_call(
        regroup_kernel,
        in_specs=[pl.BlockSpec(memory_space=pltpu.VMEM)] * len(parts) + unread(after),
        out_specs=[pl.BlockSpec(memory_space=pltpu.VMEM)] * subs,
        out_shape=[shape] * subs,
        compiler_params=params(),
        cost_estimate=cost(parts, parts),
        name="regroup",
    )(*parts, *after)


def pack_kernel(*refs):
    for i in range(refs[-1].shape[0]):
        refs[-1][i] = refs[i][...]


def pack(parts):
    return pl.pallas_call(
        pack_kernel,
        in_specs=[pl.BlockSpec(memory_space=pltpu.VMEM)] * len(parts),
        out_specs=pl.BlockSpec(memory_space=pltpu.VMEM),
        out_shape=jax.ShapeDtypeStruct((len(parts),) + parts[0].shape, parts[0].dtype),
        compiler_params=params(),
        cost_estimate=cost(parts, parts),
        name="pack",
    )(*parts)


def blocks_of(place, refs):
    request, sub, core = place[0], place[1], place[2]
    subs = len(refs) // 2
    for i, ref in enumerate(refs):
        from_core = core if i < subs else 1 - core
        for z in range(GROUP_REQUESTS):
            yield ref, z, ((request ^ z) * subs + (sub ^ i % subs)) * 2 + from_core


def pairs_kernel(place, gain_ref, weight_ref, *refs):
    subs = (len(refs) - 1) // 3
    x_refs, scale_ref, kept_ref, out_refs = (
        refs[: 2 * subs],
        refs[2 * subs],
        refs[2 * subs + 1],
        refs[2 * subs + 2 :],
    )
    request, sub, core = place[0], place[1], place[2]
    _, rows, width = x_refs[0].shape
    total = jnp.zeros((rows, LANES), jnp.float32)
    for ref in x_refs:
        for z in range(GROUP_REQUESTS):
            for piece in pieces_of(ref[z].astype(jnp.float32)):
                total += piece * piece
    mean = jnp.sum(total, axis=-1, keepdims=True) / (2 * subs * GROUP_REQUESTS * width)
    scale = lax.rsqrt(mean + eps_norm)
    scale_ref[...] = jnp.broadcast_to(scale, scale_ref.shape)
    device = (request * subs + sub) * 2 + core
    x = x_refs[0][0].astype(jnp.float32)
    mine = (x * scale * gain_ref[device]).astype(jnp.bfloat16)
    for shift in range(subs):
        pieces = []
        for z in range(GROUP_REQUESTS):
            block = weight_ref[shift * GROUP_REQUESTS + z]
            part = jnp.dot(mine, block, preferred_element_type=jnp.float32)
            if shift == 0:
                kept_ref[z] = part
            pieces += pieces_of(part)
        if shift:
            encode(out_refs[shift - 1], pieces)


def scale_and_pairs(place, gain, weight, gathered):
    subs = len(gathered) // 2
    count = gathered[0].shape[1]
    sent = jax.ShapeDtypeStruct((2 * GROUP_REQUESTS * count + TAIL, LANES), jnp.int16)
    shapes = [
        jax.ShapeDtypeStruct((count, LANES), jnp.float32),
        jax.ShapeDtypeStruct((GROUP_REQUESTS, count, PAIR), jnp.float32),
    ] + [sent] * (subs - 1)
    return pl.pallas_call(
        pairs_kernel,
        in_specs=[pl.BlockSpec(memory_space=pltpu.SMEM)]
        + [pl.BlockSpec(memory_space=pltpu.VMEM)] * (2 + len(gathered)),
        out_specs=[pl.BlockSpec(memory_space=pltpu.VMEM)] * len(shapes),
        out_shape=shapes,
        compiler_params=params(),
        cost_estimate=cost(gathered * 1, [weight], flops=2 * count * weight.size),
        name="scale_and_pairs",
    )(place, gain, weight, *gathered)


def query_kernel(place, scale_ref, gain_ref, weight_ref, cos_ref, sin_ref, *refs):
    x_refs, out_ref, held, sems = refs[:-3], refs[-3], refs[-2], refs[-1]
    _, rows, width = x_refs[0].shape
    columns = weight_ref.shape[1]
    blocks = list(blocks_of(place, x_refs))
    copies = []
    for i, (_, _, block) in enumerate(blocks):
        depth = pl.ds(pl.multiple_of(block * width, width), width)
        copies.append(pltpu.make_async_copy(weight_ref.at[depth], held.at[i], sems.at[i]))
    for copy in copies:
        copy.start()
    scale = scale_ref[:, :1]
    total = jnp.zeros((rows, columns), jnp.float32)
    for i, (ref, z, block) in enumerate(blocks):
        x = ref[z].astype(jnp.float32)
        x = (x * scale * gain_ref[block]).astype(jnp.bfloat16)
        copies[i].wait()
        total += jnp.dot(x, held[i], preferred_element_type=jnp.float32)
    for head in range(columns // HEAD_SIZE):
        part = slice(head * HEAD_SIZE, (head + 1) * HEAD_SIZE)
        turned = turn(total[:, part], cos_ref[...], sin_ref[...])
        for r in range(GROUP_REQUESTS):
            first, second = r * SAMPLES, (GROUP_REQUESTS + r) * SAMPLES
            out_ref[r, :, part] = jnp.concatenate(
                [turned[first : first + SAMPLES], turned[second : second + SAMPLES]], axis=0
            ).astype(jnp.bfloat16)


def queries(place, scale, gain, weight, cosine, sine, gathered):
    columns = weight.shape[1]
    _, rows, width = gathered[0].shape
    blocks = weight.shape[0] // width
    return pl.pallas_call(
        query_kernel,
        in_specs=[pl.BlockSpec(memory_space=pltpu.SMEM)]
        + [pl.BlockSpec(memory_space=pltpu.VMEM)] * 2
        + [pl.BlockSpec(memory_space=pltpu.HBM)]
        + [pl.BlockSpec(memory_space=pltpu.VMEM)] * (2 + len(gathered)),
        out_specs=pl.BlockSpec(memory_space=pltpu.VMEM),
        out_shape=jax.ShapeDtypeStruct((GROUP_REQUESTS, ROWS, columns), jnp.bfloat16),
        scratch_shapes=[
            pltpu.VMEM((blocks, width, columns), jnp.bfloat16),
            pltpu.SemaphoreType.DMA((blocks,)),
        ],
        compiler_params=pltpu.CompilerParams(vmem_limit_bytes=LARGE_VMEM),
        cost_estimate=cost([weight], flops=2 * rows * weight.size),
        name="queries",
    )(place, scale, gain, weight, cosine, sine, *gathered)


def attend_kernel(place, lengths, q_ref, mine_ref, other_ref, cos_ref, sin_ref, *refs):
    caches, out_ref, key_ref, value_ref = refs[:-3], refs[-3], refs[-2], refs[-1]
    request, sub, core = place[0], place[1], place[2]
    subs, span = len(caches) // 2, caches[0].shape[1]
    targets = 2 * subs
    tokens = targets * span
    quarter = q_ref.shape[2] // HEAD_SIZE
    pair = mine_ref[...] + other_ref[...]
    key_ref[...] = turn(pair[:, :HEAD_SIZE], cos_ref[...], sin_ref[...])
    value_ref[...] = pair[:, HEAD_SIZE:]
    column = lax.broadcasted_iota(jnp.int32, (1, tokens), 1)
    source, inside = column // span, column % span
    from_core = jnp.where(source < subs, core, 1 - core)
    from_sub = sub ^ source % subs
    entry = inside // PAGE_TOKENS * targets + from_sub * 2 + from_core
    position = entry * PAGE_TOKENS + inside % PAGE_TOKENS
    count = quarter * ROWS
    row = lax.broadcasted_iota(jnp.int32, (count, ROWS), 0) % ROWS
    other = lax.broadcasted_iota(jnp.int32, (count, ROWS), 1)
    own_visible = (row % SAMPLES == other % SAMPLES) & (other // SAMPLES <= row // SAMPLES)
    factor = HEAD_SIZE ** (-0.5)
    contract = (((1,), (1,)), ((), ()))
    for z in range(GROUP_REQUESTS):
        r = request ^ z
        fresh = [
            pl.ds(pl.multiple_of((step * GROUP_REQUESTS + r) * SAMPLES, SAMPLES), SAMPLES)
            for step in range(STEPS)
        ]
        new_key = jnp.concatenate([key_ref[rows] for rows in fresh], axis=0)
        new_value = jnp.concatenate([value_ref[rows] for rows in fresh], axis=0)
        new_key, new_value = new_key.astype(jnp.bfloat16), new_value.astype(jnp.bfloat16)
        keys = jnp.concatenate([ref[z, :, :HEAD_SIZE] for ref in caches], axis=0)
        values = jnp.concatenate([ref[z, :, HEAD_SIZE:] for ref in caches], axis=0)
        query = jnp.concatenate(
            [q_ref[r, :, h * HEAD_SIZE : (h + 1) * HEAD_SIZE] for h in range(quarter)], axis=0
        )
        scores = lax.dot_general(query, keys, contract, preferred_element_type=jnp.float32)
        scores = jnp.where(position < lengths[r], scores * factor, -jnp.inf)
        own = lax.dot_general(query, new_key, contract, preferred_element_type=jnp.float32)
        own = jnp.where(own_visible, own * factor, -jnp.inf)
        highest = jnp.maximum(
            jnp.max(scores, axis=-1, keepdims=True), jnp.max(own, axis=-1, keepdims=True)
        )
        scores = jnp.exp(scores - highest)
        own = jnp.exp(own - highest)
        total = jnp.sum(scores, axis=-1, keepdims=True) + jnp.sum(own, axis=-1, keepdims=True)
        mixed = jnp.dot(
            (scores / total).astype(jnp.bfloat16), values, preferred_element_type=jnp.float32
        ) + jnp.dot(
            (own / total).astype(jnp.bfloat16), new_value, preferred_element_type=jnp.float32
        )
        mixed = mixed.astype(jnp.bfloat16)
        for h in range(quarter):
            out_ref[r, :, h * HEAD_SIZE : (h + 1) * HEAD_SIZE] = mixed[
                h * ROWS : (h + 1) * ROWS
            ]


def attend(place, lengths, query, mine, other, cosine, sine, caches):
    return pl.pallas_call(
        attend_kernel,
        in_specs=[pl.BlockSpec(memory_space=pltpu.SMEM)] * 2
        + [pl.BlockSpec(memory_space=pltpu.VMEM)] * (5 + len(caches)),
        out_specs=pl.BlockSpec(memory_space=pltpu.VMEM),
        out_shape=jax.ShapeDtypeStruct(query.shape, jnp.bfloat16),
        scratch_shapes=[pltpu.VMEM(cosine.shape, jnp.float32)] * 2,
        compiler_params=params(),
        cost_estimate=cost(caches, caches, caches, flops=2**28),
        name="attend",
    )(place, lengths, query, mine, other, cosine, sine, *caches)


def output_kernel(first, x_ref, weight_ref, *refs):
    out_ref = refs[-1]
    blocks, rows, width = out_ref.shape
    x = x_ref[...].reshape(rows, -1)
    for i in range(blocks):
        part = jnp.dot(x, weight_ref[first + i], preferred_element_type=jnp.float32)
        for r in range(GROUP_REQUESTS):
            for step in range(STEPS):
                source = r * ROWS + step * SAMPLES
                target = (step * GROUP_REQUESTS + r) * SAMPLES
                out_ref[i, target : target + SAMPLES] = part[source : source + SAMPLES]


def outputs(mixed, weight, first, blocks, after=()):
    rows, width = GROUP_REQUESTS * ROWS, weight.shape[2]
    return pl.pallas_call(
        functools.partial(output_kernel, first),
        in_specs=[pl.BlockSpec(memory_space=pltpu.VMEM)] * 2 + unread(after),
        out_specs=pl.BlockSpec(memory_space=pltpu.VMEM),
        out_shape=jax.ShapeDtypeStruct((blocks, rows, width), jnp.float32),
        compiler_params=params(),
        cost_estimate=cost([mixed], flops=2 * rows * mixed.shape[2] * blocks * width),
        name="outputs",
    )(mixed, weight, *after)


def pieces_of(block):
    return [block[:, c : c + LANES] for c in range(0, block.shape[1], LANES)]


def encode(out_ref, pieces):
    rows = pieces[0].shape[0]
    peak = jnp.abs(pieces[0])
    for piece in pieces[1:]:
        peak = jnp.maximum(peak, jnp.abs(piece))
    peak = jnp.maximum(jnp.max(peak, axis=0, keepdims=True), 1e-30)
    exponent = jnp.floor(jnp.log2(peak)) - 14.0
    inverse = jnp.exp2(-exponent)
    for i, piece in enumerate(pieces):
        code = jnp.clip(jnp.floor(piece * inverse + 0.5), -32767.0, 32767.0)
        out_ref[i * rows : (i + 1) * rows] = code.astype(jnp.int32).astype(jnp.int16)
    out_ref[len(pieces) * rows :] = (
        jnp.broadcast_to(exponent, (TAIL, LANES)).astype(jnp.int32).astype(jnp.int16)
    )


def step_of(ref):
    tail = ref[ref.shape[0] - TAIL :].astype(jnp.int32).astype(jnp.float32)
    return jnp.exp2(tail[:1])


def decoded(ref, first, rows, step):
    return ref[pl.ds(first, rows)].astype(jnp.int32).astype(jnp.float32) * step


def fold_core_kernel(mine_ref, got_ref, *out_refs):
    for i, out_ref in enumerate(out_refs):
        pieces = []
        for z in HALVES[i % 2]:
            block = i // 2 * GROUP_REQUESTS + z
            pieces += pieces_of(mine_ref[block] + got_ref[block])
        encode(out_ref, pieces)


def fold_core(mine, got):
    blocks, rows, width = mine.shape
    count = 2 * (blocks // GROUP_REQUESTS)
    sent = jax.ShapeDtypeStruct((2 * width // LANES * rows + TAIL, LANES), jnp.int16)
    return pl.pallas_call(
        fold_core_kernel,
        in_specs=[pl.BlockSpec(memory_space=pltpu.VMEM)] * 2,
        out_specs=[pl.BlockSpec(memory_space=pltpu.VMEM)] * count,
        out_shape=[sent] * count,
        compiler_params=params(),
        cost_estimate=cost([mine, got]),
        name="fold_core",
    )(mine, got)


def fold_sub_kernel(order, count, own, *refs):
    own_refs, in_refs, out_refs = refs[:own], refs[own : own + count], refs[-len(order) :]
    _, rows, width = own_refs[0].shape
    steps = [step_of(ref) for ref in in_refs]
    for i, (z, out_ref) in enumerate(zip(order, out_refs)):
        block = own_refs[0][z]
        for ref in own_refs[1:]:
            block = block + ref[z]
        pieces = pieces_of(block)
        for c in range(len(pieces)):
            for ref, step in zip(in_refs, steps):
                first = (i * len(pieces) + c) * rows
                pieces[c] = pieces[c] + decoded(ref, first, rows, step)
        if z:
            encode(out_ref, pieces)
        else:
            for c, piece in enumerate(pieces):
                out_ref[:, c * LANES : (c + 1) * LANES] = piece


def fold_sub(order, own, parts, after=()):
    _, rows, width = own[0].shape
    total = jax.ShapeDtypeStruct((rows, width), jnp.float32)
    sent = jax.ShapeDtypeStruct((width // LANES * rows + TAIL, LANES), jnp.int16)
    return pl.pallas_call(
        functools.partial(fold_sub_kernel, order, len(parts), len(own)),
        in_specs=[pl.BlockSpec(memory_space=pltpu.VMEM)] * (len(own) + len(parts))
        + unread(after),
        out_specs=[pl.BlockSpec(memory_space=pltpu.VMEM)] * len(order),
        out_shape=[sent if z else total for z in order],
        compiler_params=params(),
        cost_estimate=cost(own, parts),
        name="fold_sub",
    )(*own, *parts, *after)


def fold_pairs_kernel(count, total_ref, *refs):
    rows = total_ref.shape[0]
    refs, out_ref = refs[:count], refs[-1]
    steps = [step_of(ref) for ref in refs]
    for c in range(total_ref.shape[1] // LANES):
        part = slice(c * LANES, (c + 1) * LANES)
        total = total_ref[:, part]
        for ref, step in zip(refs, steps):
            total = total + decoded(ref, c * rows, rows, step)
        out_ref[:, part] = total


def fold_pairs(total, parts, after=()):
    return pl.pallas_call(
        functools.partial(fold_pairs_kernel, len(parts)),
        in_specs=[pl.BlockSpec(memory_space=pltpu.VMEM)] * (1 + len(parts)) + unread(after),
        out_specs=pl.BlockSpec(memory_space=pltpu.VMEM),
        out_shape=jax.ShapeDtypeStruct(total.shape, jnp.float32),
        compiler_params=params(),
        cost_estimate=cost([total], parts),
        name="fold_pairs",
    )(total, *parts, *after)


def finish_kernel(rows_ref, total_ref, *refs):
    rows = total_ref.shape[0]
    steps = [step_of(ref) for ref in refs[:-1]]
    for c in range(total_ref.shape[1] // LANES):
        part = slice(c * LANES, (c + 1) * LANES)
        total = total_ref[:, part]
        for ref, step in zip(refs[:-1], steps):
            total = total + decoded(ref, c * rows, rows, step)
        refs[-1][:, part] = (total + rows_ref[0, :, part].astype(jnp.float32)).astype(
            jnp.bfloat16
        )


def finish(rows, total, parts):
    return pl.pallas_call(
        finish_kernel,
        in_specs=[pl.BlockSpec(memory_space=pltpu.VMEM)] * (2 + len(parts)),
        out_specs=pl.BlockSpec(memory_space=pltpu.VMEM),
        out_shape=jax.ShapeDtypeStruct(total.shape, jnp.bfloat16),
        compiler_params=params(),
        cost_estimate=cost([total], parts),
        name="finish",
    )(rows, total, *parts)


def passed(array, axis, shift):
    return lax.ppermute(array, axis, [(i, i ^ shift) for i in range(lax.axis_size(axis))])


def scalars(*values):
    return jnp.stack([jnp.asarray(value, jnp.int32) for value in values])


def shards(
    hidden,
    norm_gain,
    w_query,
    key_value_weight,
    w_output,
    prompt_cache_pages,
    per_page_scales,
    lengths,
    block_table,
):
    devices = lax.axis_size(DEVICES)
    subs = lax.axis_size("sub")
    device = lax.axis_index(DEVICES)
    request = lax.axis_index("req")
    sub = lax.axis_index("sub")
    core = lax.axis_index("section")
    width = hidden.shape[2]
    place = scalars(request, sub, core)

    rows = hidden.reshape(GROUP_REQUESTS * ROWS, width)
    column = [passed(rows, "req", s) for s in range(1, GROUP_REQUESTS)]
    where = scalars(request, sub * 2 + core, device * prompt_cache_pages.shape[0])
    rows, *pages = used_pages(
        prompt_cache_pages, per_page_scales, block_table, where, subs, rows
    )
    column = pack([rows] + column)
    gathered = [passed(column, "sub", s) for s in range(1, subs)]
    pages[1:] = [passed(pages[s], "req", s) for s in range(1, GROUP_REQUESTS)]
    key_value_weight, ready, gain = staged(
        place,
        key_value_weight,
        PAIR,
        pair_order(subs),
        more=[norm_gain.reshape(devices, 1, width)],
        after=[column],
    )
    gathered = [column] + list(gate(gathered, after=[ready]))
    gathered = gathered + [passed(part, "section", 1) for part in gathered]

    half = HEAD_SIZE // 2
    freqs = jnp.exp(
        -jnp.log(theta_base) * jnp.arange(half, dtype=jnp.float32) * (2.0 / HEAD_SIZE)
    )
    positions = (lengths[None, :] + jnp.arange(STEPS)[:, None]).astype(jnp.float32)
    angles = positions[..., None] * freqs
    cosine, sine = jnp.cos(angles), jnp.sin(angles)
    cosine = jnp.repeat(jnp.concatenate([cosine, cosine], axis=-1)[:, :, None], SAMPLES, axis=2)
    sine = jnp.repeat(jnp.concatenate([-sine, sine], axis=-1)[:, :, None], SAMPLES, axis=2)
    cosine = cosine.reshape(-1, HEAD_SIZE)
    sine = sine.reshape(-1, HEAD_SIZE)

    scale, kept, *parts = scale_and_pairs(place, gain, key_value_weight, gathered)
    parts = [passed(part, "sub", s + 1) for s, part in enumerate(parts)]
    query = queries(place, scale, gain, w_query, cosine, sine, gathered)
    total, *parts = fold_sub((0, 1, 2, 3), [kept], parts, after=[query])
    parts = [passed(part, "req", s + 1) for s, part in enumerate(parts)]
    pages = regroup(pages, after=[total])
    caches = [passed(pages[s], "sub", s) for s in range(1, subs)]
    w_output, ready = staged(place, w_output, width, output_order(subs), after=[query])
    mine = fold_pairs(total, parts, after=[ready])
    caches = list(pages[:1]) + list(gate(caches, after=[mine]))
    caches = caches + [passed(part, "section", 1) for part in caches]
    other = passed(mine, "section", 1)

    mixed = attend(
        place, lengths.astype(jnp.int32), query, mine, other, cosine, sine, caches
    )

    mid, end = GROUP_REQUESTS, GROUP_REQUESTS * subs
    first = outputs(mixed, w_output, end + mid, end - mid)
    got_first = passed(first, "section", 1)
    second = outputs(mixed, w_output, end, mid, after=[first])
    got_second = passed(second, "section", 1)
    kept = outputs(mixed, w_output, mid, end - mid, after=[second])
    parts = fold_core(kept, got_first)
    kept = outputs(mixed, w_output, 0, mid, after=parts[:1])
    parts = [passed(part, "sub", i // 2 + 1) for i, part in enumerate(parts)]
    last = {}
    for half, order in enumerate(HALVES):
        last.update(zip(order, fold_sub(order, [kept, got_second], parts[half::2])))
    parts = [passed(last[s], "req", s) for s in range(1, GROUP_REQUESTS)]
    return finish(gathered[0], last[0], parts).reshape(hidden.shape)


def solution(mesh):
    groups, tp, section = mesh.devices.shape
    finer = Mesh(
        mesh.devices.reshape(groups, GROUP_REQUESTS, tp // GROUP_REQUESTS, section),
        ("groups",) + DEVICES,
    )
    placed = (
        P(None, "groups", DEVICES),
        P(),
        P(None, DEVICES),
        P(DEVICES, None),
        P(DEVICES, None),
        P(("groups",) + DEVICES, None, None),
        P(("groups",) + DEVICES, None),
        P("groups"),
        P("groups", None),
    )
    return jax.shard_map(
        shards,
        mesh=finer,
        in_specs=placed,
        out_specs=P(None, "groups", DEVICES),
        check_vma=False,
    )
```

```python
import functools

import jax
import jax.numpy as jnp
from jax import lax
from jax.experimental import pallas as pl
from jax.experimental.pallas import tpu as pltpu
from jax.sharding import Mesh
from jax.sharding import PartitionSpec as P

QUERY_HEADS = 64
KEY_VALUE_HEADS = 8
HEAD_SIZE = 128
GROUP_REQUESTS = 4
SAMPLES = 8
PAGE_TOKENS = 16
STEPS = 2
ROWS = STEPS * SAMPLES
PAIR = 2 * HEAD_SIZE
LANES = 128
TAIL = 16
HALVES = ((2, 3), (0, 1))
DEVICES = ("req", "sub", "section")

theta_base = 500000.0
eps_norm = 1e-05
VMEM = 16 * 2**20
LARGE_VMEM = 51 * 2**20


def params(**more):
    return pltpu.CompilerParams(vmem_limit_bytes=VMEM, **more)


def cost(*groups, flops=0):
    size = sum(array.size * array.dtype.itemsize for arrays in groups for array in arrays)
    return pl.CostEstimate(flops=flops, bytes_accessed=size, transcendentals=0)


def unread(arrays):
    return [pl.BlockSpec(memory_space=pl.ANY)] * len(arrays)


def turn(vectors, cosine, sine):
    return vectors * cosine + pltpu.roll(vectors, HEAD_SIZE // 2, vectors.ndim - 1) * sine


def block_copies(order, place, block_ref, out_ref, sems):
    width = out_ref.shape[2]
    copies = []
    for i, block in enumerate(order):
        columns = pl.ds(pl.multiple_of(block(place) * width, width), width)
        copies.append(pltpu.make_async_copy(block_ref.at[:, columns], out_ref.at[i], sems.at[i]))
    return copies


def stage_kernel(order, count, place, block_ref, *refs):
    out_ref, token_ref, *outs, sems = refs[-3 - count :]
    copies = block_copies(order, place, block_ref, out_ref, sems)
    for i in range(count):
        copies.append(pltpu.make_async_copy(refs[i], outs[i], sems.at[len(order) + i]))
    for copy in copies:
        copy.start()
    token_ref[...] = jnp.zeros_like(token_ref)
    for copy in copies:
        copy.wait()


def staged(place, array, width, order, more=(), after=()):
    rows, count = array.shape[0], len(order)
    return pl.pallas_call(
        functools.partial(stage_kernel, order, len(more)),
        in_specs=[pl.BlockSpec(memory_space=pltpu.SMEM)]
        + [pl.BlockSpec(memory_space=pltpu.HBM)] * (1 + len(more))
        + unread(after),
        out_specs=[pl.BlockSpec(memory_space=pltpu.VMEM)] * (2 + len(more)),
        out_shape=[
            jax.ShapeDtypeStruct((count, rows, width), array.dtype),
            jax.ShapeDtypeStruct((8, LANES), jnp.float32),
        ]
        + [jax.ShapeDtypeStruct(other.shape, other.dtype) for other in more],
        scratch_shapes=[pltpu.SemaphoreType.DMA((count + len(more),))],
        compiler_params=params(),
        cost_estimate=cost([array], [array]),
        name="staged",
    )(place, array, *more, *after)


def pair_order(subs):
    return [
        lambda place, j=j, z=z: 2 * (place[0] ^ z) + (place[1] ^ j) // (subs // 2)
        for j in range(subs)
        for z in range(GROUP_REQUESTS)
    ]


def output_order(subs):
    return [
        lambda place, c=c, j=j, z=z: ((place[0] ^ z) * subs + (place[1] ^ j)) * 2 + (place[2] ^ c)
        for c in range(2)
        for j in range(subs)
        for z in range(GROUP_REQUESTS)
    ]


def gate_kernel(*refs):
    pass


def gate(arrays, after):
    count = len(arrays)
    return pl.pallas_call(
        gate_kernel,
        in_specs=[pl.BlockSpec(memory_space=pl.ANY)] * count + unread(after),
        out_specs=[pl.BlockSpec(memory_space=pl.ANY)] * count,
        out_shape=[jax.ShapeDtypeStruct(array.shape, array.dtype) for array in arrays],
        input_output_aliases={i: i for i in range(count)},
        compiler_params=params(),
        name="gate",
    )(*arrays, *after)


def pages_kernel(table, place, scales, page_ref, rows_ref, rows_out_ref, *out_refs):
    e = pl.program_id(0)
    rows_out_ref[...] = rows_ref[...]
    subs = out_refs[0].shape[0]
    targets = 2 * subs
    page = table[place[0], e * targets + place[1]] - place[2]
    for z, out_ref in enumerate(out_refs):
        for j in range(subs):
            half = (place[1] // 2 ^ j) // (subs // 2)
            head = 2 * (place[0] ^ z) + half
            for part in range(2):
                c = head * 2 + part
                columns = pl.ds(pl.multiple_of(c * HEAD_SIZE, HEAD_SIZE), HEAD_SIZE)
                block = page_ref[0, :, columns].astype(jnp.float32)
                out_ref[j, :, part * HEAD_SIZE : (part + 1) * HEAD_SIZE] = (
                    block * scales[page, c]
                ).astype(jnp.bfloat16)


def used_pages(pages, scales, table, place, subs, rows):
    targets = 2 * subs
    entries = table.shape[1] // targets
    shape = jax.ShapeDtypeStruct((subs, entries * PAGE_TOKENS, PAIR), jnp.bfloat16)
    return pl.pallas_call(
        pages_kernel,
        grid_spec=pltpu.PrefetchScalarGridSpec(
            num_scalar_prefetch=3,
            grid=(entries,),
            in_specs=[
                pl.BlockSpec(
                    (1, PAGE_TOKENS, pages.shape[2]),
                    lambda e, table, place, scales: (
                        table[place[0], e * targets + place[1]] - place[2],
                        0,
                        0,
                    ),
                ),
                pl.BlockSpec(rows.shape, lambda e, *_: (0, 0)),
            ],
            out_specs=[pl.BlockSpec(rows.shape, lambda e, *_: (0, 0))]
            + [pl.BlockSpec((subs, PAGE_TOKENS, PAIR), lambda e, *_: (0, e, 0))]
            * GROUP_REQUESTS,
        ),
        out_shape=[jax.ShapeDtypeStruct(rows.shape, rows.dtype)] + [shape] * GROUP_REQUESTS,
        compiler_params=params(),
        cost_estimate=pl.CostEstimate(
            flops=0, bytes_accessed=4 * entries * PAGE_TOKENS * pages.shape[2], transcendentals=0
        ),
        name="used_pages",
    )(table, place, scales.astype(jnp.float32), pages, rows)


def regroup_kernel(*refs):
    ins, outs = refs[:GROUP_REQUESTS], refs[-refs[0].shape[0] :]
    for j, out_ref in enumerate(outs):
        for z, ref in enumerate(ins):
            out_ref[z] = ref[j]


def regroup(parts, after=()):
    subs = parts[0].shape[0]
    shape = jax.ShapeDtypeStruct((len(parts),) + parts[0].shape[1:], parts[0].dtype)
    return pl.pallas_call(
        regroup_kernel,
        in_specs=[pl.BlockSpec(memory_space=pltpu.VMEM)] * len(parts) + unread(after),
        out_specs=[pl.BlockSpec(memory_space=pltpu.VMEM)] * subs,
        out_shape=[shape] * subs,
        compiler_params=params(),
        cost_estimate=cost(parts, parts),
        name="regroup",
    )(*parts, *after)


def pack_kernel(*refs):
    for i in range(refs[-1].shape[0]):
        refs[-1][i] = refs[i][...]


def pack(parts):
    return pl.pallas_call(
        pack_kernel,
        in_specs=[pl.BlockSpec(memory_space=pltpu.VMEM)] * len(parts),
        out_specs=pl.BlockSpec(memory_space=pltpu.VMEM),
        out_shape=jax.ShapeDtypeStruct((len(parts),) + parts[0].shape, parts[0].dtype),
        compiler_params=params(),
        cost_estimate=cost(parts, parts),
        name="pack",
    )(*parts)


def blocks_of(place, refs):
    request, sub, core = place[0], place[1], place[2]
    subs = len(refs) // 2
    for i, ref in enumerate(refs):
        from_core = core if i < subs else 1 - core
        for z in range(GROUP_REQUESTS):
            yield ref, z, ((request ^ z) * subs + (sub ^ i % subs)) * 2 + from_core


def pairs_kernel(place, gain_ref, weight_ref, *refs):
    subs = (len(refs) - 1) // 3
    x_refs, scale_ref, kept_ref, out_refs = (
        refs[: 2 * subs],
        refs[2 * subs],
        refs[2 * subs + 1],
        refs[2 * subs + 2 :],
    )
    request, sub, core = place[0], place[1], place[2]
    _, rows, width = x_refs[0].shape
    total = jnp.zeros((rows, LANES), jnp.float32)
    for ref in x_refs:
        for z in range(GROUP_REQUESTS):
            for piece in pieces_of(ref[z].astype(jnp.float32)):
                total += piece * piece
    mean = jnp.sum(total, axis=-1, keepdims=True) / (2 * subs * GROUP_REQUESTS * width)
    scale = lax.rsqrt(mean + eps_norm)
    scale_ref[...] = jnp.broadcast_to(scale, scale_ref.shape)
    device = (request * subs + sub) * 2 + core
    x = x_refs[0][0].astype(jnp.float32)
    mine = (x * scale * gain_ref[device]).astype(jnp.bfloat16)
    for shift in range(subs):
        pieces = []
        for z in range(GROUP_REQUESTS):
            block = weight_ref[shift * GROUP_REQUESTS + z]
            part = jnp.dot(mine, block, preferred_element_type=jnp.float32)
            if shift == 0:
                kept_ref[z] = part
            pieces += pieces_of(part)
        if shift:
            encode(out_refs[shift - 1], pieces)


def scale_and_pairs(place, gain, weight, gathered):
    subs = len(gathered) // 2
    count = gathered[0].shape[1]
    sent = jax.ShapeDtypeStruct((2 * GROUP_REQUESTS * count + TAIL, LANES), jnp.int16)
    shapes = [
        jax.ShapeDtypeStruct((count, LANES), jnp.float32),
        jax.ShapeDtypeStruct((GROUP_REQUESTS, count, PAIR), jnp.float32),
    ] + [sent] * (subs - 1)
    return pl.pallas_call(
        pairs_kernel,
        in_specs=[pl.BlockSpec(memory_space=pltpu.SMEM)]
        + [pl.BlockSpec(memory_space=pltpu.VMEM)] * (2 + len(gathered)),
        out_specs=[pl.BlockSpec(memory_space=pltpu.VMEM)] * len(shapes),
        out_shape=shapes,
        compiler_params=params(),
        cost_estimate=cost(gathered, [weight], flops=2 * count * weight.size),
        name="scale_and_pairs",
    )(place, gain, weight, *gathered)


def query_kernel(place, scale_ref, gain_ref, weight_ref, cos_ref, sin_ref, *refs):
    x_refs, out_ref, held, sems = refs[:-3], refs[-3], refs[-2], refs[-1]
    _, rows, width = x_refs[0].shape
    columns = weight_ref.shape[1]
    blocks = list(blocks_of(place, x_refs))
    copies = []
    for i, (_, _, block) in enumerate(blocks):
        depth = pl.ds(pl.multiple_of(block * width, width), width)
        copies.append(pltpu.make_async_copy(weight_ref.at[depth], held.at[i], sems.at[i]))
    for copy in copies:
        copy.start()
    scale = scale_ref[:, :1]
    total = jnp.zeros((rows, columns), jnp.float32)
    for i, (ref, z, block) in enumerate(blocks):
        x = ref[z].astype(jnp.float32)
        x = (x * scale * gain_ref[block]).astype(jnp.bfloat16)
        copies[i].wait()
        total += jnp.dot(x, held[i], preferred_element_type=jnp.float32)
    for head in range(columns // HEAD_SIZE):
        part = slice(head * HEAD_SIZE, (head + 1) * HEAD_SIZE)
        turned = turn(total[:, part], cos_ref[...], sin_ref[...])
        for r in range(GROUP_REQUESTS):
            first, second = r * SAMPLES, (GROUP_REQUESTS + r) * SAMPLES
            out_ref[r, :, part] = jnp.concatenate(
                [turned[first : first + SAMPLES], turned[second : second + SAMPLES]], axis=0
            ).astype(jnp.bfloat16)


def queries(place, scale, gain, weight, cosine, sine, gathered):
    columns = weight.shape[1]
    _, rows, width = gathered[0].shape
    blocks = weight.shape[0] // width
    return pl.pallas_call(
        query_kernel,
        in_specs=[pl.BlockSpec(memory_space=pltpu.SMEM)]
        + [pl.BlockSpec(memory_space=pltpu.VMEM)] * 2
        + [pl.BlockSpec(memory_space=pltpu.HBM)]
        + [pl.BlockSpec(memory_space=pltpu.VMEM)] * (2 + len(gathered)),
        out_specs=pl.BlockSpec(memory_space=pltpu.VMEM),
        out_shape=jax.ShapeDtypeStruct((GROUP_REQUESTS, ROWS, columns), jnp.bfloat16),
        scratch_shapes=[
            pltpu.VMEM((blocks, width, columns), jnp.bfloat16),
            pltpu.SemaphoreType.DMA((blocks,)),
        ],
        compiler_params=pltpu.CompilerParams(vmem_limit_bytes=LARGE_VMEM),
        cost_estimate=cost([weight], flops=2 * rows * weight.size),
        name="queries",
    )(place, scale, gain, weight, cosine, sine, *gathered)


def attend_kernel(
    order, place, lengths, q_ref, mine_ref, other_ref, cos_ref, sin_ref, block_ref, *refs
):
    caches, (out_ref, held_ref, key_ref, value_ref, sems) = refs[:-5], refs[-5:]
    copies = block_copies(order, place, block_ref, held_ref, sems)
    for copy in copies:
        copy.start()
    request, sub, core = place[0], place[1], place[2]
    subs, span = len(caches) // 2, caches[0].shape[1]
    targets = 2 * subs
    tokens = targets * span
    quarter = q_ref.shape[2] // HEAD_SIZE
    pair = mine_ref[...] + other_ref[...]
    key_ref[...] = turn(pair[:, :HEAD_SIZE], cos_ref[...], sin_ref[...])
    value_ref[...] = pair[:, HEAD_SIZE:]
    column = lax.broadcasted_iota(jnp.int32, (1, tokens), 1)
    source, inside = column // span, column % span
    from_core = jnp.where(source < subs, core, 1 - core)
    from_sub = sub ^ source % subs
    entry = inside // PAGE_TOKENS * targets + from_sub * 2 + from_core
    position = entry * PAGE_TOKENS + inside % PAGE_TOKENS
    count = quarter * ROWS
    row = lax.broadcasted_iota(jnp.int32, (count, ROWS), 0) % ROWS
    other = lax.broadcasted_iota(jnp.int32, (count, ROWS), 1)
    own_visible = (row % SAMPLES == other % SAMPLES) & (other // SAMPLES <= row // SAMPLES)
    factor = HEAD_SIZE ** (-0.5)
    contract = (((1,), (1,)), ((), ()))
    for z in range(GROUP_REQUESTS):
        r = request ^ z
        fresh = [
            pl.ds(pl.multiple_of((step * GROUP_REQUESTS + r) * SAMPLES, SAMPLES), SAMPLES)
            for step in range(STEPS)
        ]
        new_key = jnp.concatenate([key_ref[rows] for rows in fresh], axis=0)
        new_value = jnp.concatenate([value_ref[rows] for rows in fresh], axis=0)
        new_key, new_value = new_key.astype(jnp.bfloat16), new_value.astype(jnp.bfloat16)
        keys = jnp.concatenate([ref[z, :, :HEAD_SIZE] for ref in caches], axis=0)
        values = jnp.concatenate([ref[z, :, HEAD_SIZE:] for ref in caches], axis=0)
        query = jnp.concatenate(
            [q_ref[r, :, h * HEAD_SIZE : (h + 1) * HEAD_SIZE] for h in range(quarter)], axis=0
        )
        scores = lax.dot_general(query, keys, contract, preferred_element_type=jnp.float32)
        scores = jnp.where(position < lengths[r], scores * factor, -jnp.inf)
        own = lax.dot_general(query, new_key, contract, preferred_element_type=jnp.float32)
        own = jnp.where(own_visible, own * factor, -jnp.inf)
        highest = jnp.maximum(
            jnp.max(scores, axis=-1, keepdims=True), jnp.max(own, axis=-1, keepdims=True)
        )
        scores = jnp.exp(scores - highest)
        own = jnp.exp(own - highest)
        total = jnp.sum(scores, axis=-1, keepdims=True) + jnp.sum(own, axis=-1, keepdims=True)
        mixed = jnp.dot(
            (scores / total).astype(jnp.bfloat16), values, preferred_element_type=jnp.float32
        ) + jnp.dot(
            (own / total).astype(jnp.bfloat16), new_value, preferred_element_type=jnp.float32
        )
        mixed = mixed.astype(jnp.bfloat16)
        for h in range(quarter):
            out_ref[r, :, h * HEAD_SIZE : (h + 1) * HEAD_SIZE] = mixed[
                h * ROWS : (h + 1) * ROWS
            ]
    for copy in copies:
        copy.wait()


def attend(place, lengths, query, mine, other, cosine, sine, weight, width, order, caches):
    count = len(order)
    return pl.pallas_call(
        functools.partial(attend_kernel, order),
        in_specs=[pl.BlockSpec(memory_space=pltpu.SMEM)] * 2
        + [pl.BlockSpec(memory_space=pltpu.VMEM)] * 5
        + [pl.BlockSpec(memory_space=pltpu.HBM)]
        + [pl.BlockSpec(memory_space=pltpu.VMEM)] * len(caches),
        out_specs=[pl.BlockSpec(memory_space=pltpu.VMEM)] * 2,
        out_shape=[
            jax.ShapeDtypeStruct(query.shape, jnp.bfloat16),
            jax.ShapeDtypeStruct((count, weight.shape[0], width), weight.dtype),
        ],
        scratch_shapes=[pltpu.VMEM(cosine.shape, jnp.float32)] * 2
        + [pltpu.SemaphoreType.DMA((count,))],
        compiler_params=params(),
        cost_estimate=cost(caches, caches, caches, flops=2**28),
        name="attend",
    )(place, lengths, query, mine, other, cosine, sine, weight, *caches)


def output_kernel(first, x_ref, weight_ref, *refs):
    out_ref = refs[-1]
    blocks, rows, width = out_ref.shape
    x = x_ref[...].reshape(rows, -1)
    for i in range(blocks):
        part = jnp.dot(x, weight_ref[first + i], preferred_element_type=jnp.float32)
        for r in range(GROUP_REQUESTS):
            for step in range(STEPS):
                source = r * ROWS + step * SAMPLES
                target = (step * GROUP_REQUESTS + r) * SAMPLES
                out_ref[i, target : target + SAMPLES] = part[source : source + SAMPLES]


def outputs(mixed, weight, first, blocks, after=()):
    rows, width = GROUP_REQUESTS * ROWS, weight.shape[2]
    return pl.pallas_call(
        functools.partial(output_kernel, first),
        in_specs=[pl.BlockSpec(memory_space=pltpu.VMEM)] * 2 + unread(after),
        out_specs=pl.BlockSpec(memory_space=pltpu.VMEM),
        out_shape=jax.ShapeDtypeStruct((blocks, rows, width), jnp.float32),
        compiler_params=params(),
        cost_estimate=cost([mixed], flops=2 * rows * mixed.shape[2] * blocks * width),
        name="outputs",
    )(mixed, weight, *after)


def pieces_of(block):
    return [block[:, c : c + LANES] for c in range(0, block.shape[1], LANES)]


def encode(out_ref, pieces):
    rows = pieces[0].shape[0]
    peak = jnp.abs(pieces[0])
    for piece in pieces[1:]:
        peak = jnp.maximum(peak, jnp.abs(piece))
    peak = jnp.maximum(jnp.max(peak, axis=0, keepdims=True), 1e-30)
    exponent = jnp.floor(jnp.log2(peak)) - 14.0
    inverse = jnp.exp2(-exponent)
    for i, piece in enumerate(pieces):
        code = jnp.clip(jnp.floor(piece * inverse + 0.5), -32767.0, 32767.0)
        out_ref[i * rows : (i + 1) * rows] = code.astype(jnp.int32).astype(jnp.int16)
    out_ref[len(pieces) * rows :] = (
        jnp.broadcast_to(exponent, (TAIL, LANES)).astype(jnp.int32).astype(jnp.int16)
    )


def step_of(ref):
    tail = ref[ref.shape[0] - TAIL :].astype(jnp.int32).astype(jnp.float32)
    return jnp.exp2(tail[:1])


def decoded(ref, first, rows, step):
    return ref[pl.ds(first, rows)].astype(jnp.int32).astype(jnp.float32) * step


def fold_core_kernel(mine_ref, got_ref, *out_refs):
    for i, out_ref in enumerate(out_refs):
        pieces = []
        for z in HALVES[i % 2]:
            block = i // 2 * GROUP_REQUESTS + z
            pieces += pieces_of(mine_ref[block] + got_ref[block])
        encode(out_ref, pieces)


def fold_core(mine, got):
    blocks, rows, width = mine.shape
    count = 2 * (blocks // GROUP_REQUESTS)
    sent = jax.ShapeDtypeStruct((2 * width // LANES * rows + TAIL, LANES), jnp.int16)
    return pl.pallas_call(
        fold_core_kernel,
        in_specs=[pl.BlockSpec(memory_space=pltpu.VMEM)] * 2,
        out_specs=[pl.BlockSpec(memory_space=pltpu.VMEM)] * count,
        out_shape=[sent] * count,
        compiler_params=params(),
        cost_estimate=cost([mine, got]),
        name="fold_core",
    )(mine, got)


def fold_sub_kernel(order, count, own, *refs):
    own_refs, in_refs, out_refs = refs[:own], refs[own : own + count], refs[-len(order) :]
    _, rows, width = own_refs[0].shape
    steps = [step_of(ref) for ref in in_refs]
    for i, (z, out_ref) in enumerate(zip(order, out_refs)):
        block = own_refs[0][z]
        for ref in own_refs[1:]:
            block = block + ref[z]
        pieces = pieces_of(block)
        for c in range(len(pieces)):
            for ref, step in zip(in_refs, steps):
                first = (i * len(pieces) + c) * rows
                pieces[c] = pieces[c] + decoded(ref, first, rows, step)
        if z:
            encode(out_ref, pieces)
        else:
            for c, piece in enumerate(pieces):
                out_ref[:, c * LANES : (c + 1) * LANES] = piece


def fold_sub(order, own, parts, after=()):
    _, rows, width = own[0].shape
    total = jax.ShapeDtypeStruct((rows, width), jnp.float32)
    sent = jax.ShapeDtypeStruct((width // LANES * rows + TAIL, LANES), jnp.int16)
    return pl.pallas_call(
        functools.partial(fold_sub_kernel, order, len(parts), len(own)),
        in_specs=[pl.BlockSpec(memory_space=pltpu.VMEM)] * (len(own) + len(parts))
        + unread(after),
        out_specs=[pl.BlockSpec(memory_space=pltpu.VMEM)] * len(order),
        out_shape=[sent if z else total for z in order],
        compiler_params=params(),
        cost_estimate=cost(own, parts),
        name="fold_sub",
    )(*own, *parts, *after)


def fold_pairs_kernel(count, total_ref, *refs):
    rows = total_ref.shape[0]
    refs, out_ref = refs[:count], refs[-1]
    steps = [step_of(ref) for ref in refs]
    for c in range(total_ref.shape[1] // LANES):
        part = slice(c * LANES, (c + 1) * LANES)
        total = total_ref[:, part]
        for ref, step in zip(refs, steps):
            total = total + decoded(ref, c * rows, rows, step)
        out_ref[:, part] = total


def fold_pairs(total, parts, after=()):
    return pl.pallas_call(
        functools.partial(fold_pairs_kernel, len(parts)),
        in_specs=[pl.BlockSpec(memory_space=pltpu.VMEM)] * (1 + len(parts)) + unread(after),
        out_specs=pl.BlockSpec(memory_space=pltpu.VMEM),
        out_shape=jax.ShapeDtypeStruct(total.shape, jnp.float32),
        compiler_params=params(),
        cost_estimate=cost([total], parts),
        name="fold_pairs",
    )(total, *parts, *after)


def finish_kernel(rows_ref, total_ref, *refs):
    rows = total_ref.shape[0]
    steps = [step_of(ref) for ref in refs[:-1]]
    for c in range(total_ref.shape[1] // LANES):
        part = slice(c * LANES, (c + 1) * LANES)
        total = total_ref[:, part]
        for ref, step in zip(refs[:-1], steps):
            total = total + decoded(ref, c * rows, rows, step)
        refs[-1][:, part] = (total + rows_ref[0, :, part].astype(jnp.float32)).astype(
            jnp.bfloat16
        )


def finish(rows, total, parts):
    return pl.pallas_call(
        finish_kernel,
        in_specs=[pl.BlockSpec(memory_space=pltpu.VMEM)] * (2 + len(parts)),
        out_specs=pl.BlockSpec(memory_space=pltpu.VMEM),
        out_shape=jax.ShapeDtypeStruct(total.shape, jnp.bfloat16),
        compiler_params=params(),
        cost_estimate=cost([total], parts),
        name="finish",
    )(rows, total, *parts)


def passed(array, axis, shift):
    return lax.ppermute(array, axis, [(i, i ^ shift) for i in range(lax.axis_size(axis))])


def scalars(*values):
    return jnp.stack([jnp.asarray(value, jnp.int32) for value in values])


def shards(
    hidden,
    norm_gain,
    w_query,
    key_value_weight,
    w_output,
    prompt_cache_pages,
    per_page_scales,
    lengths,
    block_table,
):
    devices = lax.axis_size(DEVICES)
    subs = lax.axis_size("sub")
    device = lax.axis_index(DEVICES)
    request = lax.axis_index("req")
    sub = lax.axis_index("sub")
    core = lax.axis_index("section")
    width = hidden.shape[2]
    place = scalars(request, sub, core)

    rows = hidden.reshape(GROUP_REQUESTS * ROWS, width)
    column = [passed(rows, "req", s) for s in range(1, GROUP_REQUESTS)]
    where = scalars(request, sub * 2 + core, device * prompt_cache_pages.shape[0])
    rows, *pages = used_pages(
        prompt_cache_pages, per_page_scales, block_table, where, subs, rows
    )
    column = pack([rows] + column)
    gathered = [passed(column, "sub", s) for s in range(1, subs)]
    pages[1:] = [passed(pages[s], "req", s) for s in range(1, GROUP_REQUESTS)]
    key_value_weight, ready, gain = staged(
        place,
        key_value_weight,
        PAIR,
        pair_order(subs),
        more=[norm_gain.reshape(devices, 1, width)],
        after=[column],
    )
    gathered = [column] + list(gate(gathered, after=[ready]))
    gathered = gathered + [passed(part, "section", 1) for part in gathered]

    half = HEAD_SIZE // 2
    freqs = jnp.exp(
        -jnp.log(theta_base) * jnp.arange(half, dtype=jnp.float32) * (2.0 / HEAD_SIZE)
    )
    positions = (lengths[None, :] + jnp.arange(STEPS)[:, None]).astype(jnp.float32)
    angles = positions[..., None] * freqs
    cosine, sine = jnp.cos(angles), jnp.sin(angles)
    cosine = jnp.repeat(jnp.concatenate([cosine, cosine], axis=-1)[:, :, None], SAMPLES, axis=2)
    sine = jnp.repeat(jnp.concatenate([-sine, sine], axis=-1)[:, :, None], SAMPLES, axis=2)
    cosine = cosine.reshape(-1, HEAD_SIZE)
    sine = sine.reshape(-1, HEAD_SIZE)

    scale, kept, *parts = scale_and_pairs(place, gain, key_value_weight, gathered)
    parts = [passed(part, "sub", s + 1) for s, part in enumerate(parts)]
    query = queries(place, scale, gain, w_query, cosine, sine, gathered)
    total, *parts = fold_sub((0, 1, 2, 3), [kept], parts, after=[query])
    parts = [passed(part, "req", s + 1) for s, part in enumerate(parts)]
    pages = regroup(pages, after=[total])
    caches = [passed(pages[s], "sub", s) for s in range(1, subs)]
    mine = fold_pairs(total, parts)
    caches = list(pages[:1]) + list(gate(caches, after=[mine]))
    caches = caches + [passed(part, "section", 1) for part in caches]
    other = passed(mine, "section", 1)

    mixed, w_output = attend(
        place,
        lengths.astype(jnp.int32),
        query,
        mine,
        other,
        cosine,
        sine,
        w_output,
        width,
        output_order(subs),
        caches,
    )

    mid, end = GROUP_REQUESTS, GROUP_REQUESTS * subs
    first = outputs(mixed, w_output, end + mid, end - mid)
    got_first = passed(first, "section", 1)
    second = outputs(mixed, w_output, end, mid, after=[first])
    got_second = passed(second, "section", 1)
    kept = outputs(mixed, w_output, mid, end - mid, after=[second])
    parts = fold_core(kept, got_first)
    kept = outputs(mixed, w_output, 0, mid, after=parts[:1])
    last = {}
    for half, order in enumerate(HALVES):
        sent = parts[half::2]
        if half:
            sent = gate(sent, after=[got[0], kept])
        got = [passed(part, "sub", s + 1) for s, part in enumerate(sent)]
        last.update(zip(order, fold_sub(order, [kept, got_second], got)))
    parts = [passed(last[s], "req", s) for s in range(1, GROUP_REQUESTS)]
    return finish(gathered[0], last[0], parts).reshape(hidden.shape)


def solution(mesh):
    groups, tp, section = mesh.devices.shape
    finer = Mesh(
        mesh.devices.reshape(groups, GROUP_REQUESTS, tp // GROUP_REQUESTS, section),
        ("groups",) + DEVICES,
    )
    placed = (
        P(None, "groups", DEVICES),
        P(),
        P(None, DEVICES),
        P(DEVICES, None),
        P(DEVICES, None),
        P(("groups",) + DEVICES, None, None),
        P(("groups",) + DEVICES, None),
        P("groups"),
        P("groups", None),
    )
    return jax.shard_map(
        shards,
        mesh=finer,
        in_specs=placed,
        out_specs=P(None, "groups", DEVICES),
        check_vma=False,
    )
```

```python
import functools

import jax
import jax.numpy as jnp
from jax import lax
from jax.experimental import pallas as pl
from jax.experimental.pallas import tpu as pltpu
from jax.sharding import Mesh
from jax.sharding import PartitionSpec as P

QUERY_HEADS = 64
KEY_VALUE_HEADS = 8
HEAD_SIZE = 128
GROUP_REQUESTS = 4
SAMPLES = 8
PAGE_TOKENS = 16
STEPS = 2
ROWS = STEPS * SAMPLES
PAIR = 2 * HEAD_SIZE
LANES = 128
TAIL = 16
HALVES = ((1, 3), (0, 2))
DEVICES = ("req", "sub", "section")

theta_base = 500000.0
eps_norm = 1e-05
VMEM = 16 * 2**20
LARGE_VMEM = 51 * 2**20


def params(**more):
    return pltpu.CompilerParams(vmem_limit_bytes=VMEM, **more)


def cost(*groups, flops=0):
    size = sum(array.size * array.dtype.itemsize for arrays in groups for array in arrays)
    return pl.CostEstimate(flops=flops, bytes_accessed=size, transcendentals=0)


def unread(arrays):
    return [pl.BlockSpec(memory_space=pl.ANY)] * len(arrays)


def turn(vectors, cosine, sine):
    return vectors * cosine + pltpu.roll(vectors, HEAD_SIZE // 2, vectors.ndim - 1) * sine


def stage_kernel(order, count, place, block_ref, *refs):
    out_ref, token_ref, *outs, sems = refs[-3 - count :]
    width = out_ref.shape[2]
    copies = [
        pltpu.make_async_copy(refs[i], outs[i], sems.at[len(order) + i]) for i in range(count)
    ]
    for i, block in enumerate(order):
        columns = pl.ds(pl.multiple_of(block(place) * width, width), width)
        copies.append(pltpu.make_async_copy(block_ref.at[:, columns], out_ref.at[i], sems.at[i]))
    for copy in copies:
        copy.start()
    token_ref[...] = jnp.zeros_like(token_ref)
    for copy in copies:
        copy.wait()


def staged(place, array, width, order, more=(), after=()):
    rows, count = array.shape[0], len(order)
    return pl.pallas_call(
        functools.partial(stage_kernel, order, len(more)),
        in_specs=[pl.BlockSpec(memory_space=pltpu.SMEM)]
        + [pl.BlockSpec(memory_space=pltpu.HBM)] * (1 + len(more))
        + unread(after),
        out_specs=[pl.BlockSpec(memory_space=pltpu.VMEM)] * (2 + len(more)),
        out_shape=[
            jax.ShapeDtypeStruct((count, rows, width), array.dtype),
            jax.ShapeDtypeStruct((8, LANES), jnp.float32),
        ]
        + [jax.ShapeDtypeStruct(other.shape, other.dtype) for other in more],
        scratch_shapes=[pltpu.SemaphoreType.DMA((count + len(more),))],
        compiler_params=params(),
        cost_estimate=cost([array], [array]),
        name="staged",
    )(place, array, *more, *after)


def pair_order(subs):
    return [
        lambda place, j=j, z=z: 2 * (place[0] ^ z) + (place[1] ^ j) // (subs // 2)
        for j in range(subs)
        for z in range(GROUP_REQUESTS)
    ]


def output_order(subs):
    return [
        lambda place, c=c, j=j, z=z: ((place[0] ^ z) * subs + (place[1] ^ j)) * 2 + (place[2] ^ c)
        for c in range(2)
        for j in range(subs)
        for z in range(GROUP_REQUESTS)
    ]


def gate_kernel(*refs):
    pass


def gate(arrays, after):
    count = len(arrays)
    return pl.pallas_call(
        gate_kernel,
        in_specs=[pl.BlockSpec(memory_space=pl.ANY)] * count + unread(after),
        out_specs=[pl.BlockSpec(memory_space=pl.ANY)] * count,
        out_shape=[jax.ShapeDtypeStruct(array.shape, array.dtype) for array in arrays],
        input_output_aliases={i: i for i in range(count)},
        compiler_params=params(),
        name="gate",
    )(*arrays, *after)


def pages_kernel(table, place, scales, page_ref, rows_ref, rows_out_ref, *out_refs):
    e = pl.program_id(0)
    rows_out_ref[...] = rows_ref[...]
    subs = out_refs[0].shape[0]
    targets = 2 * subs
    page = table[place[0], e * targets + place[1]] - place[2]
    for z, out_ref in enumerate(out_refs):
        for j in range(subs):
            half = (place[1] // 2 ^ j) // (subs // 2)
            head = 2 * (place[0] ^ z) + half
            for part in range(2):
                c = head * 2 + part
                columns = pl.ds(pl.multiple_of(c * HEAD_SIZE, HEAD_SIZE), HEAD_SIZE)
                block = page_ref[0, :, columns].astype(jnp.float32)
                out_ref[j, :, part * HEAD_SIZE : (part + 1) * HEAD_SIZE] = (
                    block * scales[page, c]
                ).astype(jnp.bfloat16)


def used_pages(pages, scales, table, place, subs, rows):
    targets = 2 * subs
    entries = table.shape[1] // targets
    shape = jax.ShapeDtypeStruct((subs, entries * PAGE_TOKENS, PAIR), jnp.bfloat16)
    return pl.pallas_call(
        pages_kernel,
        grid_spec=pltpu.PrefetchScalarGridSpec(
            num_scalar_prefetch=3,
            grid=(entries,),
            in_specs=[
                pl.BlockSpec(
                    (1, PAGE_TOKENS, pages.shape[2]),
                    lambda e, table, place, scales: (
                        table[place[0], e * targets + place[1]] - place[2],
                        0,
                        0,
                    ),
                ),
                pl.BlockSpec(rows.shape, lambda e, *_: (0, 0)),
            ],
            out_specs=[pl.BlockSpec(rows.shape, lambda e, *_: (0, 0))]
            + [pl.BlockSpec((subs, PAGE_TOKENS, PAIR), lambda e, *_: (0, e, 0))]
            * GROUP_REQUESTS,
        ),
        out_shape=[jax.ShapeDtypeStruct(rows.shape, rows.dtype)] + [shape] * GROUP_REQUESTS,
        compiler_params=params(),
        cost_estimate=pl.CostEstimate(
            flops=0, bytes_accessed=4 * entries * PAGE_TOKENS * pages.shape[2], transcendentals=0
        ),
        name="used_pages",
    )(table, place, scales.astype(jnp.float32), pages, rows)


def regroup_kernel(*refs):
    ins, outs = refs[:GROUP_REQUESTS], refs[-refs[0].shape[0] :]
    for j, out_ref in enumerate(outs):
        for z, ref in enumerate(ins):
            out_ref[z] = ref[j]


def regroup(parts, after=()):
    subs = parts[0].shape[0]
    shape = jax.ShapeDtypeStruct((len(parts),) + parts[0].shape[1:], parts[0].dtype)
    return pl.pallas_call(
        regroup_kernel,
        in_specs=[pl.BlockSpec(memory_space=pltpu.VMEM)] * len(parts) + unread(after),
        out_specs=[pl.BlockSpec(memory_space=pltpu.VMEM)] * subs,
        out_shape=[shape] * subs,
        compiler_params=params(),
        cost_estimate=cost(parts, parts),
        name="regroup",
    )(*parts, *after)


def pack_kernel(*refs):
    for i in range(refs[-1].shape[0]):
        refs[-1][i] = refs[i][...]


def pack(parts):
    return pl.pallas_call(
        pack_kernel,
        in_specs=[pl.BlockSpec(memory_space=pltpu.VMEM)] * len(parts),
        out_specs=pl.BlockSpec(memory_space=pltpu.VMEM),
        out_shape=jax.ShapeDtypeStruct((len(parts),) + parts[0].shape, parts[0].dtype),
        compiler_params=params(),
        cost_estimate=cost(parts, parts),
        name="pack",
    )(*parts)


def blocks_of(place, refs):
    request, sub, core = place[0], place[1], place[2]
    subs = len(refs) // 2
    for i, ref in enumerate(refs):
        from_core = core if i < subs else 1 - core
        for z in range(GROUP_REQUESTS):
            yield ref, z, ((request ^ z) * subs + (sub ^ i % subs)) * 2 + from_core


def pairs_kernel(place, gain_ref, weight_ref, *refs):
    subs = (len(refs) - 1) // 3
    x_refs, scale_ref, kept_ref, out_refs = (
        refs[: 2 * subs],
        refs[2 * subs],
        refs[2 * subs + 1],
        refs[2 * subs + 2 :],
    )
    request, sub, core = place[0], place[1], place[2]
    _, rows, width = x_refs[0].shape
    total = jnp.zeros((rows, LANES), jnp.float32)
    for ref in x_refs:
        for z in range(GROUP_REQUESTS):
            for piece in pieces_of(ref[z].astype(jnp.float32)):
                total += piece * piece
    mean = jnp.sum(total, axis=-1, keepdims=True) / (2 * subs * GROUP_REQUESTS * width)
    scale = lax.rsqrt(mean + eps_norm)
    scale_ref[...] = jnp.broadcast_to(scale, scale_ref.shape)
    device = (request * subs + sub) * 2 + core
    x = x_refs[0][0].astype(jnp.float32)
    mine = (x * scale * gain_ref[device]).astype(jnp.bfloat16)
    for shift in range(subs):
        pieces = []
        for z in range(GROUP_REQUESTS):
            block = weight_ref[shift * GROUP_REQUESTS + z]
            part = jnp.dot(mine, block, preferred_element_type=jnp.float32)
            if shift == 0:
                kept_ref[z] = part
            pieces += pieces_of(part)
        if shift:
            encode(out_refs[shift - 1], pieces)


def scale_and_pairs(place, gain, weight, gathered):
    subs = len(gathered) // 2
    count = gathered[0].shape[1]
    sent = jax.ShapeDtypeStruct((2 * GROUP_REQUESTS * count + TAIL, LANES), jnp.int16)
    shapes = [
        jax.ShapeDtypeStruct((count, LANES), jnp.float32),
        jax.ShapeDtypeStruct((GROUP_REQUESTS, count, PAIR), jnp.float32),
    ] + [sent] * (subs - 1)
    return pl.pallas_call(
        pairs_kernel,
        in_specs=[pl.BlockSpec(memory_space=pltpu.SMEM)]
        + [pl.BlockSpec(memory_space=pltpu.VMEM)] * (2 + len(gathered)),
        out_specs=[pl.BlockSpec(memory_space=pltpu.VMEM)] * len(shapes),
        out_shape=shapes,
        compiler_params=params(),
        cost_estimate=cost(gathered, [weight], flops=2 * count * weight.size),
        name="scale_and_pairs",
    )(place, gain, weight, *gathered)


def query_kernel(place, scale_ref, gain_ref, weight_ref, cos_ref, sin_ref, *refs):
    x_refs, out_ref, held, sems = refs[:-3], refs[-3], refs[-2], refs[-1]
    _, rows, width = x_refs[0].shape
    columns = weight_ref.shape[1]
    blocks = list(blocks_of(place, x_refs))
    copies = []
    for i, (_, _, block) in enumerate(blocks):
        depth = pl.ds(pl.multiple_of(block * width, width), width)
        copies.append(pltpu.make_async_copy(weight_ref.at[depth], held.at[i], sems.at[i]))
    for copy in copies:
        copy.start()
    scale = scale_ref[:, :1]
    total = jnp.zeros((rows, columns), jnp.float32)
    for i, (ref, z, block) in enumerate(blocks):
        x = ref[z].astype(jnp.float32)
        x = (x * scale * gain_ref[block]).astype(jnp.bfloat16)
        copies[i].wait()
        total += jnp.dot(x, held[i], preferred_element_type=jnp.float32)
    for head in range(columns // HEAD_SIZE):
        part = slice(head * HEAD_SIZE, (head + 1) * HEAD_SIZE)
        turned = turn(total[:, part], cos_ref[...], sin_ref[...])
        for r in range(GROUP_REQUESTS):
            first, second = r * SAMPLES, (GROUP_REQUESTS + r) * SAMPLES
            out_ref[r, :, part] = jnp.concatenate(
                [turned[first : first + SAMPLES], turned[second : second + SAMPLES]], axis=0
            ).astype(jnp.bfloat16)


def queries(place, scale, gain, weight, cosine, sine, gathered):
    columns = weight.shape[1]
    _, rows, width = gathered[0].shape
    blocks = weight.shape[0] // width
    return pl.pallas_call(
        query_kernel,
        in_specs=[pl.BlockSpec(memory_space=pltpu.SMEM)]
        + [pl.BlockSpec(memory_space=pltpu.VMEM)] * 2
        + [pl.BlockSpec(memory_space=pltpu.HBM)]
        + [pl.BlockSpec(memory_space=pltpu.VMEM)] * (2 + len(gathered)),
        out_specs=pl.BlockSpec(memory_space=pltpu.VMEM),
        out_shape=jax.ShapeDtypeStruct((GROUP_REQUESTS, ROWS, columns), jnp.bfloat16),
        scratch_shapes=[
            pltpu.VMEM((blocks, width, columns), jnp.bfloat16),
            pltpu.SemaphoreType.DMA((blocks,)),
        ],
        compiler_params=pltpu.CompilerParams(vmem_limit_bytes=LARGE_VMEM),
        cost_estimate=cost([weight], flops=2 * rows * weight.size),
        name="queries",
    )(place, scale, gain, weight, cosine, sine, *gathered)


def attend_kernel(place, lengths, q_ref, mine_ref, other_ref, cos_ref, sin_ref, *refs):
    caches, out_ref, key_ref, value_ref = refs[:-3], refs[-3], refs[-2], refs[-1]
    request, sub, core = place[0], place[1], place[2]
    subs, span = len(caches) // 2, caches[0].shape[1]
    targets = 2 * subs
    tokens = targets * span
    quarter = q_ref.shape[2] // HEAD_SIZE
    pair = mine_ref[...] + other_ref[...]
    key_ref[...] = turn(pair[:, :HEAD_SIZE], cos_ref[...], sin_ref[...])
    value_ref[...] = pair[:, HEAD_SIZE:]
    column = lax.broadcasted_iota(jnp.int32, (1, tokens), 1)
    source, inside = column // span, column % span
    from_core = jnp.where(source < subs, core, 1 - core)
    from_sub = sub ^ source % subs
    entry = inside // PAGE_TOKENS * targets + from_sub * 2 + from_core
    position = entry * PAGE_TOKENS + inside % PAGE_TOKENS
    count = quarter * ROWS
    row = lax.broadcasted_iota(jnp.int32, (count, ROWS), 0) % ROWS
    other = lax.broadcasted_iota(jnp.int32, (count, ROWS), 1)
    own_visible = (row % SAMPLES == other % SAMPLES) & (other // SAMPLES <= row // SAMPLES)
    factor = HEAD_SIZE ** (-0.5)
    contract = (((1,), (1,)), ((), ()))
    for z in range(GROUP_REQUESTS):
        r = request ^ z
        fresh = [
            pl.ds(pl.multiple_of((step * GROUP_REQUESTS + r) * SAMPLES, SAMPLES), SAMPLES)
            for step in range(STEPS)
        ]
        new_key = jnp.concatenate([key_ref[rows] for rows in fresh], axis=0)
        new_value = jnp.concatenate([value_ref[rows] for rows in fresh], axis=0)
        new_key, new_value = new_key.astype(jnp.bfloat16), new_value.astype(jnp.bfloat16)
        keys = jnp.concatenate([ref[z, :, :HEAD_SIZE] for ref in caches], axis=0)
        values = jnp.concatenate([ref[z, :, HEAD_SIZE:] for ref in caches], axis=0)
        query = jnp.concatenate(
            [q_ref[r, :, h * HEAD_SIZE : (h + 1) * HEAD_SIZE] for h in range(quarter)], axis=0
        )
        scores = lax.dot_general(query, keys, contract, preferred_element_type=jnp.float32)
        scores = jnp.where(position < lengths[r], scores * factor, -jnp.inf)
        own = lax.dot_general(query, new_key, contract, preferred_element_type=jnp.float32)
        own = jnp.where(own_visible, own * factor, -jnp.inf)
        highest = jnp.maximum(
            jnp.max(scores, axis=-1, keepdims=True), jnp.max(own, axis=-1, keepdims=True)
        )
        scores = jnp.exp(scores - highest)
        own = jnp.exp(own - highest)
        total = jnp.sum(scores, axis=-1, keepdims=True) + jnp.sum(own, axis=-1, keepdims=True)
        mixed = jnp.dot(
            (scores / total).astype(jnp.bfloat16), values, preferred_element_type=jnp.float32
        ) + jnp.dot(
            (own / total).astype(jnp.bfloat16), new_value, preferred_element_type=jnp.float32
        )
        mixed = mixed.astype(jnp.bfloat16)
        for h in range(quarter):
            out_ref[r, :, h * HEAD_SIZE : (h + 1) * HEAD_SIZE] = mixed[
                h * ROWS : (h + 1) * ROWS
            ]


def attend(place, lengths, query, mine, other, cosine, sine, caches):
    return pl.pallas_call(
        attend_kernel,
        in_specs=[pl.BlockSpec(memory_space=pltpu.SMEM)] * 2
        + [pl.BlockSpec(memory_space=pltpu.VMEM)] * (5 + len(caches)),
        out_specs=pl.BlockSpec(memory_space=pltpu.VMEM),
        out_shape=jax.ShapeDtypeStruct(query.shape, jnp.bfloat16),
        scratch_shapes=[pltpu.VMEM(cosine.shape, jnp.float32)] * 2,
        compiler_params=params(),
        cost_estimate=cost(caches, caches, caches, flops=2**28),
        name="attend",
    )(place, lengths, query, mine, other, cosine, sine, *caches)


def output_kernel(first, x_ref, weight_ref, *refs):
    out_ref = refs[-1]
    blocks, rows, width = out_ref.shape
    x = x_ref[...].reshape(rows, -1)
    for i in range(blocks):
        part = jnp.dot(x, weight_ref[first + i], preferred_element_type=jnp.float32)
        for r in range(GROUP_REQUESTS):
            for step in range(STEPS):
                source = r * ROWS + step * SAMPLES
                target = (step * GROUP_REQUESTS + r) * SAMPLES
                out_ref[i, target : target + SAMPLES] = part[source : source + SAMPLES]


def outputs(mixed, weight, first, blocks, after=()):
    rows, width = GROUP_REQUESTS * ROWS, weight.shape[2]
    return pl.pallas_call(
        functools.partial(output_kernel, first),
        in_specs=[pl.BlockSpec(memory_space=pltpu.VMEM)] * 2 + unread(after),
        out_specs=pl.BlockSpec(memory_space=pltpu.VMEM),
        out_shape=jax.ShapeDtypeStruct((blocks, rows, width), jnp.float32),
        compiler_params=params(),
        cost_estimate=cost([mixed], flops=2 * rows * mixed.shape[2] * blocks * width),
        name="outputs",
    )(mixed, weight, *after)


def pieces_of(block):
    return [block[:, c : c + LANES] for c in range(0, block.shape[1], LANES)]


def encode(out_ref, pieces):
    rows = pieces[0].shape[0]
    peak = jnp.abs(pieces[0])
    for piece in pieces[1:]:
        peak = jnp.maximum(peak, jnp.abs(piece))
    peak = jnp.maximum(jnp.max(peak, axis=0, keepdims=True), 1e-30)
    exponent = jnp.floor(jnp.log2(peak)) - 14.0
    inverse = jnp.exp2(-exponent)
    for i, piece in enumerate(pieces):
        code = jnp.clip(jnp.floor(piece * inverse + 0.5), -32767.0, 32767.0)
        out_ref[i * rows : (i + 1) * rows] = code.astype(jnp.int32).astype(jnp.int16)
    out_ref[len(pieces) * rows :] = (
        jnp.broadcast_to(exponent, (TAIL, LANES)).astype(jnp.int32).astype(jnp.int16)
    )


def step_of(ref):
    tail = ref[ref.shape[0] - TAIL :].astype(jnp.int32).astype(jnp.float32)
    return jnp.exp2(tail[:1])


def decoded(ref, first, rows, step):
    return ref[pl.ds(first, rows)].astype(jnp.int32).astype(jnp.float32) * step


def fold_core_kernel(mine_ref, got_ref, *out_refs):
    for i, out_ref in enumerate(out_refs):
        pieces = []
        for z in HALVES[i % 2]:
            block = i // 2 * GROUP_REQUESTS + z
            pieces += pieces_of(mine_ref[block] + got_ref[block])
        encode(out_ref, pieces)


def fold_core(mine, got):
    blocks, rows, width = mine.shape
    count = 2 * (blocks // GROUP_REQUESTS)
    sent = jax.ShapeDtypeStruct((2 * width // LANES * rows + TAIL, LANES), jnp.int16)
    return pl.pallas_call(
        fold_core_kernel,
        in_specs=[pl.BlockSpec(memory_space=pltpu.VMEM)] * 2,
        out_specs=[pl.BlockSpec(memory_space=pltpu.VMEM)] * count,
        out_shape=[sent] * count,
        compiler_params=params(),
        cost_estimate=cost([mine, got]),
        name="fold_core",
    )(mine, got)


def fold_sub_kernel(order, send, keep, own, count, *refs):
    own_refs, in_refs = refs[:own], refs[own : own + count]
    outs = list(refs[-(len(send) > 0) - (len(keep) > 0) :])
    _, rows, width = own_refs[0].shape
    steps = [step_of(ref) for ref in in_refs]

    def total(z):
        block = own_refs[0][z]
        for ref in own_refs[1:]:
            block = block + ref[z]
        pieces = pieces_of(block)
        for c in range(len(pieces)):
            for ref, step in zip(in_refs, steps):
                first = (order.index(z) * len(pieces) + c) * rows
                pieces[c] = pieces[c] + decoded(ref, first, rows, step)
        return pieces

    if send:
        encode(outs.pop(0), [piece for z in send for piece in total(z)])
    for i, z in enumerate(keep):
        for c, piece in enumerate(total(z)):
            outs[0][i, :, c * LANES : (c + 1) * LANES] = piece


def fold_sub(order, send, keep, own, parts, after=()):
    _, rows, width = own[0].shape
    shapes = []
    if send:
        length = len(send) * (width // LANES) * rows + TAIL
        shapes.append(jax.ShapeDtypeStruct((length, LANES), jnp.int16))
    if keep:
        shapes.append(jax.ShapeDtypeStruct((len(keep), rows, width), jnp.float32))
    return pl.pallas_call(
        functools.partial(fold_sub_kernel, order, send, keep, len(own), len(parts)),
        in_specs=[pl.BlockSpec(memory_space=pltpu.VMEM)] * (len(own) + len(parts))
        + unread(after),
        out_specs=[pl.BlockSpec(memory_space=pltpu.VMEM)] * len(shapes),
        out_shape=shapes,
        compiler_params=params(),
        cost_estimate=cost(own, parts),
        name="fold_sub",
    )(*own, *parts, *after)


def fold_near_kernel(kept_ref, got_ref, total_ref, out_ref):
    _, rows, width = kept_ref.shape
    step = step_of(got_ref)
    count = width // LANES
    sums = []
    for i in range(2):
        for c, piece in enumerate(pieces_of(kept_ref[i])):
            sums.append(piece + decoded(got_ref, (i * count + c) * rows, rows, step))
    for c in range(count):
        total_ref[:, c * LANES : (c + 1) * LANES] = sums[c]
    encode(out_ref, sums[count:])


def fold_near(kept, got):
    _, rows, width = kept.shape
    return pl.pallas_call(
        fold_near_kernel,
        in_specs=[pl.BlockSpec(memory_space=pltpu.VMEM)] * 2,
        out_specs=[pl.BlockSpec(memory_space=pltpu.VMEM)] * 2,
        out_shape=[
            jax.ShapeDtypeStruct((rows, width), jnp.float32),
            jax.ShapeDtypeStruct((width // LANES * rows + TAIL, LANES), jnp.int16),
        ],
        compiler_params=params(),
        cost_estimate=cost([kept], [got]),
        name="fold_near",
    )(kept, got)


def fold_pairs_kernel(count, total_ref, *refs):
    rows = total_ref.shape[0]
    refs, out_ref = refs[:count], refs[-1]
    steps = [step_of(ref) for ref in refs]
    for c in range(total_ref.shape[1] // LANES):
        part = slice(c * LANES, (c + 1) * LANES)
        total = total_ref[:, part]
        for ref, step in zip(refs, steps):
            total = total + decoded(ref, c * rows, rows, step)
        out_ref[:, part] = total


def fold_pairs(total, parts, after=()):
    return pl.pallas_call(
        functools.partial(fold_pairs_kernel, len(parts)),
        in_specs=[pl.BlockSpec(memory_space=pltpu.VMEM)] * (1 + len(parts)) + unread(after),
        out_specs=pl.BlockSpec(memory_space=pltpu.VMEM),
        out_shape=jax.ShapeDtypeStruct(total.shape, jnp.float32),
        compiler_params=params(),
        cost_estimate=cost([total], parts),
        name="fold_pairs",
    )(total, *parts, *after)


def finish_kernel(rows_ref, total_ref, *refs):
    rows = total_ref.shape[0]
    steps = [step_of(ref) for ref in refs[:-1]]
    for c in range(total_ref.shape[1] // LANES):
        part = slice(c * LANES, (c + 1) * LANES)
        total = total_ref[:, part]
        for ref, step in zip(refs[:-1], steps):
            total = total + decoded(ref, c * rows, rows, step)
        refs[-1][:, part] = (total + rows_ref[0, :, part].astype(jnp.float32)).astype(
            jnp.bfloat16
        )


def finish(rows, total, parts):
    return pl.pallas_call(
        finish_kernel,
        in_specs=[pl.BlockSpec(memory_space=pltpu.VMEM)] * (2 + len(parts)),
        out_specs=pl.BlockSpec(memory_space=pltpu.VMEM),
        out_shape=jax.ShapeDtypeStruct(total.shape, jnp.bfloat16),
        compiler_params=params(),
        cost_estimate=cost([total], parts),
        name="finish",
    )(rows, total, *parts)


def passed(array, axis, shift):
    return lax.ppermute(array, axis, [(i, i ^ shift) for i in range(lax.axis_size(axis))])


def scalars(*values):
    return jnp.stack([jnp.asarray(value, jnp.int32) for value in values])


def shards(
    hidden,
    norm_gain,
    w_query,
    key_value_weight,
    w_output,
    prompt_cache_pages,
    per_page_scales,
    lengths,
    block_table,
):
    devices = lax.axis_size(DEVICES)
    subs = lax.axis_size("sub")
    device = lax.axis_index(DEVICES)
    request = lax.axis_index("req")
    sub = lax.axis_index("sub")
    core = lax.axis_index("section")
    width = hidden.shape[2]
    place = scalars(request, sub, core)

    rows = hidden.reshape(GROUP_REQUESTS * ROWS, width)
    column = [passed(rows, "req", s) for s in range(1, GROUP_REQUESTS)]
    where = scalars(request, sub * 2 + core, device * prompt_cache_pages.shape[0])
    rows, *pages = used_pages(
        prompt_cache_pages, per_page_scales, block_table, where, subs, rows
    )
    column = pack([rows] + column)
    gathered = [passed(column, "sub", s) for s in range(1, subs)]
    pages[1:] = [passed(pages[s], "req", s) for s in range(1, GROUP_REQUESTS)]
    key_value_weight, ready, gain = staged(
        place,
        key_value_weight,
        PAIR,
        pair_order(subs),
        more=[norm_gain.reshape(devices, 1, width)],
        after=[column],
    )
    gathered = [column] + list(gate(gathered, after=[ready]))
    gathered = gathered + [passed(part, "section", 1) for part in gathered]

    half = HEAD_SIZE // 2
    freqs = jnp.exp(
        -jnp.log(theta_base) * jnp.arange(half, dtype=jnp.float32) * (2.0 / HEAD_SIZE)
    )
    positions = (lengths[None, :] + jnp.arange(STEPS)[:, None]).astype(jnp.float32)
    angles = positions[..., None] * freqs
    cosine, sine = jnp.cos(angles), jnp.sin(angles)
    cosine = jnp.repeat(jnp.concatenate([cosine, cosine], axis=-1)[:, :, None], SAMPLES, axis=2)
    sine = jnp.repeat(jnp.concatenate([-sine, sine], axis=-1)[:, :, None], SAMPLES, axis=2)
    cosine = cosine.reshape(-1, HEAD_SIZE)
    sine = sine.reshape(-1, HEAD_SIZE)

    scale, kept, *parts = scale_and_pairs(place, gain, key_value_weight, gathered)
    parts = [passed(part, "sub", s + 1) for s, part in enumerate(parts)]
    query = queries(place, scale, gain, w_query, cosine, sine, gathered)
    near, kept = fold_sub((0, 1, 2, 3), (1, 3), (0, 2), [kept], parts, after=[query])
    near = passed(near, "req", 1)
    pages = regroup(pages, after=[kept])
    caches = [passed(pages[s], "sub", s) for s in range(1, subs)]
    w_output, ready = staged(place, w_output, width, output_order(subs), after=[kept])
    total, far = fold_near(kept, near)
    parts = [passed(far, "req", 2)]
    mine = fold_pairs(total, parts, after=[ready])
    caches = list(pages[:1]) + list(gate(caches, after=[mine]))
    caches = caches + [passed(part, "section", 1) for part in caches]
    other = passed(mine, "section", 1)

    mixed = attend(
        place, lengths.astype(jnp.int32), query, mine, other, cosine, sine, caches
    )

    mid, end = GROUP_REQUESTS, GROUP_REQUESTS * subs
    first = outputs(mixed, w_output, end + mid, end - mid)
    got_first = passed(first, "section", 1)
    second = outputs(mixed, w_output, end, mid, after=[first])
    got_second = passed(second, "section", 1)
    kept = outputs(mixed, w_output, mid, end - mid, after=[second])
    parts = fold_core(kept, got_first)
    kept = outputs(mixed, w_output, 0, mid, after=parts[:1])
    parts = [passed(part, "sub", i // 2 + 1) for i, part in enumerate(parts)]
    (near,) = fold_sub((1, 3), (1, 3), (), [kept, got_second], parts[0::2])
    near = passed(near, "req", 1)
    (kept,) = fold_sub((0, 2), (), (0, 2), [kept, got_second], parts[1::2])
    total, far = fold_near(kept, near)
    parts = [passed(far, "req", 2)]
    return finish(gathered[0], total, parts).reshape(hidden.shape)


def solution(mesh):
    groups, tp, section = mesh.devices.shape
    finer = Mesh(
        mesh.devices.reshape(groups, GROUP_REQUESTS, tp // GROUP_REQUESTS, section),
        ("groups",) + DEVICES,
    )
    placed = (
        P(None, "groups", DEVICES),
        P(),
        P(None, DEVICES),
        P(DEVICES, None),
        P(DEVICES, None),
        P(("groups",) + DEVICES, None, None),
        P(("groups",) + DEVICES, None),
        P("groups"),
        P("groups", None),
    )
    return jax.shard_map(
        shards,
        mesh=finer,
        in_specs=placed,
        out_specs=P(None, "groups", DEVICES),
        check_vma=False,
    )
```

```python
import functools

import jax
import jax.numpy as jnp
from jax import lax
from jax.experimental import pallas as pl
from jax.experimental.pallas import tpu as pltpu
from jax.sharding import Mesh
from jax.sharding import PartitionSpec as P

QUERY_HEADS = 64
KEY_VALUE_HEADS = 8
HEAD_SIZE = 128
GROUP_REQUESTS = 4
SAMPLES = 8
PAGE_TOKENS = 16
STEPS = 2
ROWS = STEPS * SAMPLES
PAIR = 2 * HEAD_SIZE
LANES = 128
TAIL = 16
DEVICES = ("req", "sub", "section")

theta_base = 500000.0
eps_norm = 1e-05
VMEM = 16 * 2**20
LARGE_VMEM = 51 * 2**20


def params(**more):
    return pltpu.CompilerParams(vmem_limit_bytes=VMEM, **more)


def cost(*groups, flops=0):
    size = sum(array.size * array.dtype.itemsize for arrays in groups for array in arrays)
    return pl.CostEstimate(flops=flops, bytes_accessed=size, transcendentals=0)


def unread(arrays):
    return [pl.BlockSpec(memory_space=pl.ANY)] * len(arrays)


def turn(vectors, cosine, sine):
    return vectors * cosine + pltpu.roll(vectors, HEAD_SIZE // 2, vectors.ndim - 1) * sine


def stage_kernel(order, count, place, block_ref, *refs):
    out_ref, token_ref, *outs, sems = refs[-3 - count :]
    width = out_ref.shape[2]
    copies = [
        pltpu.make_async_copy(refs[i], outs[i], sems.at[len(order) + i]) for i in range(count)
    ]
    for i, block in enumerate(order):
        columns = pl.ds(pl.multiple_of(block(place) * width, width), width)
        copies.append(pltpu.make_async_copy(block_ref.at[:, columns], out_ref.at[i], sems.at[i]))
    for copy in copies:
        copy.start()
    token_ref[...] = jnp.zeros_like(token_ref)
    for copy in copies:
        copy.wait()


def staged(place, array, width, order, more=(), after=()):
    rows, count = array.shape[0], len(order)
    return pl.pallas_call(
        functools.partial(stage_kernel, order, len(more)),
        in_specs=[pl.BlockSpec(memory_space=pltpu.SMEM)]
        + [pl.BlockSpec(memory_space=pltpu.HBM)] * (1 + len(more))
        + unread(after),
        out_specs=[pl.BlockSpec(memory_space=pltpu.VMEM)] * (2 + len(more)),
        out_shape=[
            jax.ShapeDtypeStruct((count, rows, width), array.dtype),
            jax.ShapeDtypeStruct((8, LANES), jnp.float32),
        ]
        + [jax.ShapeDtypeStruct(other.shape, other.dtype) for other in more],
        scratch_shapes=[pltpu.SemaphoreType.DMA((count + len(more),))],
        compiler_params=params(),
        cost_estimate=cost([array], [array]),
        name="staged",
    )(place, array, *more, *after)


def pair_order(subs):
    return [
        lambda place, j=j, z=z: 2 * (place[0] ^ z) + (place[1] ^ j) // (subs // 2)
        for j in range(subs)
        for z in range(GROUP_REQUESTS)
    ]


def output_order(subs):
    return [
        lambda place, c=c, j=j, z=z: ((place[0] ^ z) * subs + (place[1] ^ j)) * 2 + (place[2] ^ c)
        for c in range(2)
        for j in range(subs)
        for z in range(GROUP_REQUESTS)
    ]


def gate_kernel(*refs):
    pass


def gate(arrays, after):
    count = len(arrays)
    return pl.pallas_call(
        gate_kernel,
        in_specs=[pl.BlockSpec(memory_space=pl.ANY)] * count + unread(after),
        out_specs=[pl.BlockSpec(memory_space=pl.ANY)] * count,
        out_shape=[jax.ShapeDtypeStruct(array.shape, array.dtype) for array in arrays],
        input_output_aliases={i: i for i in range(count)},
        compiler_params=params(),
        name="gate",
    )(*arrays, *after)


def pages_kernel(table, place, scales, page_ref, rows_ref, rows_out_ref, *out_refs):
    e = pl.program_id(0)
    rows_out_ref[...] = rows_ref[...]
    subs = out_refs[0].shape[0]
    targets = 2 * subs
    page = table[place[0], e * targets + place[1]] - place[2]
    for z, out_ref in enumerate(out_refs):
        for j in range(subs):
            half = (place[1] // 2 ^ j) // (subs // 2)
            head = 2 * (place[0] ^ z) + half
            for part in range(2):
                c = head * 2 + part
                columns = pl.ds(pl.multiple_of(c * HEAD_SIZE, HEAD_SIZE), HEAD_SIZE)
                block = page_ref[0, :, columns].astype(jnp.float32)
                out_ref[j, :, part * HEAD_SIZE : (part + 1) * HEAD_SIZE] = (
                    block * scales[page, c]
                ).astype(jnp.bfloat16)


def used_pages(pages, scales, table, place, subs, rows):
    targets = 2 * subs
    entries = table.shape[1] // targets
    shape = jax.ShapeDtypeStruct((subs, entries * PAGE_TOKENS, PAIR), jnp.bfloat16)
    return pl.pallas_call(
        pages_kernel,
        grid_spec=pltpu.PrefetchScalarGridSpec(
            num_scalar_prefetch=3,
            grid=(entries,),
            in_specs=[
                pl.BlockSpec(
                    (1, PAGE_TOKENS, pages.shape[2]),
                    lambda e, table, place, scales: (
                        table[place[0], e * targets + place[1]] - place[2],
                        0,
                        0,
                    ),
                ),
                pl.BlockSpec(rows.shape, lambda e, *_: (0, 0)),
            ],
            out_specs=[pl.BlockSpec(rows.shape, lambda e, *_: (0, 0))]
            + [pl.BlockSpec((subs, PAGE_TOKENS, PAIR), lambda e, *_: (0, e, 0))]
            * GROUP_REQUESTS,
        ),
        out_shape=[jax.ShapeDtypeStruct(rows.shape, rows.dtype)] + [shape] * GROUP_REQUESTS,
        compiler_params=params(),
        cost_estimate=pl.CostEstimate(
            flops=0, bytes_accessed=4 * entries * PAGE_TOKENS * pages.shape[2], transcendentals=0
        ),
        name="used_pages",
    )(table, place, scales.astype(jnp.float32), pages, rows)


def regroup_kernel(*refs):
    ins, outs = refs[:GROUP_REQUESTS], refs[-refs[0].shape[0] :]
    for j, out_ref in enumerate(outs):
        for z, ref in enumerate(ins):
            out_ref[z] = ref[j]


def regroup(parts, after=()):
    subs = parts[0].shape[0]
    shape = jax.ShapeDtypeStruct((len(parts),) + parts[0].shape[1:], parts[0].dtype)
    return pl.pallas_call(
        regroup_kernel,
        in_specs=[pl.BlockSpec(memory_space=pltpu.VMEM)] * len(parts) + unread(after),
        out_specs=[pl.BlockSpec(memory_space=pltpu.VMEM)] * subs,
        out_shape=[shape] * subs,
        compiler_params=params(),
        cost_estimate=cost(parts, parts),
        name="regroup",
    )(*parts, *after)


def pack_kernel(*refs):
    for i in range(refs[-1].shape[0]):
        refs[-1][i] = refs[i][...]


def pack(parts):
    return pl.pallas_call(
        pack_kernel,
        in_specs=[pl.BlockSpec(memory_space=pltpu.VMEM)] * len(parts),
        out_specs=pl.BlockSpec(memory_space=pltpu.VMEM),
        out_shape=jax.ShapeDtypeStruct((len(parts),) + parts[0].shape, parts[0].dtype),
        compiler_params=params(),
        cost_estimate=cost(parts, parts),
        name="pack",
    )(*parts)


def blocks_of(place, refs):
    request, sub, core = place[0], place[1], place[2]
    subs = len(refs) // 2
    for i, ref in enumerate(refs):
        from_core = core if i < subs else 1 - core
        for z in range(GROUP_REQUESTS):
            yield ref, z, ((request ^ z) * subs + (sub ^ i % subs)) * 2 + from_core


def pairs_kernel(place, gain_ref, weight_ref, *refs):
    subs = (len(refs) - 1) // 3
    x_refs, scale_ref, kept_ref, out_refs = (
        refs[: 2 * subs],
        refs[2 * subs],
        refs[2 * subs + 1],
        refs[2 * subs + 2 :],
    )
    request, sub, core = place[0], place[1], place[2]
    _, rows, width = x_refs[0].shape
    total = jnp.zeros((rows, LANES), jnp.float32)
    for ref in x_refs:
        for z in range(GROUP_REQUESTS):
            for piece in pieces_of(ref[z].astype(jnp.float32)):
                total += piece * piece
    mean = jnp.sum(total, axis=-1, keepdims=True) / (2 * subs * GROUP_REQUESTS * width)
    scale = lax.rsqrt(mean + eps_norm)
    scale_ref[...] = jnp.broadcast_to(scale, scale_ref.shape)
    device = (request * subs + sub) * 2 + core
    x = x_refs[0][0].astype(jnp.float32)
    mine = (x * scale * gain_ref[device]).astype(jnp.bfloat16)
    for shift in range(subs):
        pieces = []
        for z in range(GROUP_REQUESTS):
            block = weight_ref[shift * GROUP_REQUESTS + z]
            part = jnp.dot(mine, block, preferred_element_type=jnp.float32)
            if shift == 0:
                kept_ref[z] = part
            pieces += pieces_of(part)
        if shift:
            encode(out_refs[shift - 1], pieces)


def scale_and_pairs(place, gain, weight, gathered):
    subs = len(gathered) // 2
    count = gathered[0].shape[1]
    sent = jax.ShapeDtypeStruct((2 * GROUP_REQUESTS * count + TAIL, LANES), jnp.int16)
    shapes = [
        jax.ShapeDtypeStruct((count, LANES), jnp.float32),
        jax.ShapeDtypeStruct((GROUP_REQUESTS, count, PAIR), jnp.float32),
    ] + [sent] * (subs - 1)
    return pl.pallas_call(
        pairs_kernel,
        in_specs=[pl.BlockSpec(memory_space=pltpu.SMEM)]
        + [pl.BlockSpec(memory_space=pltpu.VMEM)] * (2 + len(gathered)),
        out_specs=[pl.BlockSpec(memory_space=pltpu.VMEM)] * len(shapes),
        out_shape=shapes,
        compiler_params=params(),
        cost_estimate=cost(gathered, [weight], flops=2 * count * weight.size),
        name="scale_and_pairs",
    )(place, gain, weight, *gathered)


def query_kernel(place, scale_ref, gain_ref, weight_ref, cos_ref, sin_ref, *refs):
    x_refs, out_ref, held, sems = refs[:-3], refs[-3], refs[-2], refs[-1]
    _, rows, width = x_refs[0].shape
    columns = weight_ref.shape[1]
    blocks = list(blocks_of(place, x_refs))
    copies = []
    for i, (_, _, block) in enumerate(blocks):
        depth = pl.ds(pl.multiple_of(block * width, width), width)
        copies.append(pltpu.make_async_copy(weight_ref.at[depth], held.at[i], sems.at[i]))
    for copy in copies:
        copy.start()
    scale = scale_ref[:, :1]
    total = jnp.zeros((rows, columns), jnp.float32)
    for i, (ref, z, block) in enumerate(blocks):
        x = ref[z].astype(jnp.float32)
        x = (x * scale * gain_ref[block]).astype(jnp.bfloat16)
        copies[i].wait()
        total += jnp.dot(x, held[i], preferred_element_type=jnp.float32)
    for head in range(columns // HEAD_SIZE):
        part = slice(head * HEAD_SIZE, (head + 1) * HEAD_SIZE)
        turned = turn(total[:, part], cos_ref[...], sin_ref[...])
        for r in range(GROUP_REQUESTS):
            first, second = r * SAMPLES, (GROUP_REQUESTS + r) * SAMPLES
            out_ref[r, :, part] = jnp.concatenate(
                [turned[first : first + SAMPLES], turned[second : second + SAMPLES]], axis=0
            ).astype(jnp.bfloat16)


def queries(place, scale, gain, weight, cosine, sine, gathered):
    columns = weight.shape[1]
    _, rows, width = gathered[0].shape
    blocks = weight.shape[0] // width
    return pl.pallas_call(
        query_kernel,
        in_specs=[pl.BlockSpec(memory_space=pltpu.SMEM)]
        + [pl.BlockSpec(memory_space=pltpu.VMEM)] * 2
        + [pl.BlockSpec(memory_space=pltpu.HBM)]
        + [pl.BlockSpec(memory_space=pltpu.VMEM)] * (2 + len(gathered)),
        out_specs=pl.BlockSpec(memory_space=pltpu.VMEM),
        out_shape=jax.ShapeDtypeStruct((GROUP_REQUESTS, ROWS, columns), jnp.bfloat16),
        scratch_shapes=[
            pltpu.VMEM((blocks, width, columns), jnp.bfloat16),
            pltpu.SemaphoreType.DMA((blocks,)),
        ],
        compiler_params=pltpu.CompilerParams(vmem_limit_bytes=LARGE_VMEM),
        cost_estimate=cost([weight], flops=2 * rows * weight.size),
        name="queries",
    )(place, scale, gain, weight, cosine, sine, *gathered)


def attend_kernel(place, lengths, q_ref, mine_ref, other_ref, cos_ref, sin_ref, *refs):
    caches, out_ref, key_ref, value_ref = refs[:-3], refs[-3], refs[-2], refs[-1]
    request, sub, core = place[0], place[1], place[2]
    subs, span = len(caches) // 2, caches[0].shape[1]
    targets = 2 * subs
    tokens = targets * span
    quarter = q_ref.shape[2] // HEAD_SIZE
    pair = mine_ref[...] + other_ref[...]
    key_ref[...] = turn(pair[:, :HEAD_SIZE], cos_ref[...], sin_ref[...])
    value_ref[...] = pair[:, HEAD_SIZE:]
    column = lax.broadcasted_iota(jnp.int32, (1, tokens), 1)
    source, inside = column // span, column % span
    from_core = jnp.where(source < subs, core, 1 - core)
    from_sub = sub ^ source % subs
    entry = inside // PAGE_TOKENS * targets + from_sub * 2 + from_core
    position = entry * PAGE_TOKENS + inside % PAGE_TOKENS
    count = quarter * ROWS
    row = lax.broadcasted_iota(jnp.int32, (count, ROWS), 0) % ROWS
    other = lax.broadcasted_iota(jnp.int32, (count, ROWS), 1)
    own_visible = (row % SAMPLES == other % SAMPLES) & (other // SAMPLES <= row // SAMPLES)
    factor = HEAD_SIZE ** (-0.5)
    contract = (((1,), (1,)), ((), ()))
    for z in range(GROUP_REQUESTS):
        r = request ^ z
        fresh = [
            pl.ds(pl.multiple_of((step * GROUP_REQUESTS + r) * SAMPLES, SAMPLES), SAMPLES)
            for step in range(STEPS)
        ]
        new_key = jnp.concatenate([key_ref[rows] for rows in fresh], axis=0)
        new_value = jnp.concatenate([value_ref[rows] for rows in fresh], axis=0)
        new_key, new_value = new_key.astype(jnp.bfloat16), new_value.astype(jnp.bfloat16)
        keys = jnp.concatenate([ref[z, :, :HEAD_SIZE] for ref in caches], axis=0)
        values = jnp.concatenate([ref[z, :, HEAD_SIZE:] for ref in caches], axis=0)
        query = jnp.concatenate(
            [q_ref[r, :, h * HEAD_SIZE : (h + 1) * HEAD_SIZE] for h in range(quarter)], axis=0
        )
        scores = lax.dot_general(query, keys, contract, preferred_element_type=jnp.float32)
        scores = jnp.where(position < lengths[r], scores * factor, -jnp.inf)
        own = lax.dot_general(query, new_key, contract, preferred_element_type=jnp.float32)
        own = jnp.where(own_visible, own * factor, -jnp.inf)
        highest = jnp.maximum(
            jnp.max(scores, axis=-1, keepdims=True), jnp.max(own, axis=-1, keepdims=True)
        )
        scores = jnp.exp(scores - highest)
        own = jnp.exp(own - highest)
        total = jnp.sum(scores, axis=-1, keepdims=True) + jnp.sum(own, axis=-1, keepdims=True)
        share = 1.0 / total
        mixed = jnp.dot(
            (scores * share).astype(jnp.bfloat16), values, preferred_element_type=jnp.float32
        ) + jnp.dot(
            (own * share).astype(jnp.bfloat16), new_value, preferred_element_type=jnp.float32
        )
        mixed = mixed.astype(jnp.bfloat16)
        for h in range(quarter):
            out_ref[r, :, h * HEAD_SIZE : (h + 1) * HEAD_SIZE] = mixed[
                h * ROWS : (h + 1) * ROWS
            ]


def attend(place, lengths, query, mine, other, cosine, sine, caches):
    return pl.pallas_call(
        attend_kernel,
        in_specs=[pl.BlockSpec(memory_space=pltpu.SMEM)] * 2
        + [pl.BlockSpec(memory_space=pltpu.VMEM)] * (5 + len(caches)),
        out_specs=pl.BlockSpec(memory_space=pltpu.VMEM),
        out_shape=jax.ShapeDtypeStruct(query.shape, jnp.bfloat16),
        scratch_shapes=[pltpu.VMEM(cosine.shape, jnp.float32)] * 2,
        compiler_params=params(),
        cost_estimate=cost(caches, caches, caches, flops=2**28),
        name="attend",
    )(place, lengths, query, mine, other, cosine, sine, *caches)


def output_kernel(first, x_ref, weight_ref, *refs):
    out_ref = refs[-1]
    blocks, rows, width = out_ref.shape
    x = x_ref[...].reshape(rows, -1)
    for i in range(blocks):
        part = jnp.dot(x, weight_ref[first + i], preferred_element_type=jnp.float32)
        for r in range(GROUP_REQUESTS):
            for step in range(STEPS):
                source = r * ROWS + step * SAMPLES
                target = (step * GROUP_REQUESTS + r) * SAMPLES
                out_ref[i, target : target + SAMPLES] = part[source : source + SAMPLES]


def outputs(mixed, weight, first, blocks, after=()):
    rows, width = GROUP_REQUESTS * ROWS, weight.shape[2]
    return pl.pallas_call(
        functools.partial(output_kernel, first),
        in_specs=[pl.BlockSpec(memory_space=pltpu.VMEM)] * 2 + unread(after),
        out_specs=pl.BlockSpec(memory_space=pltpu.VMEM),
        out_shape=jax.ShapeDtypeStruct((blocks, rows, width), jnp.float32),
        compiler_params=params(),
        cost_estimate=cost([mixed], flops=2 * rows * mixed.shape[2] * blocks * width),
        name="outputs",
    )(mixed, weight, *after)


def pieces_of(block):
    return [block[:, c : c + LANES] for c in range(0, block.shape[1], LANES)]


def encode(out_ref, pieces):
    rows = pieces[0].shape[0]
    peak = jnp.abs(pieces[0])
    for piece in pieces[1:]:
        peak = jnp.maximum(peak, jnp.abs(piece))
    peak = jnp.maximum(jnp.max(peak, axis=0, keepdims=True), 1e-30)
    exponent = jnp.floor(jnp.log2(peak)) - 14.0
    inverse = jnp.exp2(-exponent)
    for i, piece in enumerate(pieces):
        code = jnp.clip(jnp.floor(piece * inverse + 0.5), -32767.0, 32767.0)
        out_ref[i * rows : (i + 1) * rows] = code.astype(jnp.int32).astype(jnp.int16)
    out_ref[len(pieces) * rows :] = (
        jnp.broadcast_to(exponent, (TAIL, LANES)).astype(jnp.int32).astype(jnp.int16)
    )


def step_of(ref):
    tail = ref[ref.shape[0] - TAIL :].astype(jnp.int32).astype(jnp.float32)
    return jnp.exp2(tail[:1])


def decoded(ref, first, rows, step):
    return ref[pl.ds(first, rows)].astype(jnp.int32).astype(jnp.float32) * step


def fold_core_kernel(keep, mine_ref, got_ref, *out_refs):
    for i, out_ref in enumerate(out_refs):
        block = mine_ref[i] + got_ref[i]
        if keep and i == 0:
            out_ref[...] = block
        else:
            encode(out_ref, pieces_of(block))


def fold_core(mine, got, keep):
    blocks, rows, width = mine.shape
    sent = jax.ShapeDtypeStruct((width // LANES * rows + TAIL, LANES), jnp.int16)
    kept = jax.ShapeDtypeStruct((rows, width), jnp.float32)
    return pl.pallas_call(
        functools.partial(fold_core_kernel, keep),
        in_specs=[pl.BlockSpec(memory_space=pltpu.VMEM)] * 2,
        out_specs=[pl.BlockSpec(memory_space=pltpu.VMEM)] * blocks,
        out_shape=[kept if keep and i == 0 else sent for i in range(blocks)],
        compiler_params=params(),
        cost_estimate=cost([mine, got]),
        name="fold_core",
    )(mine, got)


def fold_sub_kernel(order, count, own, *refs):
    own_refs, in_refs, out_refs = refs[:own], refs[own : own + count], refs[-len(order) :]
    _, rows, width = own_refs[0].shape
    steps = [step_of(ref) for ref in in_refs]
    for i, (z, out_ref) in enumerate(zip(order, out_refs)):
        block = own_refs[0][z]
        for ref in own_refs[1:]:
            block = block + ref[z]
        pieces = pieces_of(block)
        for c in range(len(pieces)):
            for ref, step in zip(in_refs, steps):
                first = (i * len(pieces) + c) * rows
                pieces[c] = pieces[c] + decoded(ref, first, rows, step)
        if z:
            encode(out_ref, pieces)
        else:
            for c, piece in enumerate(pieces):
                out_ref[:, c * LANES : (c + 1) * LANES] = piece


def fold_sub(order, own, parts, after=()):
    _, rows, width = own[0].shape
    total = jax.ShapeDtypeStruct((rows, width), jnp.float32)
    sent = jax.ShapeDtypeStruct((width // LANES * rows + TAIL, LANES), jnp.int16)
    return pl.pallas_call(
        functools.partial(fold_sub_kernel, order, len(parts), len(own)),
        in_specs=[pl.BlockSpec(memory_space=pltpu.VMEM)] * (len(own) + len(parts))
        + unread(after),
        out_specs=[pl.BlockSpec(memory_space=pltpu.VMEM)] * len(order),
        out_shape=[sent if z else total for z in order],
        compiler_params=params(),
        cost_estimate=cost(own, parts),
        name="fold_sub",
    )(*own, *parts, *after)


def fold_pairs_kernel(count, total_ref, *refs):
    rows = total_ref.shape[0]
    refs, out_ref = refs[:count], refs[-1]
    steps = [step_of(ref) for ref in refs]
    for c in range(total_ref.shape[1] // LANES):
        part = slice(c * LANES, (c + 1) * LANES)
        total = total_ref[:, part]
        for ref, step in zip(refs, steps):
            total = total + decoded(ref, c * rows, rows, step)
        out_ref[:, part] = total


def fold_pairs(total, parts, after=()):
    return pl.pallas_call(
        functools.partial(fold_pairs_kernel, len(parts)),
        in_specs=[pl.BlockSpec(memory_space=pltpu.VMEM)] * (1 + len(parts)) + unread(after),
        out_specs=pl.BlockSpec(memory_space=pltpu.VMEM),
        out_shape=jax.ShapeDtypeStruct(total.shape, jnp.float32),
        compiler_params=params(),
        cost_estimate=cost([total], parts),
        name="fold_pairs",
    )(total, *parts, *after)


def finish_kernel(rows_ref, total_ref, *refs):
    rows = total_ref.shape[0]
    steps = [step_of(ref) for ref in refs[:-1]]
    for c in range(total_ref.shape[1] // LANES):
        part = slice(c * LANES, (c + 1) * LANES)
        total = total_ref[:, part]
        for ref, step in zip(refs[:-1], steps):
            total = total + decoded(ref, c * rows, rows, step)
        refs[-1][:, part] = (total + rows_ref[0, :, part].astype(jnp.float32)).astype(
            jnp.bfloat16
        )


def finish(rows, total, parts):
    return pl.pallas_call(
        finish_kernel,
        in_specs=[pl.BlockSpec(memory_space=pltpu.VMEM)] * (2 + len(parts)),
        out_specs=pl.BlockSpec(memory_space=pltpu.VMEM),
        out_shape=jax.ShapeDtypeStruct(total.shape, jnp.bfloat16),
        compiler_params=params(),
        cost_estimate=cost([total], parts),
        name="finish",
    )(rows, total, *parts)


def passed(array, axis, shift):
    return lax.ppermute(array, axis, [(i, i ^ shift) for i in range(lax.axis_size(axis))])


def sent_to(array, step, shift):
    subs = lax.axis_size("sub")
    count = lax.axis_size("req") * subs
    there = [(i, ((i // subs) ^ step) * subs + (i % subs ^ shift)) for i in range(count)]
    return lax.ppermute(array, ("req", "sub"), there)


def scalars(*values):
    return jnp.stack([jnp.asarray(value, jnp.int32) for value in values])


def shards(
    hidden,
    norm_gain,
    w_query,
    key_value_weight,
    w_output,
    prompt_cache_pages,
    per_page_scales,
    lengths,
    block_table,
):
    devices = lax.axis_size(DEVICES)
    subs = lax.axis_size("sub")
    device = lax.axis_index(DEVICES)
    request = lax.axis_index("req")
    sub = lax.axis_index("sub")
    core = lax.axis_index("section")
    width = hidden.shape[2]
    place = scalars(request, sub, core)

    rows = hidden.reshape(GROUP_REQUESTS * ROWS, width)
    column = [passed(rows, "req", s) for s in range(1, GROUP_REQUESTS)]
    where = scalars(request, sub * 2 + core, device * prompt_cache_pages.shape[0])
    rows, *pages = used_pages(
        prompt_cache_pages, per_page_scales, block_table, where, subs, rows
    )
    column = pack([rows] + column)
    gathered = [passed(column, "sub", s) for s in range(1, subs)]
    pages[1:] = [passed(pages[s], "req", s) for s in range(1, GROUP_REQUESTS)]
    key_value_weight, ready, gain = staged(
        place,
        key_value_weight,
        PAIR,
        pair_order(subs),
        more=[norm_gain.reshape(devices, 1, width)],
        after=[column],
    )
    gathered = [column] + list(gate(gathered, after=[ready]))
    gathered = gathered + [passed(part, "section", 1) for part in gathered]

    half = HEAD_SIZE // 2
    freqs = jnp.exp(
        -jnp.log(theta_base) * jnp.arange(half, dtype=jnp.float32) * (2.0 / HEAD_SIZE)
    )
    positions = (lengths[None, :] + jnp.arange(STEPS)[:, None]).astype(jnp.float32)
    angles = positions[..., None] * freqs
    cosine, sine = jnp.cos(angles), jnp.sin(angles)
    cosine = jnp.repeat(jnp.concatenate([cosine, cosine], axis=-1)[:, :, None], SAMPLES, axis=2)
    sine = jnp.repeat(jnp.concatenate([-sine, sine], axis=-1)[:, :, None], SAMPLES, axis=2)
    cosine = cosine.reshape(-1, HEAD_SIZE)
    sine = sine.reshape(-1, HEAD_SIZE)

    scale, kept, *parts = scale_and_pairs(place, gain, key_value_weight, gathered)
    parts = [passed(part, "sub", s + 1) for s, part in enumerate(parts)]
    query = queries(place, scale, gain, w_query, cosine, sine, gathered)
    total, *parts = fold_sub((0, 1, 2, 3), [kept], parts, after=[query])
    parts = [passed(part, "req", s + 1) for s, part in enumerate(parts)]
    pages = regroup(pages, after=[total])
    caches = [passed(pages[s], "sub", s) for s in range(1, subs)]
    w_output, ready = staged(place, w_output, width, output_order(subs), after=[query])
    mine = fold_pairs(total, parts, after=[ready])
    caches = list(pages[:1]) + list(gate(caches, after=[mine]))
    caches = caches + [passed(part, "section", 1) for part in caches]
    other = passed(mine, "section", 1)

    mixed = attend(
        place, lengths.astype(jnp.int32), query, mine, other, cosine, sine, caches
    )

    mid, end = GROUP_REQUESTS, GROUP_REQUESTS * subs
    first = outputs(mixed, w_output, end + mid, end - mid)
    got_first = passed(first, "section", 1)
    second = outputs(mixed, w_output, end, mid, after=[first])
    got_second = passed(second, "section", 1)
    kept = outputs(mixed, w_output, mid, end - mid, after=[second])
    parts = fold_core(kept, got_first, False)
    kept = outputs(mixed, w_output, 0, mid, after=parts[:1])
    steps = [(z, j) for j in range(1, subs) for z in range(GROUP_REQUESTS)]
    parts = [sent_to(part, *step) for part, step in zip(parts, steps)]
    total, *near = fold_core(kept, got_second, True)
    parts += [sent_to(part, z + 1, 0) for z, part in enumerate(near)]
    return finish(gathered[0], total, parts).reshape(hidden.shape)


def solution(mesh):
    groups, tp, section = mesh.devices.shape
    finer = Mesh(
        mesh.devices.reshape(groups, GROUP_REQUESTS, tp // GROUP_REQUESTS, section),
        ("groups",) + DEVICES,
    )
    placed = (
        P(None, "groups", DEVICES),
        P(),
        P(None, DEVICES),
        P(DEVICES, None),
        P(DEVICES, None),
        P(("groups",) + DEVICES, None, None),
        P(("groups",) + DEVICES, None),
        P("groups"),
        P("groups", None),
    )
    return jax.shard_map(
        shards,
        mesh=finer,
        in_specs=placed,
        out_specs=P(None, "groups", DEVICES),
        check_vma=False,
    )
```

```python
import functools

import jax
import jax.numpy as jnp
from jax import lax
from jax.experimental import pallas as pl
from jax.experimental.pallas import tpu as pltpu
from jax.sharding import Mesh
from jax.sharding import PartitionSpec as P

QUERY_HEADS = 64
KEY_VALUE_HEADS = 8
HEAD_SIZE = 128
GROUP_REQUESTS = 4
SAMPLES = 8
PAGE_TOKENS = 16
STEPS = 2
ROWS = STEPS * SAMPLES
PAIR = 2 * HEAD_SIZE
LANES = 128
TAIL = 16
HALVES = ((2, 3), (0, 1))
DEVICES = ("req", "sub", "section")

theta_base = 500000.0
eps_norm = 1e-05
VMEM = 16 * 2**20
LARGE_VMEM = 51 * 2**20


def params(**more):
    return pltpu.CompilerParams(vmem_limit_bytes=VMEM, **more)


def cost(*groups, flops=0):
    size = sum(array.size * array.dtype.itemsize for arrays in groups for array in arrays)
    return pl.CostEstimate(flops=flops, bytes_accessed=size, transcendentals=0)


def unread(arrays):
    return [pl.BlockSpec(memory_space=pl.ANY)] * len(arrays)


def turn(vectors, cosine, sine):
    return vectors * cosine + pltpu.roll(vectors, HEAD_SIZE // 2, vectors.ndim - 1) * sine


def stage_kernel(order, count, place, block_ref, *refs):
    out_ref, token_ref, *outs, sems = refs[-3 - count :]
    width = out_ref.shape[2]
    copies = [
        pltpu.make_async_copy(refs[i], outs[i], sems.at[len(order) + i]) for i in range(count)
    ]
    for i, block in enumerate(order):
        columns = pl.ds(pl.multiple_of(block(place) * width, width), width)
        copies.append(pltpu.make_async_copy(block_ref.at[:, columns], out_ref.at[i], sems.at[i]))
    for copy in copies:
        copy.start()
    token_ref[...] = jnp.zeros_like(token_ref)
    for copy in copies:
        copy.wait()


def staged(place, array, width, order, more=(), after=()):
    rows, count = array.shape[0], len(order)
    return pl.pallas_call(
        functools.partial(stage_kernel, order, len(more)),
        in_specs=[pl.BlockSpec(memory_space=pltpu.SMEM)]
        + [pl.BlockSpec(memory_space=pltpu.HBM)] * (1 + len(more))
        + unread(after),
        out_specs=[pl.BlockSpec(memory_space=pltpu.VMEM)] * (2 + len(more)),
        out_shape=[
            jax.ShapeDtypeStruct((count, rows, width), array.dtype),
            jax.ShapeDtypeStruct((8, LANES), jnp.float32),
        ]
        + [jax.ShapeDtypeStruct(other.shape, other.dtype) for other in more],
        scratch_shapes=[pltpu.SemaphoreType.DMA((count + len(more),))],
        compiler_params=params(),
        cost_estimate=cost([array], [array]),
        name="staged",
    )(place, array, *more, *after)


def pair_order(subs):
    return [
        lambda place, j=j, z=z: 2 * (place[0] ^ z) + (place[1] ^ j) // (subs // 2)
        for j in range(subs)
        for z in range(GROUP_REQUESTS)
    ]


def output_order(subs):
    return [
        lambda place, c=c, j=j, z=z: ((place[0] ^ z) * subs + (place[1] ^ j)) * 2 + (place[2] ^ c)
        for c in range(2)
        for j in range(subs)
        for z in range(GROUP_REQUESTS)
    ]


def gate_kernel(*refs):
    pass


def gate(arrays, after):
    count = len(arrays)
    return pl.pallas_call(
        gate_kernel,
        in_specs=[pl.BlockSpec(memory_space=pl.ANY)] * count + unread(after),
        out_specs=[pl.BlockSpec(memory_space=pl.ANY)] * count,
        out_shape=[jax.ShapeDtypeStruct(array.shape, array.dtype) for array in arrays],
        input_output_aliases={i: i for i in range(count)},
        compiler_params=params(),
        name="gate",
    )(*arrays, *after)


def page_of(length, targets, e, place, facts):
    index = place[0] * length + e * targets + place[1]
    return facts[index].astype(jnp.int32) - place[2]


def pages_kernel(length, place, facts, page_ref, rows_ref, rows_out_ref, *out_refs):
    e = pl.program_id(0)
    rows_out_ref[...] = rows_ref[...]
    subs = out_refs[0].shape[0]
    targets = 2 * subs
    page = page_of(length, targets, e, place, facts)
    scales = GROUP_REQUESTS * length + page * (2 * KEY_VALUE_HEADS)
    for z, out_ref in enumerate(out_refs):
        for j in range(subs):
            half = (place[1] // 2 ^ j) // (subs // 2)
            head = 2 * (place[0] ^ z) + half
            for part in range(2):
                c = head * 2 + part
                columns = pl.ds(pl.multiple_of(c * HEAD_SIZE, HEAD_SIZE), HEAD_SIZE)
                block = page_ref[0, :, columns].astype(jnp.float32)
                out_ref[j, :, part * HEAD_SIZE : (part + 1) * HEAD_SIZE] = (
                    block * facts[scales + c]
                ).astype(jnp.bfloat16)


def used_pages(pages, scales, table, place, subs, rows):
    targets = 2 * subs
    length = table.shape[1]
    entries = length // targets
    facts = jnp.concatenate(
        [table.astype(jnp.float32).reshape(-1), scales.astype(jnp.float32).reshape(-1)]
    )
    shape = jax.ShapeDtypeStruct((subs, entries * PAGE_TOKENS, PAIR), jnp.bfloat16)
    return pl.pallas_call(
        functools.partial(pages_kernel, length),
        grid_spec=pltpu.PrefetchScalarGridSpec(
            num_scalar_prefetch=2,
            grid=(entries,),
            in_specs=[
                pl.BlockSpec(
                    (1, PAGE_TOKENS, pages.shape[2]),
                    lambda e, place, facts: (page_of(length, targets, e, place, facts), 0, 0),
                ),
                pl.BlockSpec(rows.shape, lambda e, *_: (0, 0)),
            ],
            out_specs=[pl.BlockSpec(rows.shape, lambda e, *_: (0, 0))]
            + [pl.BlockSpec((subs, PAGE_TOKENS, PAIR), lambda e, *_: (0, e, 0))]
            * GROUP_REQUESTS,
        ),
        out_shape=[jax.ShapeDtypeStruct(rows.shape, rows.dtype)] + [shape] * GROUP_REQUESTS,
        compiler_params=params(),
        cost_estimate=pl.CostEstimate(
            flops=0, bytes_accessed=4 * entries * PAGE_TOKENS * pages.shape[2], transcendentals=0
        ),
        name="used_pages",
    )(place, facts, pages, rows)


def regroup_kernel(*refs):
    ins, outs = refs[:GROUP_REQUESTS], refs[-refs[0].shape[0] :]
    for j, out_ref in enumerate(outs):
        for z, ref in enumerate(ins):
            out_ref[z] = ref[j]


def regroup(parts, after=()):
    subs = parts[0].shape[0]
    shape = jax.ShapeDtypeStruct((len(parts),) + parts[0].shape[1:], parts[0].dtype)
    return pl.pallas_call(
        regroup_kernel,
        in_specs=[pl.BlockSpec(memory_space=pltpu.VMEM)] * len(parts) + unread(after),
        out_specs=[pl.BlockSpec(memory_space=pltpu.VMEM)] * subs,
        out_shape=[shape] * subs,
        compiler_params=params(),
        cost_estimate=cost(parts, parts),
        name="regroup",
    )(*parts, *after)


def pack_kernel(*refs):
    for i in range(refs[-1].shape[0]):
        refs[-1][i] = refs[i][...]


def pack(parts):
    return pl.pallas_call(
        pack_kernel,
        in_specs=[pl.BlockSpec(memory_space=pltpu.VMEM)] * len(parts),
        out_specs=pl.BlockSpec(memory_space=pltpu.VMEM),
        out_shape=jax.ShapeDtypeStruct((len(parts),) + parts[0].shape, parts[0].dtype),
        compiler_params=params(),
        cost_estimate=cost(parts, parts),
        name="pack",
    )(*parts)


def blocks_of(place, refs):
    request, sub, core = place[0], place[1], place[2]
    subs = len(refs) // 2
    for i, ref in enumerate(refs):
        from_core = core if i < subs else 1 - core
        for z in range(GROUP_REQUESTS):
            yield ref, z, ((request ^ z) * subs + (sub ^ i % subs)) * 2 + from_core


def pairs_kernel(place, gain_ref, weight_ref, *refs):
    subs = (len(refs) - 1) // 3
    x_refs, scale_ref, kept_ref, out_refs = (
        refs[: 2 * subs],
        refs[2 * subs],
        refs[2 * subs + 1],
        refs[2 * subs + 2 :],
    )
    request, sub, core = place[0], place[1], place[2]
    _, rows, width = x_refs[0].shape
    total = jnp.zeros((rows, LANES), jnp.float32)
    for ref in x_refs:
        for z in range(GROUP_REQUESTS):
            for piece in pieces_of(ref[z].astype(jnp.float32)):
                total += piece * piece
    mean = jnp.sum(total, axis=-1, keepdims=True) / (2 * subs * GROUP_REQUESTS * width)
    scale = lax.rsqrt(mean + eps_norm)
    scale_ref[...] = jnp.broadcast_to(scale, scale_ref.shape)
    device = (request * subs + sub) * 2 + core
    x = x_refs[0][0].astype(jnp.float32)
    mine = (x * scale * gain_ref[device]).astype(jnp.bfloat16)
    for shift in range(subs):
        pieces = []
        for z in range(GROUP_REQUESTS):
            block = weight_ref[shift * GROUP_REQUESTS + z]
            part = jnp.dot(mine, block, preferred_element_type=jnp.float32)
            if shift == 0:
                kept_ref[z] = part
            pieces += pieces_of(part)
        if shift:
            encode(out_refs[shift - 1], pieces)


def scale_and_pairs(place, gain, weight, gathered):
    subs = len(gathered) // 2
    count = gathered[0].shape[1]
    sent = jax.ShapeDtypeStruct((2 * GROUP_REQUESTS * count + TAIL, LANES), jnp.int16)
    shapes = [
        jax.ShapeDtypeStruct((count, LANES), jnp.float32),
        jax.ShapeDtypeStruct((GROUP_REQUESTS, count, PAIR), jnp.float32),
    ] + [sent] * (subs - 1)
    return pl.pallas_call(
        pairs_kernel,
        in_specs=[pl.BlockSpec(memory_space=pltpu.SMEM)]
        + [pl.BlockSpec(memory_space=pltpu.VMEM)] * (2 + len(gathered)),
        out_specs=[pl.BlockSpec(memory_space=pltpu.VMEM)] * len(shapes),
        out_shape=shapes,
        compiler_params=params(),
        cost_estimate=cost(gathered, [weight], flops=2 * count * weight.size),
        name="scale_and_pairs",
    )(place, gain, weight, *gathered)


def query_kernel(place, scale_ref, gain_ref, weight_ref, cos_ref, sin_ref, *refs):
    x_refs, out_ref, held, sems = refs[:-3], refs[-3], refs[-2], refs[-1]
    _, rows, width = x_refs[0].shape
    columns = weight_ref.shape[1]
    blocks = list(blocks_of(place, x_refs))
    copies = []
    for i, (_, _, block) in enumerate(blocks):
        depth = pl.ds(pl.multiple_of(block * width, width), width)
        copies.append(pltpu.make_async_copy(weight_ref.at[depth], held.at[i], sems.at[i]))
    for copy in copies:
        copy.start()
    scale = scale_ref[:, :1]
    total = jnp.zeros((rows, columns), jnp.float32)
    for i, (ref, z, block) in enumerate(blocks):
        x = ref[z].astype(jnp.float32)
        x = (x * scale * gain_ref[block]).astype(jnp.bfloat16)
        copies[i].wait()
        total += jnp.dot(x, held[i], preferred_element_type=jnp.float32)
    for head in range(columns // HEAD_SIZE):
        part = slice(head * HEAD_SIZE, (head + 1) * HEAD_SIZE)
        turned = turn(total[:, part], cos_ref[...], sin_ref[...])
        for r in range(GROUP_REQUESTS):
            first, second = r * SAMPLES, (GROUP_REQUESTS + r) * SAMPLES
            out_ref[r, :, part] = jnp.concatenate(
                [turned[first : first + SAMPLES], turned[second : second + SAMPLES]], axis=0
            ).astype(jnp.bfloat16)


def queries(place, scale, gain, weight, cosine, sine, gathered):
    columns = weight.shape[1]
    _, rows, width = gathered[0].shape
    blocks = weight.shape[0] // width
    return pl.pallas_call(
        query_kernel,
        in_specs=[pl.BlockSpec(memory_space=pltpu.SMEM)]
        + [pl.BlockSpec(memory_space=pltpu.VMEM)] * 2
        + [pl.BlockSpec(memory_space=pltpu.HBM)]
        + [pl.BlockSpec(memory_space=pltpu.VMEM)] * (2 + len(gathered)),
        out_specs=pl.BlockSpec(memory_space=pltpu.VMEM),
        out_shape=jax.ShapeDtypeStruct((GROUP_REQUESTS, ROWS, columns), jnp.bfloat16),
        scratch_shapes=[
            pltpu.VMEM((blocks, width, columns), jnp.bfloat16),
            pltpu.SemaphoreType.DMA((blocks,)),
        ],
        compiler_params=pltpu.CompilerParams(vmem_limit_bytes=LARGE_VMEM),
        cost_estimate=cost([weight], flops=2 * rows * weight.size),
        name="queries",
    )(place, scale, gain, weight, cosine, sine, *gathered)


def attend_kernel(place, lengths, q_ref, mine_ref, other_ref, cos_ref, sin_ref, *refs):
    caches, out_ref, key_ref, value_ref = refs[:-3], refs[-3], refs[-2], refs[-1]
    request, sub, core = place[0], place[1], place[2]
    subs, span = len(caches) // 2, caches[0].shape[1]
    targets = 2 * subs
    tokens = targets * span
    quarter = q_ref.shape[2] // HEAD_SIZE
    pair = mine_ref[...] + other_ref[...]
    key_ref[...] = turn(pair[:, :HEAD_SIZE], cos_ref[...], sin_ref[...])
    value_ref[...] = pair[:, HEAD_SIZE:]
    column = lax.broadcasted_iota(jnp.int32, (1, tokens), 1)
    source, inside = column // span, column % span
    from_core = jnp.where(source < subs, core, 1 - core)
    from_sub = sub ^ source % subs
    entry = inside // PAGE_TOKENS * targets + from_sub * 2 + from_core
    position = entry * PAGE_TOKENS + inside % PAGE_TOKENS
    count = quarter * ROWS
    row = lax.broadcasted_iota(jnp.int32, (count, ROWS), 0) % ROWS
    other = lax.broadcasted_iota(jnp.int32, (count, ROWS), 1)
    own_visible = (row % SAMPLES == other % SAMPLES) & (other // SAMPLES <= row // SAMPLES)
    factor = HEAD_SIZE ** (-0.5)
    contract = (((1,), (1,)), ((), ()))
    for z in range(GROUP_REQUESTS):
        r = request ^ z
        fresh = [
            pl.ds(pl.multiple_of((step * GROUP_REQUESTS + r) * SAMPLES, SAMPLES), SAMPLES)
            for step in range(STEPS)
        ]
        new_key = jnp.concatenate([key_ref[rows] for rows in fresh], axis=0)
        new_value = jnp.concatenate([value_ref[rows] for rows in fresh], axis=0)
        new_key, new_value = new_key.astype(jnp.bfloat16), new_value.astype(jnp.bfloat16)
        keys = [ref[z, :, :HEAD_SIZE] for ref in caches]
        values = [ref[z, :, HEAD_SIZE:] for ref in caches]
        if span % LANES:
            keys = [jnp.concatenate(keys, axis=0)]
            values = [jnp.concatenate(values, axis=0)]
        query = jnp.concatenate(
            [q_ref[r, :, h * HEAD_SIZE : (h + 1) * HEAD_SIZE] for h in range(quarter)], axis=0
        )
        scores = jnp.concatenate(
            [
                lax.dot_general(query, part, contract, preferred_element_type=jnp.float32)
                for part in keys
            ],
            axis=1,
        )
        scores = jnp.where(position < lengths[r], scores * factor, -jnp.inf)
        own = lax.dot_general(query, new_key, contract, preferred_element_type=jnp.float32)
        own = jnp.where(own_visible, own * factor, -jnp.inf)
        highest = jnp.maximum(
            jnp.max(scores, axis=-1, keepdims=True), jnp.max(own, axis=-1, keepdims=True)
        )
        scores = jnp.exp(scores - highest)
        own = jnp.exp(own - highest)
        total = jnp.sum(scores, axis=-1, keepdims=True) + jnp.sum(own, axis=-1, keepdims=True)
        share = 1.0 / total
        scores = (scores * share).astype(jnp.bfloat16)
        own = (own * share).astype(jnp.bfloat16)
        mixed = jnp.dot(own, new_value, preferred_element_type=jnp.float32)
        first = 0
        for part in values:
            weights = scores[:, first : first + part.shape[0]]
            mixed += jnp.dot(weights, part, preferred_element_type=jnp.float32)
            first += part.shape[0]
        mixed = mixed.astype(jnp.bfloat16)
        for h in range(quarter):
            out_ref[r, :, h * HEAD_SIZE : (h + 1) * HEAD_SIZE] = mixed[
                h * ROWS : (h + 1) * ROWS
            ]


def attend(place, lengths, query, mine, other, cosine, sine, caches):
    return pl.pallas_call(
        attend_kernel,
        in_specs=[pl.BlockSpec(memory_space=pltpu.SMEM)] * 2
        + [pl.BlockSpec(memory_space=pltpu.VMEM)] * (5 + len(caches)),
        out_specs=pl.BlockSpec(memory_space=pltpu.VMEM),
        out_shape=jax.ShapeDtypeStruct(query.shape, jnp.bfloat16),
        scratch_shapes=[pltpu.VMEM(cosine.shape, jnp.float32)] * 2,
        compiler_params=params(),
        cost_estimate=cost(caches, caches, caches, flops=2**28),
        name="attend",
    )(place, lengths, query, mine, other, cosine, sine, *caches)


def output_kernel(first, x_ref, weight_ref, *refs):
    out_ref = refs[-1]
    blocks, rows, width = out_ref.shape
    x = x_ref[...].reshape(rows, -1)
    for i in range(blocks):
        part = jnp.dot(x, weight_ref[first + i], preferred_element_type=jnp.float32)
        for r in range(GROUP_REQUESTS):
            for step in range(STEPS):
                source = r * ROWS + step * SAMPLES
                target = (step * GROUP_REQUESTS + r) * SAMPLES
                out_ref[i, target : target + SAMPLES] = part[source : source + SAMPLES]


def outputs(mixed, weight, first, blocks, after=()):
    rows, width = GROUP_REQUESTS * ROWS, weight.shape[2]
    return pl.pallas_call(
        functools.partial(output_kernel, first),
        in_specs=[pl.BlockSpec(memory_space=pltpu.VMEM)] * 2 + unread(after),
        out_specs=pl.BlockSpec(memory_space=pltpu.VMEM),
        out_shape=jax.ShapeDtypeStruct((blocks, rows, width), jnp.float32),
        compiler_params=params(),
        cost_estimate=cost([mixed], flops=2 * rows * mixed.shape[2] * blocks * width),
        name="outputs",
    )(mixed, weight, *after)


def pieces_of(block):
    return [block[:, c : c + LANES] for c in range(0, block.shape[1], LANES)]


def encode(out_ref, pieces):
    rows = pieces[0].shape[0]
    peak = jnp.abs(pieces[0])
    for piece in pieces[1:]:
        peak = jnp.maximum(peak, jnp.abs(piece))
    peak = jnp.maximum(jnp.max(peak, axis=0, keepdims=True), 1e-30)
    exponent = jnp.floor(jnp.log2(peak)) - 14.0
    inverse = jnp.exp2(-exponent)
    for i, piece in enumerate(pieces):
        code = jnp.clip(jnp.floor(piece * inverse + 0.5), -32767.0, 32767.0)
        out_ref[i * rows : (i + 1) * rows] = code.astype(jnp.int32).astype(jnp.int16)
    out_ref[len(pieces) * rows :] = (
        jnp.broadcast_to(exponent, (TAIL, LANES)).astype(jnp.int32).astype(jnp.int16)
    )


def step_of(ref):
    tail = ref[ref.shape[0] - TAIL :].astype(jnp.int32).astype(jnp.float32)
    return jnp.exp2(tail[:1])


def decoded(ref, first, rows, step):
    return ref[pl.ds(first, rows)].astype(jnp.int32).astype(jnp.float32) * step


def fold_core_kernel(mine_ref, got_ref, *out_refs):
    for i, out_ref in enumerate(out_refs):
        pieces = []
        for z in HALVES[i % 2]:
            block = i // 2 * GROUP_REQUESTS + z
            pieces += pieces_of(mine_ref[block] + got_ref[block])
        encode(out_ref, pieces)


def fold_core(mine, got):
    blocks, rows, width = mine.shape
    count = 2 * (blocks // GROUP_REQUESTS)
    sent = jax.ShapeDtypeStruct((2 * width // LANES * rows + TAIL, LANES), jnp.int16)
    return pl.pallas_call(
        fold_core_kernel,
        in_specs=[pl.BlockSpec(memory_space=pltpu.VMEM)] * 2,
        out_specs=[pl.BlockSpec(memory_space=pltpu.VMEM)] * count,
        out_shape=[sent] * count,
        compiler_params=params(),
        cost_estimate=cost([mine, got]),
        name="fold_core",
    )(mine, got)


def fold_sub_kernel(order, count, own, *refs):
    own_refs, in_refs, out_refs = refs[:own], refs[own : own + count], refs[-len(order) :]
    _, rows, width = own_refs[0].shape
    steps = [step_of(ref) for ref in in_refs]
    for i, (z, out_ref) in enumerate(zip(order, out_refs)):
        block = own_refs[0][z]
        for ref in own_refs[1:]:
            block = block + ref[z]
        pieces = pieces_of(block)
        for c in range(len(pieces)):
            for ref, step in zip(in_refs, steps):
                first = (i * len(pieces) + c) * rows
                pieces[c] = pieces[c] + decoded(ref, first, rows, step)
        if z:
            encode(out_ref, pieces)
        else:
            for c, piece in enumerate(pieces):
                out_ref[:, c * LANES : (c + 1) * LANES] = piece


def fold_sub(order, own, parts, after=()):
    _, rows, width = own[0].shape
    total = jax.ShapeDtypeStruct((rows, width), jnp.float32)
    sent = jax.ShapeDtypeStruct((width // LANES * rows + TAIL, LANES), jnp.int16)
    return pl.pallas_call(
        functools.partial(fold_sub_kernel, order, len(parts), len(own)),
        in_specs=[pl.BlockSpec(memory_space=pltpu.VMEM)] * (len(own) + len(parts))
        + unread(after),
        out_specs=[pl.BlockSpec(memory_space=pltpu.VMEM)] * len(order),
        out_shape=[sent if z else total for z in order],
        compiler_params=params(),
        cost_estimate=cost(own, parts),
        name="fold_sub",
    )(*own, *parts, *after)


def fold_pairs_kernel(count, total_ref, *refs):
    rows = total_ref.shape[0]
    refs, out_ref = refs[:count], refs[-1]
    steps = [step_of(ref) for ref in refs]
    for c in range(total_ref.shape[1] // LANES):
        part = slice(c * LANES, (c + 1) * LANES)
        total = total_ref[:, part]
        for ref, step in zip(refs, steps):
            total = total + decoded(ref, c * rows, rows, step)
        out_ref[:, part] = total


def fold_pairs(total, parts, after=()):
    return pl.pallas_call(
        functools.partial(fold_pairs_kernel, len(parts)),
        in_specs=[pl.BlockSpec(memory_space=pltpu.VMEM)] * (1 + len(parts)) + unread(after),
        out_specs=pl.BlockSpec(memory_space=pltpu.VMEM),
        out_shape=jax.ShapeDtypeStruct(total.shape, jnp.float32),
        compiler_params=params(),
        cost_estimate=cost([total], parts),
        name="fold_pairs",
    )(total, *parts, *after)


def finish_kernel(rows_ref, total_ref, *refs):
    rows = total_ref.shape[0]
    steps = [step_of(ref) for ref in refs[:-1]]
    for c in range(total_ref.shape[1] // LANES):
        part = slice(c * LANES, (c + 1) * LANES)
        total = total_ref[:, part]
        for ref, step in zip(refs[:-1], steps):
            total = total + decoded(ref, c * rows, rows, step)
        refs[-1][:, part] = (total + rows_ref[0, :, part].astype(jnp.float32)).astype(
            jnp.bfloat16
        )


def finish(rows, total, parts):
    return pl.pallas_call(
        finish_kernel,
        in_specs=[pl.BlockSpec(memory_space=pltpu.VMEM)] * (2 + len(parts)),
        out_specs=pl.BlockSpec(memory_space=pltpu.VMEM),
        out_shape=jax.ShapeDtypeStruct(total.shape, jnp.bfloat16),
        compiler_params=params(),
        cost_estimate=cost([total], parts),
        name="finish",
    )(rows, total, *parts)


def passed(array, axis, shift):
    return lax.ppermute(array, axis, [(i, i ^ shift) for i in range(lax.axis_size(axis))])


def scalars(*values):
    return jnp.stack([jnp.asarray(value, jnp.int32) for value in values])


def shards(
    hidden,
    norm_gain,
    w_query,
    key_value_weight,
    w_output,
    prompt_cache_pages,
    per_page_scales,
    lengths,
    block_table,
):
    devices = lax.axis_size(DEVICES)
    subs = lax.axis_size("sub")
    device = lax.axis_index(DEVICES)
    request = lax.axis_index("req")
    sub = lax.axis_index("sub")
    core = lax.axis_index("section")
    width = hidden.shape[2]
    place = scalars(request, sub, core)

    rows = hidden.reshape(GROUP_REQUESTS * ROWS, width)
    column = [passed(rows, "req", s) for s in range(1, GROUP_REQUESTS)]
    where = scalars(request, sub * 2 + core, device * prompt_cache_pages.shape[0])
    rows, *pages = used_pages(
        prompt_cache_pages, per_page_scales, block_table, where, subs, rows
    )
    column = pack([rows] + column)
    gathered = [passed(column, "sub", s) for s in range(1, subs)]
    pages[1:] = [passed(pages[s], "req", s) for s in range(1, GROUP_REQUESTS)]
    key_value_weight, ready, gain = staged(
        place,
        key_value_weight,
        PAIR,
        pair_order(subs),
        more=[norm_gain.reshape(devices, 1, width)],
        after=[column],
    )
    gathered = [column] + list(gate(gathered, after=[ready]))
    gathered = gathered + [passed(part, "section", 1) for part in gathered]

    half = HEAD_SIZE // 2
    freqs = jnp.exp(
        -jnp.log(theta_base) * jnp.arange(half, dtype=jnp.float32) * (2.0 / HEAD_SIZE)
    )
    positions = (lengths[None, :] + jnp.arange(STEPS)[:, None]).astype(jnp.float32)
    angles = positions[..., None] * freqs
    cosine, sine = jnp.cos(angles), jnp.sin(angles)
    cosine = jnp.repeat(jnp.concatenate([cosine, cosine], axis=-1)[:, :, None], SAMPLES, axis=2)
    sine = jnp.repeat(jnp.concatenate([-sine, sine], axis=-1)[:, :, None], SAMPLES, axis=2)
    cosine = cosine.reshape(-1, HEAD_SIZE)
    sine = sine.reshape(-1, HEAD_SIZE)

    scale, kept, *parts = scale_and_pairs(place, gain, key_value_weight, gathered)
    parts = [passed(part, "sub", s + 1) for s, part in enumerate(parts)]
    query = queries(place, scale, gain, w_query, cosine, sine, gathered)
    total, *parts = fold_sub((0, 1, 2, 3), [kept], parts, after=[query])
    parts = [passed(part, "req", s + 1) for s, part in enumerate(parts)]
    pages = regroup(pages, after=[total])
    caches = [passed(pages[s], "sub", s) for s in range(1, subs)]
    w_output, ready = staged(place, w_output, width, output_order(subs), after=[query])
    mine = fold_pairs(total, parts, after=[ready])
    caches = list(pages[:1]) + list(gate(caches, after=[mine]))
    caches = caches + [passed(part, "section", 1) for part in caches]
    other = passed(mine, "section", 1)

    mixed = attend(
        place, lengths.astype(jnp.int32), query, mine, other, cosine, sine, caches
    )

    mid, end = GROUP_REQUESTS, GROUP_REQUESTS * subs
    first = outputs(mixed, w_output, end + mid, end - mid)
    got_first = passed(first, "section", 1)
    second = outputs(mixed, w_output, end, mid, after=[first])
    got_second = passed(second, "section", 1)
    kept = outputs(mixed, w_output, mid, end - mid, after=[second])
    parts = fold_core(kept, got_first)
    kept = outputs(mixed, w_output, 0, mid, after=parts[:1])
    last = {}
    for half, order in enumerate(HALVES):
        sent = parts[half::2]
        if half:
            sent = gate(sent, after=[got[0], kept])
        got = [passed(part, "sub", s + 1) for s, part in enumerate(sent)]
        last.update(zip(order, fold_sub(order, [kept, got_second], got)))
    parts = [passed(last[s], "req", s) for s in range(1, GROUP_REQUESTS)]
    return finish(gathered[0], last[0], parts).reshape(hidden.shape)


def solution(mesh):
    groups, tp, section = mesh.devices.shape
    finer = Mesh(
        mesh.devices.reshape(groups, GROUP_REQUESTS, tp // GROUP_REQUESTS, section),
        ("groups",) + DEVICES,
    )
    placed = (
        P(None, "groups", DEVICES),
        P(),
        P(None, DEVICES),
        P(DEVICES, None),
        P(DEVICES, None),
        P(("groups",) + DEVICES, None, None),
        P(("groups",) + DEVICES, None),
        P("groups"),
        P("groups", None),
    )
    return jax.shard_map(
        shards,
        mesh=finer,
        in_specs=placed,
        out_specs=P(None, "groups", DEVICES),
        check_vma=False,
    )
```

```python
import functools

import jax
import jax.numpy as jnp
from jax import lax
from jax.experimental import pallas as pl
from jax.experimental.pallas import tpu as pltpu
from jax.sharding import Mesh
from jax.sharding import PartitionSpec as P

QUERY_HEADS = 64
KEY_VALUE_HEADS = 8
HEAD_SIZE = 128
GROUP_REQUESTS = 4
SAMPLES = 8
PAGE_TOKENS = 16
STEPS = 2
ROWS = STEPS * SAMPLES
PAIR = 2 * HEAD_SIZE
LANES = 128
TAIL = 16
HALVES = ((2, 3), (0, 1))
DEVICES = ("req", "sub", "section")

theta_base = 500000.0
eps_norm = 1e-05
VMEM = 16 * 2**20
LARGE_VMEM = 51 * 2**20


def params(**more):
    return pltpu.CompilerParams(vmem_limit_bytes=VMEM, **more)


def cost(*groups, flops=0):
    size = sum(array.size * array.dtype.itemsize for arrays in groups for array in arrays)
    return pl.CostEstimate(flops=flops, bytes_accessed=size, transcendentals=0)


def unread(arrays):
    return [pl.BlockSpec(memory_space=pl.ANY)] * len(arrays)


def turn(vectors, cosine, sine):
    return vectors * cosine + pltpu.roll(vectors, HEAD_SIZE // 2, vectors.ndim - 1) * sine


def stage_kernel(order, count, place, block_ref, *refs):
    out_ref, token_ref, *outs, sems = refs[-3 - count :]
    width = out_ref.shape[2]
    copies = [
        pltpu.make_async_copy(refs[i], outs[i], sems.at[len(order) + i]) for i in range(count)
    ]
    for i, block in enumerate(order):
        columns = pl.ds(pl.multiple_of(block(place) * width, width), width)
        copies.append(pltpu.make_async_copy(block_ref.at[:, columns], out_ref.at[i], sems.at[i]))
    for copy in copies:
        copy.start()
    token_ref[...] = jnp.zeros_like(token_ref)
    for copy in copies:
        copy.wait()


def staged(place, array, width, order, more=(), after=(), limit=VMEM):
    rows, count = array.shape[0], len(order)
    return pl.pallas_call(
        functools.partial(stage_kernel, order, len(more)),
        in_specs=[pl.BlockSpec(memory_space=pltpu.SMEM)]
        + [pl.BlockSpec(memory_space=pltpu.HBM)] * (1 + len(more))
        + unread(after),
        out_specs=[pl.BlockSpec(memory_space=pltpu.VMEM)] * (2 + len(more)),
        out_shape=[
            jax.ShapeDtypeStruct((count, rows, width), array.dtype),
            jax.ShapeDtypeStruct((8, LANES), jnp.float32),
        ]
        + [jax.ShapeDtypeStruct(other.shape, other.dtype) for other in more],
        scratch_shapes=[pltpu.SemaphoreType.DMA((count + len(more),))],
        compiler_params=pltpu.CompilerParams(vmem_limit_bytes=limit),
        cost_estimate=cost([array], [array]),
        name="staged",
    )(place, array, *more, *after)


def pair_order(subs):
    return [
        lambda place, j=j, z=z: 2 * (place[0] ^ z) + (place[1] ^ j) // (subs // 2)
        for j in range(subs)
        for z in range(GROUP_REQUESTS)
    ]


def output_order(subs):
    return [
        lambda place, c=c, j=j, z=z: ((place[0] ^ z) * subs + (place[1] ^ j)) * 2 + (place[2] ^ c)
        for c in range(2)
        for j in range(subs)
        for z in range(GROUP_REQUESTS)
    ]


def gate_kernel(*refs):
    pass


def gate(arrays, after):
    count = len(arrays)
    return pl.pallas_call(
        gate_kernel,
        in_specs=[pl.BlockSpec(memory_space=pl.ANY)] * count + unread(after),
        out_specs=[pl.BlockSpec(memory_space=pl.ANY)] * count,
        out_shape=[jax.ShapeDtypeStruct(array.shape, array.dtype) for array in arrays],
        input_output_aliases={i: i for i in range(count)},
        compiler_params=params(),
        name="gate",
    )(*arrays, *after)


def pages_kernel(table, place, scales, page_ref, rows_ref, rows_out_ref, *out_refs):
    e = pl.program_id(0)
    rows_out_ref[...] = rows_ref[...]
    subs = out_refs[0].shape[0]
    targets = 2 * subs
    page = table[place[0], e * targets + place[1]] - place[2]
    for z, out_ref in enumerate(out_refs):
        for j in range(subs):
            half = (place[1] // 2 ^ j) // (subs // 2)
            head = 2 * (place[0] ^ z) + half
            for part in range(2):
                c = head * 2 + part
                columns = pl.ds(pl.multiple_of(c * HEAD_SIZE, HEAD_SIZE), HEAD_SIZE)
                block = page_ref[0, :, columns].astype(jnp.float32)
                out_ref[j, :, part * HEAD_SIZE : (part + 1) * HEAD_SIZE] = (
                    block * scales[page, c]
                ).astype(jnp.bfloat16)


def used_pages(pages, scales, table, place, subs, rows):
    targets = 2 * subs
    entries = table.shape[1] // targets
    shape = jax.ShapeDtypeStruct((subs, entries * PAGE_TOKENS, PAIR), jnp.bfloat16)
    return pl.pallas_call(
        pages_kernel,
        grid_spec=pltpu.PrefetchScalarGridSpec(
            num_scalar_prefetch=3,
            grid=(entries,),
            in_specs=[
                pl.BlockSpec(
                    (1, PAGE_TOKENS, pages.shape[2]),
                    lambda e, table, place, scales: (
                        table[place[0], e * targets + place[1]] - place[2],
                        0,
                        0,
                    ),
                ),
                pl.BlockSpec(rows.shape, lambda e, *_: (0, 0)),
            ],
            out_specs=[pl.BlockSpec(rows.shape, lambda e, *_: (0, 0))]
            + [pl.BlockSpec((subs, PAGE_TOKENS, PAIR), lambda e, *_: (0, e, 0))]
            * GROUP_REQUESTS,
        ),
        out_shape=[jax.ShapeDtypeStruct(rows.shape, rows.dtype)] + [shape] * GROUP_REQUESTS,
        compiler_params=params(),
        cost_estimate=pl.CostEstimate(
            flops=0, bytes_accessed=4 * entries * PAGE_TOKENS * pages.shape[2], transcendentals=0
        ),
        name="used_pages",
    )(table, place, scales.astype(jnp.float32), pages, rows)


def regroup_kernel(*refs):
    ins, outs = refs[:GROUP_REQUESTS], refs[-refs[0].shape[0] :]
    for j, out_ref in enumerate(outs):
        for z, ref in enumerate(ins):
            out_ref[z] = ref[j]


def regroup(parts, after=()):
    subs = parts[0].shape[0]
    shape = jax.ShapeDtypeStruct((len(parts),) + parts[0].shape[1:], parts[0].dtype)
    return pl.pallas_call(
        regroup_kernel,
        in_specs=[pl.BlockSpec(memory_space=pltpu.VMEM)] * len(parts) + unread(after),
        out_specs=[pl.BlockSpec(memory_space=pltpu.VMEM)] * subs,
        out_shape=[shape] * subs,
        compiler_params=params(),
        cost_estimate=cost(parts, parts),
        name="regroup",
    )(*parts, *after)


def pack_kernel(*refs):
    for i in range(refs[-1].shape[0]):
        refs[-1][i] = refs[i][...]


def pack(parts):
    return pl.pallas_call(
        pack_kernel,
        in_specs=[pl.BlockSpec(memory_space=pltpu.VMEM)] * len(parts),
        out_specs=pl.BlockSpec(memory_space=pltpu.VMEM),
        out_shape=jax.ShapeDtypeStruct((len(parts),) + parts[0].shape, parts[0].dtype),
        compiler_params=params(),
        cost_estimate=cost(parts, parts),
        name="pack",
    )(*parts)


def blocks_of(place, refs):
    request, sub, core = place[0], place[1], place[2]
    subs = len(refs) // 2
    for i, ref in enumerate(refs):
        from_core = core if i < subs else 1 - core
        for z in range(GROUP_REQUESTS):
            yield ref, z, ((request ^ z) * subs + (sub ^ i % subs)) * 2 + from_core


def pairs_kernel(place, gain_ref, weight_ref, *refs):
    subs = (len(refs) - 1) // 3
    x_refs, scale_ref, kept_ref, out_refs = (
        refs[: 2 * subs],
        refs[2 * subs],
        refs[2 * subs + 1],
        refs[2 * subs + 2 :],
    )
    request, sub, core = place[0], place[1], place[2]
    _, rows, width = x_refs[0].shape
    total = jnp.zeros((rows, LANES), jnp.float32)
    for ref in x_refs:
        for z in range(GROUP_REQUESTS):
            for piece in pieces_of(ref[z].astype(jnp.float32)):
                total += piece * piece
    mean = jnp.sum(total, axis=-1, keepdims=True) / (2 * subs * GROUP_REQUESTS * width)
    scale = lax.rsqrt(mean + eps_norm)
    scale_ref[...] = jnp.broadcast_to(scale, scale_ref.shape)
    device = (request * subs + sub) * 2 + core
    x = x_refs[0][0].astype(jnp.float32)
    mine = (x * scale * gain_ref[device]).astype(jnp.bfloat16)
    for shift in range(subs):
        pieces = []
        for z in range(GROUP_REQUESTS):
            block = weight_ref[shift * GROUP_REQUESTS + z]
            part = jnp.dot(mine, block, preferred_element_type=jnp.float32)
            if shift == 0:
                kept_ref[z] = part
            pieces += pieces_of(part)
        if shift:
            encode(out_refs[shift - 1], pieces)


def scale_and_pairs(place, gain, weight, gathered):
    subs = len(gathered) // 2
    count = gathered[0].shape[1]
    sent = jax.ShapeDtypeStruct((2 * GROUP_REQUESTS * count + TAIL, LANES), jnp.int16)
    shapes = [
        jax.ShapeDtypeStruct((count, LANES), jnp.float32),
        jax.ShapeDtypeStruct((GROUP_REQUESTS, count, PAIR), jnp.float32),
    ] + [sent] * (subs - 1)
    return pl.pallas_call(
        pairs_kernel,
        in_specs=[pl.BlockSpec(memory_space=pltpu.SMEM)]
        + [pl.BlockSpec(memory_space=pltpu.VMEM)] * (2 + len(gathered)),
        out_specs=[pl.BlockSpec(memory_space=pltpu.VMEM)] * len(shapes),
        out_shape=shapes,
        compiler_params=params(),
        cost_estimate=cost(gathered, [weight], flops=2 * count * weight.size),
        name="scale_and_pairs",
    )(place, gain, weight, *gathered)


def query_kernel(place, scale_ref, gain_ref, weight_ref, cos_ref, sin_ref, *refs):
    x_refs, out_ref, held, sems = refs[:-3], refs[-3], refs[-2], refs[-1]
    _, rows, width = x_refs[0].shape
    columns = weight_ref.shape[1]
    blocks = list(blocks_of(place, x_refs))
    copies = []
    for i, (_, _, block) in enumerate(blocks):
        depth = pl.ds(pl.multiple_of(block * width, width), width)
        copies.append(pltpu.make_async_copy(weight_ref.at[depth], held.at[i], sems.at[i]))
    for copy in copies:
        copy.start()
    scale = scale_ref[:, :1]
    total = jnp.zeros((rows, columns), jnp.float32)
    for i, (ref, z, block) in enumerate(blocks):
        x = ref[z].astype(jnp.float32)
        x = (x * scale * gain_ref[block]).astype(jnp.bfloat16)
        copies[i].wait()
        total += jnp.dot(x, held[i], preferred_element_type=jnp.float32)
    for head in range(columns // HEAD_SIZE):
        part = slice(head * HEAD_SIZE, (head + 1) * HEAD_SIZE)
        turned = turn(total[:, part], cos_ref[...], sin_ref[...])
        for r in range(GROUP_REQUESTS):
            first, second = r * SAMPLES, (GROUP_REQUESTS + r) * SAMPLES
            out_ref[r, :, part] = jnp.concatenate(
                [turned[first : first + SAMPLES], turned[second : second + SAMPLES]], axis=0
            ).astype(jnp.bfloat16)


def queries(place, scale, gain, weight, cosine, sine, gathered):
    columns = weight.shape[1]
    _, rows, width = gathered[0].shape
    blocks = weight.shape[0] // width
    return pl.pallas_call(
        query_kernel,
        in_specs=[pl.BlockSpec(memory_space=pltpu.SMEM)]
        + [pl.BlockSpec(memory_space=pltpu.VMEM)] * 2
        + [pl.BlockSpec(memory_space=pltpu.HBM)]
        + [pl.BlockSpec(memory_space=pltpu.VMEM)] * (2 + len(gathered)),
        out_specs=pl.BlockSpec(memory_space=pltpu.VMEM),
        out_shape=jax.ShapeDtypeStruct((GROUP_REQUESTS, ROWS, columns), jnp.bfloat16),
        scratch_shapes=[
            pltpu.VMEM((blocks, width, columns), jnp.bfloat16),
            pltpu.SemaphoreType.DMA((blocks,)),
        ],
        compiler_params=pltpu.CompilerParams(vmem_limit_bytes=LARGE_VMEM),
        cost_estimate=cost([weight], flops=2 * rows * weight.size),
        name="queries",
    )(place, scale, gain, weight, cosine, sine, *gathered)


def attend_kernel(place, lengths, q_ref, mine_ref, other_ref, cos_ref, sin_ref, *refs):
    caches, out_ref, key_ref, value_ref = refs[:-3], refs[-3], refs[-2], refs[-1]
    request, sub, core = place[0], place[1], place[2]
    subs, span = len(caches) // 2, caches[0].shape[1]
    targets = 2 * subs
    tokens = targets * span
    quarter = q_ref.shape[2] // HEAD_SIZE
    pair = mine_ref[...] + other_ref[...]
    key_ref[...] = turn(pair[:, :HEAD_SIZE], cos_ref[...], sin_ref[...])
    value_ref[...] = pair[:, HEAD_SIZE:]
    column = lax.broadcasted_iota(jnp.int32, (1, tokens), 1)
    source, inside = column // span, column % span
    from_core = jnp.where(source < subs, core, 1 - core)
    from_sub = sub ^ source % subs
    entry = inside // PAGE_TOKENS * targets + from_sub * 2 + from_core
    position = entry * PAGE_TOKENS + inside % PAGE_TOKENS
    count = quarter * ROWS
    row = lax.broadcasted_iota(jnp.int32, (count, ROWS), 0) % ROWS
    other = lax.broadcasted_iota(jnp.int32, (count, ROWS), 1)
    own_visible = (row % SAMPLES == other % SAMPLES) & (other // SAMPLES <= row // SAMPLES)
    factor = HEAD_SIZE ** (-0.5)
    contract = (((1,), (1,)), ((), ()))
    for z in range(GROUP_REQUESTS):
        r = request ^ z
        fresh = [
            pl.ds(pl.multiple_of((step * GROUP_REQUESTS + r) * SAMPLES, SAMPLES), SAMPLES)
            for step in range(STEPS)
        ]
        new_key = jnp.concatenate([key_ref[rows] for rows in fresh], axis=0)
        new_value = jnp.concatenate([value_ref[rows] for rows in fresh], axis=0)
        new_key, new_value = new_key.astype(jnp.bfloat16), new_value.astype(jnp.bfloat16)
        keys = jnp.concatenate([ref[z, :, :HEAD_SIZE] for ref in caches], axis=0)
        values = jnp.concatenate([ref[z, :, HEAD_SIZE:] for ref in caches], axis=0)
        query = jnp.concatenate(
            [q_ref[r, :, h * HEAD_SIZE : (h + 1) * HEAD_SIZE] for h in range(quarter)], axis=0
        )
        scores = lax.dot_general(query, keys, contract, preferred_element_type=jnp.float32)
        scores = jnp.where(position < lengths[r], scores * factor, -jnp.inf)
        own = lax.dot_general(query, new_key, contract, preferred_element_type=jnp.float32)
        own = jnp.where(own_visible, own * factor, -jnp.inf)
        highest = jnp.maximum(
            jnp.max(scores, axis=-1, keepdims=True), jnp.max(own, axis=-1, keepdims=True)
        )
        scores = jnp.exp(scores - highest)
        own = jnp.exp(own - highest)
        total = jnp.sum(scores, axis=-1, keepdims=True) + jnp.sum(own, axis=-1, keepdims=True)
        mixed = jnp.dot(
            (scores / total).astype(jnp.bfloat16), values, preferred_element_type=jnp.float32
        ) + jnp.dot(
            (own / total).astype(jnp.bfloat16), new_value, preferred_element_type=jnp.float32
        )
        mixed = mixed.astype(jnp.bfloat16)
        for h in range(quarter):
            out_ref[r, :, h * HEAD_SIZE : (h + 1) * HEAD_SIZE] = mixed[
                h * ROWS : (h + 1) * ROWS
            ]


def attend(place, lengths, query, mine, other, cosine, sine, caches):
    return pl.pallas_call(
        attend_kernel,
        in_specs=[pl.BlockSpec(memory_space=pltpu.SMEM)] * 2
        + [pl.BlockSpec(memory_space=pltpu.VMEM)] * (5 + len(caches)),
        out_specs=pl.BlockSpec(memory_space=pltpu.VMEM),
        out_shape=jax.ShapeDtypeStruct(query.shape, jnp.bfloat16),
        scratch_shapes=[pltpu.VMEM(cosine.shape, jnp.float32)] * 2,
        compiler_params=params(),
        cost_estimate=cost(caches, caches, caches, flops=2**28),
        name="attend",
    )(place, lengths, query, mine, other, cosine, sine, *caches)


def output_kernel(first, x_ref, weight_ref, *refs):
    out_ref = refs[-1]
    blocks, rows, width = out_ref.shape
    x = x_ref[...].reshape(rows, -1)
    for i in range(blocks):
        part = jnp.dot(x, weight_ref[first + i], preferred_element_type=jnp.float32)
        for r in range(GROUP_REQUESTS):
            for step in range(STEPS):
                source = r * ROWS + step * SAMPLES
                target = (step * GROUP_REQUESTS + r) * SAMPLES
                out_ref[i, target : target + SAMPLES] = part[source : source + SAMPLES]


def outputs(mixed, weight, first, blocks, after=()):
    rows, width = GROUP_REQUESTS * ROWS, weight.shape[2]
    return pl.pallas_call(
        functools.partial(output_kernel, first),
        in_specs=[pl.BlockSpec(memory_space=pltpu.VMEM)] * 2 + unread(after),
        out_specs=pl.BlockSpec(memory_space=pltpu.VMEM),
        out_shape=jax.ShapeDtypeStruct((blocks, rows, width), jnp.float32),
        compiler_params=params(),
        cost_estimate=cost([mixed], flops=2 * rows * mixed.shape[2] * blocks * width),
        name="outputs",
    )(mixed, weight, *after)


def pieces_of(block):
    return [block[:, c : c + LANES] for c in range(0, block.shape[1], LANES)]


def encode(out_ref, pieces):
    rows = pieces[0].shape[0]
    peak = jnp.abs(pieces[0])
    for piece in pieces[1:]:
        peak = jnp.maximum(peak, jnp.abs(piece))
    peak = jnp.maximum(jnp.max(peak, axis=0, keepdims=True), 1e-30)
    exponent = jnp.floor(jnp.log2(peak)) - 14.0
    inverse = jnp.exp2(-exponent)
    for i, piece in enumerate(pieces):
        code = jnp.clip(jnp.floor(piece * inverse + 0.5), -32767.0, 32767.0)
        out_ref[i * rows : (i + 1) * rows] = code.astype(jnp.int32).astype(jnp.int16)
    out_ref[len(pieces) * rows :] = (
        jnp.broadcast_to(exponent, (TAIL, LANES)).astype(jnp.int32).astype(jnp.int16)
    )


def step_of(ref):
    tail = ref[ref.shape[0] - TAIL :].astype(jnp.int32).astype(jnp.float32)
    return jnp.exp2(tail[:1])


def decoded(ref, first, rows, step):
    return ref[pl.ds(first, rows)].astype(jnp.int32).astype(jnp.float32) * step


def fold_core_kernel(mine_ref, got_ref, *out_refs):
    for i, out_ref in enumerate(out_refs):
        pieces = []
        for z in HALVES[i % 2]:
            block = i // 2 * GROUP_REQUESTS + z
            pieces += pieces_of(mine_ref[block] + got_ref[block])
        encode(out_ref, pieces)


def fold_core(mine, got):
    blocks, rows, width = mine.shape
    count = 2 * (blocks // GROUP_REQUESTS)
    sent = jax.ShapeDtypeStruct((2 * width // LANES * rows + TAIL, LANES), jnp.int16)
    return pl.pallas_call(
        fold_core_kernel,
        in_specs=[pl.BlockSpec(memory_space=pltpu.VMEM)] * 2,
        out_specs=[pl.BlockSpec(memory_space=pltpu.VMEM)] * count,
        out_shape=[sent] * count,
        compiler_params=params(),
        cost_estimate=cost([mine, got]),
        name="fold_core",
    )(mine, got)


def fold_sub_kernel(order, count, own, *refs):
    own_refs, in_refs, out_refs = refs[:own], refs[own : own + count], refs[-len(order) :]
    _, rows, width = own_refs[0].shape
    steps = [step_of(ref) for ref in in_refs]
    for i, (z, out_ref) in enumerate(zip(order, out_refs)):
        block = own_refs[0][z]
        for ref in own_refs[1:]:
            block = block + ref[z]
        pieces = pieces_of(block)
        for c in range(len(pieces)):
            for ref, step in zip(in_refs, steps):
                first = (i * len(pieces) + c) * rows
                pieces[c] = pieces[c] + decoded(ref, first, rows, step)
        if z:
            encode(out_ref, pieces)
        else:
            for c, piece in enumerate(pieces):
                out_ref[:, c * LANES : (c + 1) * LANES] = piece


def fold_sub(order, own, parts, after=()):
    _, rows, width = own[0].shape
    total = jax.ShapeDtypeStruct((rows, width), jnp.float32)
    sent = jax.ShapeDtypeStruct((width // LANES * rows + TAIL, LANES), jnp.int16)
    return pl.pallas_call(
        functools.partial(fold_sub_kernel, order, len(parts), len(own)),
        in_specs=[pl.BlockSpec(memory_space=pltpu.VMEM)] * (len(own) + len(parts))
        + unread(after),
        out_specs=[pl.BlockSpec(memory_space=pltpu.VMEM)] * len(order),
        out_shape=[sent if z else total for z in order],
        compiler_params=params(),
        cost_estimate=cost(own, parts),
        name="fold_sub",
    )(*own, *parts, *after)


def fold_pairs_kernel(count, total_ref, *refs):
    rows = total_ref.shape[0]
    refs, out_ref = refs[:count], refs[-1]
    steps = [step_of(ref) for ref in refs]
    for c in range(total_ref.shape[1] // LANES):
        part = slice(c * LANES, (c + 1) * LANES)
        total = total_ref[:, part]
        for ref, step in zip(refs, steps):
            total = total + decoded(ref, c * rows, rows, step)
        out_ref[:, part] = total


def fold_pairs(total, parts, after=()):
    return pl.pallas_call(
        functools.partial(fold_pairs_kernel, len(parts)),
        in_specs=[pl.BlockSpec(memory_space=pltpu.VMEM)] * (1 + len(parts)) + unread(after),
        out_specs=pl.BlockSpec(memory_space=pltpu.VMEM),
        out_shape=jax.ShapeDtypeStruct(total.shape, jnp.float32),
        compiler_params=params(),
        cost_estimate=cost([total], parts),
        name="fold_pairs",
    )(total, *parts, *after)


def finish_kernel(rows_ref, total_ref, *refs):
    rows = total_ref.shape[0]
    steps = [step_of(ref) for ref in refs[:-1]]
    for c in range(total_ref.shape[1] // LANES):
        part = slice(c * LANES, (c + 1) * LANES)
        total = total_ref[:, part]
        for ref, step in zip(refs[:-1], steps):
            total = total + decoded(ref, c * rows, rows, step)
        refs[-1][:, part] = (total + rows_ref[0, :, part].astype(jnp.float32)).astype(
            jnp.bfloat16
        )


def finish(rows, total, parts):
    return pl.pallas_call(
        finish_kernel,
        in_specs=[pl.BlockSpec(memory_space=pltpu.VMEM)] * (2 + len(parts)),
        out_specs=pl.BlockSpec(memory_space=pltpu.VMEM),
        out_shape=jax.ShapeDtypeStruct(total.shape, jnp.bfloat16),
        compiler_params=params(),
        cost_estimate=cost([total], parts),
        name="finish",
    )(rows, total, *parts)


def passed(array, axis, shift):
    return lax.ppermute(array, axis, [(i, i ^ shift) for i in range(lax.axis_size(axis))])


def scalars(*values):
    return jnp.stack([jnp.asarray(value, jnp.int32) for value in values])


def shards(
    hidden,
    norm_gain,
    w_query,
    key_value_weight,
    w_output,
    prompt_cache_pages,
    per_page_scales,
    lengths,
    block_table,
):
    devices = lax.axis_size(DEVICES)
    subs = lax.axis_size("sub")
    device = lax.axis_index(DEVICES)
    request = lax.axis_index("req")
    sub = lax.axis_index("sub")
    core = lax.axis_index("section")
    width = hidden.shape[2]
    place = scalars(request, sub, core)

    rows = hidden.reshape(GROUP_REQUESTS * ROWS, width)
    column = [passed(rows, "req", s) for s in range(1, GROUP_REQUESTS)]
    where = scalars(request, sub * 2 + core, device * prompt_cache_pages.shape[0])
    rows, *pages = used_pages(
        prompt_cache_pages, per_page_scales, block_table, where, subs, rows
    )
    column = pack([rows] + column)
    gathered = [passed(column, "sub", s) for s in range(1, subs)]
    pages[1:] = gate(pages[1:], after=[column])
    pages[1:] = [passed(pages[s], "req", s) for s in range(1, GROUP_REQUESTS)]
    key_value_weight, ready, gain = staged(
        place,
        key_value_weight,
        PAIR,
        pair_order(subs),
        more=[norm_gain.reshape(devices, 1, width)],
        after=[column],
        limit=LARGE_VMEM,
    )
    gathered = [column] + list(gate(gathered, after=[ready, pages[1]]))
    gathered = gathered + [passed(part, "section", 1) for part in gathered]

    half = HEAD_SIZE // 2
    freqs = jnp.exp(
        -jnp.log(theta_base) * jnp.arange(half, dtype=jnp.float32) * (2.0 / HEAD_SIZE)
    )
    positions = (lengths[None, :] + jnp.arange(STEPS)[:, None]).astype(jnp.float32)
    angles = positions[..., None] * freqs
    cosine, sine = jnp.cos(angles), jnp.sin(angles)
    cosine = jnp.repeat(jnp.concatenate([cosine, cosine], axis=-1)[:, :, None], SAMPLES, axis=2)
    sine = jnp.repeat(jnp.concatenate([-sine, sine], axis=-1)[:, :, None], SAMPLES, axis=2)
    cosine = cosine.reshape(-1, HEAD_SIZE)
    sine = sine.reshape(-1, HEAD_SIZE)

    scale, kept, *parts = scale_and_pairs(place, gain, key_value_weight, gathered)
    parts = [passed(part, "sub", s + 1) for s, part in enumerate(parts)]
    query = queries(place, scale, gain, w_query, cosine, sine, gathered)
    total, *parts = fold_sub((0, 1, 2, 3), [kept], parts, after=[query])
    parts = [passed(part, "req", s + 1) for s, part in enumerate(parts)]
    pages = regroup(pages, after=[total])
    caches = [passed(pages[s], "sub", s) for s in range(1, subs)]
    w_output, ready = staged(place, w_output, width, output_order(subs), after=[query])
    mine = fold_pairs(total, parts, after=[ready])
    caches = list(pages[:1]) + list(gate(caches, after=[mine]))
    caches = caches + [passed(part, "section", 1) for part in caches]
    other = passed(mine, "section", 1)

    mixed = attend(
        place, lengths.astype(jnp.int32), query, mine, other, cosine, sine, caches
    )

    mid, end = GROUP_REQUESTS, GROUP_REQUESTS * subs
    first = outputs(mixed, w_output, end + mid, end - mid)
    got_first = passed(first, "section", 1)
    second = outputs(mixed, w_output, end, mid, after=[first])
    got_second = passed(second, "section", 1)
    kept = outputs(mixed, w_output, mid, end - mid, after=[second])
    parts = fold_core(kept, got_first)
    kept = outputs(mixed, w_output, 0, mid, after=parts[:1])
    last = {}
    for half, order in enumerate(HALVES):
        sent = parts[half::2]
        if half:
            sent = gate(sent, after=[got[0], kept])
        got = [passed(part, "sub", s + 1) for s, part in enumerate(sent)]
        last.update(zip(order, fold_sub(order, [kept, got_second], got)))
    parts = [passed(last[s], "req", s) for s in range(1, GROUP_REQUESTS)]
    return finish(gathered[0], last[0], parts).reshape(hidden.shape)


def solution(mesh):
    groups, tp, section = mesh.devices.shape
    finer = Mesh(
        mesh.devices.reshape(groups, GROUP_REQUESTS, tp // GROUP_REQUESTS, section),
        ("groups",) + DEVICES,
    )
    placed = (
        P(None, "groups", DEVICES),
        P(),
        P(None, DEVICES),
        P(DEVICES, None),
        P(DEVICES, None),
        P(("groups",) + DEVICES, None, None),
        P(("groups",) + DEVICES, None),
        P("groups"),
        P("groups", None),
    )
    return jax.shard_map(
        shards,
        mesh=finer,
        in_specs=placed,
        out_specs=P(None, "groups", DEVICES),
        check_vma=False,
    )
```

```python
import functools

import jax
import jax.numpy as jnp
from jax import lax
from jax.experimental import pallas as pl
from jax.experimental.pallas import tpu as pltpu
from jax.sharding import Mesh
from jax.sharding import PartitionSpec as P

QUERY_HEADS = 64
KEY_VALUE_HEADS = 8
HEAD_SIZE = 128
GROUP_REQUESTS = 4
SAMPLES = 8
PAGE_TOKENS = 16
STEPS = 2
ROWS = STEPS * SAMPLES
PAIR = 2 * HEAD_SIZE
LANES = 128
TAIL = 16
HALVES = ((2, 3), (0, 1))
DEVICES = ("req", "sub", "section")

theta_base = 500000.0
eps_norm = 1e-05
VMEM = 16 * 2**20
LARGE_VMEM = 51 * 2**20


def params(**more):
    return pltpu.CompilerParams(vmem_limit_bytes=VMEM, **more)


def cost(*groups, flops=0):
    size = sum(array.size * array.dtype.itemsize for arrays in groups for array in arrays)
    return pl.CostEstimate(flops=flops, bytes_accessed=size, transcendentals=0)


def unread(arrays):
    return [pl.BlockSpec(memory_space=pl.ANY)] * len(arrays)


def turn(vectors, cosine, sine):
    return vectors * cosine + pltpu.roll(vectors, HEAD_SIZE // 2, vectors.ndim - 1) * sine


def stage_kernel(order, count, place, block_ref, *refs):
    out_ref, token_ref, *outs, sems = refs[-3 - count :]
    width = out_ref.shape[2]
    copies = [
        pltpu.make_async_copy(refs[i], outs[i], sems.at[len(order) + i]) for i in range(count)
    ]
    for i, block in enumerate(order):
        columns = pl.ds(pl.multiple_of(block(place) * width, width), width)
        copies.append(pltpu.make_async_copy(block_ref.at[:, columns], out_ref.at[i], sems.at[i]))
    for copy in copies:
        copy.start()
    token_ref[...] = jnp.zeros_like(token_ref)
    for copy in copies:
        copy.wait()


def staged(place, array, width, order, more=(), after=(), limit=VMEM):
    rows, count = array.shape[0], len(order)
    return pl.pallas_call(
        functools.partial(stage_kernel, order, len(more)),
        in_specs=[pl.BlockSpec(memory_space=pltpu.SMEM)]
        + [pl.BlockSpec(memory_space=pltpu.HBM)] * (1 + len(more))
        + unread(after),
        out_specs=[pl.BlockSpec(memory_space=pltpu.VMEM)] * (2 + len(more)),
        out_shape=[
            jax.ShapeDtypeStruct((count, rows, width), array.dtype),
            jax.ShapeDtypeStruct((8, LANES), jnp.float32),
        ]
        + [jax.ShapeDtypeStruct(other.shape, other.dtype) for other in more],
        scratch_shapes=[pltpu.SemaphoreType.DMA((count + len(more),))],
        compiler_params=pltpu.CompilerParams(vmem_limit_bytes=limit),
        cost_estimate=cost([array], [array]),
        name="staged",
    )(place, array, *more, *after)


def pair_order(subs):
    return [
        lambda place, j=j, z=z: 2 * (place[0] ^ z) + (place[1] ^ j) // (subs // 2)
        for j in range(subs)
        for z in range(GROUP_REQUESTS)
    ]


def output_order(subs):
    return [
        lambda place, c=c, j=j, z=z: ((place[0] ^ z) * subs + (place[1] ^ j)) * 2 + (place[2] ^ c)
        for c in range(2)
        for j in range(subs)
        for z in range(GROUP_REQUESTS)
    ]


def gate_kernel(*refs):
    pass


def gate(arrays, after):
    count = len(arrays)
    return pl.pallas_call(
        gate_kernel,
        in_specs=[pl.BlockSpec(memory_space=pl.ANY)] * count + unread(after),
        out_specs=[pl.BlockSpec(memory_space=pl.ANY)] * count,
        out_shape=[jax.ShapeDtypeStruct(array.shape, array.dtype) for array in arrays],
        input_output_aliases={i: i for i in range(count)},
        compiler_params=params(),
        name="gate",
    )(*arrays, *after)


def pages_kernel(table, place, scales, page_ref, rows_ref, rows_out_ref, *out_refs):
    e = pl.program_id(0)
    rows_out_ref[...] = rows_ref[...]
    subs = out_refs[0].shape[0]
    targets = 2 * subs
    page = table[place[0], e * targets + place[1]] - place[2]
    for z, out_ref in enumerate(out_refs):
        for j in range(subs):
            half = (place[1] // 2 ^ j) // (subs // 2)
            head = 2 * (place[0] ^ z) + half
            for part in range(2):
                c = head * 2 + part
                columns = pl.ds(pl.multiple_of(c * HEAD_SIZE, HEAD_SIZE), HEAD_SIZE)
                block = page_ref[0, :, columns].astype(jnp.float32)
                out_ref[j, :, part * HEAD_SIZE : (part + 1) * HEAD_SIZE] = (
                    block * scales[page, c]
                ).astype(jnp.bfloat16)


def used_pages(pages, scales, table, place, subs, rows):
    targets = 2 * subs
    entries = table.shape[1] // targets
    shape = jax.ShapeDtypeStruct((subs, entries * PAGE_TOKENS, PAIR), jnp.bfloat16)
    return pl.pallas_call(
        pages_kernel,
        grid_spec=pltpu.PrefetchScalarGridSpec(
            num_scalar_prefetch=3,
            grid=(entries,),
            in_specs=[
                pl.BlockSpec(
                    (1, PAGE_TOKENS, pages.shape[2]),
                    lambda e, table, place, scales: (
                        table[place[0], e * targets + place[1]] - place[2],
                        0,
                        0,
                    ),
                ),
                pl.BlockSpec(rows.shape, lambda e, *_: (0, 0)),
            ],
            out_specs=[pl.BlockSpec(rows.shape, lambda e, *_: (0, 0))]
            + [pl.BlockSpec((subs, PAGE_TOKENS, PAIR), lambda e, *_: (0, e, 0))]
            * GROUP_REQUESTS,
        ),
        out_shape=[jax.ShapeDtypeStruct(rows.shape, rows.dtype)] + [shape] * GROUP_REQUESTS,
        compiler_params=params(),
        cost_estimate=pl.CostEstimate(
            flops=0, bytes_accessed=4 * entries * PAGE_TOKENS * pages.shape[2], transcendentals=0
        ),
        name="used_pages",
    )(table, place, scales.astype(jnp.float32), pages, rows)


def regroup_kernel(*refs):
    ins, outs = refs[:GROUP_REQUESTS], refs[-refs[0].shape[0] :]
    for j, out_ref in enumerate(outs):
        for z, ref in enumerate(ins):
            out_ref[z] = ref[j]


def regroup(parts, after=()):
    subs = parts[0].shape[0]
    shape = jax.ShapeDtypeStruct((len(parts),) + parts[0].shape[1:], parts[0].dtype)
    return pl.pallas_call(
        regroup_kernel,
        in_specs=[pl.BlockSpec(memory_space=pltpu.VMEM)] * len(parts) + unread(after),
        out_specs=[pl.BlockSpec(memory_space=pltpu.VMEM)] * subs,
        out_shape=[shape] * subs,
        compiler_params=params(),
        cost_estimate=cost(parts, parts),
        name="regroup",
    )(*parts, *after)


def pack_kernel(*refs):
    for i in range(refs[-1].shape[0]):
        refs[-1][i] = refs[i][...]


def pack(parts):
    return pl.pallas_call(
        pack_kernel,
        in_specs=[pl.BlockSpec(memory_space=pltpu.VMEM)] * len(parts),
        out_specs=pl.BlockSpec(memory_space=pltpu.VMEM),
        out_shape=jax.ShapeDtypeStruct((len(parts),) + parts[0].shape, parts[0].dtype),
        compiler_params=params(),
        cost_estimate=cost(parts, parts),
        name="pack",
    )(*parts)


def blocks_of(place, refs):
    request, sub, core = place[0], place[1], place[2]
    subs = len(refs) // 2
    for i, ref in enumerate(refs):
        from_core = core if i < subs else 1 - core
        for z in range(GROUP_REQUESTS):
            yield ref, z, ((request ^ z) * subs + (sub ^ i % subs)) * 2 + from_core


def pairs_kernel(place, gain_ref, weight_ref, *refs):
    subs = (len(refs) - 1) // 3
    x_refs, scale_ref, kept_ref, out_refs = (
        refs[: 2 * subs],
        refs[2 * subs],
        refs[2 * subs + 1],
        refs[2 * subs + 2 :],
    )
    request, sub, core = place[0], place[1], place[2]
    _, rows, width = x_refs[0].shape
    total = jnp.zeros((rows, LANES), jnp.float32)
    for ref in x_refs:
        for z in range(GROUP_REQUESTS):
            for piece in pieces_of(ref[z].astype(jnp.float32)):
                total += piece * piece
    mean = jnp.sum(total, axis=-1, keepdims=True) / (2 * subs * GROUP_REQUESTS * width)
    scale = lax.rsqrt(mean + eps_norm)
    scale_ref[...] = jnp.broadcast_to(scale, scale_ref.shape)
    device = (request * subs + sub) * 2 + core
    x = x_refs[0][0].astype(jnp.float32)
    mine = (x * scale * gain_ref[device]).astype(jnp.bfloat16)
    for shift in range(subs):
        pieces = []
        for z in range(GROUP_REQUESTS):
            block = weight_ref[shift * GROUP_REQUESTS + z]
            part = jnp.dot(mine, block, preferred_element_type=jnp.float32)
            if shift == 0:
                kept_ref[z] = part
            pieces += pieces_of(part)
        if shift:
            encode(out_refs[shift - 1], pieces)


def scale_and_pairs(place, gain, weight, gathered):
    subs = len(gathered) // 2
    count = gathered[0].shape[1]
    sent = jax.ShapeDtypeStruct((2 * GROUP_REQUESTS * count + TAIL, LANES), jnp.int16)
    shapes = [
        jax.ShapeDtypeStruct((count, LANES), jnp.float32),
        jax.ShapeDtypeStruct((GROUP_REQUESTS, count, PAIR), jnp.float32),
    ] + [sent] * (subs - 1)
    return pl.pallas_call(
        pairs_kernel,
        in_specs=[pl.BlockSpec(memory_space=pltpu.SMEM)]
        + [pl.BlockSpec(memory_space=pltpu.VMEM)] * (2 + len(gathered)),
        out_specs=[pl.BlockSpec(memory_space=pltpu.VMEM)] * len(shapes),
        out_shape=shapes,
        compiler_params=params(),
        cost_estimate=cost(gathered, [weight], flops=2 * count * weight.size),
        name="scale_and_pairs",
    )(place, gain, weight, *gathered)


def query_kernel(place, scale_ref, gain_ref, weight_ref, cos_ref, sin_ref, *refs):
    x_refs, out_ref, held, sems = refs[:-3], refs[-3], refs[-2], refs[-1]
    _, rows, width = x_refs[0].shape
    columns = weight_ref.shape[1]
    blocks = list(blocks_of(place, x_refs))
    copies = []
    for i, (_, _, block) in enumerate(blocks):
        depth = pl.ds(pl.multiple_of(block * width, width), width)
        copies.append(pltpu.make_async_copy(weight_ref.at[depth], held.at[i], sems.at[i]))
    for copy in copies:
        copy.start()
    scale = scale_ref[:, :1]
    total = jnp.zeros((rows, columns), jnp.float32)
    for i, (ref, z, block) in enumerate(blocks):
        x = ref[z].astype(jnp.float32)
        x = (x * scale * gain_ref[block]).astype(jnp.bfloat16)
        copies[i].wait()
        total += jnp.dot(x, held[i], preferred_element_type=jnp.float32)
    for head in range(columns // HEAD_SIZE):
        part = slice(head * HEAD_SIZE, (head + 1) * HEAD_SIZE)
        turned = turn(total[:, part], cos_ref[...], sin_ref[...])
        for r in range(GROUP_REQUESTS):
            first, second = r * SAMPLES, (GROUP_REQUESTS + r) * SAMPLES
            out_ref[r, :, part] = jnp.concatenate(
                [turned[first : first + SAMPLES], turned[second : second + SAMPLES]], axis=0
            ).astype(jnp.bfloat16)


def queries(place, scale, gain, weight, cosine, sine, gathered):
    columns = weight.shape[1]
    _, rows, width = gathered[0].shape
    blocks = weight.shape[0] // width
    return pl.pallas_call(
        query_kernel,
        in_specs=[pl.BlockSpec(memory_space=pltpu.SMEM)]
        + [pl.BlockSpec(memory_space=pltpu.VMEM)] * 2
        + [pl.BlockSpec(memory_space=pltpu.HBM)]
        + [pl.BlockSpec(memory_space=pltpu.VMEM)] * (2 + len(gathered)),
        out_specs=pl.BlockSpec(memory_space=pltpu.VMEM),
        out_shape=jax.ShapeDtypeStruct((GROUP_REQUESTS, ROWS, columns), jnp.bfloat16),
        scratch_shapes=[
            pltpu.VMEM((blocks, width, columns), jnp.bfloat16),
            pltpu.SemaphoreType.DMA((blocks,)),
        ],
        compiler_params=pltpu.CompilerParams(vmem_limit_bytes=LARGE_VMEM),
        cost_estimate=cost([weight], flops=2 * rows * weight.size),
        name="queries",
    )(place, scale, gain, weight, cosine, sine, *gathered)


def attend_kernel(place, lengths, q_ref, mine_ref, other_ref, cos_ref, sin_ref, *refs):
    caches, out_ref, key_ref, value_ref = refs[:-3], refs[-3], refs[-2], refs[-1]
    request, sub, core = place[0], place[1], place[2]
    subs, span = len(caches) // 2, caches[0].shape[1]
    targets = 2 * subs
    tokens = targets * span
    quarter = q_ref.shape[2] // HEAD_SIZE
    pair = mine_ref[...] + other_ref[...]
    key_ref[...] = turn(pair[:, :HEAD_SIZE], cos_ref[...], sin_ref[...])
    value_ref[...] = pair[:, HEAD_SIZE:]
    column = lax.broadcasted_iota(jnp.int32, (1, tokens), 1)
    source, inside = column // span, column % span
    from_core = jnp.where(source < subs, core, 1 - core)
    from_sub = sub ^ source % subs
    entry = inside // PAGE_TOKENS * targets + from_sub * 2 + from_core
    position = entry * PAGE_TOKENS + inside % PAGE_TOKENS
    count = quarter * ROWS
    row = lax.broadcasted_iota(jnp.int32, (count, ROWS), 0) % ROWS
    other = lax.broadcasted_iota(jnp.int32, (count, ROWS), 1)
    own_visible = (row % SAMPLES == other % SAMPLES) & (other // SAMPLES <= row // SAMPLES)
    factor = HEAD_SIZE ** (-0.5)
    contract = (((1,), (1,)), ((), ()))
    for z in range(GROUP_REQUESTS):
        r = request ^ z
        fresh = [
            pl.ds(pl.multiple_of((step * GROUP_REQUESTS + r) * SAMPLES, SAMPLES), SAMPLES)
            for step in range(STEPS)
        ]
        new_key = jnp.concatenate([key_ref[rows] for rows in fresh], axis=0)
        new_value = jnp.concatenate([value_ref[rows] for rows in fresh], axis=0)
        new_key, new_value = new_key.astype(jnp.bfloat16), new_value.astype(jnp.bfloat16)
        keys = jnp.concatenate([ref[z, :, :HEAD_SIZE] for ref in caches], axis=0)
        values = jnp.concatenate([ref[z, :, HEAD_SIZE:] for ref in caches], axis=0)
        query = jnp.concatenate(
            [q_ref[r, :, h * HEAD_SIZE : (h + 1) * HEAD_SIZE] for h in range(quarter)], axis=0
        )
        scores = lax.dot_general(query, keys, contract, preferred_element_type=jnp.float32)
        scores = jnp.where(position < lengths[r], scores * factor, -jnp.inf)
        own = lax.dot_general(query, new_key, contract, preferred_element_type=jnp.float32)
        own = jnp.where(own_visible, own * factor, -jnp.inf)
        highest = jnp.maximum(
            jnp.max(scores, axis=-1, keepdims=True), jnp.max(own, axis=-1, keepdims=True)
        )
        scores = jnp.exp(scores - highest)
        own = jnp.exp(own - highest)
        total = jnp.sum(scores, axis=-1, keepdims=True) + jnp.sum(own, axis=-1, keepdims=True)
        mixed = jnp.dot(
            (scores / total).astype(jnp.bfloat16), values, preferred_element_type=jnp.float32
        ) + jnp.dot(
            (own / total).astype(jnp.bfloat16), new_value, preferred_element_type=jnp.float32
        )
        mixed = mixed.astype(jnp.bfloat16)
        for h in range(quarter):
            out_ref[r, :, h * HEAD_SIZE : (h + 1) * HEAD_SIZE] = mixed[
                h * ROWS : (h + 1) * ROWS
            ]


def attend(place, lengths, query, mine, other, cosine, sine, caches):
    return pl.pallas_call(
        attend_kernel,
        in_specs=[pl.BlockSpec(memory_space=pltpu.SMEM)] * 2
        + [pl.BlockSpec(memory_space=pltpu.VMEM)] * (5 + len(caches)),
        out_specs=pl.BlockSpec(memory_space=pltpu.VMEM),
        out_shape=jax.ShapeDtypeStruct(query.shape, jnp.bfloat16),
        scratch_shapes=[pltpu.VMEM(cosine.shape, jnp.float32)] * 2,
        compiler_params=params(),
        cost_estimate=cost(caches, caches, caches, flops=2**28),
        name="attend",
    )(place, lengths, query, mine, other, cosine, sine, *caches)


def output_kernel(first, x_ref, weight_ref, *refs):
    out_ref = refs[-1]
    blocks, rows, width = out_ref.shape
    x = x_ref[...].reshape(rows, -1)
    for i in range(blocks):
        part = jnp.dot(x, weight_ref[first + i], preferred_element_type=jnp.float32)
        for r in range(GROUP_REQUESTS):
            for step in range(STEPS):
                source = r * ROWS + step * SAMPLES
                target = (step * GROUP_REQUESTS + r) * SAMPLES
                out_ref[i, target : target + SAMPLES] = part[source : source + SAMPLES]


def outputs(mixed, weight, first, blocks, after=()):
    rows, width = GROUP_REQUESTS * ROWS, weight.shape[2]
    return pl.pallas_call(
        functools.partial(output_kernel, first),
        in_specs=[pl.BlockSpec(memory_space=pltpu.VMEM)] * 2 + unread(after),
        out_specs=pl.BlockSpec(memory_space=pltpu.VMEM),
        out_shape=jax.ShapeDtypeStruct((blocks, rows, width), jnp.float32),
        compiler_params=params(),
        cost_estimate=cost([mixed], flops=2 * rows * mixed.shape[2] * blocks * width),
        name="outputs",
    )(mixed, weight, *after)


def pieces_of(block):
    return [block[:, c : c + LANES] for c in range(0, block.shape[1], LANES)]


def encode(out_ref, pieces):
    rows = pieces[0].shape[0]
    peak = jnp.abs(pieces[0])
    for piece in pieces[1:]:
        peak = jnp.maximum(peak, jnp.abs(piece))
    peak = jnp.maximum(jnp.max(peak, axis=0, keepdims=True), 1e-30)
    exponent = jnp.floor(jnp.log2(peak)) - 14.0
    inverse = jnp.exp2(-exponent)
    for i, piece in enumerate(pieces):
        code = jnp.clip(jnp.floor(piece * inverse + 0.5), -32767.0, 32767.0)
        out_ref[i * rows : (i + 1) * rows] = code.astype(jnp.int32).astype(jnp.int16)
    out_ref[len(pieces) * rows :] = (
        jnp.broadcast_to(exponent, (TAIL, LANES)).astype(jnp.int32).astype(jnp.int16)
    )


def step_of(ref):
    tail = ref[ref.shape[0] - TAIL :].astype(jnp.int32).astype(jnp.float32)
    return jnp.exp2(tail[:1])


def decoded(ref, first, rows, step):
    return ref[pl.ds(first, rows)].astype(jnp.int32).astype(jnp.float32) * step


def fold_core_kernel(mine_ref, got_ref, *out_refs):
    for i, out_ref in enumerate(out_refs):
        pieces = []
        for z in HALVES[i % 2]:
            block = i // 2 * GROUP_REQUESTS + z
            pieces += pieces_of(mine_ref[block] + got_ref[block])
        encode(out_ref, pieces)


def fold_core(mine, got):
    blocks, rows, width = mine.shape
    count = 2 * (blocks // GROUP_REQUESTS)
    sent = jax.ShapeDtypeStruct((2 * width // LANES * rows + TAIL, LANES), jnp.int16)
    return pl.pallas_call(
        fold_core_kernel,
        in_specs=[pl.BlockSpec(memory_space=pltpu.VMEM)] * 2,
        out_specs=[pl.BlockSpec(memory_space=pltpu.VMEM)] * count,
        out_shape=[sent] * count,
        compiler_params=params(),
        cost_estimate=cost([mine, got]),
        name="fold_core",
    )(mine, got)


def fold_sub_kernel(order, count, own, *refs):
    own_refs, in_refs, out_refs = refs[:own], refs[own : own + count], refs[-len(order) :]
    _, rows, width = own_refs[0].shape
    steps = [step_of(ref) for ref in in_refs]
    for i, (z, out_ref) in enumerate(zip(order, out_refs)):
        block = own_refs[0][z]
        for ref in own_refs[1:]:
            block = block + ref[z]
        pieces = pieces_of(block)
        for c in range(len(pieces)):
            for ref, step in zip(in_refs, steps):
                first = (i * len(pieces) + c) * rows
                pieces[c] = pieces[c] + decoded(ref, first, rows, step)
        if z:
            encode(out_ref, pieces)
        else:
            for c, piece in enumerate(pieces):
                out_ref[:, c * LANES : (c + 1) * LANES] = piece


def fold_sub(order, own, parts, after=()):
    _, rows, width = own[0].shape
    total = jax.ShapeDtypeStruct((rows, width), jnp.float32)
    sent = jax.ShapeDtypeStruct((width // LANES * rows + TAIL, LANES), jnp.int16)
    return pl.pallas_call(
        functools.partial(fold_sub_kernel, order, len(parts), len(own)),
        in_specs=[pl.BlockSpec(memory_space=pltpu.VMEM)] * (len(own) + len(parts))
        + unread(after),
        out_specs=[pl.BlockSpec(memory_space=pltpu.VMEM)] * len(order),
        out_shape=[sent if z else total for z in order],
        compiler_params=params(),
        cost_estimate=cost(own, parts),
        name="fold_sub",
    )(*own, *parts, *after)


def fold_pairs_kernel(count, total_ref, *refs):
    rows = total_ref.shape[0]
    refs, out_ref = refs[:count], refs[-1]
    steps = [step_of(ref) for ref in refs]
    for c in range(total_ref.shape[1] // LANES):
        part = slice(c * LANES, (c + 1) * LANES)
        total = total_ref[:, part]
        for ref, step in zip(refs, steps):
            total = total + decoded(ref, c * rows, rows, step)
        out_ref[:, part] = total


def fold_pairs(total, parts, after=()):
    return pl.pallas_call(
        functools.partial(fold_pairs_kernel, len(parts)),
        in_specs=[pl.BlockSpec(memory_space=pltpu.VMEM)] * (1 + len(parts)) + unread(after),
        out_specs=pl.BlockSpec(memory_space=pltpu.VMEM),
        out_shape=jax.ShapeDtypeStruct(total.shape, jnp.float32),
        compiler_params=params(),
        cost_estimate=cost([total], parts),
        name="fold_pairs",
    )(total, *parts, *after)


def finish_kernel(rows_ref, total_ref, *refs):
    rows = total_ref.shape[0]
    steps = [step_of(ref) for ref in refs[:-1]]
    for c in range(total_ref.shape[1] // LANES):
        part = slice(c * LANES, (c + 1) * LANES)
        total = total_ref[:, part]
        for ref, step in zip(refs[:-1], steps):
            total = total + decoded(ref, c * rows, rows, step)
        refs[-1][:, part] = (total + rows_ref[0, :, part].astype(jnp.float32)).astype(
            jnp.bfloat16
        )


def finish(rows, total, parts):
    return pl.pallas_call(
        finish_kernel,
        in_specs=[pl.BlockSpec(memory_space=pltpu.VMEM)] * (2 + len(parts)),
        out_specs=pl.BlockSpec(memory_space=pltpu.VMEM),
        out_shape=jax.ShapeDtypeStruct(total.shape, jnp.bfloat16),
        compiler_params=params(),
        cost_estimate=cost([total], parts),
        name="finish",
    )(rows, total, *parts)


def passed(array, axis, shift):
    return lax.ppermute(array, axis, [(i, i ^ shift) for i in range(lax.axis_size(axis))])


def scalars(*values):
    return jnp.stack([jnp.asarray(value, jnp.int32) for value in values])


def shards(
    hidden,
    norm_gain,
    w_query,
    key_value_weight,
    w_output,
    prompt_cache_pages,
    per_page_scales,
    lengths,
    block_table,
):
    devices = lax.axis_size(DEVICES)
    subs = lax.axis_size("sub")
    device = lax.axis_index(DEVICES)
    request = lax.axis_index("req")
    sub = lax.axis_index("sub")
    core = lax.axis_index("section")
    width = hidden.shape[2]
    place = scalars(request, sub, core)

    rows = hidden.reshape(GROUP_REQUESTS * ROWS, width)
    column = [passed(rows, "req", s) for s in range(1, GROUP_REQUESTS)]
    where = scalars(request, sub * 2 + core, device * prompt_cache_pages.shape[0])
    rows, *pages = used_pages(
        prompt_cache_pages, per_page_scales, block_table, where, subs, rows
    )
    column = pack([rows] + column)
    gathered = [passed(column, "sub", s) for s in range(1, subs)]
    pages[3:] = gate(pages[3:], after=[column])
    pages[1:] = [passed(pages[s], "req", s) for s in range(1, GROUP_REQUESTS)]
    key_value_weight, ready, gain = staged(
        place,
        key_value_weight,
        PAIR,
        pair_order(subs),
        more=[norm_gain.reshape(devices, 1, width)],
        after=[column],
        limit=LARGE_VMEM,
    )
    gathered = [column] + list(gate(gathered, after=[ready]))
    gathered = gathered + [passed(part, "section", 1) for part in gathered]

    half = HEAD_SIZE // 2
    freqs = jnp.exp(
        -jnp.log(theta_base) * jnp.arange(half, dtype=jnp.float32) * (2.0 / HEAD_SIZE)
    )
    positions = (lengths[None, :] + jnp.arange(STEPS)[:, None]).astype(jnp.float32)
    angles = positions[..., None] * freqs
    cosine, sine = jnp.cos(angles), jnp.sin(angles)
    cosine = jnp.repeat(jnp.concatenate([cosine, cosine], axis=-1)[:, :, None], SAMPLES, axis=2)
    sine = jnp.repeat(jnp.concatenate([-sine, sine], axis=-1)[:, :, None], SAMPLES, axis=2)
    cosine = cosine.reshape(-1, HEAD_SIZE)
    sine = sine.reshape(-1, HEAD_SIZE)

    scale, kept, *parts = scale_and_pairs(place, gain, key_value_weight, gathered)
    parts = [passed(part, "sub", s + 1) for s, part in enumerate(parts)]
    query = queries(place, scale, gain, w_query, cosine, sine, gathered)
    total, *parts = fold_sub((0, 1, 2, 3), [kept], parts, after=[query])
    parts = [passed(part, "req", s + 1) for s, part in enumerate(parts)]
    pages = regroup(pages, after=[total])
    caches = [passed(pages[s], "sub", s) for s in range(1, subs)]
    w_output, ready = staged(place, w_output, width, output_order(subs), after=[query])
    mine = fold_pairs(total, parts, after=[ready])
    caches = list(pages[:1]) + list(gate(caches, after=[mine]))
    caches = caches + [passed(part, "section", 1) for part in caches]
    other = passed(mine, "section", 1)

    mixed = attend(
        place, lengths.astype(jnp.int32), query, mine, other, cosine, sine, caches
    )

    mid, end = GROUP_REQUESTS, GROUP_REQUESTS * subs
    first = outputs(mixed, w_output, end + mid, end - mid)
    got_first = passed(first, "section", 1)
    second = outputs(mixed, w_output, end, mid, after=[first])
    got_second = passed(second, "section", 1)
    kept = outputs(mixed, w_output, mid, end - mid, after=[second])
    parts = fold_core(kept, got_first)
    kept = outputs(mixed, w_output, 0, mid, after=parts[:1])
    last = {}
    for half, order in enumerate(HALVES):
        sent = parts[half::2]
        if half:
            sent = gate(sent, after=[got[0], kept])
        got = [passed(part, "sub", s + 1) for s, part in enumerate(sent)]
        last.update(zip(order, fold_sub(order, [kept, got_second], got)))
    parts = [passed(last[s], "req", s) for s in range(1, GROUP_REQUESTS)]
    return finish(gathered[0], last[0], parts).reshape(hidden.shape)


def solution(mesh):
    groups, tp, section = mesh.devices.shape
    finer = Mesh(
        mesh.devices.reshape(groups, GROUP_REQUESTS, tp // GROUP_REQUESTS, section),
        ("groups",) + DEVICES,
    )
    placed = (
        P(None, "groups", DEVICES),
        P(),
        P(None, DEVICES),
        P(DEVICES, None),
        P(DEVICES, None),
        P(("groups",) + DEVICES, None, None),
        P(("groups",) + DEVICES, None),
        P("groups"),
        P("groups", None),
    )
    return jax.shard_map(
        shards,
        mesh=finer,
        in_specs=placed,
        out_specs=P(None, "groups", DEVICES),
        check_vma=False,
    )
```
